32 devices in a mesh: ctx: 8 (over y, x, core), head: 4 (over z).
Axes of the slice: x: 2, y: 2, z: 4, core: 2. Of those that a mesh axis runs over, the one named last changes fastest.
Arguments:
- hidden_in: bfloat16 [2048, 2048], P('ctx'), may hold values from -6 to 6
- gain_attn: float32 [2048], replicated, may hold values from 0.1 to 1.9
- w_qkv: bfloat16 [2048, 3, 2048], P(None, None, 'head'), may hold values from -0.125 to 0.125
- conv_w: float32 [4, 3, 2048], P(None, None, 'head'), may hold values from -3 to 3
- log_decay: float32 [2048, 16], P('ctx', 'head'), may hold values from -1 to 0, as said below
- norm_gain: float32 [2048], P('head'), may hold values from 0.1 to 1.9
- w_out: bfloat16 [2048, 2048], P('head'), may hold values from -0.125 to 0.125
- gain_moe: float32 [2048], replicated, may hold values from 0.1 to 1.9
- expert_ids: int32 [2048, 8], P('ctx'), may hold values from 0 to 15, all different within a row; in each aligned block of 256 rows (0 to 255, 256 to 511, ...) at most 192 rows name the same one
- route_weights: float32 [2048, 8], P('ctx'), may hold values from 0.05 to 1
- w_gate: bfloat16 [32, 2048, 512], P(('ctx', 'head')), may hold values from -0.125 to 0.125
- w_up: bfloat16 [32, 2048, 512], P(('ctx', 'head')), may hold values from -0.125 to 0.125
- w_down: bfloat16 [32, 512, 2048], P(('ctx', 'head')), may hold values from -0.1875 to 0.1875
- grad_core: bfloat16 [2048, 2048], P('ctx', 'head'), may hold values from -6 to 6
Outputs:
- layer_out: bfloat16 [2048, 2048], P('ctx', 'head')
- grad_q: bfloat16 [2048, 2048], P('ctx', 'head')
- grad_k: bfloat16 [2048, 2048], P('ctx', 'head')
- grad_v: bfloat16 [2048, 2048], P('ctx', 'head')
The draws below stay inside these ranges and needn't reach their ends.
Inputs may be any that keep to these rules, and one draw needn't show every extreme that they name: `expert_ids`: in each aligned block of 256 rows (the tokens of one index of ctx) no expert is chosen by more than 192 rows, a bound that some block reaches; the 8 experts of a row differ. `log_decay`: every entry is negative.
All inputs are finite; a program needn't handle non-finite values.
Results may differ from the reference program's by a relative error of at most 0.023.
Values may be sent and summed in bfloat16 or wider, within the bound.
No kernel may reach another device: no remote copies, remote signals or barrier semaphores. Data moves between devices by JAX's collectives and lax.ppermute only.
A program may use at most 128 MiB of HBM per device.

```python
import math
import jax
import jax.numpy as jnp
import numpy as np
from jax import lax

D = 2048
ATTENDER_NUMBER = 16
DH = 128
HD = 2048
KERNEL = 4
FFE = 1024
TOP = 8
TOK_DEV = 256
SEGMENT_WORDS = 2048
EXPERTS = 16
SHARDS = 2
FF_DEV = 512
CAP = 192
N_CTX = 8


def draw_log_decay(key, part):
    lookup_array = jax.random.split(jax.random.fold_in(key, 7), 6)
    share = 0.5
    quick = jax.random.uniform(lookup_array[0], (ATTENDER_NUMBER,)) < share
    fast = jnp.exp(jax.random.uniform(lookup_array[1], (ATTENDER_NUMBER,), minval=math.log(1.0 / 50.0), maxval=math.log(1.0 / 30.0)))
    slow = jnp.exp(jax.random.uniform(lookup_array[2], (ATTENDER_NUMBER,), minval=math.log(0.1), maxval=math.log(0.5))) / SEGMENT_WORDS
    forgetting_speed = jnp.where(quick, fast, slow)
    multiplier_coefficient = jnp.exp(jax.random.uniform(lookup_array[3], (SEGMENT_WORDS, ATTENDER_NUMBER), minval=math.log(0.5), maxval=math.log(2.0)))
    spurt_extent = jax.random.uniform(lookup_array[4], (SEGMENT_WORDS, ATTENDER_NUMBER)) < 2.0 / SEGMENT_WORDS
    discarded_words = jnp.log(jax.random.uniform(lookup_array[5], (SEGMENT_WORDS, ATTENDER_NUMBER), minval=0.5, maxval=0.8))
    return (-forgetting_speed[None, :] * multiplier_coefficient + jnp.where(spurt_extent, discarded_words, 0.0)).astype(jnp.float32)


def shard_levels(own_key, extent, cuts, least, top_value):
    level, own = 1.0, jax.random.fold_in(own_key, 6)
    for axis_at, blocks in cuts:
        steps = jnp.exp(jax.random.uniform(jax.random.fold_in(own, axis_at), (blocks,), jnp.float32, least / len(cuts), top_value / len(cuts)))
        level = level * jnp.repeat(steps, extent[axis_at] // blocks).reshape([-1 if axis == axis_at else 1 for axis in range(len(extent))])
    return level


def shared_out(stream_key, own, number, rows, amount, top, bound, skew):
    ranking = jax.random.permutation(stream_key, amount)
    packed, ordinary = load_shares(amount, rows * top, bound, skew, True), load_shares(amount, rows * top, bound, skew, False)
    places = jnp.arange(amount)

    def named(sizes, rotation):
        used = int((sizes > 0).sum())
        fixed = max(1, used // 4)
        shifted = fixed + (places - fixed + rotation * (used - fixed)) % max(1, amount - fixed)
        return jnp.zeros((amount,), jnp.int32).at[ranking[jnp.where(places < fixed, places, shifted)]].set(jnp.asarray(sizes, jnp.int32))

    sizes = jnp.where(number % 4 == 0, named(packed, number // 4), named(ordinary, number - number // 4 - 1))
    mixed = jax.random.permutation(jax.random.fold_in(own, 3), amount)
    giver, taker = mixed[0:amount // 2 * 2:2], mixed[1:amount // 2 * 2:2]
    slack = jnp.minimum(sizes[giver] - 1, bound - sizes[taker]) // 2
    slack = jnp.where((giver == ranking[0]) | (taker == ranking[0]) | (sizes[taker] == 0), 0, jnp.maximum(slack, 0))
    shifted = jax.random.randint(jax.random.fold_in(own, 4), (amount // 2,), 0, 1 << 20) % (slack + 1)
    sizes = sizes.at[giver].add(-shifted).at[taker].add(shifted)
    items = jnp.searchsorted(jnp.cumsum(sizes), jnp.arange(rows * top), side="right").astype(jnp.int32)
    table = items.reshape(top, rows).T
    table = table[jax.random.permutation(jax.random.fold_in(own, 1), rows)]
    rotation = jax.random.randint(jax.random.fold_in(own, 2), (rows, 1), 0, top)
    return jnp.take_along_axis(table, (jnp.arange(top)[None, :] + rotation) % top, axis=1)


def load_shares(amount, total, bound, lean, full):
    portions = [(1 << 20) // math.isqrt(standing ** lean) + 1 for standing in range(1, amount + 1)]
    largest = bound if full else min(bound, max(-(-total // amount), total * portions[0] // sum(portions)))
    least = 1 if total - largest >= amount - 1 else 0
    given, spare = [largest] + [least] * (amount - 1), total - largest - least * (amount - 1)
    while spare > 0:
        movable = [i for i in range(1, amount) if given[i] < largest] or [i for i in range(1, amount) if given[i] < bound]
        pool, budget = sum([portions[i] for i in movable]), spare
        for i in movable:
            extra = min(bound - given[i], max(1, budget * portions[i] // pool), spare)
            given[i] = given[i] + extra
            spare = spare - extra
    return np.array(given)


def centred(own_key, extent, width, reach, cuts=(), kind=jnp.bfloat16):
    values = width * jax.random.normal(own_key, extent, jnp.float32)
    if cuts:
        values = values * shard_levels(own_key, extent, cuts, -0.22, 0.18)
    return jnp.clip(values, -reach, reach).astype(kind)


def setup_inputs(seed: int = 0) -> dict:
    splits = jax.random.split(jax.random.key(seed), 15)
    hidden_in = centred(splits[0], (SEGMENT_WORDS, D), 1.0, 6.0, ((0, 8),))
    gain_attn = jnp.clip(1.0 + 0.18 * jax.random.normal(splits[1], (D,), jnp.float32), 0.1, 1.9)
    w_qkv = centred(splits[2], (D, 3, HD), D ** -0.5, 0.125, ((2, 4),))
    conv_w = centred(splits[3], (KERNEL, 3, HD), KERNEL ** -0.5, 3.0, ((2, 4),), jnp.float32)
    log_decay = draw_log_decay(jax.random.fold_in(splits[14], 71), 0)
    norm_gain = jnp.clip(1.0 + 0.18 * jax.random.normal(splits[5], (HD,), jnp.float32), 0.1, 1.9)
    w_out = centred(splits[6], (HD, D), HD ** -0.5, 0.125, ((0, 4),))
    gain_moe = jnp.clip(1.0 + 0.18 * jax.random.normal(splits[7], (D,), jnp.float32), 0.1, 1.9)
    expert_ids_keys = jax.random.split(jax.random.fold_in(splits[8], 1), SEGMENT_WORDS // TOK_DEV)
    expert_ids_turns = jax.random.permutation(jax.random.fold_in(splits[8], 3), SEGMENT_WORDS // TOK_DEV)
    expert_ids = jax.vmap(lambda own, number: shared_out(jax.random.fold_in(splits[8], 2), own, number, TOK_DEV, EXPERTS, TOP, CAP, 2))(expert_ids_keys, expert_ids_turns).reshape((SEGMENT_WORDS, TOP))
    route_weights = jnp.clip(jnp.exp(math.log(1.0) - 2.9957323 * jax.random.uniform(splits[9], (SEGMENT_WORDS, TOP), jnp.float32) ** shard_levels(splits[9], (SEGMENT_WORDS, TOP), ((0, 8),), -0.2, 0.2)), 0.05, 1.0)
    w_gate = centred(splits[10], (EXPERTS * SHARDS, D, FF_DEV), D ** -0.5, 0.125, ((0, 32),))
    w_up = centred(splits[11], (EXPERTS * SHARDS, D, FF_DEV), D ** -0.5, 0.125, ((0, 32),))
    w_down = centred(splits[12], (EXPERTS * SHARDS, FF_DEV, D), FFE ** -0.5, 0.1875, ((0, 32),))
    grad_core = centred(splits[13], (SEGMENT_WORDS, HD), 1.0, 6.0, ((0, 8), (1, 4)))
    return {"hidden_in": hidden_in, "gain_attn": gain_attn, "w_qkv": w_qkv, "conv_w": conv_w, "log_decay": log_decay, "norm_gain": norm_gain, "w_out": w_out, "gain_moe": gain_moe, "expert_ids": expert_ids, "route_weights": route_weights, "w_gate": w_gate, "w_up": w_up, "w_down": w_down, "grad_core": grad_core}


def rms_norm(values, gain):
    return values * lax.rsqrt(lax.optimization_barrier(jnp.mean(values * values, axis=-1, keepdims=True)) + 1e-06) * gain

def short_conv(mixed, conv_w):
    lead = jnp.zeros((KERNEL - 1,) + mixed.shape[1:], jnp.float32)
    padded = jnp.concatenate([lead, mixed.astype(jnp.float32)], axis=0)
    total = jnp.zeros(mixed.shape, jnp.float32)
    for offset in range(KERNEL):
        total = total + conv_w[offset] * padded[KERNEL - 1 - offset:KERNEL - 1 - offset + mixed.shape[0]]
    return total

def linear_core(query_f, key_f, value_f, log_steps):
    blocks = SEGMENT_WORDS // TOK_DEV
    hi = lax.Precision.HIGHEST

    def block_step(state, items):
        q_blk, k_blk, v_blk, g_blk = items
        cum = jnp.cumsum(g_blk, axis=0)
        cum_t = cum.T
        diff = cum_t[:, :, None] - cum_t[:, None, :]
        lower = (jnp.arange(TOK_DEV)[:, None] >= jnp.arange(TOK_DEV)[None, :])[None]
        weights = jnp.where(lower, jnp.exp(jnp.where(lower, diff, 0.0)), 0.0)
        scores = jnp.einsum('thd,shd->hts', q_blk, k_blk, precision=hi) * weights
        local = jnp.einsum('hts,shd->thd', scores, v_blk, precision=hi)
        carried = jnp.einsum('thd,hde->the', q_blk, state, precision=hi) * jnp.exp(cum)[:, :, None]
        tail = jnp.exp(cum[-1][None, :] - cum)
        fresh = jnp.einsum('shd,she->hde', k_blk * tail[:, :, None], v_blk, precision=hi)
        new_state = jnp.exp(cum[-1])[:, None, None] * state + fresh
        return (new_state, local + carried)
    shaped = (blocks, TOK_DEV, ATTENDER_NUMBER, DH)
    items = (query_f.reshape(shaped), key_f.reshape(shaped), value_f.reshape(shaped), log_steps.reshape(blocks, TOK_DEV, ATTENDER_NUMBER))
    _, outs = lax.scan(block_step, jnp.zeros((ATTENDER_NUMBER, DH, DH), jnp.float32), items)
    return outs.reshape(SEGMENT_WORDS, ATTENDER_NUMBER, DH)

def mixture(moe_in, expert_ids, route_weights, w_gate, w_up, w_down):
    hi = lax.Precision.HIGHEST
    ids = expert_ids.reshape(N_CTX, TOK_DEV, TOP)
    hot = (ids[..., None] == jnp.arange(EXPERTS, dtype=jnp.int32)).astype(jnp.int32)
    counts = lax.optimization_barrier(jnp.sum(hot, axis=2))
    ranks = jnp.cumsum(counts, axis=1) - counts
    slot = lax.optimization_barrier(jnp.sum(hot * ranks[:, :, None, :], axis=-1))
    source = jnp.broadcast_to(jnp.arange(N_CTX, dtype=jnp.int32)[:, None, None], ids.shape)
    token = source * TOK_DEV + jnp.broadcast_to(jnp.arange(TOK_DEV, dtype=jnp.int32)[None, :, None], ids.shape)
    position = source * CAP + slot
    tok_table = jnp.full((EXPERTS, N_CTX * CAP), SEGMENT_WORDS, jnp.int32)
    tok_table = tok_table.at[ids.reshape(-1), position.reshape(-1)].set(token.reshape(-1))
    wt_table = jnp.zeros((EXPERTS, N_CTX * CAP), jnp.float32)
    wt_table = wt_table.at[ids.reshape(-1), position.reshape(-1)].set(route_weights.reshape(-1))
    padded_rows = jnp.concatenate([moe_in, jnp.zeros((1, D), jnp.bfloat16)], axis=0)
    gates = w_gate.reshape(EXPERTS, SHARDS, D, FF_DEV)
    ups = w_up.reshape(EXPERTS, SHARDS, D, FF_DEV)
    downs = w_down.reshape(EXPERTS, SHARDS, FF_DEV, D)

    def expert_step(total, items):
        row_index, row_weight, gate_e, up_e, down_e = items
        rows = padded_rows[row_index].astype(jnp.float32)
        summed = jnp.zeros((N_CTX * CAP, D), jnp.float32)
        for shard in range(SHARDS):
            gate_val = jnp.dot(rows, gate_e[shard].astype(jnp.float32), precision=hi)
            up_val = jnp.dot(rows, up_e[shard].astype(jnp.float32), precision=hi)
            inner = (jax.nn.silu(gate_val) * up_val).astype(jnp.bfloat16)
            part = jnp.dot(inner.astype(jnp.float32), down_e[shard].astype(jnp.float32), precision=hi)
            part = lax.optimization_barrier(part.astype(jnp.bfloat16))
            summed = summed + part.astype(jnp.float32)
        total = total.at[row_index].add(row_weight[:, None] * summed)
        return (total, None)
    start = jnp.zeros((SEGMENT_WORDS + 1, D), jnp.float32)
    total, _ = lax.scan(expert_step, start, (tok_table, wt_table, gates, ups, downs))
    return total[:SEGMENT_WORDS]

def reference(hidden_in, gain_attn, w_qkv, conv_w, log_decay, norm_gain, w_out, gain_moe, expert_ids, route_weights, w_gate, w_up, w_down, grad_core):
    x_float = hidden_in.astype(jnp.float32)
    normed = rms_norm(x_float, gain_attn).astype(jnp.bfloat16)
    mixed = jnp.dot(normed, w_qkv.reshape(D, 3 * HD), preferred_element_type=jnp.float32)
    mixed = mixed.astype(jnp.bfloat16).reshape(SEGMENT_WORDS, 3, HD)
    activ = jax.nn.silu(short_conv(mixed, conv_w))
    shape3 = (SEGMENT_WORDS, ATTENDER_NUMBER, DH)
    queries = (activ[:, 0] * DH ** (-0.5)).astype(jnp.bfloat16).astype(jnp.float32).reshape(shape3)
    key_rows = activ[:, 1].astype(jnp.bfloat16).astype(jnp.float32).reshape(shape3)
    val_rows = activ[:, 2].astype(jnp.bfloat16).astype(jnp.float32).reshape(shape3)

    def core_of(query_f, key_f, value_f):
        return linear_core(query_f, key_f, value_f, log_decay)
    attended, pullback = jax.vjp(core_of, queries, key_rows, val_rows)
    grad_q, grad_k, grad_v = pullback(grad_core.astype(jnp.float32).reshape(shape3))
    headed = rms_norm(attended, norm_gain.reshape(ATTENDER_NUMBER, DH)).reshape(SEGMENT_WORDS, HD).astype(jnp.bfloat16)
    resid = x_float + jnp.dot(headed, w_out, preferred_element_type=jnp.float32)
    moe_in = rms_norm(resid, gain_moe).astype(jnp.bfloat16)
    moe_out = mixture(moe_in, expert_ids, route_weights, w_gate, w_up, w_down)
    layer_out = (resid + moe_out).astype(jnp.bfloat16)
    return (layer_out, grad_q.reshape(SEGMENT_WORDS, HD).astype(jnp.bfloat16), grad_k.reshape(SEGMENT_WORDS, HD).astype(jnp.bfloat16), grad_v.reshape(SEGMENT_WORDS, HD).astype(jnp.bfloat16))
```

```python
import functools

import jax
import jax.numpy as jnp
from jax import lax
from jax.experimental import pallas as pl
from jax.experimental.pallas import tpu as pltpu
from jax.sharding import PartitionSpec as P

KERNEL = 4
EXP_CTX = 2
LANES = 128
RIM = 16
VMEM_BYTES = 48 * 1024 * 1024
HI = lax.Precision.HIGHEST
BF = jnp.bfloat16
F32 = jnp.float32
NT = (((1,), (1,)), ((), ()))
TN = (((0,), (0,)), ((), ()))
NN = (((1,), (0,)), ((), ()))


def params():
    return pltpu.CompilerParams(vmem_limit_bytes=VMEM_BYTES)


def mm(a, b, dims=NN):
    return lax.dot_general(a, b, dims, preferred_element_type=F32)


def pick_block(extent, target):
    return target if extent % target == 0 else extent


def qkv_kernel(x_ref, gain_ref, w_ref, mixed_ref, rim_ref, normed_ref):
    @pl.when(pl.program_id(0) == 0)
    def _():
        values = x_ref[...].astype(F32)
        scale = lax.rsqrt(jnp.mean(values * values, axis=-1, keepdims=True) + 1e-06)
        normed_ref[...] = (values * scale * gain_ref[...]).astype(BF)

    out = mm(normed_ref[...], w_ref[0]).astype(BF)
    mixed_ref[0] = out
    rim_ref[0] = out[out.shape[0] - RIM :]


def project(x, gain, weights):
    rows, width = x.shape
    kinds, _, chans = weights.shape
    block = pick_block(chans, 256)
    per = chans // block
    return pl.pallas_call(
        qkv_kernel,
        grid=(kinds * per,),
        in_specs=[
            pl.BlockSpec((rows, width), lambda i: (0, 0)),
            pl.BlockSpec((1, width), lambda i: (0, 0)),
            pl.BlockSpec((1, width, block), lambda i: (i // per, 0, i % per)),
        ],
        out_specs=[
            pl.BlockSpec((1, rows, block), lambda i: (i // per, 0, i % per)),
            pl.BlockSpec((1, RIM, block), lambda i: (i // per, 0, i % per)),
        ],
        out_shape=[
            jax.ShapeDtypeStruct((kinds, rows, chans), BF),
            jax.ShapeDtypeStruct((kinds, RIM, chans), BF),
        ],
        scratch_shapes=[pltpu.VMEM((rows, width), BF)],
        compiler_params=params(),
        name="qkv_projection",
    )(x, gain.reshape(1, width), weights)


def decay_sums(steps):
    rows = steps.shape[1]
    row_at = lax.broadcasted_iota(jnp.int32, (rows, rows), 0)
    col_at = lax.broadcasted_iota(jnp.int32, (rows, rows), 1)
    lower = row_at >= col_at
    tri = jnp.where(lower, 1.0, 0.0).astype(F32)
    along = lax.dot_general(steps, tri, NT, precision=HI, preferred_element_type=F32)
    down = lax.dot_general(tri, steps, NT, precision=HI, preferred_element_type=F32)
    return along, down, lower


def payload_tail(total, size):
    full = jnp.broadcast_to(total, (RIM, size))
    first = full.astype(BF).astype(F32)
    second = (full - first).astype(BF).astype(F32)
    third = full - first - second
    at = lax.broadcasted_iota(jnp.int32, (RIM, size), 0)
    return jnp.where(at == 0, first, jnp.where(at == 1, second, jnp.where(at == 2, third, 0.0)))


def conv_kernel(mixed_ref, rim_ref, taps_ref, steps_ref, cot_ref, qkv_ref, fwd_ref, bwd_ref, pad_ref):
    kinds, rows, chans = mixed_ref.shape
    heads = steps_ref.shape[0]
    size = chans // heads
    along, down, _ = decay_sums(steps_ref[...])
    for kind in range(kinds):
        pad_ref[:RIM] = rim_ref[kind].astype(F32)
        pad_ref[RIM:] = mixed_ref[kind].astype(F32)
        total = taps_ref[kind, 0:1, :] * pad_ref[RIM:]
        for offset in range(1, KERNEL):
            total += taps_ref[kind, offset : offset + 1, :] * pad_ref[RIM - offset : RIM - offset + rows]
        activ = total * jax.nn.sigmoid(total)
        if kind == 0:
            activ = activ * size ** (-0.5)
        qkv_ref[kind] = activ.astype(BF)
    for head in range(heads):
        at = slice(head * size, (head + 1) * size)
        last = along[head : head + 1, rows - 1 : rows]
        lead = jnp.exp(down[:, head : head + 1])
        tail = jnp.exp(last - down[:, head : head + 1])
        key_out = (qkv_ref[1, :, at].astype(F32) * tail).astype(BF)
        query_out = (qkv_ref[0, :, at].astype(F32) * lead).astype(BF)
        ends = payload_tail(last, size).astype(BF)
        fwd_ref[head, :size] = mm(key_out, qkv_ref[2, :, at], TN).astype(BF)
        fwd_ref[head, size:] = ends
        bwd_ref[head, :size] = mm(query_out, cot_ref[:, at], TN).astype(BF)
        bwd_ref[head, size:] = ends


def local_states(mixed, rim, taps, steps, cot):
    kinds, rows, chans = mixed.shape
    heads = steps.shape[0]
    size = chans // heads
    state = jax.ShapeDtypeStruct((heads, size + RIM, size), BF)
    return pl.pallas_call(
        conv_kernel,
        out_shape=[jax.ShapeDtypeStruct((kinds, rows, chans), BF), state, state],
        scratch_shapes=[pltpu.VMEM((rows + RIM, chans), F32)],
        compiler_params=params(),
        name="conv_states",
    )(mixed, rim, taps, steps, cot)


def entering(states_ref, head, size, first, last, step):
    def hop(count, total):
        at = first + count * step
        ends = states_ref[at, head, size:, :].astype(F32)
        factor = jnp.exp(ends[0:1] + ends[1:2] + ends[2:3])
        return factor * total + states_ref[at, head, :size, :].astype(F32)

    return lax.fori_loop(0, (last - first) * step, hop, jnp.zeros((size, size), F32))


def core_kernel(me_ref, qkv_ref, steps_ref, states_ref, gain_ref, w_ref, out_ref, headed_ref):
    _, rows, chans = qkv_ref.shape
    heads = steps_ref.shape[0]
    size = chans // heads
    along, down, lower = decay_sums(steps_ref[...])
    for head in range(heads):
        at = slice(head * size, (head + 1) * size)
        state = entering(states_ref, head, size, 0, me_ref[0], 1).astype(BF)
        diff = down[:, head : head + 1] - along[head : head + 1, :]
        mask = jnp.exp(jnp.where(lower, diff, -jnp.inf))
        query = qkv_ref[0, :, at]
        scores = (mm(query, qkv_ref[1, :, at], NT) * mask).astype(BF)
        attended = mm(scores, qkv_ref[2, :, at])
        attended += mm(query, state) * jnp.exp(down[:, head : head + 1])
        scale = lax.rsqrt(jnp.mean(attended * attended, axis=-1, keepdims=True) + 1e-06)
        headed_ref[:, at] = (attended * scale * gain_ref[:, at]).astype(BF)
    out_ref[...] = mm(headed_ref[...], w_ref[...]).astype(BF)


def core_out(me, qkv, steps, states, gain, w_out):
    _, rows, chans = qkv.shape
    vmem = pl.BlockSpec(memory_space=pltpu.VMEM)
    return pl.pallas_call(
        core_kernel,
        in_specs=[pl.BlockSpec(memory_space=pltpu.SMEM)] + [vmem] * 5,
        out_shape=jax.ShapeDtypeStruct((rows, w_out.shape[1]), BF),
        scratch_shapes=[pltpu.VMEM((rows, chans), BF)],
        compiler_params=params(),
        name="core_out",
    )(me, qkv, steps, states, gain.reshape(1, chans), w_out)


def grad_kernel(count, me_ref, qkv_ref, cot_ref, steps_ref, fwd_ref, bwd_ref, gq_ref, gk_ref, gv_ref):
    _, rows, chans = qkv_ref.shape
    heads = steps_ref.shape[0]
    size = chans // heads
    along, down, lower = decay_sums(steps_ref[...])
    for head in range(heads):
        at = slice(head * size, (head + 1) * size)
        state = entering(fwd_ref, head, size, 0, me_ref[0], 1).astype(BF)
        after = entering(bwd_ref, head, size, count - 1, me_ref[0], -1).astype(BF)
        here = down[:, head : head + 1]
        lead = jnp.exp(here)
        tail = jnp.exp(along[head : head + 1, rows - 1 : rows] - here)
        mask = jnp.exp(jnp.where(lower, here - along[head : head + 1, :], -jnp.inf))
        query, key, val = qkv_ref[0, :, at], qkv_ref[1, :, at], qkv_ref[2, :, at]
        cot = cot_ref[:, at]
        scores = (mm(query, key, NT) * mask).astype(BF)
        dov = (mm(cot, val, NT) * mask).astype(BF)
        gq_ref[:, at] = (mm(dov, key) + lead * mm(cot, state, NT)).astype(BF)
        gk_ref[:, at] = (mm(dov, query, TN) + tail * mm(val, after, NT)).astype(BF)
        gv_ref[:, at] = (mm(scores, cot, TN) + tail * mm(key, after)).astype(BF)


def core_grads(count, me, qkv, cot, steps, fwd, bwd):
    _, rows, chans = qkv.shape
    vmem = pl.BlockSpec(memory_space=pltpu.VMEM)
    return pl.pallas_call(
        functools.partial(grad_kernel, count),
        in_specs=[pl.BlockSpec(memory_space=pltpu.SMEM)] + [vmem] * 5,
        out_shape=[jax.ShapeDtypeStruct((rows, chans), BF)] * 3,
        compiler_params=params(),
        name="core_grads",
    )(me, qkv, cot, steps, fwd, bwd)


def norm_kernel(head_ref, x_ref, attn_ref, gain_ref, routes_ref, out_ref):
    rows, width = attn_ref.shape
    start = pl.multiple_of(head_ref[0] * rows, rows)
    resid = x_ref[pl.ds(start, rows), :].astype(F32) + attn_ref[...].astype(F32)
    scale = lax.rsqrt(jnp.mean(resid * resid, axis=-1, keepdims=True) + 1e-06)
    out_ref[:, :width] = (resid * scale * gain_ref[...]).astype(BF)
    out_ref[:, width:] = routes_ref[pl.ds(start, rows), :]


def norm_rows(my_head, x, attn, gain, routes):
    rows, width = attn.shape
    vmem = pl.BlockSpec(memory_space=pltpu.VMEM)
    return pl.pallas_call(
        norm_kernel,
        in_specs=[pl.BlockSpec(memory_space=pltpu.SMEM)] + [vmem] * 4,
        out_shape=jax.ShapeDtypeStruct((rows, width + routes.shape[1]), BF),
        compiler_params=params(),
        name="moe_norm",
    )(my_head, x, attn, gain.reshape(1, width), routes)


def expert_kernel(experts, where_ref, rows_ref, gate_ref, up_ref, down_ref, attn_ref, out_ref):
    _, blocks, rows, cols = out_ref.shape
    width = blocks * cols
    part = attn_ref.shape[0]
    tokens = rows_ref[:, :width]
    routes = rows_ref[:, width:].astype(F32)
    lane = lax.broadcasted_iota(jnp.int32, routes.shape, 1)
    mine = (lane == where_ref[2]) | (lane == where_ref[2] + experts) | (lane == where_ref[2] + 2 * experts)
    weight = jnp.sum(jnp.where(mine, routes, 0.0), axis=1, keepdims=True)
    gate = mm(tokens, gate_ref[0])
    inner = (gate * jax.nn.sigmoid(gate) * mm(tokens, up_ref[0])).astype(BF)
    for block in range(blocks):
        at = slice(block * cols, (block + 1) * cols)
        out_ref[0, block] = (mm(inner, down_ref[0, :, at]) * weight).astype(BF)

    @pl.when(pl.program_id(0) == where_ref[0])
    def _():
        start = pl.multiple_of(where_ref[1] * part, part)
        for block in range(blocks):
            at = slice(block * cols, (block + 1) * cols)
            mine = out_ref[0, block, pl.ds(start, part), :].astype(F32)
            out_ref[0, block, pl.ds(start, part), :] = (mine + attn_ref[:, at].astype(F32)).astype(BF)


def expert_pieces(experts, where, rows, gate, up, down, attn, n_ctx, n_head):
    total, padded = rows.shape
    width = gate.shape[1]
    hidden = gate.shape[2]
    tok, cols = total // n_ctx, width // n_head
    once = pl.Buffered(1)
    return pl.pallas_call(
        functools.partial(expert_kernel, experts),
        grid=(n_ctx,),
        in_specs=[
            pl.BlockSpec(memory_space=pltpu.SMEM),
            pl.BlockSpec((tok, padded), lambda i: (i, 0)),
            pl.BlockSpec((1, width, hidden), lambda i: (0, 0, 0), pipeline_mode=once),
            pl.BlockSpec((1, width, hidden), lambda i: (0, 0, 0), pipeline_mode=once),
            pl.BlockSpec((1, hidden, width), lambda i: (0, 0, 0), pipeline_mode=once),
            pl.BlockSpec(attn.shape, lambda i: (0, 0), pipeline_mode=once),
        ],
        out_specs=pl.BlockSpec((1, n_head, tok, cols), lambda i: (i, 0, 0, 0)),
        out_shape=jax.ShapeDtypeStruct((n_ctx, n_head, tok, cols), BF),
        compiler_params=params(),
        name="expert_pieces",
    )(where, rows, gate, up, down, attn)


def route_table(expert_ids, route_weights, experts):
    hot = expert_ids[:, :, None] == jnp.arange(experts, dtype=jnp.int32)
    table = jnp.sum(jnp.where(hot, route_weights[:, :, None], 0.0), axis=1)
    first = table.astype(BF)
    left = table - first.astype(F32)
    second = left.astype(BF)
    third = (left - second.astype(F32)).astype(BF)
    joined = jnp.concatenate([first, second, third], axis=1)
    return jnp.pad(joined, ((0, 0), (0, -joined.shape[1] % LANES)))


def body(
    hidden_in,
    gain_attn,
    w_qkv,
    conv_w,
    log_decay,
    norm_gain,
    w_out,
    gain_moe,
    expert_ids,
    route_weights,
    w_gate,
    w_up,
    w_down,
    grad_core,
):
    n_ctx, n_head = lax.axis_size("ctx"), lax.axis_size("head")
    my_ctx, my_head = lax.axis_index("ctx"), lax.axis_index("head")
    tok_dev, width = hidden_in.shape
    experts = EXP_CTX * n_ctx
    shards = n_head // EXP_CTX
    cols = width // n_head
    me = my_ctx.astype(jnp.int32).reshape(1)
    head_at = my_head.astype(jnp.int32).reshape(1)
    routes = route_table(expert_ids, route_weights, experts)
    steps = log_decay.T

    mixed, rim = project(hidden_in, gain_attn, jnp.transpose(w_qkv, (1, 0, 2)))
    rim = lax.ppermute(rim, "ctx", [(at, at + 1) for at in range(n_ctx - 1)])
    qkv, fwd, bwd = local_states(mixed, rim, jnp.transpose(conv_w, (1, 0, 2)), steps, grad_core)
    fwd = lax.all_gather(fwd, "ctx")
    bwd = lax.all_gather(bwd, "ctx")
    partial = core_out(me, qkv, steps, fwd, norm_gain, w_out)
    attn = lax.psum_scatter(partial, "head", scatter_dimension=0, tiled=True)
    packed = norm_rows(head_at, hidden_in, attn, gain_moe, routes)
    rows = lax.all_gather(packed, ("ctx", "head"), tiled=True)
    where = jnp.stack([my_ctx, my_head, EXP_CTX * my_ctx + my_head // shards]).astype(jnp.int32)
    pieces = expert_pieces(experts, where, rows, w_gate, w_up, w_down, attn, n_ctx, n_head)
    moe = lax.psum_scatter(
        pieces.reshape(n_ctx * n_head, tok_dev, cols), ("ctx", "head"), scatter_dimension=0, tiled=True
    )
    grads = core_grads(n_ctx, me, qkv, grad_core, steps, fwd, bwd)
    own = lax.dynamic_slice_in_dim(hidden_in, my_head * cols, cols, 1)
    layer_out = (own.astype(F32) + moe[0].astype(F32)).astype(BF)
    return (layer_out, *grads)


def solution(mesh):
    in_specs = (
        P("ctx", None),
        P(),
        P(None, None, "head"),
        P(None, None, "head"),
        P("ctx", "head"),
        P("head"),
        P("head", None),
        P(),
        P("ctx", None),
        P("ctx", None),
        P(("ctx", "head"), None, None),
        P(("ctx", "head"), None, None),
        P(("ctx", "head"), None, None),
        P("ctx", "head"),
    )
    out_specs = (P("ctx", "head"), P("ctx", "head"), P("ctx", "head"), P("ctx", "head"))
    return jax.shard_map(body, mesh=mesh, in_specs=in_specs, out_specs=out_specs, check_vma=False)
```

```python
import functools

import jax
import jax.numpy as jnp
from jax import lax
from jax.experimental import pallas as pl
from jax.experimental.pallas import tpu as pltpu
from jax.sharding import PartitionSpec as P

KERNEL = 4
EXP_CTX = 2
LANES = 128
RIM = 16
MIB = 1024 * 1024
HI = lax.Precision.HIGHEST
BF = jnp.bfloat16
F32 = jnp.float32
NT = (((1,), (1,)), ((), ()))
TN = (((0,), (0,)), ((), ()))
NN = (((1,), (0,)), ((), ()))


def params(mib):
    return pltpu.CompilerParams(vmem_limit_bytes=mib * MIB)


def mm(a, b, dims=NN):
    return lax.dot_general(a, b, dims, preferred_element_type=F32)


def pick_block(extent, target):
    return target if extent % target == 0 else extent


def qkv_kernel(x_ref, gain_ref, w_ref, mixed_ref, rim_ref, normed_ref):
    @pl.when(pl.program_id(0) == 0)
    def _():
        values = x_ref[...].astype(F32)
        scale = lax.rsqrt(jnp.mean(values * values, axis=-1, keepdims=True) + 1e-06)
        normed_ref[...] = (values * scale * gain_ref[...]).astype(BF)

    out = mm(normed_ref[...], w_ref[0]).astype(BF)
    mixed_ref[0] = out
    rim_ref[0] = out[out.shape[0] - RIM :]


def project(x, gain, weights):
    rows, width = x.shape
    kinds, _, chans = weights.shape
    block = pick_block(chans, 256)
    per = chans // block
    return pl.pallas_call(
        qkv_kernel,
        grid=(kinds * per,),
        in_specs=[
            pl.BlockSpec((rows, width), lambda i: (0, 0)),
            pl.BlockSpec((1, width), lambda i: (0, 0)),
            pl.BlockSpec((1, width, block), lambda i: (i // per, 0, i % per)),
        ],
        out_specs=[
            pl.BlockSpec((1, rows, block), lambda i: (i // per, 0, i % per)),
            pl.BlockSpec((1, RIM, block), lambda i: (i // per, 0, i % per)),
        ],
        out_shape=[
            jax.ShapeDtypeStruct((kinds, rows, chans), BF),
            jax.ShapeDtypeStruct((kinds, RIM, chans), BF),
        ],
        scratch_shapes=[pltpu.VMEM((rows, width), BF)],
        compiler_params=params(12),
        name="qkv_projection",
    )(x, gain.reshape(1, width), weights)


def decay_sums(steps):
    rows = steps.shape[1]
    row_at = lax.broadcasted_iota(jnp.int32, (rows, rows), 0)
    col_at = lax.broadcasted_iota(jnp.int32, (rows, rows), 1)
    lower = row_at >= col_at
    tri = jnp.where(lower, 1.0, 0.0).astype(F32)
    along = lax.dot_general(steps, tri, NT, precision=HI, preferred_element_type=F32)
    down = lax.dot_general(tri, steps, NT, precision=HI, preferred_element_type=F32)
    return along, down, lower


def payload_tail(total, size):
    full = jnp.broadcast_to(total, (RIM, size))
    first = full.astype(BF).astype(F32)
    second = (full - first).astype(BF).astype(F32)
    third = full - first - second
    at = lax.broadcasted_iota(jnp.int32, (RIM, size), 0)
    return jnp.where(at == 0, first, jnp.where(at == 1, second, jnp.where(at == 2, third, 0.0)))


def conv_kernel(mixed_ref, rim_ref, taps_ref, steps_ref, cot_ref, qkv_ref, fwd_ref, bwd_ref, pad_ref):
    kinds, rows, chans = mixed_ref.shape
    heads = steps_ref.shape[0]
    size = chans // heads
    along, down, _ = decay_sums(steps_ref[...])
    for kind in range(kinds):
        pad_ref[:RIM] = rim_ref[kind].astype(F32)
        pad_ref[RIM:] = mixed_ref[kind].astype(F32)
        total = taps_ref[kind, 0:1, :] * pad_ref[RIM:]
        for offset in range(1, KERNEL):
            total += taps_ref[kind, offset : offset + 1, :] * pad_ref[RIM - offset : RIM - offset + rows]
        activ = total * jax.nn.sigmoid(total)
        if kind == 0:
            activ = activ * size ** (-0.5)
        qkv_ref[kind] = activ.astype(BF)
    for head in range(heads):
        at = slice(head * size, (head + 1) * size)
        last = along[head : head + 1, rows - 1 : rows]
        lead = jnp.exp(down[:, head : head + 1])
        tail = jnp.exp(last - down[:, head : head + 1])
        key_out = (qkv_ref[1, :, at].astype(F32) * tail).astype(BF)
        query_out = (qkv_ref[0, :, at].astype(F32) * lead).astype(BF)
        ends = payload_tail(last, size).astype(BF)
        fwd_ref[head, :size] = mm(key_out, qkv_ref[2, :, at], TN).astype(BF)
        fwd_ref[head, size:] = ends
        bwd_ref[head, :size] = mm(query_out, cot_ref[:, at], TN).astype(BF)
        bwd_ref[head, size:] = ends


def local_states(mixed, rim, taps, steps, cot):
    kinds, rows, chans = mixed.shape
    heads = steps.shape[0]
    size = chans // heads
    state = jax.ShapeDtypeStruct((heads, size + RIM, size), BF)
    return pl.pallas_call(
        conv_kernel,
        out_shape=[jax.ShapeDtypeStruct((kinds, rows, chans), BF), state, state],
        scratch_shapes=[pltpu.VMEM((rows + RIM, chans), F32)],
        compiler_params=params(12),
        name="conv_states",
    )(mixed, rim, taps, steps, cot)


def arrange(me_ref, state_refs, held_ref):
    for at, ref in enumerate(state_refs):
        held_ref[me_ref[0] ^ at] = ref[...]


def entering(held_ref, head, size, first, last, step):
    def hop(count, total):
        at = first + count * step
        ends = held_ref[at, head, size:, :].astype(F32)
        factor = jnp.exp(ends[0:1] + ends[1:2] + ends[2:3])
        return factor * total + held_ref[at, head, :size, :].astype(F32)

    return lax.fori_loop(0, (last - first) * step, hop, jnp.zeros((size, size), F32))


def core_kernel(count, me_ref, qkv_ref, steps_ref, gain_ref, w_ref, *refs):
    state_refs, (out_ref, headed_ref, held_ref) = refs[:count], refs[count:]
    _, rows, chans = qkv_ref.shape
    heads = steps_ref.shape[0]
    size = chans // heads
    arrange(me_ref, state_refs, held_ref)
    along, down, lower = decay_sums(steps_ref[...])
    for head in range(heads):
        at = slice(head * size, (head + 1) * size)
        state = entering(held_ref, head, size, 0, me_ref[0], 1).astype(BF)
        diff = down[:, head : head + 1] - along[head : head + 1, :]
        mask = jnp.exp(jnp.where(lower, diff, -jnp.inf))
        query = qkv_ref[0, :, at]
        scores = (mm(query, qkv_ref[1, :, at], NT) * mask).astype(BF)
        attended = mm(scores, qkv_ref[2, :, at])
        attended += mm(query, state) * jnp.exp(down[:, head : head + 1])
        scale = lax.rsqrt(jnp.mean(attended * attended, axis=-1, keepdims=True) + 1e-06)
        headed_ref[:, at] = (attended * scale * gain_ref[:, at]).astype(BF)
    out_ref[...] = mm(headed_ref[...], w_ref[...]).astype(BF)


def core_out(me, qkv, steps, states, gain, w_out):
    _, rows, chans = qkv.shape
    count = len(states)
    vmem = pl.BlockSpec(memory_space=pltpu.VMEM)
    return pl.pallas_call(
        functools.partial(core_kernel, count),
        in_specs=[pl.BlockSpec(memory_space=pltpu.SMEM)] + [vmem] * (4 + count),
        out_shape=jax.ShapeDtypeStruct((rows, w_out.shape[1]), BF),
        scratch_shapes=[pltpu.VMEM((rows, chans), BF), pltpu.VMEM((count, *states[0].shape), BF)],
        compiler_params=params(16),
        name="core_out",
    )(me, qkv, steps, gain.reshape(1, chans), w_out, *states)


def grad_kernel(count, me_ref, qkv_ref, cot_ref, steps_ref, *refs):
    fwd_refs, bwd_refs = refs[:count], refs[count : 2 * count]
    gq_ref, gk_ref, gv_ref, fwd_ref, bwd_ref = refs[2 * count :]
    _, rows, chans = qkv_ref.shape
    heads = steps_ref.shape[0]
    size = chans // heads
    arrange(me_ref, fwd_refs, fwd_ref)
    arrange(me_ref, bwd_refs, bwd_ref)
    along, down, lower = decay_sums(steps_ref[...])
    for head in range(heads):
        at = slice(head * size, (head + 1) * size)
        state = entering(fwd_ref, head, size, 0, me_ref[0], 1).astype(BF)
        after = entering(bwd_ref, head, size, count - 1, me_ref[0], -1).astype(BF)
        here = down[:, head : head + 1]
        lead = jnp.exp(here)
        tail = jnp.exp(along[head : head + 1, rows - 1 : rows] - here)
        mask = jnp.exp(jnp.where(lower, here - along[head : head + 1, :], -jnp.inf))
        query, key, val = qkv_ref[0, :, at], qkv_ref[1, :, at], qkv_ref[2, :, at]
        cot = cot_ref[:, at]
        scores = (mm(query, key, NT) * mask).astype(BF)
        dov = (mm(cot, val, NT) * mask).astype(BF)
        gq_ref[:, at] = (mm(dov, key) + lead * mm(cot, state, NT)).astype(BF)
        gk_ref[:, at] = (mm(dov, query, TN) + tail * mm(val, after, NT)).astype(BF)
        gv_ref[:, at] = (mm(scores, cot, TN) + tail * mm(key, after)).astype(BF)


def core_grads(me, qkv, cot, steps, fwd, bwd):
    _, rows, chans = qkv.shape
    count = len(fwd)
    held = pltpu.VMEM((count, *fwd[0].shape), BF)
    vmem = pl.BlockSpec(memory_space=pltpu.VMEM)
    return pl.pallas_call(
        functools.partial(grad_kernel, count),
        in_specs=[pl.BlockSpec(memory_space=pltpu.SMEM)] + [vmem] * (3 + 2 * count),
        out_shape=[jax.ShapeDtypeStruct((rows, chans), BF)] * 3,
        scratch_shapes=[held, held],
        compiler_params=params(20),
        name="core_grads",
    )(me, qkv, cot, steps, *fwd, *bwd)


def norm_kernel(head_ref, x_ref, attn_ref, gain_ref, out_ref):
    rows = attn_ref.shape[0]
    start = pl.multiple_of(head_ref[0] * rows, rows)
    resid = x_ref[pl.ds(start, rows), :].astype(F32) + attn_ref[...].astype(F32)
    scale = lax.rsqrt(jnp.mean(resid * resid, axis=-1, keepdims=True) + 1e-06)
    out_ref[...] = (resid * scale * gain_ref[...]).astype(BF)


def norm_rows(my_head, x, attn, gain):
    rows, width = attn.shape
    vmem = pl.BlockSpec(memory_space=pltpu.VMEM)
    return pl.pallas_call(
        norm_kernel,
        in_specs=[pl.BlockSpec(memory_space=pltpu.SMEM)] + [vmem] * 3,
        out_shape=jax.ShapeDtypeStruct((rows, width), BF),
        compiler_params=params(8),
        name="moe_norm",
    )(my_head, x, attn, gain.reshape(1, width))


def expert_kernel(layout, masks, experts, where_ref, gate_ref, up_ref, down_ref, routes_ref, *refs):
    parts = 1 + max(operand for block in layout for operand, _ in block)
    row_refs, (out_ref, rows_ref, sems) = refs[:parts], refs[parts:]
    step = pl.program_id(0)
    slot = lax.rem(step, 2)

    def copies(at, block):
        for operand, start in layout[block]:
            size = row_refs[operand].shape[0]
            yield pltpu.make_async_copy(
                row_refs[operand], rows_ref.at[at, pl.ds(start, size)], sems.at[at]
            )

    @pl.when(step == 0)
    def _():
        for copy in copies(0, 0):
            copy.start()

    for block in range(1, len(layout)):

        @pl.when(step == block - 1)
        def _(block=block):
            for copy in copies(block % 2, block):
                copy.start()

    pltpu.make_async_copy(rows_ref.at[slot], rows_ref.at[slot], sems.at[slot]).wait()

    relative = jnp.int32(masks[0])
    for block in range(1, len(layout)):
        relative = jnp.where(step == block, masks[block], relative)
    routes = routes_ref[where_ref[0] ^ relative].astype(F32)
    lane = lax.broadcasted_iota(jnp.int32, routes.shape, 1)
    mine = (lane == where_ref[1]) | (lane == where_ref[1] + experts) | (lane == where_ref[1] + 2 * experts)
    weight = jnp.sum(jnp.where(mine, routes, 0.0), axis=1, keepdims=True)
    tokens = rows_ref[slot]
    gate = mm(tokens, gate_ref[0])
    inner = (gate * jax.nn.sigmoid(gate) * mm(tokens, up_ref[0])).astype(BF)
    width = out_ref.shape[2]
    cols = pick_block(width, 512)
    for start in range(0, width, cols):
        at = slice(start, start + cols)
        out_ref[0, :, at] = (mm(inner, down_ref[0, :, at]) * weight).astype(BF)


def expert_pieces(where, blocks, masks, gate, up, down, routes):
    tok, lanes = routes.shape[1:]
    width, hidden = gate.shape[1:]
    operands, layout = [], []
    for block in blocks:
        start, entry = 0, []
        for part in block:
            entry.append((len(operands), start))
            operands.append(part)
            start += part.shape[0]
        layout.append(tuple(entry))
    once = pl.Buffered(1)
    count = len(blocks)
    experts = EXP_CTX * routes.shape[0]
    return pl.pallas_call(
        functools.partial(expert_kernel, tuple(layout), tuple(masks), experts),
        grid=(count,),
        in_specs=[
            pl.BlockSpec(memory_space=pltpu.SMEM),
            pl.BlockSpec((1, width, hidden), lambda i: (0, 0, 0), pipeline_mode=once),
            pl.BlockSpec((1, width, hidden), lambda i: (0, 0, 0), pipeline_mode=once),
            pl.BlockSpec((1, hidden, width), lambda i: (0, 0, 0), pipeline_mode=once),
            pl.BlockSpec(routes.shape, lambda i: (0, 0, 0), pipeline_mode=once),
        ]
        + [pl.BlockSpec(memory_space=pl.ANY)] * len(operands),
        out_specs=pl.BlockSpec((1, tok, width), lambda i: (i, 0, 0)),
        out_shape=jax.ShapeDtypeStruct((count, tok, width), BF),
        scratch_shapes=[pltpu.VMEM((2, tok, width), BF), pltpu.SemaphoreType.DMA((2,))],
        compiler_params=params(24),
        cost_estimate=pl.CostEstimate(
            flops=6 * count * tok * width * hidden,
            bytes_accessed=2 * (2 * count * tok * width + 3 * width * hidden),
            transcendentals=count * tok * hidden,
        ),
        name="expert_pieces",
    )(where, gate, up, down, routes, *operands)


def route_table(expert_ids, route_weights, experts):
    hot = expert_ids[:, :, None] == jnp.arange(experts, dtype=jnp.int32)
    table = jnp.sum(jnp.where(hot, route_weights[:, :, None], 0.0), axis=1)
    first = table.astype(BF)
    left = table - first.astype(F32)
    second = left.astype(BF)
    third = (left - second.astype(F32)).astype(BF)
    joined = jnp.concatenate([first, second, third], axis=1)
    return jnp.pad(joined, ((0, 0), (0, -joined.shape[1] % LANES)))


CORE, ROW, COL = 1, 2, 4
PLANE = 8


def swap(value, mask, keep=None):
    count = lax.axis_size("ctx")
    pairs = [(at, at ^ mask) for at in range(count)]
    return lax.ppermute(value, "ctx", [pair for pair in pairs if keep is None or keep(*pair)])


def spread_states(own, keep):
    count = lax.axis_size("ctx")
    near = jnp.stack([own] + [swap(own, mask, keep) for mask in range(2, count, 2)])
    far = swap(near, CORE)
    return [(far if mask % 2 else near)[mask // 2] for mask in range(count)]


def spread_rows(own):
    count = lax.axis_size("ctx")
    rows = own.shape[0]
    near = {0: [own]}
    if count == PLANE:
        half = rows // 2
        near[ROW] = [swap(own, ROW)]
        near[COL] = [swap(own, COL)]
        near[ROW | COL] = [swap(near[ROW][0][:half], COL), swap(near[COL][0][half:], ROW)]
    else:
        for mask in range(2, count, 2):
            near[mask] = [swap(own, mask)]
    far = {mask | CORE: [swap(part, CORE) for part in parts] for mask, parts in near.items()}
    return near | far


def plus(*terms):
    return functools.reduce(jnp.add, [term.astype(F32) for term in terms]).astype(BF)


def collect_terms(near, far, evens):
    arrived = swap(far, CORE)
    sums = {mask: (near[at], arrived[at]) for at, mask in enumerate(evens)}
    if lax.axis_size("ctx") == PLANE:
        half = near.shape[1] // 2
        across, along, down = sums[ROW | COL], sums[ROW], sums[COL]
        lower = swap(plus(across[0][:half], across[1][:half]), ROW)
        upper = swap(plus(across[0][half:], across[1][half:]), COL)
        none = jnp.zeros_like(lower)
        others = [
            swap(plus(*along, jnp.concatenate([none, upper])), ROW),
            swap(plus(*down, jnp.concatenate([lower, none])), COL),
        ]
    else:
        others = [swap(plus(*sums[mask]), mask) for mask in evens[1:]]
    return arrived, others


def sum_kernel(head_ref, attn_ref, near_ref, arrived_ref, *refs):
    others, out_ref = refs[:-1], refs[-1]
    part = attn_ref.shape[0]
    total = near_ref[0].astype(F32) + arrived_ref[0].astype(F32)
    for ref in others:
        total += ref[...].astype(F32)
    out_ref[0] = total.astype(BF)
    start = pl.multiple_of(head_ref[0] * part, part)
    mine = near_ref[0, pl.ds(start, part), :].astype(F32) + arrived_ref[0, pl.ds(start, part), :].astype(F32)
    for ref in others:
        mine += ref[pl.ds(start, part), :].astype(F32)
    out_ref[0, pl.ds(start, part), :] = (mine + attn_ref[...].astype(F32)).astype(BF)


def sum_terms(my_head, attn, near, arrived, others, n_head):
    _, tok, width = near.shape
    part = attn.shape[0]
    cols = width // n_head
    first = pl.BlockSpec((1, tok, cols), lambda i: (0, 0, i))
    return pl.pallas_call(
        sum_kernel,
        grid=(n_head,),
        in_specs=[
            pl.BlockSpec(memory_space=pltpu.SMEM),
            pl.BlockSpec((part, cols), lambda i: (0, i)),
            first,
            first,
        ]
        + [pl.BlockSpec((tok, cols), lambda i: (0, i))] * len(others),
        out_specs=pl.BlockSpec((1, tok, cols), lambda i: (i, 0, 0)),
        out_shape=jax.ShapeDtypeStruct((n_head, tok, cols), BF),
        compiler_params=params(16),
        name="sum_terms",
    )(my_head, attn, near, arrived, *others)


def body(
    hidden_in,
    gain_attn,
    w_qkv,
    conv_w,
    log_decay,
    norm_gain,
    w_out,
    gain_moe,
    expert_ids,
    route_weights,
    w_gate,
    w_up,
    w_down,
    grad_core,
):
    n_ctx, n_head = lax.axis_size("ctx"), lax.axis_size("head")
    my_ctx, my_head = lax.axis_index("ctx"), lax.axis_index("head")
    tok_dev, width = hidden_in.shape
    experts = EXP_CTX * n_ctx
    shards = n_head // EXP_CTX
    cols = width // n_head
    me = my_ctx.astype(jnp.int32).reshape(1)
    head_at = my_head.astype(jnp.int32).reshape(1)
    routes = route_table(expert_ids, route_weights, experts)
    steps = log_decay.T

    routes = lax.all_gather(routes, "ctx")
    mixed, rim = project(hidden_in, gain_attn, jnp.transpose(w_qkv, (1, 0, 2)))
    rim = lax.ppermute(rim, "ctx", [(at, at + 1) for at in range(n_ctx - 1)])
    qkv, fwd, bwd = local_states(mixed, rim, jnp.transpose(conv_w, (1, 0, 2)), steps, grad_core)
    fwd = spread_states(fwd, lambda source, target: source < target)
    bwd = spread_states(bwd, lambda source, target: source > target)
    partial = core_out(me, qkv, steps, fwd, norm_gain, w_out)
    attn = lax.psum_scatter(partial, "head", scatter_dimension=0, tiled=True)
    normed = norm_rows(head_at, hidden_in, attn, gain_moe)
    rows = spread_rows(lax.all_gather(normed, "head", tiled=True))
    where = jnp.stack([my_ctx, EXP_CTX * my_ctx + my_head // shards]).astype(jnp.int32)
    evens = list(range(0, n_ctx, 2))
    odds = [mask | CORE for mask in evens]
    near, far = (
        expert_pieces(where, [rows[mask] for mask in masks], masks, w_gate, w_up, w_down, routes)
        for masks in (evens, odds)
    )
    arrived, others = collect_terms(near, far, evens)
    total = sum_terms(head_at, attn, near, arrived, others, n_head)
    moe = lax.psum_scatter(total, "head", scatter_dimension=0, tiled=True)
    grads = core_grads(me, qkv, grad_core, steps, fwd, bwd)
    own = lax.dynamic_slice_in_dim(hidden_in, my_head * cols, cols, 1)
    layer_out = (own.astype(F32) + moe[0].astype(F32)).astype(BF)
    return (layer_out, *grads)


def solution(mesh):
    in_specs = (
        P("ctx", None),
        P(),
        P(None, None, "head"),
        P(None, None, "head"),
        P("ctx", "head"),
        P("head"),
        P("head", None),
        P(),
        P("ctx", None),
        P("ctx", None),
        P(("ctx", "head"), None, None),
        P(("ctx", "head"), None, None),
        P(("ctx", "head"), None, None),
        P("ctx", "head"),
    )
    out_specs = (P("ctx", "head"), P("ctx", "head"), P("ctx", "head"), P("ctx", "head"))
    return jax.shard_map(body, mesh=mesh, in_specs=in_specs, out_specs=out_specs, check_vma=False)
```

```python
import functools

import jax
import jax.numpy as jnp
from jax import lax
from jax.experimental import pallas as pl
from jax.experimental.pallas import tpu as pltpu
from jax.sharding import PartitionSpec as P

KERNEL = 4
EXP_CTX = 2
LANES = 128
RIM = 16
MIB = 1024 * 1024
HI = lax.Precision.HIGHEST
BF = jnp.bfloat16
F32 = jnp.float32
NT = (((1,), (1,)), ((), ()))
TN = (((0,), (0,)), ((), ()))
NN = (((1,), (0,)), ((), ()))


def params(mib):
    return pltpu.CompilerParams(vmem_limit_bytes=mib * MIB)


def mm(a, b, dims=NN):
    return lax.dot_general(a, b, dims, preferred_element_type=F32)


def pick_block(extent, target):
    return target if extent % target == 0 else extent


def qkv_kernel(x_hbm, gain_ref, w_hbm, mixed_ref, rim_ref, x_ref, w_ref, normed_ref, x_sem, sems):
    kinds, width, chans = w_ref.shape
    load = pltpu.make_async_copy(x_hbm, x_ref, x_sem)
    load.start()
    copies = [pltpu.make_async_copy(w_hbm.at[kind], w_ref.at[kind], sems.at[kind]) for kind in range(kinds)]
    for copy in copies:
        copy.start()
    load.wait()
    values = x_ref[...].astype(F32)
    scale = lax.rsqrt(jnp.mean(values * values, axis=-1, keepdims=True) + 1e-06)
    normed_ref[...] = (values * scale * gain_ref[...]).astype(BF)
    for kind in range(kinds):
        copies[kind].wait()
        out = mm(normed_ref[...], w_ref[kind]).astype(BF)
        mixed_ref[kind] = out
        rim_ref[kind] = out[out.shape[0] - RIM :]


def project(x, gain, weights):
    rows, width = x.shape
    kinds, _, chans = weights.shape
    vmem = pl.BlockSpec(memory_space=pltpu.VMEM)
    hbm = pl.BlockSpec(memory_space=pltpu.HBM)
    return pl.pallas_call(
        qkv_kernel,
        in_specs=[hbm, vmem, hbm],
        out_shape=[
            jax.ShapeDtypeStruct((kinds, rows, chans), BF),
            jax.ShapeDtypeStruct((kinds, RIM, chans), BF),
        ],
        scratch_shapes=[
            pltpu.VMEM((rows, width), BF),
            pltpu.VMEM((kinds, width, chans), BF),
            pltpu.VMEM((rows, width), BF),
            pltpu.SemaphoreType.DMA,
            pltpu.SemaphoreType.DMA((kinds,)),
        ],
        compiler_params=params(24),
        name="qkv_projection",
    )(x, gain.reshape(1, width), weights)


def decay_sums(steps):
    rows = steps.shape[1]
    row_at = lax.broadcasted_iota(jnp.int32, (rows, rows), 0)
    col_at = lax.broadcasted_iota(jnp.int32, (rows, rows), 1)
    lower = row_at >= col_at
    tri = jnp.where(lower, 1.0, 0.0).astype(F32)
    along = lax.dot_general(steps, tri, NT, precision=HI, preferred_element_type=F32)
    down = lax.dot_general(tri, steps, NT, precision=HI, preferred_element_type=F32)
    return along, down, lower


def payload_tail(total, size):
    full = jnp.broadcast_to(total, (RIM, size))
    first = full.astype(BF).astype(F32)
    second = (full - first).astype(BF).astype(F32)
    third = full - first - second
    at = lax.broadcasted_iota(jnp.int32, (RIM, size), 0)
    return jnp.where(at == 0, first, jnp.where(at == 1, second, jnp.where(at == 2, third, 0.0)))


def route_rows(ids_ref, weights_ref, experts):
    top, tok = ids_ref.shape
    expert = lax.broadcasted_iota(jnp.int32, (experts, tok), 0)
    table = jnp.zeros((experts, tok), F32)
    for choice in range(top):
        table += jnp.where(expert == ids_ref[choice : choice + 1, :], weights_ref[choice : choice + 1, :], 0.0)
    first = table.astype(BF).astype(F32)
    second = (table - first).astype(BF).astype(F32)
    return jnp.concatenate([first, second, table - first - second], axis=0)


def conv_kernel(
    experts, mixed_ref, rim_ref, taps_ref, steps_ref, cot_ref, ids_ref, weights_ref, qkv_ref, fwd_ref, bwd_ref, pad_ref
):
    kinds, rows, chans = mixed_ref.shape
    heads = steps_ref.shape[0]
    size = chans // heads
    along, down, _ = decay_sums(steps_ref[...])
    for kind in range(kinds):
        pad_ref[:RIM] = rim_ref[kind].astype(F32)
        pad_ref[RIM:] = mixed_ref[kind].astype(F32)
        total = taps_ref[kind, 0:1, :] * pad_ref[RIM:]
        for offset in range(1, KERNEL):
            total += taps_ref[kind, offset : offset + 1, :] * pad_ref[RIM - offset : RIM - offset + rows]
        activ = total * jax.nn.sigmoid(total)
        if kind == 0:
            activ = activ * size ** (-0.5)
        qkv_ref[kind] = activ.astype(BF)
    for head in range(heads):
        at = slice(head * size, (head + 1) * size)
        base = head * (size + RIM)
        last = along[head : head + 1, rows - 1 : rows]
        lead = jnp.exp(down[:, head : head + 1])
        tail = jnp.exp(last - down[:, head : head + 1])
        key_out = (qkv_ref[1, :, at].astype(F32) * tail).astype(BF)
        query_out = (qkv_ref[0, :, at].astype(F32) * lead).astype(BF)
        ends = payload_tail(last, size).astype(BF)
        fwd_ref[base : base + size] = mm(key_out, qkv_ref[2, :, at], TN).astype(BF)
        fwd_ref[base + size : base + size + RIM] = ends
        bwd_ref[base : base + size] = mm(query_out, cot_ref[:, at], TN).astype(BF)
        bwd_ref[base + size : base + size + RIM] = ends
    base = heads * (size + RIM)
    table = route_rows(ids_ref, weights_ref, experts).astype(BF)
    for part in range(rows // LANES):
        bwd_ref[base : base + 3 * experts] = table[:, part * LANES : (part + 1) * LANES]
        base += 3 * experts


def local_states(mixed, rim, taps, steps, cot, ids, weights, experts):
    kinds, rows, chans = mixed.shape
    heads = steps.shape[0]
    size = chans // heads
    states = heads * (size + RIM)
    return pl.pallas_call(
        functools.partial(conv_kernel, experts),
        out_shape=[
            jax.ShapeDtypeStruct((kinds, rows, chans), BF),
            jax.ShapeDtypeStruct((states, size), BF),
            jax.ShapeDtypeStruct((states + rows // LANES * 3 * experts, size), BF),
        ],
        scratch_shapes=[pltpu.VMEM((rows + RIM, chans), F32)],
        compiler_params=params(12),
        name="conv_states",
    )(mixed, rim, taps, steps, cot, ids, weights)


def arrange(me_ref, near_ref, far_ref, held_ref):
    for at in range(near_ref.shape[0]):
        held_ref[me_ref[0] ^ (2 * at)] = near_ref[at]
        held_ref[me_ref[0] ^ (2 * at + 1)] = far_ref[at]


def entering(held_ref, head, size, first, last, step):
    base = head * (size + RIM)

    def hop(count, total):
        at = first + count * step
        ends = held_ref[at, base + size : base + size + RIM, :].astype(F32)
        factor = jnp.exp(ends[0:1] + ends[1:2] + ends[2:3])
        return factor * total + held_ref[at, base : base + size, :].astype(F32)

    return lax.fori_loop(0, (last - first) * step, hop, jnp.zeros((size, size), F32))


def core_kernel(me_ref, qkv_ref, steps_ref, gain_ref, near_ref, far_ref, w_hbm, *refs):
    out_refs, (headed_ref, held_ref, w_ref, sem) = refs[:-4], refs[-4:]
    load = pltpu.make_async_copy(w_hbm, w_ref, sem)
    load.start()
    _, rows, chans = qkv_ref.shape
    heads = steps_ref.shape[0]
    size = chans // heads
    arrange(me_ref, near_ref, far_ref, held_ref)
    along, down, lower = decay_sums(steps_ref[...])
    for head in range(heads):
        at = slice(head * size, (head + 1) * size)
        state = entering(held_ref, head, size, 0, me_ref[0], 1).astype(BF)
        diff = down[:, head : head + 1] - along[head : head + 1, :]
        mask = jnp.exp(jnp.where(lower, diff, -jnp.inf))
        query = qkv_ref[0, :, at]
        scores = (mm(query, qkv_ref[1, :, at], NT) * mask).astype(BF)
        attended = mm(scores, qkv_ref[2, :, at])
        attended += mm(query, state) * jnp.exp(down[:, head : head + 1])
        scale = lax.rsqrt(jnp.mean(attended * attended, axis=-1, keepdims=True) + 1e-06)
        headed_ref[:, at] = (attended * scale * gain_ref[:, at]).astype(BF)
    load.wait()
    part = rows // len(out_refs)
    out = mm(headed_ref[...], w_ref[...]).astype(BF)
    for chunk, ref in enumerate(out_refs):
        ref[...] = out[chunk * part : (chunk + 1) * part]


def core_out(me, qkv, steps, near, far, gain, w_out, chunks):
    _, rows, chans = qkv.shape
    width = w_out.shape[1]
    vmem = pl.BlockSpec(memory_space=pltpu.VMEM)
    return pl.pallas_call(
        core_kernel,
        in_specs=[pl.BlockSpec(memory_space=pltpu.SMEM)] + [vmem] * 5 + [pl.BlockSpec(memory_space=pltpu.HBM)],
        out_shape=[jax.ShapeDtypeStruct((rows // chunks, width), BF)] * chunks,
        scratch_shapes=[
            pltpu.VMEM((rows, chans), BF),
            pltpu.VMEM((2 * near.shape[0], *near.shape[1:]), BF),
            pltpu.VMEM(w_out.shape, BF),
            pltpu.SemaphoreType.DMA,
        ],
        compiler_params=params(20),
        name="core_out",
    )(me, qkv, steps, gain.reshape(1, chans), near, far, w_out)


def grad_kernel(
    experts, me_ref, qkv_ref, cot_ref, steps_ref, fwd_near, fwd_far, bwd_near, bwd_far, gate_hbm, up_hbm, down_hbm,
    gq_ref, gk_ref, gv_ref, columns_ref, gate_ref, up_ref, down_ref, fwd_ref, bwd_ref, sems,
):
    copies = [
        pltpu.make_async_copy(source, target, sems.at[at])
        for at, (source, target) in enumerate(((gate_hbm, gate_ref), (up_hbm, up_ref), (down_hbm, down_ref)))
    ]
    for copy in copies:
        copy.start()
    _, rows, chans = qkv_ref.shape
    heads = steps_ref.shape[0]
    size = chans // heads
    count = fwd_ref.shape[0]
    arrange(me_ref, fwd_near, fwd_far, fwd_ref)
    arrange(me_ref, bwd_near, bwd_far, bwd_ref)
    along, down, lower = decay_sums(steps_ref[...])
    for head in range(heads):
        at = slice(head * size, (head + 1) * size)
        state = entering(fwd_ref, head, size, 0, me_ref[0], 1).astype(BF)
        after = entering(bwd_ref, head, size, count - 1, me_ref[0], -1).astype(BF)
        here = down[:, head : head + 1]
        lead = jnp.exp(here)
        tail = jnp.exp(along[head : head + 1, rows - 1 : rows] - here)
        mask = jnp.exp(jnp.where(lower, here - along[head : head + 1, :], -jnp.inf))
        query, key, val = qkv_ref[0, :, at], qkv_ref[1, :, at], qkv_ref[2, :, at]
        cot = cot_ref[:, at]
        scores = (mm(query, key, NT) * mask).astype(BF)
        dov = (mm(cot, val, NT) * mask).astype(BF)
        gq_ref[:, at] = (mm(dov, key) + lead * mm(cot, state, NT)).astype(BF)
        gk_ref[:, at] = (mm(dov, query, TN) + tail * mm(val, after, NT)).astype(BF)
        gv_ref[:, at] = (mm(scores, cot, TN) + tail * mm(key, after)).astype(BF)

    here = lax.broadcasted_iota(jnp.int32, (3 * experts, LANES), 0)
    mine = (here == me_ref[1]) | (here == me_ref[1] + experts) | (here == me_ref[1] + 2 * experts)
    diagonal = lax.broadcasted_iota(jnp.int32, (LANES, LANES), 0) == lax.broadcasted_iota(jnp.int32, (LANES, LANES), 1)
    for mask in range(count):
        source = bwd_far if mask % 2 else bwd_near
        base = heads * (size + RIM)
        for part in range(rows // LANES):
            table = source[mask // 2, base : base + 3 * experts, :].astype(F32)
            row = jnp.sum(jnp.where(mine, table, 0.0), axis=0, keepdims=True)
            column = jnp.sum(jnp.where(diagonal, jnp.broadcast_to(row, (LANES, LANES)), 0.0), axis=1, keepdims=True)
            columns_ref[mask, part * LANES : (part + 1) * LANES, :] = jnp.broadcast_to(column, (LANES, LANES))
            base += 3 * experts
    for copy in copies:
        copy.wait()


def core_grads(where, qkv, cot, steps, fwd, bwd, gate, up, down, experts):
    _, rows, chans = qkv.shape
    count = 2 * fwd[0].shape[0]
    vmem = pl.BlockSpec(memory_space=pltpu.VMEM)
    hbm = pl.BlockSpec(memory_space=pltpu.HBM)
    grad = jax.ShapeDtypeStruct((rows, chans), BF)
    return pl.pallas_call(
        functools.partial(grad_kernel, experts),
        in_specs=[pl.BlockSpec(memory_space=pltpu.SMEM)] + [vmem] * 7 + [hbm] * 3,
        out_specs=[vmem] * 7,
        out_shape=[grad, grad, grad, jax.ShapeDtypeStruct((count, rows, LANES), F32)]
        + [jax.ShapeDtypeStruct(part.shape, BF) for part in (gate, up, down)],
        scratch_shapes=[
            pltpu.VMEM((count, *fwd[0].shape[1:]), BF),
            pltpu.VMEM((count, *bwd[0].shape[1:]), BF),
            pltpu.SemaphoreType.DMA((3,)),
        ],
        compiler_params=params(24),
        name="core_grads",
    )(where, qkv, cot, steps, *fwd, *bwd, gate, up, down)


def norm_kernel(chunk, head_ref, x_ref, attn_ref, gain_ref, out_ref):
    rows = attn_ref.shape[0]
    start = pl.multiple_of(chunk + head_ref[0] * rows, rows)
    resid = x_ref[pl.ds(start, rows), :].astype(F32) + attn_ref[...].astype(F32)
    scale = lax.rsqrt(jnp.mean(resid * resid, axis=-1, keepdims=True) + 1e-06)
    out_ref[...] = (resid * scale * gain_ref[...]).astype(BF)


def norm_rows(chunk, my_head, x, attn, gain):
    rows, width = attn.shape
    vmem = pl.BlockSpec(memory_space=pltpu.VMEM)
    return pl.pallas_call(
        functools.partial(norm_kernel, chunk),
        in_specs=[pl.BlockSpec(memory_space=pltpu.SMEM)] + [vmem] * 3,
        out_shape=jax.ShapeDtypeStruct((rows, width), BF),
        compiler_params=params(8),
        name="moe_norm",
    )(my_head, x, attn, gain.reshape(1, width))


PAIR = 2


def expert_kernel(masks, chunk, gate_ref, up_ref, down_ref, columns_ref, *refs):
    row_refs, (out_ref, rows_ref, sems) = refs[: len(masks)], refs[len(masks) :]
    _, tok, width = out_ref.shape
    steps = len(masks) // PAIR
    step = pl.program_id(0)
    slot = lax.rem(step, 2)

    def start(at):
        for part in range(PAIR):
            target = rows_ref.at[at % 2, pl.ds(part * tok, tok)]
            pltpu.make_async_copy(row_refs[PAIR * at + part], target, sems.at[at % 2]).start()

    @pl.when(step == 0)
    def _():
        start(0)

    for at in range(1, steps):

        @pl.when(step == at - 1)
        def _(at=at):
            start(at)

    pltpu.make_async_copy(rows_ref.at[slot], rows_ref.at[slot], sems.at[slot]).wait()
    tokens = rows_ref[slot]
    gate = mm(tokens, gate_ref[0])
    inner = (gate * jax.nn.sigmoid(gate) * mm(tokens, up_ref[0])).astype(BF)
    cols = pick_block(width, 512)
    weights = []
    for part in range(PAIR):
        mask = jnp.int32(masks[part])
        for at in range(1, steps):
            mask = jnp.where(step == at, masks[PAIR * at + part], mask)
        weights.append(columns_ref[mask, chunk : chunk + tok, :1])
    for begin in range(0, width, cols):
        piece = mm(inner, down_ref[0, :, begin : begin + cols])
        for part in range(PAIR):
            scaled = piece[part * tok : (part + 1) * tok] * weights[part]
            out_ref[part, :, begin : begin + cols] = scaled.astype(BF)


def expert_pieces(chunk, blocks, masks, gate, up, down, columns):
    tok, width = blocks[0].shape
    hidden = gate.shape[2]
    count = len(blocks)
    vmem = pl.BlockSpec(memory_space=pltpu.VMEM)
    return pl.pallas_call(
        functools.partial(expert_kernel, tuple(masks), chunk),
        grid=(count // PAIR,),
        in_specs=[vmem] * 4 + [pl.BlockSpec(memory_space=pl.ANY)] * count,
        out_specs=pl.BlockSpec((PAIR, tok, width), lambda i: (i, 0, 0)),
        out_shape=jax.ShapeDtypeStruct((count, tok, width), BF),
        scratch_shapes=[pltpu.VMEM((2, PAIR * tok, width), BF), pltpu.SemaphoreType.DMA((2,))],
        compiler_params=params(16),
        cost_estimate=pl.CostEstimate(
            flops=6 * count * tok * width * hidden,
            bytes_accessed=4 * count * tok * width,
            transcendentals=count * tok * hidden,
        ),
        name="expert_pieces",
    )(gate, up, down, columns, *blocks)


CORE, ROW, COL = 1, 2, 4
PLANE = 8


def swap(value, mask, keep=None):
    count = lax.axis_size("ctx")
    pairs = [(at, at ^ mask) for at in range(count)]
    return lax.ppermute(value, "ctx", [pair for pair in pairs if keep is None or keep(*pair)])


def spread_states(own, keep=None):
    near = jnp.stack([own] + [swap(own, mask, keep) for mask in range(2, lax.axis_size("ctx"), 2)])
    return near, swap(near, CORE)


def hops(chunk):
    return (ROW, COL) if chunk % 2 == 0 else (COL, ROW)


def spread_rows(own, chunk):
    count = lax.axis_size("ctx")
    near = {0: own}
    if count == PLANE:
        first, second = hops(chunk)
        near[first] = swap(own, first)
        near[second] = swap(own, second)
        near[ROW | COL] = swap(near[first], second)
    else:
        for mask in range(2, count, 2):
            near[mask] = swap(own, mask)
    return near | {mask | CORE: swap(rows, CORE) for mask, rows in near.items()}


def plus(*terms):
    return functools.reduce(jnp.add, [term.astype(F32) for term in terms]).astype(BF)


def collect_terms(near, far, evens, chunk):
    arrived = swap(far, CORE)
    sums = {mask: (near[at], arrived[at]) for at, mask in enumerate(evens)}
    if lax.axis_size("ctx") == PLANE:
        first, second = hops(chunk)
        across = swap(plus(*sums[ROW | COL]), second)
        direct, across = lax.optimization_barrier((plus(*sums[second]), across))
        others = [swap(plus(*sums[first], across), first), swap(direct, second)]
    else:
        others = [swap(plus(*sums[mask]), mask) for mask in evens[1:]]
    return arrived, others


def sum_kernel(head_ref, attn_ref, near_ref, arrived_ref, *refs):
    others, out_ref = refs[:-1], refs[-1]
    part = attn_ref.shape[0]
    total = near_ref[0].astype(F32) + arrived_ref[0].astype(F32)
    for ref in others:
        total += ref[...].astype(F32)
    out_ref[0] = total.astype(BF)
    start = pl.multiple_of(head_ref[0] * part, part)
    mine = near_ref[0, pl.ds(start, part), :].astype(F32) + arrived_ref[0, pl.ds(start, part), :].astype(F32)
    for ref in others:
        mine += ref[pl.ds(start, part), :].astype(F32)
    out_ref[0, pl.ds(start, part), :] = (mine + attn_ref[...].astype(F32)).astype(BF)


def sum_terms(my_head, attn, near, arrived, others, n_head):
    _, tok, width = near.shape
    part = attn.shape[0]
    cols = width // n_head
    first = pl.BlockSpec((1, tok, cols), lambda i: (0, 0, i))
    return pl.pallas_call(
        sum_kernel,
        grid=(n_head,),
        in_specs=[
            pl.BlockSpec(memory_space=pltpu.SMEM),
            pl.BlockSpec((part, cols), lambda i: (0, i)),
            first,
            first,
        ]
        + [pl.BlockSpec((tok, cols), lambda i: (0, i))] * len(others),
        out_specs=pl.BlockSpec((1, tok, cols), lambda i: (i, 0, 0)),
        out_shape=jax.ShapeDtypeStruct((n_head, tok, cols), BF),
        compiler_params=params(16),
        name="sum_terms",
    )(my_head, attn, near, arrived, *others)


def final_kernel(head_ref, x_ref, *refs):
    del head_ref
    moe_refs, out_ref = refs[:-1], refs[-1]
    rows = moe_refs[0].shape[1]
    for chunk, ref in enumerate(moe_refs):
        at = slice(chunk * rows, (chunk + 1) * rows)
        out_ref[at] = (x_ref[at].astype(F32) + ref[0].astype(F32)).astype(BF)


def final_sum(my_head, x, moe):
    rows = x.shape[0]
    cols = moe[0].shape[2]
    return pl.pallas_call(
        final_kernel,
        grid_spec=pltpu.PrefetchScalarGridSpec(
            num_scalar_prefetch=1,
            grid=(1,),
            in_specs=[pl.BlockSpec((rows, cols), lambda i, head: (0, head[0]))]
            + [pl.BlockSpec(part.shape, lambda i, head: (0, 0, 0)) for part in moe],
            out_specs=pl.BlockSpec((rows, cols), lambda i, head: (0, 0)),
        ),
        out_shape=jax.ShapeDtypeStruct((rows, cols), BF),
        compiler_params=params(8),
        name="layer_out",
    )(my_head, x, *moe)


CHUNKS = 2


def body(
    hidden_in,
    gain_attn,
    w_qkv,
    conv_w,
    log_decay,
    norm_gain,
    w_out,
    gain_moe,
    expert_ids,
    route_weights,
    w_gate,
    w_up,
    w_down,
    grad_core,
):
    n_ctx, n_head = lax.axis_size("ctx"), lax.axis_size("head")
    my_ctx, my_head = lax.axis_index("ctx"), lax.axis_index("head")
    tok_dev = hidden_in.shape[0]
    experts = EXP_CTX * n_ctx
    shards = n_head // EXP_CTX
    where = jnp.stack([my_ctx, EXP_CTX * my_ctx + my_head // shards]).astype(jnp.int32)
    head_at = my_head.astype(jnp.int32).reshape(1)
    steps = log_decay.T
    chunk_rows = tok_dev // CHUNKS

    mixed, rim = project(hidden_in, gain_attn, jnp.transpose(w_qkv, (1, 0, 2)))
    rim = lax.ppermute(rim, "ctx", [(at, at + 1) for at in range(n_ctx - 1)])
    qkv, fwd, bwd = local_states(
        mixed, rim, jnp.transpose(conv_w, (1, 0, 2)), steps, grad_core, expert_ids.T, route_weights.T, experts
    )
    fwd = spread_states(fwd, lambda source, target: source < target)
    partials = core_out(where, qkv, steps, *fwd, norm_gain, w_out, CHUNKS)
    bwd, partials = lax.optimization_barrier((bwd, partials))
    attn = [lax.psum_scatter(part, "head", scatter_dimension=0, tiled=True) for part in partials]
    bwd = spread_states(bwd)
    *grads, columns, gate, up, down = core_grads(
        where, qkv, grad_core, steps, fwd, bwd, w_gate, w_up, w_down, experts
    )
    attn[0], columns = lax.optimization_barrier((attn[0], columns))
    own = []
    for chunk in range(CHUNKS):
        normed = norm_rows(chunk * chunk_rows, head_at, hidden_in, attn[chunk], gain_moe)
        own.append(lax.all_gather(normed, "head", tiled=True))
    moe = []
    for chunk in range(CHUNKS):
        rows = spread_rows(own[chunk], chunk)
        evens = [mask for mask in rows if not mask & CORE]
        near, far = (
            expert_pieces(chunk * chunk_rows, [rows[mask] for mask in masks], masks, gate, up, down, columns)
            for masks in (evens, [mask | CORE for mask in evens])
        )
        arrived, others = collect_terms(near, far, evens, chunk)
        total = sum_terms(head_at, attn[chunk], near, arrived, others, n_head)
        moe.append(lax.psum_scatter(total, "head", scatter_dimension=0, tiled=True))
    return (final_sum(head_at, hidden_in, moe), *grads)


def solution(mesh):
    in_specs = (
        P("ctx", None),
        P(),
        P(None, None, "head"),
        P(None, None, "head"),
        P("ctx", "head"),
        P("head"),
        P("head", None),
        P(),
        P("ctx", None),
        P("ctx", None),
        P(("ctx", "head"), None, None),
        P(("ctx", "head"), None, None),
        P(("ctx", "head"), None, None),
        P("ctx", "head"),
    )
    out_specs = (P("ctx", "head"), P("ctx", "head"), P("ctx", "head"), P("ctx", "head"))
    return jax.shard_map(body, mesh=mesh, in_specs=in_specs, out_specs=out_specs, check_vma=False)
```

```python
import functools

import jax
import jax.numpy as jnp
from jax import lax
from jax.experimental import pallas as pl
from jax.experimental.pallas import tpu as pltpu
from jax.sharding import PartitionSpec as P

KERNEL = 4
EXP_CTX = 2
LANES = 128
RIM = 16
MIB = 1024 * 1024
HI = lax.Precision.HIGHEST
BF = jnp.bfloat16
F32 = jnp.float32
NT = (((1,), (1,)), ((), ()))
TN = (((0,), (0,)), ((), ()))
NN = (((1,), (0,)), ((), ()))


def params(mib):
    return pltpu.CompilerParams(vmem_limit_bytes=mib * MIB)


def mm(a, b, dims=NN):
    return lax.dot_general(a, b, dims, preferred_element_type=F32)


def pick_block(extent, target):
    return target if extent % target == 0 else extent


def qkv_kernel(x_hbm, gain_ref, w_hbm, mixed_ref, rim_ref, x_ref, w_ref, normed_ref, x_sem, sems):
    kinds, width, chans = w_ref.shape
    load = pltpu.make_async_copy(x_hbm, x_ref, x_sem)
    load.start()
    copies = [pltpu.make_async_copy(w_hbm.at[kind], w_ref.at[kind], sems.at[kind]) for kind in range(kinds)]
    for copy in copies:
        copy.start()
    load.wait()
    values = x_ref[...].astype(F32)
    scale = lax.rsqrt(jnp.mean(values * values, axis=-1, keepdims=True) + 1e-06)
    normed_ref[...] = (values * scale * gain_ref[...]).astype(BF)
    for kind in range(kinds):
        copies[kind].wait()
        out = mm(normed_ref[...], w_ref[kind]).astype(BF)
        mixed_ref[kind] = out
        rim_ref[kind] = out[out.shape[0] - RIM :]


def project(x, gain, weights):
    rows, width = x.shape
    kinds, _, chans = weights.shape
    vmem = pl.BlockSpec(memory_space=pltpu.VMEM)
    hbm = pl.BlockSpec(memory_space=pltpu.HBM)
    return pl.pallas_call(
        qkv_kernel,
        in_specs=[hbm, vmem, hbm],
        out_shape=[
            jax.ShapeDtypeStruct((kinds, rows, chans), BF),
            jax.ShapeDtypeStruct((kinds, RIM, chans), BF),
        ],
        scratch_shapes=[
            pltpu.VMEM((rows, width), BF),
            pltpu.VMEM((kinds, width, chans), BF),
            pltpu.VMEM((rows, width), BF),
            pltpu.SemaphoreType.DMA,
            pltpu.SemaphoreType.DMA((kinds,)),
        ],
        compiler_params=params(61),
        name="qkv_projection",
    )(x, gain.reshape(1, width), weights)


def decay_sums(steps):
    rows = steps.shape[1]
    row_at = lax.broadcasted_iota(jnp.int32, (rows, rows), 0)
    col_at = lax.broadcasted_iota(jnp.int32, (rows, rows), 1)
    lower = row_at >= col_at
    tri = jnp.where(lower, 1.0, 0.0).astype(F32)
    along = lax.dot_general(steps, tri, NT, precision=HI, preferred_element_type=F32)
    down = lax.dot_general(tri, steps, NT, precision=HI, preferred_element_type=F32)
    return along, down, lower


def payload_tail(total, size):
    full = jnp.broadcast_to(total, (RIM, size))
    first = full.astype(BF).astype(F32)
    second = (full - first).astype(BF).astype(F32)
    third = full - first - second
    at = lax.broadcasted_iota(jnp.int32, (RIM, size), 0)
    return jnp.where(at == 0, first, jnp.where(at == 1, second, jnp.where(at == 2, third, 0.0)))


def route_rows(ids_ref, weights_ref, experts):
    top, tok = ids_ref.shape
    expert = lax.broadcasted_iota(jnp.int32, (experts, tok), 0)
    table = jnp.zeros((experts, tok), F32)
    for choice in range(top):
        table += jnp.where(expert == ids_ref[choice : choice + 1, :], weights_ref[choice : choice + 1, :], 0.0)
    first = table.astype(BF).astype(F32)
    second = (table - first).astype(BF).astype(F32)
    return jnp.concatenate([first, second, table - first - second], axis=0)


def conv_kernel(
    experts, mixed_ref, rim_ref, taps_ref, steps_ref, cot_ref, ids_ref, weights_ref, qkv_ref, fwd_ref, bwd_ref, pad_ref
):
    kinds, rows, chans = mixed_ref.shape
    heads = steps_ref.shape[0]
    size = chans // heads
    along, down, _ = decay_sums(steps_ref[...])
    for kind in range(kinds):
        pad_ref[:RIM] = rim_ref[kind].astype(F32)
        pad_ref[RIM:] = mixed_ref[kind].astype(F32)
        total = taps_ref[kind, 0:1, :] * pad_ref[RIM:]
        for offset in range(1, KERNEL):
            total += taps_ref[kind, offset : offset + 1, :] * pad_ref[RIM - offset : RIM - offset + rows]
        activ = total * jax.nn.sigmoid(total)
        if kind == 0:
            activ = activ * size ** (-0.5)
        qkv_ref[kind] = activ.astype(BF)
    routes = rows // LANES * 3 * experts
    table = route_rows(ids_ref, weights_ref, experts).astype(BF)
    for part in range(rows // LANES):
        bwd_ref[part * 3 * experts : (part + 1) * 3 * experts] = table[:, part * LANES : (part + 1) * LANES]
    for head in range(heads):
        at = slice(head * size, (head + 1) * size)
        base = head * (size + RIM)
        last = along[head : head + 1, rows - 1 : rows]
        lead = jnp.exp(down[:, head : head + 1])
        tail = jnp.exp(last - down[:, head : head + 1])
        key_out = (qkv_ref[1, :, at].astype(F32) * tail).astype(BF)
        query_out = (qkv_ref[0, :, at].astype(F32) * lead).astype(BF)
        ends = payload_tail(last, size).astype(BF)
        fwd_ref[base : base + size] = mm(key_out, qkv_ref[2, :, at], TN).astype(BF)
        fwd_ref[base + size : base + size + RIM] = ends
        base += routes
        bwd_ref[base : base + size] = mm(query_out, cot_ref[:, at], TN).astype(BF)
        bwd_ref[base + size : base + size + RIM] = ends


def local_states(mixed, rim, taps, steps, cot, ids, weights, experts):
    kinds, rows, chans = mixed.shape
    heads = steps.shape[0]
    size = chans // heads
    states = heads * (size + RIM)
    return pl.pallas_call(
        functools.partial(conv_kernel, experts),
        out_shape=[
            jax.ShapeDtypeStruct((kinds, rows, chans), BF),
            jax.ShapeDtypeStruct((states, size), BF),
            jax.ShapeDtypeStruct((states + rows // LANES * 3 * experts, size), BF),
        ],
        scratch_shapes=[pltpu.VMEM((rows + RIM, chans), F32)],
        compiler_params=params(12),
        name="conv_states",
    )(mixed, rim, taps, steps, cot, ids, weights)


def arrange(me_ref, near_ref, far_ref, held_ref):
    for at in range(near_ref.shape[0]):
        held_ref[me_ref[0] ^ (2 * at)] = near_ref[at]
        held_ref[me_ref[0] ^ (2 * at + 1)] = far_ref[at]


def entering(held_ref, heads, head, size, first, last, step):
    base = held_ref.shape[1] - (heads - head) * (size + RIM)

    def hop(count, total):
        at = first + count * step
        ends = held_ref[at, base + size : base + size + RIM, :].astype(F32)
        factor = jnp.exp(ends[0:1] + ends[1:2] + ends[2:3])
        return factor * total + held_ref[at, base : base + size, :].astype(F32)

    return lax.fori_loop(0, (last - first) * step, hop, jnp.zeros((size, size), F32))


def core_kernel(parts, me_ref, qkv_ref, steps_ref, gain_ref, near_ref, far_ref, w_hbm, *refs):
    out_refs, (headed_ref, held_ref, w_ref, whole_ref, sem) = refs[:-5], refs[-5:]
    load = pltpu.make_async_copy(w_hbm, w_ref, sem)
    load.start()
    _, rows, chans = qkv_ref.shape
    heads = steps_ref.shape[0]
    size = chans // heads
    arrange(me_ref, near_ref, far_ref, held_ref)
    along, down, lower = decay_sums(steps_ref[...])
    for head in range(heads):
        at = slice(head * size, (head + 1) * size)
        state = entering(held_ref, heads, head, size, 0, me_ref[0], 1).astype(BF)
        diff = down[:, head : head + 1] - along[head : head + 1, :]
        mask = jnp.exp(jnp.where(lower, diff, -jnp.inf))
        query = qkv_ref[0, :, at]
        scores = (mm(query, qkv_ref[1, :, at], NT) * mask).astype(BF)
        attended = mm(scores, qkv_ref[2, :, at])
        attended += mm(query, state) * jnp.exp(down[:, head : head + 1])
        scale = lax.rsqrt(jnp.mean(attended * attended, axis=-1, keepdims=True) + 1e-06)
        headed_ref[:, at] = (attended * scale * gain_ref[:, at]).astype(BF)
    load.wait()
    whole_ref[...] = mm(headed_ref[...], w_ref[...]).astype(BF)
    part = rows // len(out_refs)
    for at, ref in enumerate(out_refs):
        chunk, mask = divmod(at, parts)
        start = chunk * parts * part + (me_ref[2] ^ mask) * part
        ref[...] = whole_ref[pl.ds(pl.multiple_of(start, part), part), :]


def core_out(where, qkv, steps, near, far, gain, w_out, chunks, parts):
    _, rows, chans = qkv.shape
    width = w_out.shape[1]
    vmem = pl.BlockSpec(memory_space=pltpu.VMEM)
    outs = pl.pallas_call(
        functools.partial(core_kernel, parts),
        in_specs=[pl.BlockSpec(memory_space=pltpu.SMEM)] + [vmem] * 5 + [pl.BlockSpec(memory_space=pltpu.HBM)],
        out_shape=[jax.ShapeDtypeStruct((rows // chunks // parts, width), BF)] * (chunks * parts),
        scratch_shapes=[
            pltpu.VMEM((rows, chans), BF),
            pltpu.VMEM((2 * near.shape[0], *near.shape[1:]), BF),
            pltpu.VMEM(w_out.shape, BF),
            pltpu.VMEM((rows, width), BF),
            pltpu.SemaphoreType.DMA,
        ],
        compiler_params=params(56),
        name="core_out",
    )(where, qkv, steps, gain.reshape(1, chans), near, far, w_out)
    return [outs[chunk * parts : (chunk + 1) * parts] for chunk in range(chunks)]


def grad_kernel(
    me_ref, qkv_ref, cot_ref, steps_ref, fwd_near, fwd_far, bwd_near, bwd_far, gq_ref, gk_ref, gv_ref, fwd_ref, bwd_ref
):
    _, rows, chans = qkv_ref.shape
    heads = steps_ref.shape[0]
    size = chans // heads
    count = fwd_ref.shape[0]
    arrange(me_ref, fwd_near, fwd_far, fwd_ref)
    arrange(me_ref, bwd_near, bwd_far, bwd_ref)
    along, down, lower = decay_sums(steps_ref[...])
    for head in range(heads):
        at = slice(head * size, (head + 1) * size)
        state = entering(fwd_ref, heads, head, size, 0, me_ref[0], 1).astype(BF)
        after = entering(bwd_ref, heads, head, size, count - 1, me_ref[0], -1).astype(BF)
        here = down[:, head : head + 1]
        lead = jnp.exp(here)
        tail = jnp.exp(along[head : head + 1, rows - 1 : rows] - here)
        mask = jnp.exp(jnp.where(lower, here - along[head : head + 1, :], -jnp.inf))
        query, key, val = qkv_ref[0, :, at], qkv_ref[1, :, at], qkv_ref[2, :, at]
        cot = cot_ref[:, at]
        scores = (mm(query, key, NT) * mask).astype(BF)
        dov = (mm(cot, val, NT) * mask).astype(BF)
        gq_ref[:, at] = (mm(dov, key) + lead * mm(cot, state, NT)).astype(BF)
        gk_ref[:, at] = (mm(dov, query, TN) + tail * mm(val, after, NT)).astype(BF)
        gv_ref[:, at] = (mm(scores, cot, TN) + tail * mm(key, after)).astype(BF)


def core_grads(where, qkv, cot, steps, fwd, bwd):
    _, rows, chans = qkv.shape
    count = 2 * fwd[0].shape[0]
    vmem = pl.BlockSpec(memory_space=pltpu.VMEM)
    return pl.pallas_call(
        grad_kernel,
        in_specs=[pl.BlockSpec(memory_space=pltpu.SMEM)] + [vmem] * 7,
        out_shape=[jax.ShapeDtypeStruct((rows, chans), BF)] * 3,
        scratch_shapes=[pltpu.VMEM((count, *fwd[0].shape[1:]), BF), pltpu.VMEM((count, *bwd[0].shape[1:]), BF)],
        compiler_params=params(24),
        name="core_grads",
    )(where, qkv, cot, steps, *fwd, *bwd)


def norm_kernel(where_ref, x_ref, gain_ref, *refs):
    del where_ref
    parts, (out_ref, attn_ref) = refs[:-2], refs[-2:]
    attn = functools.reduce(jnp.add, [part[...].astype(F32) for part in parts])
    attn_ref[...] = attn
    resid = x_ref[...].astype(F32) + attn
    scale = lax.rsqrt(jnp.mean(resid * resid, axis=-1, keepdims=True) + 1e-06)
    out_ref[...] = (resid * scale * gain_ref[...]).astype(BF)


def norm_rows(chunk, where, x, parts, gain):
    rows, width = parts[0].shape
    count = len(parts)
    block = pl.BlockSpec((rows, width), lambda i, where: (0, 0))
    return pl.pallas_call(
        norm_kernel,
        grid_spec=pltpu.PrefetchScalarGridSpec(
            num_scalar_prefetch=1,
            grid=(1,),
            in_specs=[
                pl.BlockSpec((rows, width), lambda i, where: (chunk * count + where[2], 0)),
                pl.BlockSpec((1, width), lambda i, where: (0, 0)),
            ]
            + [block] * count,
            out_specs=[block, block],
        ),
        out_shape=[jax.ShapeDtypeStruct((rows, width), BF), jax.ShapeDtypeStruct((rows, width), F32)],
        compiler_params=params(56),
        name="moe_norm",
    )(where, x, gain.reshape(1, width), *parts)


def join_kernel(where_ref, *refs):
    parts, out_ref = refs[:-1], refs[-1]
    rows = parts[0].shape[0]
    for mask, ref in enumerate(parts):
        out_ref[pl.ds(pl.multiple_of((where_ref[2] ^ mask) * rows, rows), rows), :] = ref[...]


def join_rows(where, parts):
    rows, width = parts[0].shape
    vmem = pl.BlockSpec(memory_space=pltpu.VMEM)
    return pl.pallas_call(
        join_kernel,
        in_specs=[pl.BlockSpec(memory_space=pltpu.SMEM)] + [vmem] * len(parts),
        out_shape=jax.ShapeDtypeStruct((len(parts) * rows, width), BF),
        compiler_params=params(16),
        name="join_rows",
    )(where, *parts)


PAIR = 2


def expert_kernel(masks, chunk, experts, where_ref, routes_ref, gate_hbm, up_hbm, down_hbm, *refs):
    row_refs, (out_ref, rows_ref, gate_ref, up_ref, down_ref, sems, weight_sems) = refs[: len(masks)], refs[len(masks) :]
    _, tok, width = out_ref.shape
    steps = len(masks) // PAIR
    step = pl.program_id(0)
    slot = lax.rem(step, 2)
    loads = [
        pltpu.make_async_copy(source.at[0], target, weight_sems.at[at])
        for at, (source, target) in enumerate(((gate_hbm, gate_ref), (up_hbm, up_ref), (down_hbm, down_ref)))
    ]

    def start(at):
        for part in range(PAIR):
            target = rows_ref.at[at % 2, pl.ds(part * tok, tok)]
            pltpu.make_async_copy(row_refs[PAIR * at + part], target, sems.at[at % 2]).start()

    def ready(at):
        @pl.when(step == 0)
        def _():
            loads[at].wait()

    @pl.when(step == 0)
    def _():
        start(0)
        for load in loads:
            load.start()

    for at in range(1, steps):

        @pl.when(step == at - 1)
        def _(at=at):
            start(at)

    here = lax.broadcasted_iota(jnp.int32, (3 * experts, LANES), 0)
    mine = (here == where_ref[1]) | (here == where_ref[1] + experts) | (here == where_ref[1] + 2 * experts)
    square = (LANES, LANES)
    diagonal = lax.broadcasted_iota(jnp.int32, square, 0) == lax.broadcasted_iota(jnp.int32, square, 1)
    weights = []
    for part in range(PAIR):
        index = jnp.int32(masks[part] // 2)
        for at in range(1, steps):
            index = jnp.where(step == at, masks[PAIR * at + part] // 2, index)
        for block in range(tok // LANES):
            base = (chunk // LANES + block) * 3 * experts
            table = routes_ref[index, base : base + 3 * experts, :].astype(F32)
            row = jnp.sum(jnp.where(mine, table, 0.0), axis=0, keepdims=True)
            weights.append(jnp.sum(jnp.where(diagonal, jnp.broadcast_to(row, square), 0.0), axis=1, keepdims=True))

    pltpu.make_async_copy(rows_ref.at[slot], rows_ref.at[slot], sems.at[slot]).wait()
    tokens = rows_ref[slot]
    ready(0)
    gate = mm(tokens, gate_ref[...])
    ready(1)
    inner = (gate * jax.nn.sigmoid(gate) * mm(tokens, up_ref[...])).astype(BF)
    ready(2)
    cols = pick_block(width, 512)
    for begin in range(0, width, cols):
        piece = mm(inner, down_ref[:, begin : begin + cols])
        for at, weight in enumerate(weights):
            part, row = divmod(at * LANES, tok)
            scaled = piece[at * LANES : (at + 1) * LANES] * weight
            out_ref[part, row : row + LANES, begin : begin + cols] = scaled.astype(BF)


def expert_pieces(chunk, where, blocks, masks, gate, up, down, routes):
    tok, width = blocks[0].shape
    hidden = gate.shape[2]
    count = len(blocks)
    experts = 2 * EXP_CTX * routes.shape[0]
    route_rows = CHUNKS * tok // LANES * 3 * experts
    hbm = pl.BlockSpec(memory_space=pltpu.HBM)
    return pl.pallas_call(
        functools.partial(expert_kernel, tuple(masks), chunk, experts),
        grid=(count // PAIR,),
        in_specs=[
            pl.BlockSpec(memory_space=pltpu.SMEM),
            pl.BlockSpec((routes.shape[0], route_rows, LANES), lambda i: (0, 0, 0)),
        ]
        + [hbm] * 3
        + [pl.BlockSpec(memory_space=pl.ANY)] * count,
        out_specs=pl.BlockSpec((PAIR, tok, width), lambda i: (i, 0, 0)),
        out_shape=jax.ShapeDtypeStruct((count, tok, width), BF),
        scratch_shapes=[
            pltpu.VMEM((2, PAIR * tok, width), BF),
            pltpu.VMEM(gate.shape[1:], BF),
            pltpu.VMEM(up.shape[1:], BF),
            pltpu.VMEM(down.shape[1:], BF),
            pltpu.SemaphoreType.DMA((2,)),
            pltpu.SemaphoreType.DMA((3,)),
        ],
        compiler_params=params(60),
        cost_estimate=pl.CostEstimate(
            flops=6 * count * tok * width * hidden,
            bytes_accessed=4 * count * tok * width,
            transcendentals=count * tok * hidden,
        ),
        name="expert_pieces",
    )(where, routes, gate, up, down, *blocks)


CORE, ROW, COL = 1, 2, 4
PLANE = 8


def swap(value, mask, keep=None):
    count = lax.axis_size("ctx")
    pairs = [(at, at ^ mask) for at in range(count)]
    return lax.ppermute(value, "ctx", [pair for pair in pairs if keep is None or keep(*pair)])


def send_heads(parts):
    count = lax.axis_size("head")
    return [parts[0]] + [
        lax.ppermute(parts[mask], "head", [(at, at ^ mask) for at in range(count)]) for mask in range(1, count)
    ]


def spread_states(own, keep=None):
    near = jnp.stack([own] + [swap(own, mask, keep) for mask in range(2, lax.axis_size("ctx"), 2)])
    return near, swap(near, CORE)


def hops(chunk):
    return (ROW, COL) if chunk % 2 == 0 else (COL, ROW)


def spread_rows(own, chunk):
    count = lax.axis_size("ctx")
    near = {0: own}
    if count == PLANE:
        first, second = hops(chunk)
        near[first] = swap(own, first)
        near[second] = swap(own, second)
        near[ROW | COL] = swap(near[first], second)
    else:
        for mask in range(2, count, 2):
            near[mask] = swap(own, mask)
    return near | {mask | CORE: swap(rows, CORE) for mask, rows in near.items()}


def plus(*terms):
    return functools.reduce(jnp.add, [term.astype(F32) for term in terms]).astype(BF)


def collect_terms(near, far, evens, chunk):
    arrived = swap(far, CORE)
    sums = {mask: (near[at], arrived[at]) for at, mask in enumerate(evens)}
    if lax.axis_size("ctx") == PLANE:
        first, second = hops(chunk)
        across = swap(plus(*sums[ROW | COL]), second)
        direct, across = lax.optimization_barrier((plus(*sums[second]), across))
        others = [swap(plus(*sums[first], across), first), swap(direct, second)]
    else:
        others = [swap(plus(*sums[mask]), mask) for mask in evens[1:]]
    return arrived, others


def sum_kernel(where_ref, attn_ref, near_ref, arrived_ref, *refs):
    parts = attn_ref.shape[1] // refs[-1].shape[1]
    others, outs, total_ref = refs[: -parts - 1], refs[-parts - 1 : -1], refs[-1]
    part, width = attn_ref.shape
    cols = width // parts
    own = pl.ds(pl.multiple_of(where_ref[2] * part, part), part)
    for mask, out_ref in enumerate(outs):
        at = pl.ds(pl.multiple_of((where_ref[2] ^ mask) * cols, cols), cols)
        total = near_ref[0, :, at].astype(F32) + arrived_ref[0, :, at].astype(F32)
        for ref in others:
            total += ref[:, at].astype(F32)
        total_ref[...] = total
        total_ref[own, :] += attn_ref[:, at]
        out_ref[...] = total_ref[...].astype(BF)


def sum_terms(where, attn, near, arrived, others, parts):
    _, tok, width = near.shape
    part = attn.shape[0]
    cols = width // parts
    first = pl.BlockSpec((1, tok, width), lambda i: (0, 0, 0))
    return pl.pallas_call(
        sum_kernel,
        grid=(1,),
        in_specs=[
            pl.BlockSpec(memory_space=pltpu.SMEM),
            pl.BlockSpec((part, width), lambda i: (0, 0)),
            first,
            first,
        ]
        + [pl.BlockSpec((tok, width), lambda i: (0, 0))] * len(others),
        out_specs=[pl.BlockSpec((tok, cols), lambda i: (0, 0))] * parts,
        out_shape=[jax.ShapeDtypeStruct((tok, cols), BF)] * parts,
        scratch_shapes=[pltpu.VMEM((tok, cols), F32)],
        compiler_params=params(24),
        name="sum_terms",
    )(where, attn, near, arrived, *others)


def final_kernel(where_ref, x_ref, *refs):
    del where_ref
    out_ref = refs[-1]
    terms = [x_ref[...]] + [ref[...] for ref in refs[:-1]]
    out_ref[...] = functools.reduce(jnp.add, [term.astype(F32) for term in terms]).astype(BF)


def final_sum(chunk, where, x, parts):
    rows, cols = parts[0].shape
    block = pl.BlockSpec((rows, cols), lambda i, where: (0, 0))
    return pl.pallas_call(
        final_kernel,
        grid_spec=pltpu.PrefetchScalarGridSpec(
            num_scalar_prefetch=1,
            grid=(1,),
            in_specs=[pl.BlockSpec((rows, cols), lambda i, where: (chunk, where[2]))] + [block] * len(parts),
            out_specs=block,
        ),
        out_shape=jax.ShapeDtypeStruct((rows, cols), BF),
        compiler_params=params(56),
        name="layer_out",
    )(where, x, *parts)


CHUNKS = 2


def body(
    hidden_in,
    gain_attn,
    w_qkv,
    conv_w,
    log_decay,
    norm_gain,
    w_out,
    gain_moe,
    expert_ids,
    route_weights,
    w_gate,
    w_up,
    w_down,
    grad_core,
):
    n_ctx, n_head = lax.axis_size("ctx"), lax.axis_size("head")
    my_ctx, my_head = lax.axis_index("ctx"), lax.axis_index("head")
    experts = EXP_CTX * n_ctx
    shards = n_head // EXP_CTX
    where = jnp.stack([my_ctx, EXP_CTX * my_ctx + my_head // shards, my_head]).astype(jnp.int32)
    steps = log_decay.T
    chunk_rows = hidden_in.shape[0] // CHUNKS

    mixed, rim = project(hidden_in, gain_attn, jnp.transpose(w_qkv, (1, 0, 2)))
    rim = lax.ppermute(rim, "ctx", [(at, at + 1) for at in range(n_ctx - 1)])
    qkv, fwd, bwd = local_states(
        mixed, rim, jnp.transpose(conv_w, (1, 0, 2)), steps, grad_core, expert_ids.T, route_weights.T, experts
    )
    fwd = spread_states(fwd, lambda source, target: source < target)
    partials = core_out(where, qkv, steps, *fwd, norm_gain, w_out, CHUNKS, n_head)
    bwd, partials = lax.optimization_barrier((bwd, partials))
    parts = [send_heads(chunk) for chunk in partials]
    bwd = spread_states(bwd)
    parts[1], bwd = lax.optimization_barrier((parts[1], bwd))
    attn, own = [], []
    for chunk in range(CHUNKS):
        normed, total = norm_rows(chunk, where, hidden_in, parts[chunk], gain_moe)
        attn.append(total)
        own.append(join_rows(where, send_heads([normed] * n_head)))
    layer_out = []
    for chunk in range(CHUNKS):
        rows = spread_rows(own[chunk], chunk)
        evens = [mask for mask in rows if not mask & CORE]
        near, far = (
            expert_pieces(
                chunk * chunk_rows, where, [rows[mask] for mask in masks], masks, w_gate, w_up, w_down, routes
            )
            for masks, routes in ((evens, bwd[0]), ([mask | CORE for mask in evens], bwd[1]))
        )
        arrived, others = collect_terms(near, far, evens, chunk)
        sums = send_heads(sum_terms(where, attn[chunk], near, arrived, others, n_head))
        layer_out.append(final_sum(chunk, where, hidden_in, sums))
    grads = core_grads(where, qkv, grad_core, steps, fwd, bwd)
    return (jnp.concatenate(layer_out), *grads)


def solution(mesh):
    in_specs = (
        P("ctx", None),
        P(),
        P(None, None, "head"),
        P(None, None, "head"),
        P("ctx", "head"),
        P("head"),
        P("head", None),
        P(),
        P("ctx", None),
        P("ctx", None),
        P(("ctx", "head"), None, None),
        P(("ctx", "head"), None, None),
        P(("ctx", "head"), None, None),
        P("ctx", "head"),
    )
    out_specs = (P("ctx", "head"), P("ctx", "head"), P("ctx", "head"), P("ctx", "head"))
    return jax.shard_map(body, mesh=mesh, in_specs=in_specs, out_specs=out_specs, check_vma=False)
```

```python
import functools

import jax
import jax.numpy as jnp
from jax import lax
from jax.experimental import pallas as pl
from jax.experimental.pallas import tpu as pltpu
from jax.sharding import PartitionSpec as P

KERNEL = 4
EXP_CTX = 2
LANES = 128
RIM = 16
MIB = 1024 * 1024
HI = lax.Precision.HIGHEST
BF = jnp.bfloat16
F32 = jnp.float32
NT = (((1,), (1,)), ((), ()))
TN = (((0,), (0,)), ((), ()))
NN = (((1,), (0,)), ((), ()))


def params(mib):
    return pltpu.CompilerParams(vmem_limit_bytes=mib * MIB)


def mm(a, b, dims=NN):
    return lax.dot_general(a, b, dims, preferred_element_type=F32)


def pick_block(extent, target):
    return target if extent % target == 0 else extent


def qkv_kernel(x_hbm, gain_ref, w_hbm, mixed_ref, rim_ref, x_ref, w_ref, normed_ref, x_sem, sems):
    kinds, width, chans = w_ref.shape
    load = pltpu.make_async_copy(x_hbm, x_ref, x_sem)
    load.start()
    copies = [pltpu.make_async_copy(w_hbm.at[kind], w_ref.at[kind], sems.at[kind]) for kind in range(kinds)]
    for copy in copies:
        copy.start()
    load.wait()
    values = x_ref[...].astype(F32)
    scale = lax.rsqrt(jnp.mean(values * values, axis=-1, keepdims=True) + 1e-06)
    normed_ref[...] = (values * scale * gain_ref[...]).astype(BF)
    for kind in range(kinds):
        copies[kind].wait()
        out = mm(normed_ref[...], w_ref[kind]).astype(BF)
        mixed_ref[kind] = out
        rim_ref[kind] = out[out.shape[0] - RIM :]


def project(x, gain, weights):
    rows, width = x.shape
    kinds, _, chans = weights.shape
    vmem = pl.BlockSpec(memory_space=pltpu.VMEM)
    hbm = pl.BlockSpec(memory_space=pltpu.HBM)
    return pl.pallas_call(
        qkv_kernel,
        in_specs=[hbm, vmem, hbm],
        out_shape=[
            jax.ShapeDtypeStruct((kinds, rows, chans), BF),
            jax.ShapeDtypeStruct((kinds, RIM, chans), BF),
        ],
        scratch_shapes=[
            pltpu.VMEM((rows, width), BF),
            pltpu.VMEM((kinds, width, chans), BF),
            pltpu.VMEM((rows, width), BF),
            pltpu.SemaphoreType.DMA,
            pltpu.SemaphoreType.DMA((kinds,)),
        ],
        compiler_params=params(61),
        name="qkv_projection",
    )(x, gain.reshape(1, width), weights)


def decay_sums(steps):
    rows = steps.shape[1]
    row_at = lax.broadcasted_iota(jnp.int32, (rows, rows), 0)
    col_at = lax.broadcasted_iota(jnp.int32, (rows, rows), 1)
    lower = row_at >= col_at
    tri = jnp.where(lower, 1.0, 0.0).astype(F32)
    along = lax.dot_general(steps, tri, NT, precision=HI, preferred_element_type=F32)
    down = lax.dot_general(tri, steps, NT, precision=HI, preferred_element_type=F32)
    return along, down, lower


def payload_tail(total, size):
    full = jnp.broadcast_to(total, (RIM, size))
    first = full.astype(BF).astype(F32)
    second = (full - first).astype(BF).astype(F32)
    third = full - first - second
    at = lax.broadcasted_iota(jnp.int32, (RIM, size), 0)
    return jnp.where(at == 0, first, jnp.where(at == 1, second, jnp.where(at == 2, third, 0.0)))


def route_rows(ids_ref, weights_ref, experts):
    top, tok = ids_ref.shape
    expert = lax.broadcasted_iota(jnp.int32, (experts, tok), 0)
    table = jnp.zeros((experts, tok), F32)
    for choice in range(top):
        table += jnp.where(expert == ids_ref[choice : choice + 1, :], weights_ref[choice : choice + 1, :], 0.0)
    first = table.astype(BF).astype(F32)
    second = (table - first).astype(BF).astype(F32)
    return jnp.concatenate([first, second, table - first - second], axis=0)


def conv_kernel(
    experts, mixed_ref, rim_ref, taps_ref, steps_ref, cot_ref, ids_ref, weights_ref, qkv_ref, fwd_ref, bwd_ref, pad_ref
):
    kinds, rows, chans = mixed_ref.shape
    heads = steps_ref.shape[0]
    size = chans // heads
    along, down, _ = decay_sums(steps_ref[...])
    for kind in range(kinds):
        pad_ref[:RIM] = rim_ref[kind].astype(F32)
        pad_ref[RIM:] = mixed_ref[kind].astype(F32)
        total = taps_ref[kind, 0:1, :] * pad_ref[RIM:]
        for offset in range(1, KERNEL):
            total += taps_ref[kind, offset : offset + 1, :] * pad_ref[RIM - offset : RIM - offset + rows]
        activ = total * jax.nn.sigmoid(total)
        if kind == 0:
            activ = activ * size ** (-0.5)
        qkv_ref[kind] = activ.astype(BF)
    routes = rows // LANES * 3 * experts
    table = route_rows(ids_ref, weights_ref, experts).astype(BF)
    for part in range(rows // LANES):
        bwd_ref[part * 3 * experts : (part + 1) * 3 * experts] = table[:, part * LANES : (part + 1) * LANES]
    for head in range(heads):
        at = slice(head * size, (head + 1) * size)
        base = head * (size + RIM)
        last = along[head : head + 1, rows - 1 : rows]
        lead = jnp.exp(down[:, head : head + 1])
        tail = jnp.exp(last - down[:, head : head + 1])
        key_out = (qkv_ref[1, :, at].astype(F32) * tail).astype(BF)
        query_out = (qkv_ref[0, :, at].astype(F32) * lead).astype(BF)
        ends = payload_tail(last, size).astype(BF)
        fwd_ref[base : base + size] = mm(key_out, qkv_ref[2, :, at], TN).astype(BF)
        fwd_ref[base + size : base + size + RIM] = ends
        base += routes
        bwd_ref[base : base + size] = mm(query_out, cot_ref[:, at], TN).astype(BF)
        bwd_ref[base + size : base + size + RIM] = ends


def local_states(mixed, rim, taps, steps, cot, ids, weights, experts):
    kinds, rows, chans = mixed.shape
    heads = steps.shape[0]
    size = chans // heads
    states = heads * (size + RIM)
    return pl.pallas_call(
        functools.partial(conv_kernel, experts),
        out_shape=[
            jax.ShapeDtypeStruct((kinds, rows, chans), BF),
            jax.ShapeDtypeStruct((states, size), BF),
            jax.ShapeDtypeStruct((states + rows // LANES * 3 * experts, size), BF),
        ],
        scratch_shapes=[pltpu.VMEM((rows + RIM, chans), F32)],
        compiler_params=params(12),
        name="conv_states",
    )(mixed, rim, taps, steps, cot, ids, weights)


def arrange(me_ref, near_ref, far_ref, held_ref):
    for at in range(near_ref.shape[0]):
        held_ref[me_ref[0] ^ (2 * at)] = near_ref[at]
        held_ref[me_ref[0] ^ (2 * at + 1)] = far_ref[at]


def entering(held_ref, heads, head, size, first, last, step):
    base = held_ref.shape[1] - (heads - head) * (size + RIM)

    def hop(count, total):
        at = first + count * step
        ends = held_ref[at, base + size : base + size + RIM, :].astype(F32)
        factor = jnp.exp(ends[0:1] + ends[1:2] + ends[2:3])
        return factor * total + held_ref[at, base : base + size, :].astype(F32)

    return lax.fori_loop(0, (last - first) * step, hop, jnp.zeros((size, size), F32))


def core_kernel(chunks, me_ref, qkv_ref, steps_ref, gain_ref, near_ref, far_ref, w_hbm, *refs):
    out_refs, (headed_ref, held_ref, w_ref, whole_ref, sem) = refs[:-5], refs[-5:]
    load = pltpu.make_async_copy(w_hbm, w_ref, sem)
    load.start()
    _, rows, chans = qkv_ref.shape
    heads = steps_ref.shape[0]
    size = chans // heads
    arrange(me_ref, near_ref, far_ref, held_ref)
    along, down, lower = decay_sums(steps_ref[...])
    for head in range(heads):
        at = slice(head * size, (head + 1) * size)
        state = entering(held_ref, heads, head, size, 0, me_ref[0], 1).astype(BF)
        diff = down[:, head : head + 1] - along[head : head + 1, :]
        mask = jnp.exp(jnp.where(lower, diff, -jnp.inf))
        query = qkv_ref[0, :, at]
        scores = (mm(query, qkv_ref[1, :, at], NT) * mask).astype(BF)
        attended = mm(scores, qkv_ref[2, :, at])
        attended += mm(query, state) * jnp.exp(down[:, head : head + 1])
        scale = lax.rsqrt(jnp.mean(attended * attended, axis=-1, keepdims=True) + 1e-06)
        headed_ref[:, at] = (attended * scale * gain_ref[:, at]).astype(BF)
    load.wait()
    whole_ref[...] = mm(headed_ref[...], w_ref[...]).astype(BF)
    part = rows // len(out_refs) // chunks
    for mask, ref in enumerate(out_refs):
        for chunk in range(chunks):
            start = chunk * len(out_refs) * part + (me_ref[2] ^ mask) * part
            ref[chunk * part : (chunk + 1) * part] = whole_ref[pl.ds(pl.multiple_of(start, part), part), :]


def core_out(where, qkv, steps, near, far, gain, w_out, chunks, parts):
    _, rows, chans = qkv.shape
    width = w_out.shape[1]
    vmem = pl.BlockSpec(memory_space=pltpu.VMEM)
    return pl.pallas_call(
        functools.partial(core_kernel, chunks),
        in_specs=[pl.BlockSpec(memory_space=pltpu.SMEM)] + [vmem] * 5 + [pl.BlockSpec(memory_space=pltpu.HBM)],
        out_shape=[jax.ShapeDtypeStruct((rows // parts, width), BF)] * parts,
        scratch_shapes=[
            pltpu.VMEM((rows, chans), BF),
            pltpu.VMEM((2 * near.shape[0], *near.shape[1:]), BF),
            pltpu.VMEM(w_out.shape, BF),
            pltpu.VMEM((rows, width), BF),
            pltpu.SemaphoreType.DMA,
        ],
        compiler_params=params(56),
        name="core_out",
    )(where, qkv, steps, gain.reshape(1, chans), near, far, w_out)


def grad_kernel(
    me_ref, qkv_ref, cot_ref, steps_ref, fwd_near, fwd_far, bwd_near, bwd_far, gq_ref, gk_ref, gv_ref, fwd_ref, bwd_ref
):
    _, rows, chans = qkv_ref.shape
    heads = steps_ref.shape[0]
    size = chans // heads
    count = fwd_ref.shape[0]
    arrange(me_ref, fwd_near, fwd_far, fwd_ref)
    arrange(me_ref, bwd_near, bwd_far, bwd_ref)
    along, down, lower = decay_sums(steps_ref[...])
    for head in range(heads):
        at = slice(head * size, (head + 1) * size)
        state = entering(fwd_ref, heads, head, size, 0, me_ref[0], 1).astype(BF)
        after = entering(bwd_ref, heads, head, size, count - 1, me_ref[0], -1).astype(BF)
        here = down[:, head : head + 1]
        lead = jnp.exp(here)
        tail = jnp.exp(along[head : head + 1, rows - 1 : rows] - here)
        mask = jnp.exp(jnp.where(lower, here - along[head : head + 1, :], -jnp.inf))
        query, key, val = qkv_ref[0, :, at], qkv_ref[1, :, at], qkv_ref[2, :, at]
        cot = cot_ref[:, at]
        scores = (mm(query, key, NT) * mask).astype(BF)
        dov = (mm(cot, val, NT) * mask).astype(BF)
        gq_ref[:, at] = (mm(dov, key) + lead * mm(cot, state, NT)).astype(BF)
        gk_ref[:, at] = (mm(dov, query, TN) + tail * mm(val, after, NT)).astype(BF)
        gv_ref[:, at] = (mm(scores, cot, TN) + tail * mm(key, after)).astype(BF)


def core_grads(where, qkv, cot, steps, fwd, bwd):
    _, rows, chans = qkv.shape
    count = 2 * fwd[0].shape[0]
    vmem = pl.BlockSpec(memory_space=pltpu.VMEM)
    return pl.pallas_call(
        grad_kernel,
        in_specs=[pl.BlockSpec(memory_space=pltpu.SMEM)] + [vmem] * 7,
        out_shape=[jax.ShapeDtypeStruct((rows, chans), BF)] * 3,
        scratch_shapes=[pltpu.VMEM((count, *fwd[0].shape[1:]), BF), pltpu.VMEM((count, *bwd[0].shape[1:]), BF)],
        compiler_params=params(24),
        name="core_grads",
    )(where, qkv, cot, steps, *fwd, *bwd)


def norm_kernel(count, where_ref, x_ref, gain_ref, *refs):
    chunks = (len(refs) - count) // 2
    parts, outs, attns = refs[:count], refs[count : count + chunks], refs[count + chunks :]
    rows = outs[0].shape[0]
    for chunk, (out_ref, attn_ref) in enumerate(zip(outs, attns)):
        at = slice(chunk * rows, (chunk + 1) * rows)
        attn = functools.reduce(jnp.add, [part[at].astype(F32) for part in parts])
        attn_ref[...] = attn
        start = pl.multiple_of((chunk * count + where_ref[2]) * rows, rows)
        resid = x_ref[pl.ds(start, rows), :].astype(F32) + attn
        scale = lax.rsqrt(jnp.mean(resid * resid, axis=-1, keepdims=True) + 1e-06)
        out_ref[...] = (resid * scale * gain_ref[...]).astype(BF)


def norm_rows(where, x, parts, gain, chunks):
    rows, width = parts[0].shape[0] // chunks, parts[0].shape[1]
    vmem = pl.BlockSpec(memory_space=pltpu.VMEM)
    outs = pl.pallas_call(
        functools.partial(norm_kernel, len(parts)),
        in_specs=[pl.BlockSpec(memory_space=pltpu.SMEM)] + [vmem] * (2 + len(parts)),
        out_shape=[jax.ShapeDtypeStruct((rows, width), BF)] * chunks
        + [jax.ShapeDtypeStruct((rows, width), F32)] * chunks,
        compiler_params=params(12),
        name="moe_norm",
    )(where, x, gain.reshape(1, width), *parts)
    return outs[:chunks], outs[chunks:]


def join_kernel(where_ref, *refs):
    parts, out_ref = refs[:-1], refs[-1]
    rows = parts[0].shape[0]
    for mask, ref in enumerate(parts):
        out_ref[pl.ds(pl.multiple_of((where_ref[2] ^ mask) * rows, rows), rows), :] = ref[...]


def join_rows(where, parts):
    rows, width = parts[0].shape
    vmem = pl.BlockSpec(memory_space=pltpu.VMEM)
    return pl.pallas_call(
        join_kernel,
        in_specs=[pl.BlockSpec(memory_space=pltpu.SMEM)] + [vmem] * len(parts),
        out_shape=jax.ShapeDtypeStruct((len(parts) * rows, width), BF),
        compiler_params=params(16),
        name="join_rows",
    )(where, *parts)


PAIR = 2


def expert_kernel(masks, chunk, experts, where_ref, near_routes, far_routes, gate_hbm, up_hbm, down_hbm, *refs):
    row_refs, (near_ref, far_ref, rows_ref, gate_ref, up_ref, down_ref, sems, weight_sems) = (
        refs[: len(masks)],
        refs[len(masks) :],
    )
    _, tok, width = near_ref.shape
    steps = len(masks) // PAIR
    step = pl.program_id(0)
    slot = lax.rem(step, 2)
    loads = [
        pltpu.make_async_copy(source.at[0], target, weight_sems.at[at])
        for at, (source, target) in enumerate(((gate_hbm, gate_ref), (up_hbm, up_ref), (down_hbm, down_ref)))
    ]

    def start(at):
        for part in range(PAIR):
            target = rows_ref.at[at % 2, pl.ds(part * tok, tok)]
            pltpu.make_async_copy(row_refs[PAIR * at + part], target, sems.at[at % 2]).start()

    def ready(at):
        @pl.when(step == 0)
        def _():
            loads[at].wait()

    @pl.when(step == 0)
    def _():
        start(0)
        for load in loads:
            load.start()

    for at in range(1, steps):

        @pl.when(step == at - 1)
        def _(at=at):
            start(at)

    here = lax.broadcasted_iota(jnp.int32, (3 * experts, LANES), 0)
    mine = (here == where_ref[1]) | (here == where_ref[1] + experts) | (here == where_ref[1] + 2 * experts)
    square = (LANES, LANES)
    diagonal = lax.broadcasted_iota(jnp.int32, square, 0) == lax.broadcasted_iota(jnp.int32, square, 1)
    is_near = step < steps // 2
    weights = []
    for part in range(PAIR):
        index = jnp.int32(masks[part] // 2)
        for at in range(1, steps):
            index = jnp.where(step == at, masks[PAIR * at + part] // 2, index)
        for block in range(tok // LANES):
            base = (chunk // LANES + block) * 3 * experts
            at = slice(base, base + 3 * experts)
            table = jnp.where(is_near, near_routes[index, at, :].astype(F32), far_routes[index, at, :].astype(F32))
            row = jnp.sum(jnp.where(mine, table, 0.0), axis=0, keepdims=True)
            weights.append(jnp.sum(jnp.where(diagonal, jnp.broadcast_to(row, square), 0.0), axis=1, keepdims=True))

    pltpu.make_async_copy(rows_ref.at[slot], rows_ref.at[slot], sems.at[slot]).wait()
    tokens = rows_ref[slot]
    ready(0)
    gate = mm(tokens, gate_ref[...])
    ready(1)
    inner = (gate * jax.nn.sigmoid(gate) * mm(tokens, up_ref[...])).astype(BF)
    ready(2)
    cols = pick_block(width, 512)
    for begin in range(0, width, cols):
        piece = mm(inner, down_ref[:, begin : begin + cols])
        for at, weight in enumerate(weights):
            part, row = divmod(at * LANES, tok)
            scaled = (piece[at * LANES : (at + 1) * LANES] * weight).astype(BF)

            @pl.when(is_near)
            def _(scaled=scaled, part=part, row=row):
                near_ref[part, row : row + LANES, begin : begin + cols] = scaled

            @pl.when(jnp.logical_not(is_near))
            def _(scaled=scaled, part=part, row=row):
                far_ref[part, row : row + LANES, begin : begin + cols] = scaled


def expert_pieces(chunk, where, rows, evens, gate, up, down, routes):
    masks = list(evens) + [mask | CORE for mask in evens]
    blocks = [rows[mask] for mask in masks]
    tok, width = blocks[0].shape
    hidden = gate.shape[2]
    count = len(blocks)
    half = count // PAIR // 2
    experts = EXP_CTX * count
    route_rows = CHUNKS * tok // LANES * 3 * experts
    hbm = pl.BlockSpec(memory_space=pltpu.HBM)
    piece = jax.ShapeDtypeStruct((count // 2, tok, width), BF)
    table = pl.BlockSpec((count // 2, route_rows, LANES), lambda i: (0, 0, 0))
    return pl.pallas_call(
        functools.partial(expert_kernel, tuple(masks), chunk, experts),
        grid=(count // PAIR,),
        in_specs=[pl.BlockSpec(memory_space=pltpu.SMEM), table, table]
        + [hbm] * 3
        + [pl.BlockSpec(memory_space=pl.ANY)] * count,
        out_specs=[
            pl.BlockSpec((PAIR, tok, width), lambda i: (jnp.minimum(i, half - 1), 0, 0)),
            pl.BlockSpec((PAIR, tok, width), lambda i: (jnp.maximum(i - half, 0), 0, 0)),
        ],
        out_shape=[piece, piece],
        scratch_shapes=[
            pltpu.VMEM((2, PAIR * tok, width), BF),
            pltpu.VMEM(gate.shape[1:], BF),
            pltpu.VMEM(up.shape[1:], BF),
            pltpu.VMEM(down.shape[1:], BF),
            pltpu.SemaphoreType.DMA((2,)),
            pltpu.SemaphoreType.DMA((3,)),
        ],
        compiler_params=params(60),
        cost_estimate=pl.CostEstimate(
            flops=6 * count * tok * width * hidden,
            bytes_accessed=4 * count * tok * width,
            transcendentals=count * tok * hidden,
        ),
        name="expert_pieces",
    )(where, *routes, gate, up, down, *blocks)


CORE = 1


def swap(value, mask, keep=None):
    count = lax.axis_size("ctx")
    pairs = [(at, at ^ mask) for at in range(count)]
    return lax.ppermute(value, "ctx", [pair for pair in pairs if keep is None or keep(*pair)])


def send_heads(parts):
    count = lax.axis_size("head")
    return [parts[0]] + [
        lax.ppermute(parts[mask], "head", [(at, at ^ mask) for at in range(count)]) for mask in range(1, count)
    ]


def spread_near(own, keep=None):
    return jnp.stack([own] + [swap(own, mask, keep) for mask in range(2, lax.axis_size("ctx"), 2)])


def plus(*terms):
    return functools.reduce(jnp.add, [term.astype(F32) for term in terms]).astype(BF)


def after(value, other):
    return lax.optimization_barrier((value, other))[0]


def sum_kernel(where_ref, attn_ref, near_ref, arrived_ref, *refs):
    parts = attn_ref.shape[1] // refs[-1].shape[1]
    others, outs, total_ref = refs[: -parts - 1], refs[-parts - 1 : -1], refs[-1]
    part, width = attn_ref.shape
    cols = width // parts
    own = pl.ds(pl.multiple_of(where_ref[2] * part, part), part)
    for mask, out_ref in enumerate(outs):
        at = pl.ds(pl.multiple_of((where_ref[2] ^ mask) * cols, cols), cols)
        total = near_ref[0, :, at].astype(F32) + arrived_ref[0, :, at].astype(F32)
        for ref in others:
            total += ref[:, at].astype(F32)
        total_ref[...] = total
        total_ref[own, :] += attn_ref[:, at]
        out_ref[...] = total_ref[...].astype(BF)


def sum_terms(where, attn, near, arrived, others, parts):
    _, tok, width = near.shape
    part = attn.shape[0]
    cols = width // parts
    first = pl.BlockSpec((1, tok, width), lambda i: (0, 0, 0))
    return pl.pallas_call(
        sum_kernel,
        grid=(1,),
        in_specs=[
            pl.BlockSpec(memory_space=pltpu.SMEM),
            pl.BlockSpec((part, width), lambda i: (0, 0)),
            first,
            first,
        ]
        + [pl.BlockSpec((tok, width), lambda i: (0, 0))] * len(others),
        out_specs=[pl.BlockSpec((tok, cols), lambda i: (0, 0))] * parts,
        out_shape=[jax.ShapeDtypeStruct((tok, cols), BF)] * parts,
        scratch_shapes=[pltpu.VMEM((tok, cols), F32)],
        compiler_params=params(24),
        name="sum_terms",
    )(where, attn, near, arrived, *others)


def final_kernel(count, where_ref, x_ref, *refs):
    del where_ref
    out_ref = refs[-1]
    rows = refs[0].shape[0]
    for chunk in range((len(refs) - 1) // count):
        at = slice(chunk * rows, (chunk + 1) * rows)
        terms = [x_ref[at]] + [ref[...] for ref in refs[chunk * count : (chunk + 1) * count]]
        out_ref[at] = functools.reduce(jnp.add, [term.astype(F32) for term in terms]).astype(BF)


def final_sum(where, x, parts):
    rows, cols = parts[0][0].shape
    total = len(parts) * rows
    block = pl.BlockSpec((rows, cols), lambda i, where: (0, 0))
    return pl.pallas_call(
        functools.partial(final_kernel, len(parts[0])),
        grid_spec=pltpu.PrefetchScalarGridSpec(
            num_scalar_prefetch=1,
            grid=(1,),
            in_specs=[pl.BlockSpec((total, cols), lambda i, where: (0, where[2]))]
            + [block] * (len(parts) * len(parts[0])),
            out_specs=pl.BlockSpec((total, cols), lambda i, where: (0, 0)),
        ),
        out_shape=jax.ShapeDtypeStruct((total, cols), BF),
        compiler_params=params(12),
        name="layer_out",
    )(where, x, *[part for chunk in parts for part in chunk])


CHUNKS = 2


def body(
    hidden_in,
    gain_attn,
    w_qkv,
    conv_w,
    log_decay,
    norm_gain,
    w_out,
    gain_moe,
    expert_ids,
    route_weights,
    w_gate,
    w_up,
    w_down,
    grad_core,
):
    n_ctx, n_head = lax.axis_size("ctx"), lax.axis_size("head")
    my_ctx, my_head = lax.axis_index("ctx"), lax.axis_index("head")
    experts = EXP_CTX * n_ctx
    shards = n_head // EXP_CTX
    where = jnp.stack([my_ctx, EXP_CTX * my_ctx + my_head // shards, my_head]).astype(jnp.int32)
    steps = log_decay.T
    chunk_rows = hidden_in.shape[0] // CHUNKS

    mixed, rim = project(hidden_in, gain_attn, jnp.transpose(w_qkv, (1, 0, 2)))
    rim = lax.ppermute(rim, "ctx", [(at, at + 1) for at in range(n_ctx - 1)])
    qkv, fwd, bwd = local_states(
        mixed, rim, jnp.transpose(conv_w, (1, 0, 2)), steps, grad_core, expert_ids.T, route_weights.T, experts
    )
    fwd = spread_near(fwd, lambda source, target: source < target)
    fwd = (fwd, swap(fwd, CORE))
    parts = core_out(where, qkv, steps, *fwd, norm_gain, w_out, CHUNKS, n_head)
    bwd = spread_near(after(bwd, parts))
    normed, attn = norm_rows(where, hidden_in, after(send_heads(parts), bwd), gain_moe, CHUNKS)
    bwd = after(bwd, normed)
    bwd = (bwd, swap(bwd, CORE))

    evens = list(range(0, n_ctx, 2))
    near, rows = [], []
    own = join_rows(where, send_heads([normed[0]] * n_head))
    for chunk in range(CHUNKS):
        near.append([own] + [swap(own, mask) for mask in evens[1:]])
        if chunk + 1 < CHUNKS:
            own = join_rows(where, send_heads([after(normed[chunk + 1], own)] * n_head))
            near[chunk] = after(near[chunk], own)
    for chunk in range(CHUNKS):
        rows.append({mask: part for mask, part in zip(evens, near[chunk])})
        rows[chunk] |= {mask | CORE: swap(part, CORE) for mask, part in rows[chunk].items()}

    sums, pending = [], []
    for chunk in range(CHUNKS):
        here, far = expert_pieces(chunk * chunk_rows, where, rows[chunk], evens, w_gate, w_up, w_down, bwd)
        arrived = swap(far, CORE)
        leaving = [plus(here[at], arrived[at]) for at in range(1, len(evens))]
        if chunk + 1 < CHUNKS:
            rows[chunk + 1] = after(rows[chunk + 1], leaving)
        others = [swap(part, mask) for part, mask in zip(leaving, evens[1:])]
        pending.append((here, arrived, others, leaving))
    for chunk in range(CHUNKS):
        here, arrived, others, _ = pending[chunk]
        if chunk + 1 < CHUNKS:
            others = after(others, pending[chunk + 1][3])
        sums.append(send_heads(sum_terms(where, attn[chunk], here, arrived, others, n_head)))
    grads = core_grads(where, qkv, grad_core, steps, fwd, bwd)
    return (final_sum(where, hidden_in, sums), *grads)


def solution(mesh):
    in_specs = (
        P("ctx", None),
        P(),
        P(None, None, "head"),
        P(None, None, "head"),
        P("ctx", "head"),
        P("head"),
        P("head", None),
        P(),
        P("ctx", None),
        P("ctx", None),
        P(("ctx", "head"), None, None),
        P(("ctx", "head"), None, None),
        P(("ctx", "head"), None, None),
        P("ctx", "head"),
    )
    out_specs = (P("ctx", "head"), P("ctx", "head"), P("ctx", "head"), P("ctx", "head"))
    return jax.shard_map(body, mesh=mesh, in_specs=in_specs, out_specs=out_specs, check_vma=False)
```

```python
import functools

import jax
import jax.numpy as jnp
from jax import lax
from jax.experimental import pallas as pl
from jax.experimental.pallas import tpu as pltpu
from jax.sharding import PartitionSpec as P

KERNEL = 4
EXP_CTX = 2
LANES = 128
RIM = 16
MIB = 1024 * 1024
HI = lax.Precision.HIGHEST
BF = jnp.bfloat16
F32 = jnp.float32
NT = (((1,), (1,)), ((), ()))
TN = (((0,), (0,)), ((), ()))
NN = (((1,), (0,)), ((), ()))


def params(mib):
    return pltpu.CompilerParams(vmem_limit_bytes=mib * MIB)


def mm(a, b, dims=NN):
    return lax.dot_general(a, b, dims, preferred_element_type=F32)


def pick_block(extent, target):
    return target if extent % target == 0 else extent


def qkv_kernel(x_hbm, gain_ref, w_hbm, mixed_ref, rim_ref, x_ref, w_ref, normed_ref, x_sem, sems):
    kinds, width, chans = w_ref.shape
    load = pltpu.make_async_copy(x_hbm, x_ref, x_sem)
    load.start()
    copies = [pltpu.make_async_copy(w_hbm.at[kind], w_ref.at[kind], sems.at[kind]) for kind in range(kinds)]
    for copy in copies:
        copy.start()
    load.wait()
    values = x_ref[...].astype(F32)
    scale = lax.rsqrt(jnp.mean(values * values, axis=-1, keepdims=True) + 1e-06)
    normed_ref[...] = (values * scale * gain_ref[...]).astype(BF)
    for kind in range(kinds):
        copies[kind].wait()
        out = mm(normed_ref[...], w_ref[kind]).astype(BF)
        mixed_ref[kind] = out
        rim_ref[kind] = out[out.shape[0] - RIM :]


def project(x, gain, weights):
    rows, width = x.shape
    kinds, _, chans = weights.shape
    vmem = pl.BlockSpec(memory_space=pltpu.VMEM)
    hbm = pl.BlockSpec(memory_space=pltpu.HBM)
    return pl.pallas_call(
        qkv_kernel,
        in_specs=[hbm, vmem, hbm],
        out_shape=[
            jax.ShapeDtypeStruct((kinds, rows, chans), BF),
            jax.ShapeDtypeStruct((kinds, RIM, chans), BF),
        ],
        scratch_shapes=[
            pltpu.VMEM((rows, width), BF),
            pltpu.VMEM((kinds, width, chans), BF),
            pltpu.VMEM((rows, width), BF),
            pltpu.SemaphoreType.DMA,
            pltpu.SemaphoreType.DMA((kinds,)),
        ],
        compiler_params=params(61),
        name="qkv_projection",
    )(x, gain.reshape(1, width), weights)


def decay_sums(steps):
    rows = steps.shape[1]
    row_at = lax.broadcasted_iota(jnp.int32, (rows, rows), 0)
    col_at = lax.broadcasted_iota(jnp.int32, (rows, rows), 1)
    lower = row_at >= col_at
    tri = jnp.where(lower, 1.0, 0.0).astype(F32)
    along = lax.dot_general(steps, tri, NT, precision=HI, preferred_element_type=F32)
    down = lax.dot_general(tri, steps, NT, precision=HI, preferred_element_type=F32)
    return along, down, lower


def payload_tail(total, size):
    full = jnp.broadcast_to(total, (RIM, size))
    first = full.astype(BF).astype(F32)
    second = (full - first).astype(BF).astype(F32)
    third = full - first - second
    at = lax.broadcasted_iota(jnp.int32, (RIM, size), 0)
    return jnp.where(at == 0, first, jnp.where(at == 1, second, jnp.where(at == 2, third, 0.0)))


def route_rows(ids_ref, weights_ref, experts):
    top, tok = ids_ref.shape
    expert = lax.broadcasted_iota(jnp.int32, (experts, tok), 0)
    table = jnp.zeros((experts, tok), F32)
    for choice in range(top):
        table += jnp.where(expert == ids_ref[choice : choice + 1, :], weights_ref[choice : choice + 1, :], 0.0)
    first = table.astype(BF).astype(F32)
    second = (table - first).astype(BF).astype(F32)
    return jnp.concatenate([first, second, table - first - second], axis=0)


def conv_kernel(
    experts, mixed_ref, rim_ref, taps_ref, steps_ref, cot_ref, ids_ref, weights_ref, qkv_ref, fwd_ref, bwd_ref, pad_ref
):
    kinds, rows, chans = mixed_ref.shape
    heads = steps_ref.shape[0]
    size = chans // heads
    along, down, _ = decay_sums(steps_ref[...])
    for kind in range(kinds):
        pad_ref[:RIM] = rim_ref[kind].astype(F32)
        pad_ref[RIM:] = mixed_ref[kind].astype(F32)
        total = taps_ref[kind, 0:1, :] * pad_ref[RIM:]
        for offset in range(1, KERNEL):
            total += taps_ref[kind, offset : offset + 1, :] * pad_ref[RIM - offset : RIM - offset + rows]
        activ = total * jax.nn.sigmoid(total)
        if kind == 0:
            activ = activ * size ** (-0.5)
        qkv_ref[kind] = activ.astype(BF)
    routes = rows // LANES * 3 * experts
    table = route_rows(ids_ref, weights_ref, experts).astype(BF)
    for part in range(rows // LANES):
        bwd_ref[part * 3 * experts : (part + 1) * 3 * experts] = table[:, part * LANES : (part + 1) * LANES]
    for head in range(heads):
        at = slice(head * size, (head + 1) * size)
        base = head * (size + RIM)
        last = along[head : head + 1, rows - 1 : rows]
        lead = jnp.exp(down[:, head : head + 1])
        tail = jnp.exp(last - down[:, head : head + 1])
        key_out = (qkv_ref[1, :, at].astype(F32) * tail).astype(BF)
        query_out = (qkv_ref[0, :, at].astype(F32) * lead).astype(BF)
        ends = payload_tail(last, size).astype(BF)
        fwd_ref[base : base + size] = mm(key_out, qkv_ref[2, :, at], TN).astype(BF)
        fwd_ref[base + size : base + size + RIM] = ends
        base += routes
        bwd_ref[base : base + size] = mm(query_out, cot_ref[:, at], TN).astype(BF)
        bwd_ref[base + size : base + size + RIM] = ends


def local_states(mixed, rim, taps, steps, cot, ids, weights, experts):
    kinds, rows, chans = mixed.shape
    heads = steps.shape[0]
    size = chans // heads
    states = heads * (size + RIM)
    return pl.pallas_call(
        functools.partial(conv_kernel, experts),
        out_shape=[
            jax.ShapeDtypeStruct((kinds, rows, chans), BF),
            jax.ShapeDtypeStruct((states, size), BF),
            jax.ShapeDtypeStruct((states + rows // LANES * 3 * experts, size), BF),
        ],
        scratch_shapes=[pltpu.VMEM((rows + RIM, chans), F32)],
        compiler_params=params(12),
        name="conv_states",
    )(mixed, rim, taps, steps, cot, ids, weights)


def arrange(me_ref, near_ref, far_ref, held_ref):
    for at in range(near_ref.shape[0]):
        held_ref[me_ref[0] ^ (2 * at)] = near_ref[at]
        held_ref[me_ref[0] ^ (2 * at + 1)] = far_ref[at]


def entering(held_ref, heads, head, size, first, last, step):
    base = held_ref.shape[1] - (heads - head) * (size + RIM)

    def hop(count, total):
        at = first + count * step
        ends = held_ref[at, base + size : base + size + RIM, :].astype(F32)
        factor = jnp.exp(ends[0:1] + ends[1:2] + ends[2:3])
        return factor * total + held_ref[at, base : base + size, :].astype(F32)

    return lax.fori_loop(0, (last - first) * step, hop, jnp.zeros((size, size), F32))


def core_kernel(chunks, me_ref, qkv_ref, steps_ref, gain_ref, near_ref, far_ref, w_hbm, *refs):
    out_refs, (headed_ref, held_ref, w_ref, whole_ref, sem) = refs[:-5], refs[-5:]
    load = pltpu.make_async_copy(w_hbm, w_ref, sem)
    load.start()
    _, rows, chans = qkv_ref.shape
    heads = steps_ref.shape[0]
    size = chans // heads
    arrange(me_ref, near_ref, far_ref, held_ref)
    along, down, lower = decay_sums(steps_ref[...])
    for head in range(heads):
        at = slice(head * size, (head + 1) * size)
        state = entering(held_ref, heads, head, size, 0, me_ref[0], 1).astype(BF)
        diff = down[:, head : head + 1] - along[head : head + 1, :]
        mask = jnp.exp(jnp.where(lower, diff, -jnp.inf))
        query = qkv_ref[0, :, at]
        scores = (mm(query, qkv_ref[1, :, at], NT) * mask).astype(BF)
        attended = mm(scores, qkv_ref[2, :, at])
        attended += mm(query, state) * jnp.exp(down[:, head : head + 1])
        scale = lax.rsqrt(jnp.mean(attended * attended, axis=-1, keepdims=True) + 1e-06)
        headed_ref[:, at] = (attended * scale * gain_ref[:, at]).astype(BF)
    load.wait()
    whole_ref[...] = mm(headed_ref[...], w_ref[...]).astype(BF)
    part = rows // len(out_refs) // chunks
    for mask, ref in enumerate(out_refs):
        for chunk in range(chunks):
            start = chunk * len(out_refs) * part + (me_ref[2] ^ mask) * part
            ref[chunk * part : (chunk + 1) * part] = whole_ref[pl.ds(pl.multiple_of(start, part), part), :]


def core_out(where, qkv, steps, near, far, gain, w_out, chunks, parts):
    _, rows, chans = qkv.shape
    width = w_out.shape[1]
    vmem = pl.BlockSpec(memory_space=pltpu.VMEM)
    return pl.pallas_call(
        functools.partial(core_kernel, chunks),
        in_specs=[pl.BlockSpec(memory_space=pltpu.SMEM)] + [vmem] * 5 + [pl.BlockSpec(memory_space=pltpu.HBM)],
        out_shape=[jax.ShapeDtypeStruct((rows // parts, width), BF)] * parts,
        scratch_shapes=[
            pltpu.VMEM((rows, chans), BF),
            pltpu.VMEM((2 * near.shape[0], *near.shape[1:]), BF),
            pltpu.VMEM(w_out.shape, BF),
            pltpu.VMEM((rows, width), BF),
            pltpu.SemaphoreType.DMA,
        ],
        compiler_params=params(56),
        name="core_out",
    )(where, qkv, steps, gain.reshape(1, chans), near, far, w_out)


def grad_kernel(
    me_ref, qkv_ref, cot_ref, steps_ref, fwd_near, fwd_far, bwd_near, bwd_far, gq_ref, gk_ref, gv_ref, fwd_ref, bwd_ref
):
    _, rows, chans = qkv_ref.shape
    heads = steps_ref.shape[0]
    size = chans // heads
    count = fwd_ref.shape[0]
    arrange(me_ref, fwd_near, fwd_far, fwd_ref)
    arrange(me_ref, bwd_near, bwd_far, bwd_ref)
    along, down, lower = decay_sums(steps_ref[...])
    for head in range(heads):
        at = slice(head * size, (head + 1) * size)
        state = entering(fwd_ref, heads, head, size, 0, me_ref[0], 1).astype(BF)
        after = entering(bwd_ref, heads, head, size, count - 1, me_ref[0], -1).astype(BF)
        here = down[:, head : head + 1]
        lead = jnp.exp(here)
        tail = jnp.exp(along[head : head + 1, rows - 1 : rows] - here)
        mask = jnp.exp(jnp.where(lower, here - along[head : head + 1, :], -jnp.inf))
        query, key, val = qkv_ref[0, :, at], qkv_ref[1, :, at], qkv_ref[2, :, at]
        cot = cot_ref[:, at]
        scores = (mm(query, key, NT) * mask).astype(BF)
        dov = (mm(cot, val, NT) * mask).astype(BF)
        gq_ref[:, at] = (mm(dov, key) + lead * mm(cot, state, NT)).astype(BF)
        gk_ref[:, at] = (mm(dov, query, TN) + tail * mm(val, after, NT)).astype(BF)
        gv_ref[:, at] = (mm(scores, cot, TN) + tail * mm(key, after)).astype(BF)


def core_grads(where, qkv, cot, steps, fwd, bwd):
    _, rows, chans = qkv.shape
    count = 2 * fwd[0].shape[0]
    vmem = pl.BlockSpec(memory_space=pltpu.VMEM)
    return pl.pallas_call(
        grad_kernel,
        in_specs=[pl.BlockSpec(memory_space=pltpu.SMEM)] + [vmem] * 7,
        out_shape=[jax.ShapeDtypeStruct((rows, chans), BF)] * 3,
        scratch_shapes=[pltpu.VMEM((count, *fwd[0].shape[1:]), BF), pltpu.VMEM((count, *bwd[0].shape[1:]), BF)],
        compiler_params=params(24),
        name="core_grads",
    )(where, qkv, cot, steps, *fwd, *bwd)


def norm_kernel(count, where_ref, x_ref, gain_ref, *refs):
    chunks = (len(refs) - count) // 2
    parts, outs, attns = refs[:count], refs[count : count + chunks], refs[count + chunks :]
    rows = outs[0].shape[0]
    for chunk, (out_ref, attn_ref) in enumerate(zip(outs, attns)):
        at = slice(chunk * rows, (chunk + 1) * rows)
        attn = functools.reduce(jnp.add, [part[at].astype(F32) for part in parts])
        attn_ref[...] = attn
        start = pl.multiple_of((chunk * count + where_ref[2]) * rows, rows)
        resid = x_ref[pl.ds(start, rows), :].astype(F32) + attn
        scale = lax.rsqrt(jnp.mean(resid * resid, axis=-1, keepdims=True) + 1e-06)
        out_ref[...] = (resid * scale * gain_ref[...]).astype(BF)


def norm_rows(where, x, parts, gain, chunks):
    rows, width = parts[0].shape[0] // chunks, parts[0].shape[1]
    vmem = pl.BlockSpec(memory_space=pltpu.VMEM)
    outs = pl.pallas_call(
        functools.partial(norm_kernel, len(parts)),
        in_specs=[pl.BlockSpec(memory_space=pltpu.SMEM)] + [vmem] * (2 + len(parts)),
        out_shape=[jax.ShapeDtypeStruct((rows, width), BF)] * chunks
        + [jax.ShapeDtypeStruct((rows, width), F32)] * chunks,
        compiler_params=params(12),
        name="moe_norm",
    )(where, x, gain.reshape(1, width), *parts)
    return list(outs[:chunks]), list(outs[chunks:])


def join_kernel(where_ref, *refs):
    parts, out_ref = refs[:-1], refs[-1]
    rows = parts[0].shape[0]
    for mask, ref in enumerate(parts):
        out_ref[pl.ds(pl.multiple_of((where_ref[2] ^ mask) * rows, rows), rows), :] = ref[...]


def join_rows(where, parts):
    rows, width = parts[0].shape
    vmem = pl.BlockSpec(memory_space=pltpu.VMEM)
    return pl.pallas_call(
        join_kernel,
        in_specs=[pl.BlockSpec(memory_space=pltpu.SMEM)] + [vmem] * len(parts),
        out_shape=jax.ShapeDtypeStruct((len(parts) * rows, width), BF),
        compiler_params=params(16),
        name="join_rows",
    )(where, *parts)


PAIR = 2


def expert_kernel(masks, chunk, experts, where_ref, near_routes, far_routes, gate_ref, up_ref, down_ref, *refs):
    row_refs, (near_ref, far_ref, rows_ref, sems) = refs[: len(masks)], refs[len(masks) :]
    _, tok, width = near_ref.shape
    steps = len(masks) // PAIR
    step = pl.program_id(0)
    slot = lax.rem(step, 2)

    def start(at):
        for part in range(PAIR):
            target = rows_ref.at[at % 2, pl.ds(part * tok, tok)]
            pltpu.make_async_copy(row_refs[PAIR * at + part], target, sems.at[at % 2]).start()

    @pl.when(step == 0)
    def _():
        start(0)

    for at in range(1, steps):

        @pl.when(step == at - 1)
        def _(at=at):
            start(at)

    here = lax.broadcasted_iota(jnp.int32, (3 * experts, LANES), 0)
    mine = (here == where_ref[1]) | (here == where_ref[1] + experts) | (here == where_ref[1] + 2 * experts)
    square = (LANES, LANES)
    diagonal = lax.broadcasted_iota(jnp.int32, square, 0) == lax.broadcasted_iota(jnp.int32, square, 1)
    is_near = step < steps // 2
    weights = []
    for part in range(PAIR):
        index = jnp.int32(masks[part] // 2)
        for at in range(1, steps):
            index = jnp.where(step == at, masks[PAIR * at + part] // 2, index)
        for block in range(tok // LANES):
            base = (chunk // LANES + block) * 3 * experts
            at = slice(base, base + 3 * experts)
            table = jnp.where(is_near, near_routes[index, at, :].astype(F32), far_routes[index, at, :].astype(F32))
            row = jnp.sum(jnp.where(mine, table, 0.0), axis=0, keepdims=True)
            weights.append(jnp.sum(jnp.where(diagonal, jnp.broadcast_to(row, square), 0.0), axis=1, keepdims=True))

    pltpu.make_async_copy(rows_ref.at[slot], rows_ref.at[slot], sems.at[slot]).wait()
    tokens = rows_ref[slot]
    gate = mm(tokens, gate_ref[0])
    inner = (gate * jax.nn.sigmoid(gate) * mm(tokens, up_ref[0])).astype(BF)
    cols = pick_block(width, 512)
    for begin in range(0, width, cols):
        piece = mm(inner, down_ref[0, :, begin : begin + cols])
        for at, weight in enumerate(weights):
            part, row = divmod(at * LANES, tok)
            scaled = (piece[at * LANES : (at + 1) * LANES] * weight).astype(BF)

            @pl.when(is_near)
            def _(scaled=scaled, part=part, row=row):
                near_ref[part, row : row + LANES, begin : begin + cols] = scaled

            @pl.when(jnp.logical_not(is_near))
            def _(scaled=scaled, part=part, row=row):
                far_ref[part, row : row + LANES, begin : begin + cols] = scaled


def stage_kernel(where_ref, *refs):
    out_ref = refs[-1]
    for at in range(where_ref.shape[0]):
        out_ref[at] = where_ref[at]


def stage(where, *weights):
    smem = pl.BlockSpec(memory_space=pltpu.SMEM)
    return pl.pallas_call(
        stage_kernel,
        in_specs=[smem] + [pl.BlockSpec(memory_space=pltpu.VMEM)] * len(weights),
        out_specs=smem,
        out_shape=jax.ShapeDtypeStruct(where.shape, where.dtype),
        compiler_params=params(2),
        name="stage_weights",
    )(where, *weights)


def expert_pieces(chunk, where, rows, evens, gate, up, down, routes):
    masks = list(evens) + [mask | CORE for mask in evens]
    blocks = [rows[mask] for mask in masks]
    tok, width = blocks[0].shape
    hidden = gate.shape[2]
    count = len(blocks)
    half = count // PAIR // 2
    experts = EXP_CTX * count
    route_rows = CHUNKS * tok // LANES * 3 * experts
    vmem = pl.BlockSpec(memory_space=pltpu.VMEM)
    piece = jax.ShapeDtypeStruct((count // 2, tok, width), BF)
    table = pl.BlockSpec((count // 2, route_rows, LANES), lambda i: (0, 0, 0))
    return pl.pallas_call(
        functools.partial(expert_kernel, tuple(masks), chunk, experts),
        grid=(count // PAIR,),
        in_specs=[pl.BlockSpec(memory_space=pltpu.SMEM), table, table]
        + [vmem] * 3
        + [pl.BlockSpec(memory_space=pl.ANY)] * count,
        out_specs=[
            pl.BlockSpec((PAIR, tok, width), lambda i: (jnp.minimum(i, half - 1), 0, 0)),
            pl.BlockSpec((PAIR, tok, width), lambda i: (jnp.maximum(i - half, 0), 0, 0)),
        ],
        out_shape=[piece, piece],
        scratch_shapes=[
            pltpu.VMEM((2, PAIR * tok, width), BF),
            pltpu.SemaphoreType.DMA((2,)),
        ],
        compiler_params=params(20),
        cost_estimate=pl.CostEstimate(
            flops=6 * count * tok * width * hidden,
            bytes_accessed=4 * count * tok * width,
            transcendentals=count * tok * hidden,
        ),
        name="expert_pieces",
    )(where, *routes, gate, up, down, *blocks)


CORE = 1


def swap(value, mask, keep=None):
    count = lax.axis_size("ctx")
    pairs = [(at, at ^ mask) for at in range(count)]
    return lax.ppermute(value, "ctx", [pair for pair in pairs if keep is None or keep(*pair)])


def send_heads(parts):
    count = lax.axis_size("head")
    return [parts[0]] + [
        lax.ppermute(parts[mask], "head", [(at, at ^ mask) for at in range(count)]) for mask in range(1, count)
    ]


def spread_near(own, keep=None):
    return jnp.stack([own] + [swap(own, mask, keep) for mask in range(2, lax.axis_size("ctx"), 2)])


def plus(*terms):
    return functools.reduce(jnp.add, [term.astype(F32) for term in terms]).astype(BF)


def after(value, other):
    return lax.optimization_barrier((value, other))[0]


def sum_kernel(where_ref, attn_ref, near_ref, arrived_ref, *refs):
    parts = attn_ref.shape[1] // refs[-1].shape[1]
    others, outs, total_ref = refs[: -parts - 1], refs[-parts - 1 : -1], refs[-1]
    part, width = attn_ref.shape
    cols = width // parts
    own = pl.ds(pl.multiple_of(where_ref[2] * part, part), part)
    for mask, out_ref in enumerate(outs):
        at = pl.ds(pl.multiple_of((where_ref[2] ^ mask) * cols, cols), cols)
        total = near_ref[0, :, at].astype(F32) + arrived_ref[0, :, at].astype(F32)
        for ref in others:
            total += ref[:, at].astype(F32)
        total_ref[...] = total
        total_ref[own, :] += attn_ref[:, at]
        out_ref[...] = total_ref[...].astype(BF)


def sum_terms(where, attn, near, arrived, others, parts):
    _, tok, width = near.shape
    part = attn.shape[0]
    cols = width // parts
    first = pl.BlockSpec((1, tok, width), lambda i: (0, 0, 0))
    return pl.pallas_call(
        sum_kernel,
        grid=(1,),
        in_specs=[
            pl.BlockSpec(memory_space=pltpu.SMEM),
            pl.BlockSpec((part, width), lambda i: (0, 0)),
            first,
            first,
        ]
        + [pl.BlockSpec((tok, width), lambda i: (0, 0))] * len(others),
        out_specs=[pl.BlockSpec((tok, cols), lambda i: (0, 0))] * parts,
        out_shape=[jax.ShapeDtypeStruct((tok, cols), BF)] * parts,
        scratch_shapes=[pltpu.VMEM((tok, cols), F32)],
        compiler_params=params(24),
        name="sum_terms",
    )(where, attn, near, arrived, *others)


def final_kernel(count, where_ref, x_ref, *refs):
    del where_ref
    out_ref = refs[-1]
    rows = refs[0].shape[0]
    for chunk in range((len(refs) - 1) // count):
        at = slice(chunk * rows, (chunk + 1) * rows)
        terms = [x_ref[at]] + [ref[...] for ref in refs[chunk * count : (chunk + 1) * count]]
        out_ref[at] = functools.reduce(jnp.add, [term.astype(F32) for term in terms]).astype(BF)


def final_sum(where, x, parts):
    rows, cols = parts[0][0].shape
    total = len(parts) * rows
    block = pl.BlockSpec((rows, cols), lambda i, where: (0, 0))
    return pl.pallas_call(
        functools.partial(final_kernel, len(parts[0])),
        grid_spec=pltpu.PrefetchScalarGridSpec(
            num_scalar_prefetch=1,
            grid=(1,),
            in_specs=[pl.BlockSpec((total, cols), lambda i, where: (0, where[2]))]
            + [block] * (len(parts) * len(parts[0])),
            out_specs=pl.BlockSpec((total, cols), lambda i, where: (0, 0)),
        ),
        out_shape=jax.ShapeDtypeStruct((total, cols), BF),
        compiler_params=params(12),
        name="layer_out",
    )(where, x, *[part for chunk in parts for part in chunk])


CHUNKS = 2


def body(
    hidden_in,
    gain_attn,
    w_qkv,
    conv_w,
    log_decay,
    norm_gain,
    w_out,
    gain_moe,
    expert_ids,
    route_weights,
    w_gate,
    w_up,
    w_down,
    grad_core,
):
    n_ctx, n_head = lax.axis_size("ctx"), lax.axis_size("head")
    my_ctx, my_head = lax.axis_index("ctx"), lax.axis_index("head")
    experts = EXP_CTX * n_ctx
    shards = n_head // EXP_CTX
    where = jnp.stack([my_ctx, EXP_CTX * my_ctx + my_head // shards, my_head]).astype(jnp.int32)
    steps = log_decay.T
    chunk_rows = hidden_in.shape[0] // CHUNKS

    mixed, rim = project(hidden_in, gain_attn, jnp.transpose(w_qkv, (1, 0, 2)))
    rim = lax.ppermute(rim, "ctx", [(at, at + 1) for at in range(n_ctx - 1)])
    qkv, fwd, bwd = local_states(
        mixed, rim, jnp.transpose(conv_w, (1, 0, 2)), steps, grad_core, expert_ids.T, route_weights.T, experts
    )
    fwd = spread_near(fwd, lambda source, target: source < target)
    fwd = (fwd, swap(fwd, CORE))
    parts = core_out(where, qkv, steps, *fwd, norm_gain, w_out, CHUNKS, n_head)
    where = stage(after(where, parts), w_gate, w_up, w_down)
    bwd = spread_near(after(bwd, parts))
    normed, attn = norm_rows(where, hidden_in, after(send_heads(parts), bwd), gain_moe, CHUNKS)

    evens = list(range(0, n_ctx, 2))
    near, rows = [], []
    own = join_rows(where, send_heads([normed[0]] * n_head))
    bwd = (bwd, swap(after(bwd, own), CORE))
    for chunk in range(CHUNKS):
        near.append([own] + [swap(own, mask) for mask in evens[1:]])
        if chunk + 1 < CHUNKS:
            own = join_rows(where, send_heads([after(normed[chunk + 1], own)] * n_head))
            near[chunk] = after(near[chunk], own)
    for chunk in range(CHUNKS):
        rows.append({mask: part for mask, part in zip(evens, near[chunk])})
        rows[chunk] |= {mask | CORE: swap(part, CORE) for mask, part in rows[chunk].items()}

    sums, pending = [], []
    for chunk in range(CHUNKS):
        here, far = expert_pieces(chunk * chunk_rows, where, rows[chunk], evens, w_gate, w_up, w_down, bwd)
        arrived = swap(after(far, near[chunk + 1] if chunk + 1 < CHUNKS else pending[-1][2]), CORE)
        leaving = [plus(here[at], arrived[at]) for at in range(1, len(evens))]
        if chunk + 1 < CHUNKS:
            rows[chunk + 1] = after(rows[chunk + 1], leaving)
        others = [swap(part, mask) for part, mask in zip(leaving, evens[1:])]
        pending.append((here, arrived, others, leaving))
    for chunk in range(CHUNKS):
        here, arrived, others, _ = pending[chunk]
        if chunk + 1 < CHUNKS:
            others = after(others, pending[chunk + 1][3])
        sums.append(send_heads(sum_terms(where, attn[chunk], here, arrived, others, n_head)))
    grads = core_grads(where, qkv, grad_core, steps, fwd, bwd)
    return (final_sum(where, hidden_in, sums), *grads)


def solution(mesh):
    in_specs = (
        P("ctx", None),
        P(),
        P(None, None, "head"),
        P(None, None, "head"),
        P("ctx", "head"),
        P("head"),
        P("head", None),
        P(),
        P("ctx", None),
        P("ctx", None),
        P(("ctx", "head"), None, None),
        P(("ctx", "head"), None, None),
        P(("ctx", "head"), None, None),
        P("ctx", "head"),
    )
    out_specs = (P("ctx", "head"), P("ctx", "head"), P("ctx", "head"), P("ctx", "head"))
    return jax.shard_map(body, mesh=mesh, in_specs=in_specs, out_specs=out_specs, check_vma=False)
```

```python
import functools

import jax
import jax.numpy as jnp
from jax import lax
from jax.experimental import pallas as pl
from jax.experimental.pallas import tpu as pltpu
from jax.sharding import PartitionSpec as P

KERNEL = 4
EXP_CTX = 2
LANES = 128
RIM = 16
MIB = 1024 * 1024
HI = lax.Precision.HIGHEST
BF = jnp.bfloat16
F32 = jnp.float32
NT = (((1,), (1,)), ((), ()))
TN = (((0,), (0,)), ((), ()))
NN = (((1,), (0,)), ((), ()))


def params(mib):
    return pltpu.CompilerParams(vmem_limit_bytes=mib * MIB)


def mm(a, b, dims=NN):
    return lax.dot_general(a, b, dims, preferred_element_type=F32)


def pick_block(extent, target):
    return target if extent % target == 0 else extent


def qkv_kernel(x_hbm, gain_ref, w_hbm, mixed_ref, rim_ref, x_ref, w_ref, normed_ref, x_sem, sems):
    kinds, width, chans = w_ref.shape
    load = pltpu.make_async_copy(x_hbm, x_ref, x_sem)
    load.start()
    copies = [pltpu.make_async_copy(w_hbm.at[kind], w_ref.at[kind], sems.at[kind]) for kind in range(kinds)]
    for copy in copies:
        copy.start()
    load.wait()
    values = x_ref[...].astype(F32)
    scale = lax.rsqrt(jnp.mean(values * values, axis=-1, keepdims=True) + 1e-06)
    normed_ref[...] = (values * scale * gain_ref[...]).astype(BF)
    for kind in range(kinds):
        copies[kind].wait()
        out = mm(normed_ref[...], w_ref[kind]).astype(BF)
        mixed_ref[kind] = out
        rim_ref[kind] = out[out.shape[0] - RIM :]


def project(x, gain, weights):
    rows, width = x.shape
    kinds, _, chans = weights.shape
    vmem = pl.BlockSpec(memory_space=pltpu.VMEM)
    hbm = pl.BlockSpec(memory_space=pltpu.HBM)
    return pl.pallas_call(
        qkv_kernel,
        in_specs=[hbm, vmem, hbm],
        out_specs=[vmem, vmem],
        out_shape=[
            jax.ShapeDtypeStruct((kinds, rows, chans), BF),
            jax.ShapeDtypeStruct((kinds, RIM, chans), BF),
        ],
        scratch_shapes=[
            pltpu.VMEM((rows, width), BF),
            pltpu.VMEM((kinds, width, chans), BF),
            pltpu.VMEM((rows, width), BF),
            pltpu.SemaphoreType.DMA,
            pltpu.SemaphoreType.DMA((kinds,)),
        ],
        compiler_params=params(60),
        name="qkv_projection",
    )(x, gain.reshape(1, width), weights)


def decay_sums(steps):
    rows = steps.shape[1]
    row_at = lax.broadcasted_iota(jnp.int32, (rows, rows), 0)
    col_at = lax.broadcasted_iota(jnp.int32, (rows, rows), 1)
    lower = row_at >= col_at
    tri = jnp.where(lower, 1.0, 0.0).astype(F32)
    along = lax.dot_general(steps, tri, NT, precision=HI, preferred_element_type=F32)
    down = lax.dot_general(tri, steps, NT, precision=HI, preferred_element_type=F32)
    return along, down, lower


def payload_tail(total, size):
    full = jnp.broadcast_to(total, (RIM, size))
    first = full.astype(BF).astype(F32)
    second = (full - first).astype(BF).astype(F32)
    third = full - first - second
    at = lax.broadcasted_iota(jnp.int32, (RIM, size), 0)
    return jnp.where(at == 0, first, jnp.where(at == 1, second, jnp.where(at == 2, third, 0.0)))


def route_rows(ids_ref, weights_ref, experts):
    top, tok = ids_ref.shape
    expert = lax.broadcasted_iota(jnp.int32, (experts, tok), 0)
    table = jnp.zeros((experts, tok), F32)
    for choice in range(top):
        table += jnp.where(expert == ids_ref[choice : choice + 1, :], weights_ref[choice : choice + 1, :], 0.0)
    first = table.astype(BF).astype(F32)
    second = (table - first).astype(BF).astype(F32)
    return jnp.concatenate([first, second, table - first - second], axis=0)


def conv_kernel(
    experts, mixed_ref, rim_ref, taps_ref, steps_ref, cot_ref, ids_ref, weights_ref, qkv_ref, fwd_ref, bwd_ref, pad_ref
):
    kinds, rows, chans = mixed_ref.shape
    heads = steps_ref.shape[0]
    size = chans // heads
    along, down, _ = decay_sums(steps_ref[...])
    for kind in range(kinds):
        pad_ref[:RIM] = rim_ref[kind].astype(F32)
        pad_ref[RIM:] = mixed_ref[kind].astype(F32)
        total = taps_ref[kind, 0:1, :] * pad_ref[RIM:]
        for offset in range(1, KERNEL):
            total += taps_ref[kind, offset : offset + 1, :] * pad_ref[RIM - offset : RIM - offset + rows]
        activ = total * jax.nn.sigmoid(total)
        if kind == 0:
            activ = activ * size ** (-0.5)
        qkv_ref[kind] = activ.astype(BF)
    routes = rows // LANES * 3 * experts
    table = route_rows(ids_ref, weights_ref, experts).astype(BF)
    for part in range(rows // LANES):
        bwd_ref[part * 3 * experts : (part + 1) * 3 * experts] = table[:, part * LANES : (part + 1) * LANES]
    for head in range(heads):
        at = slice(head * size, (head + 1) * size)
        base = head * (size + RIM)
        last = along[head : head + 1, rows - 1 : rows]
        lead = jnp.exp(down[:, head : head + 1])
        tail = jnp.exp(last - down[:, head : head + 1])
        key_out = (qkv_ref[1, :, at].astype(F32) * tail).astype(BF)
        query_out = (qkv_ref[0, :, at].astype(F32) * lead).astype(BF)
        ends = payload_tail(last, size).astype(BF)
        fwd_ref[base : base + size] = mm(key_out, qkv_ref[2, :, at], TN).astype(BF)
        fwd_ref[base + size : base + size + RIM] = ends
        base += routes
        bwd_ref[base : base + size] = mm(query_out, cot_ref[:, at], TN).astype(BF)
        bwd_ref[base + size : base + size + RIM] = ends


def local_states(mixed, rim, taps, steps, cot, ids, weights, experts):
    kinds, rows, chans = mixed.shape
    heads = steps.shape[0]
    size = chans // heads
    states = heads * (size + RIM)
    return pl.pallas_call(
        functools.partial(conv_kernel, experts),
        out_specs=[pl.BlockSpec(memory_space=pltpu.VMEM)] * 3,
        out_shape=[
            jax.ShapeDtypeStruct((kinds, rows, chans), BF),
            jax.ShapeDtypeStruct((states, size), BF),
            jax.ShapeDtypeStruct((states + rows // LANES * 3 * experts, size), BF),
        ],
        scratch_shapes=[pltpu.VMEM((rows + RIM, chans), F32)],
        compiler_params=params(12),
        name="conv_states",
    )(mixed, rim, taps, steps, cot, ids, weights)


def arrange(me_ref, near_ref, far_ref, held_ref):
    for at in range(near_ref.shape[0]):
        held_ref[me_ref[0] ^ (2 * at)] = near_ref[at]
        held_ref[me_ref[0] ^ (2 * at + 1)] = far_ref[at]


def entering(held_ref, heads, head, size, first, last, step):
    base = held_ref.shape[1] - (heads - head) * (size + RIM)

    def hop(count, total):
        at = first + count * step
        ends = held_ref[at, base + size : base + size + RIM, :].astype(F32)
        factor = jnp.exp(ends[0:1] + ends[1:2] + ends[2:3])
        return factor * total + held_ref[at, base : base + size, :].astype(F32)

    return lax.fori_loop(0, (last - first) * step, hop, jnp.zeros((size, size), F32))


def core_kernel(chunks, me_ref, qkv_ref, steps_ref, gain_ref, near_ref, far_ref, w_ref, *refs):
    out_refs, (headed_ref, held_ref, whole_ref) = refs[:-3], refs[-3:]
    _, rows, chans = qkv_ref.shape
    heads = steps_ref.shape[0]
    size = chans // heads
    arrange(me_ref, near_ref, far_ref, held_ref)
    along, down, lower = decay_sums(steps_ref[...])
    for head in range(heads):
        at = slice(head * size, (head + 1) * size)
        state = entering(held_ref, heads, head, size, 0, me_ref[0], 1).astype(BF)
        diff = down[:, head : head + 1] - along[head : head + 1, :]
        mask = jnp.exp(jnp.where(lower, diff, -jnp.inf))
        query = qkv_ref[0, :, at]
        scores = (mm(query, qkv_ref[1, :, at], NT) * mask).astype(BF)
        attended = mm(scores, qkv_ref[2, :, at])
        attended += mm(query, state) * jnp.exp(down[:, head : head + 1])
        scale = lax.rsqrt(jnp.mean(attended * attended, axis=-1, keepdims=True) + 1e-06)
        headed_ref[:, at] = (attended * scale * gain_ref[:, at]).astype(BF)
    whole_ref[...] = mm(headed_ref[...], w_ref[...]).astype(BF)
    part = rows // len(out_refs) // chunks
    for mask, ref in enumerate(out_refs):
        for chunk in range(chunks):
            start = chunk * len(out_refs) * part + (me_ref[2] ^ mask) * part
            ref[chunk * part : (chunk + 1) * part] = whole_ref[pl.ds(pl.multiple_of(start, part), part), :]


def core_out(where, qkv, steps, near, far, gain, w_out, chunks, parts):
    _, rows, chans = qkv.shape
    width = w_out.shape[1]
    vmem = pl.BlockSpec(memory_space=pltpu.VMEM)
    return pl.pallas_call(
        functools.partial(core_kernel, chunks),
        in_specs=[pl.BlockSpec(memory_space=pltpu.SMEM)] + [vmem] * 6,
        out_shape=[jax.ShapeDtypeStruct((rows // parts, width), BF)] * parts,
        scratch_shapes=[
            pltpu.VMEM((rows, chans), BF),
            pltpu.VMEM((2 * near.shape[0], *near.shape[1:]), BF),
            pltpu.VMEM((rows, width), BF),
        ],
        compiler_params=params(16),
        name="core_out",
    )(where, qkv, steps, gain.reshape(1, chans), near, far, w_out)


def grad_kernel(
    me_ref, qkv_ref, cot_ref, steps_ref, fwd_near, fwd_far, bwd_near, bwd_far, gq_ref, gk_ref, gv_ref, fwd_ref, bwd_ref
):
    _, rows, chans = qkv_ref.shape
    heads = steps_ref.shape[0]
    size = chans // heads
    count = fwd_ref.shape[0]
    arrange(me_ref, fwd_near, fwd_far, fwd_ref)
    arrange(me_ref, bwd_near, bwd_far, bwd_ref)
    along, down, lower = decay_sums(steps_ref[...])
    for head in range(heads):
        at = slice(head * size, (head + 1) * size)
        state = entering(fwd_ref, heads, head, size, 0, me_ref[0], 1).astype(BF)
        after = entering(bwd_ref, heads, head, size, count - 1, me_ref[0], -1).astype(BF)
        here = down[:, head : head + 1]
        lead = jnp.exp(here)
        tail = jnp.exp(along[head : head + 1, rows - 1 : rows] - here)
        mask = jnp.exp(jnp.where(lower, here - along[head : head + 1, :], -jnp.inf))
        query, key, val = qkv_ref[0, :, at], qkv_ref[1, :, at], qkv_ref[2, :, at]
        cot = cot_ref[:, at]
        scores = (mm(query, key, NT) * mask).astype(BF)
        dov = (mm(cot, val, NT) * mask).astype(BF)
        gq_ref[:, at] = (mm(dov, key) + lead * mm(cot, state, NT)).astype(BF)
        gk_ref[:, at] = (mm(dov, query, TN) + tail * mm(val, after, NT)).astype(BF)
        gv_ref[:, at] = (mm(scores, cot, TN) + tail * mm(key, after)).astype(BF)


def core_grads(where, qkv, cot, steps, fwd, bwd):
    _, rows, chans = qkv.shape
    count = 2 * fwd[0].shape[0]
    vmem = pl.BlockSpec(memory_space=pltpu.VMEM)
    return pl.pallas_call(
        grad_kernel,
        in_specs=[pl.BlockSpec(memory_space=pltpu.SMEM)] + [vmem] * 7,
        out_shape=[jax.ShapeDtypeStruct((rows, chans), BF)] * 3,
        scratch_shapes=[pltpu.VMEM((count, *fwd[0].shape[1:]), BF), pltpu.VMEM((count, *bwd[0].shape[1:]), BF)],
        compiler_params=params(24),
        name="core_grads",
    )(where, qkv, cot, steps, *fwd, *bwd)


def norm_kernel(count, where_ref, x_ref, gain_ref, *refs):
    chunks = (len(refs) - count) // 2
    parts, outs, attns = refs[:count], refs[count : count + chunks], refs[count + chunks :]
    rows = outs[0].shape[0]
    for chunk, (out_ref, attn_ref) in enumerate(zip(outs, attns)):
        at = slice(chunk * rows, (chunk + 1) * rows)
        attn = functools.reduce(jnp.add, [part[at].astype(F32) for part in parts])
        attn_ref[...] = attn
        start = pl.multiple_of((chunk * count + where_ref[2]) * rows, rows)
        resid = x_ref[pl.ds(start, rows), :].astype(F32) + attn
        scale = lax.rsqrt(jnp.mean(resid * resid, axis=-1, keepdims=True) + 1e-06)
        out_ref[...] = (resid * scale * gain_ref[...]).astype(BF)


def norm_rows(where, x, parts, gain, chunks):
    rows, width = parts[0].shape[0] // chunks, parts[0].shape[1]
    vmem = pl.BlockSpec(memory_space=pltpu.VMEM)
    outs = pl.pallas_call(
        functools.partial(norm_kernel, len(parts)),
        in_specs=[pl.BlockSpec(memory_space=pltpu.SMEM)] + [vmem] * (2 + len(parts)),
        out_shape=[jax.ShapeDtypeStruct((rows, width), BF)] * chunks
        + [jax.ShapeDtypeStruct((rows, width), F32)] * chunks,
        compiler_params=params(12),
        name="moe_norm",
    )(where, x, gain.reshape(1, width), *parts)
    return list(outs[:chunks]), list(outs[chunks:])


def join_kernel(where_ref, *refs):
    parts, out_ref = refs[:-1], refs[-1]
    rows = parts[0].shape[0]
    for mask, ref in enumerate(parts):
        out_ref[pl.ds(pl.multiple_of((where_ref[2] ^ mask) * rows, rows), rows), :] = ref[...]


def join_rows(where, parts):
    rows, width = parts[0].shape
    vmem = pl.BlockSpec(memory_space=pltpu.VMEM)
    return pl.pallas_call(
        join_kernel,
        in_specs=[pl.BlockSpec(memory_space=pltpu.SMEM)] + [vmem] * len(parts),
        out_shape=jax.ShapeDtypeStruct((len(parts) * rows, width), BF),
        compiler_params=params(16),
        name="join_rows",
    )(where, *parts)


PAIR = 2


def expert_kernel(masks, chunk, experts, where_ref, near_routes, far_routes, gate_ref, up_ref, down_ref, *refs):
    row_refs, (near_ref, far_ref, rows_ref, sems) = refs[: len(masks)], refs[len(masks) :]
    _, tok, width = near_ref.shape
    steps = len(masks) // PAIR
    step = pl.program_id(0)
    slot = lax.rem(step, 2)

    def start(at):
        for part in range(PAIR):
            target = rows_ref.at[at % 2, pl.ds(part * tok, tok)]
            pltpu.make_async_copy(row_refs[PAIR * at + part], target, sems.at[at % 2]).start()

    @pl.when(step == 0)
    def _():
        start(0)

    for at in range(1, steps):

        @pl.when(step == at - 1)
        def _(at=at):
            start(at)

    here = lax.broadcasted_iota(jnp.int32, (3 * experts, LANES), 0)
    mine = (here == where_ref[1]) | (here == where_ref[1] + experts) | (here == where_ref[1] + 2 * experts)
    square = (LANES, LANES)
    diagonal = lax.broadcasted_iota(jnp.int32, square, 0) == lax.broadcasted_iota(jnp.int32, square, 1)
    is_near = step < steps // 2
    weights = []
    for part in range(PAIR):
        index = jnp.int32(masks[part] // 2)
        for at in range(1, steps):
            index = jnp.where(step == at, masks[PAIR * at + part] // 2, index)
        for block in range(tok // LANES):
            base = (chunk // LANES + block) * 3 * experts
            at = slice(base, base + 3 * experts)
            table = jnp.where(is_near, near_routes[index, at, :].astype(F32), far_routes[index, at, :].astype(F32))
            row = jnp.sum(jnp.where(mine, table, 0.0), axis=0, keepdims=True)
            weights.append(jnp.sum(jnp.where(diagonal, jnp.broadcast_to(row, square), 0.0), axis=1, keepdims=True))

    pltpu.make_async_copy(rows_ref.at[slot], rows_ref.at[slot], sems.at[slot]).wait()
    tokens = rows_ref[slot]
    gate = mm(tokens, gate_ref[0])
    inner = (gate * jax.nn.sigmoid(gate) * mm(tokens, up_ref[0])).astype(BF)
    cols = pick_block(width, 512)
    for begin in range(0, width, cols):
        piece = mm(inner, down_ref[0, :, begin : begin + cols])
        for at, weight in enumerate(weights):
            part, row = divmod(at * LANES, tok)
            scaled = (piece[at * LANES : (at + 1) * LANES] * weight).astype(BF)

            @pl.when(is_near)
            def _(scaled=scaled, part=part, row=row):
                near_ref[part, row : row + LANES, begin : begin + cols] = scaled

            @pl.when(jnp.logical_not(is_near))
            def _(scaled=scaled, part=part, row=row):
                far_ref[part, row : row + LANES, begin : begin + cols] = scaled


def stage_kernel(where_ref, *refs):
    out_ref = refs[-1]
    for at in range(where_ref.shape[0]):
        out_ref[at] = where_ref[at]


def stage(where, *weights):
    smem = pl.BlockSpec(memory_space=pltpu.SMEM)
    return pl.pallas_call(
        stage_kernel,
        in_specs=[smem] + [pl.BlockSpec(memory_space=pltpu.VMEM)] * len(weights),
        out_specs=smem,
        out_shape=jax.ShapeDtypeStruct(where.shape, where.dtype),
        compiler_params=params(2),
        name="stage_weights",
    )(where, *weights)


def expert_pieces(chunk, where, rows, evens, gate, up, down, routes):
    masks = list(evens) + [mask | CORE for mask in evens]
    blocks = [rows[mask] for mask in masks]
    tok, width = blocks[0].shape
    hidden = gate.shape[2]
    count = len(blocks)
    half = count // PAIR // 2
    experts = EXP_CTX * count
    route_rows = CHUNKS * tok // LANES * 3 * experts
    vmem = pl.BlockSpec(memory_space=pltpu.VMEM)
    piece = jax.ShapeDtypeStruct((count // 2, tok, width), BF)
    table = pl.BlockSpec((count // 2, route_rows, LANES), lambda i: (0, 0, 0))
    return pl.pallas_call(
        functools.partial(expert_kernel, tuple(masks), chunk, experts),
        grid=(count // PAIR,),
        in_specs=[pl.BlockSpec(memory_space=pltpu.SMEM), table, table]
        + [vmem] * 3
        + [pl.BlockSpec(memory_space=pl.ANY)] * count,
        out_specs=[
            pl.BlockSpec((PAIR, tok, width), lambda i: (jnp.minimum(i, half - 1), 0, 0)),
            pl.BlockSpec((PAIR, tok, width), lambda i: (jnp.maximum(i - half, 0), 0, 0)),
        ],
        out_shape=[piece, piece],
        scratch_shapes=[
            pltpu.VMEM((2, PAIR * tok, width), BF),
            pltpu.SemaphoreType.DMA((2,)),
        ],
        compiler_params=params(20),
        cost_estimate=pl.CostEstimate(
            flops=6 * count * tok * width * hidden,
            bytes_accessed=4 * count * tok * width,
            transcendentals=count * tok * hidden,
        ),
        name="expert_pieces",
    )(where, *routes, gate, up, down, *blocks)


CORE, ROW, COL = 1, 2, 4
PLANE = 8


def swap(value, mask, keep=None):
    count = lax.axis_size("ctx")
    pairs = [(at, at ^ mask) for at in range(count)]
    return lax.ppermute(value, "ctx", [pair for pair in pairs if keep is None or keep(*pair)])


def send_heads(parts):
    count = lax.axis_size("head")
    return [parts[0]] + [
        lax.ppermute(parts[mask], "head", [(at, at ^ mask) for at in range(count)]) for mask in range(1, count)
    ]


def spread_near(own, keep=None):
    return jnp.stack([own] + [swap(own, mask, keep) for mask in range(2, lax.axis_size("ctx"), 2)])


def plus(*terms):
    return functools.reduce(jnp.add, [term.astype(F32) for term in terms]).astype(BF)


def after(value, other):
    return lax.optimization_barrier((value, other))[0]


def depart(own):
    masks = (ROW, COL) if lax.axis_size("ctx") == PLANE else range(2, lax.axis_size("ctx"), 2)
    return {mask: swap(own, mask) for mask in masks}


def forward(own, came):
    came = {0: own} | came
    if lax.axis_size("ctx") == PLANE:
        half = own.shape[0] // 2
        upper, lower = swap(came[ROW][:half], COL), swap(came[COL][half:], ROW)
        came[ROW | COL] = jnp.concatenate([upper, lower])
    return [came[mask] for mask in range(0, lax.axis_size("ctx"), 2)]


def first_sums(here, arrived):
    if lax.axis_size("ctx") != PLANE:
        return [(2 * at, 0, plus(here[at], arrived[at])) for at in range(1, here.shape[0])]
    half = here.shape[1] // 2
    row, col, across = ROW // 2, COL // 2, (ROW | COL) // 2
    upper, lower = slice(0, half), slice(half, 2 * half)
    return [
        (ROW, 0, plus(here[across, upper], arrived[across, upper])),
        (COL, half, plus(here[across, lower], arrived[across, lower])),
        (ROW, 0, plus(here[row, upper], arrived[row, upper])),
        (COL, half, plus(here[col, lower], arrived[col, lower])),
    ]


def last_sums(here, arrived, came):
    if lax.axis_size("ctx") != PLANE:
        return []
    half = here.shape[1] // 2
    row, col = ROW // 2, COL // 2
    return [
        (COL, 0, plus(here[col, :half], arrived[col, :half], came[0])),
        (ROW, half, plus(here[row, half:], arrived[row, half:], came[1])),
    ]


def send_sums(sums):
    return [swap(rows, mask) for mask, _, rows in sums]


def sum_kernel(starts, where_ref, attn_ref, near_ref, arrived_ref, *refs):
    parts = attn_ref.shape[1] // refs[-1].shape[1]
    others, outs, total_ref = refs[: -parts - 1], refs[-parts - 1 : -1], refs[-1]
    part, width = attn_ref.shape
    cols = width // parts
    own = pl.ds(pl.multiple_of(where_ref[2] * part, part), part)
    for mask, out_ref in enumerate(outs):
        at = pl.ds(pl.multiple_of((where_ref[2] ^ mask) * cols, cols), cols)
        total = near_ref[0, :, at].astype(F32) + arrived_ref[0, :, at].astype(F32)
        total_ref[...] = total
        for start, ref in zip(starts, others):
            total_ref[start : start + ref.shape[0]] += ref[:, at].astype(F32)
        total_ref[own, :] += attn_ref[:, at]
        out_ref[...] = total_ref[...].astype(BF)


def sum_terms(where, attn, near, arrived, others, starts, parts):
    _, tok, width = near.shape
    part = attn.shape[0]
    cols = width // parts
    first = pl.BlockSpec((1, tok, width), lambda i: (0, 0, 0))
    return pl.pallas_call(
        functools.partial(sum_kernel, tuple(starts)),
        grid=(1,),
        in_specs=[
            pl.BlockSpec(memory_space=pltpu.SMEM),
            pl.BlockSpec((part, width), lambda i: (0, 0)),
            first,
            first,
        ]
        + [pl.BlockSpec(part.shape, lambda i: (0, 0)) for part in others],
        out_specs=[pl.BlockSpec((tok, cols), lambda i: (0, 0))] * parts,
        out_shape=[jax.ShapeDtypeStruct((tok, cols), BF)] * parts,
        scratch_shapes=[pltpu.VMEM((tok, cols), F32)],
        compiler_params=params(24),
        name="sum_terms",
    )(where, attn, near, arrived, *others)


def final_kernel(count, where_ref, x_ref, *refs):
    del where_ref
    out_ref = refs[-1]
    rows = refs[0].shape[0]
    for chunk in range((len(refs) - 1) // count):
        at = slice(chunk * rows, (chunk + 1) * rows)
        terms = [x_ref[at]] + [ref[...] for ref in refs[chunk * count : (chunk + 1) * count]]
        out_ref[at] = functools.reduce(jnp.add, [term.astype(F32) for term in terms]).astype(BF)


def final_sum(where, x, parts):
    rows, cols = parts[0][0].shape
    total = len(parts) * rows
    block = pl.BlockSpec((rows, cols), lambda i, where: (0, 0))
    return pl.pallas_call(
        functools.partial(final_kernel, len(parts[0])),
        grid_spec=pltpu.PrefetchScalarGridSpec(
            num_scalar_prefetch=1,
            grid=(1,),
            in_specs=[pl.BlockSpec((total, cols), lambda i, where: (0, where[2]))]
            + [block] * (len(parts) * len(parts[0])),
            out_specs=pl.BlockSpec((total, cols), lambda i, where: (0, 0)),
        ),
        out_shape=jax.ShapeDtypeStruct((total, cols), BF),
        compiler_params=params(12),
        name="layer_out",
    )(where, x, *[part for chunk in parts for part in chunk])


CHUNKS = 2


def body(
    hidden_in,
    gain_attn,
    w_qkv,
    conv_w,
    log_decay,
    norm_gain,
    w_out,
    gain_moe,
    expert_ids,
    route_weights,
    w_gate,
    w_up,
    w_down,
    grad_core,
):
    n_ctx, n_head = lax.axis_size("ctx"), lax.axis_size("head")
    my_ctx, my_head = lax.axis_index("ctx"), lax.axis_index("head")
    experts = EXP_CTX * n_ctx
    shards = n_head // EXP_CTX
    where = jnp.stack([my_ctx, EXP_CTX * my_ctx + my_head // shards, my_head]).astype(jnp.int32)
    steps = log_decay.T
    chunk_rows = hidden_in.shape[0] // CHUNKS

    mixed, rim = project(hidden_in, gain_attn, jnp.transpose(w_qkv, (1, 0, 2)))
    rim = lax.ppermute(rim, "ctx", [(at, at + 1) for at in range(n_ctx - 1)])
    qkv, fwd, bwd = local_states(
        mixed, rim, jnp.transpose(conv_w, (1, 0, 2)), steps, grad_core, expert_ids.T, route_weights.T, experts
    )
    fwd = spread_near(fwd, lambda source, target: source < target)
    fwd = (fwd, swap(fwd, CORE))
    where = stage(after(where, qkv), w_out)
    parts = core_out(where, qkv, steps, *fwd, norm_gain, w_out, CHUNKS, n_head)
    where = stage(after(where, parts), w_gate, w_up, w_down)
    normed, attn = norm_rows(where, hidden_in, send_heads(parts), gain_moe, CHUNKS)
    bwd = spread_near(after(bwd, normed))

    near, came, owns = [], [], []
    own = join_rows(where, send_heads([normed[0]] * n_head))
    bwd = (bwd, swap(after(bwd, own), CORE))
    for chunk in range(CHUNKS):
        owns.append(own)
        came.append(depart(own))
        if chunk + 1 < CHUNKS:
            own = join_rows(where, send_heads([after(normed[chunk + 1], own)] * n_head))
            came[chunk] = after(came[chunk], own)
    evens = list(range(0, n_ctx, 2))
    rows = []
    for chunk in range(CHUNKS):
        near = forward(owns[chunk], came[chunk])
        rows.append({mask: part for mask, part in zip(evens, near)})
        rows[chunk] |= {mask | CORE: swap(part, CORE) for mask, part in rows[chunk].items()}

    pending, sums = [], []
    for chunk in range(CHUNKS):
        here, far = expert_pieces(chunk * chunk_rows, where, rows[chunk], evens, w_gate, w_up, w_down, bwd)
        arrived = swap(after(far, came[chunk + 1] if chunk + 1 < CHUNKS else pending[-1][3]), CORE)
        if pending:
            pending[-1] += (last_sums(*pending[-1][:2], pending[-1][3]),)
            arrived = after(arrived, [part for _, _, part in pending[-1][4]])
        first = first_sums(here, arrived)
        if chunk + 1 < CHUNKS:
            rows[chunk + 1] = after(rows[chunk + 1], [part for _, _, part in first])
        pending.append((here, arrived, first, send_sums(first)))
    pending[-1] += (last_sums(*pending[-1][:2], pending[-1][3]),)
    for chunk in range(CHUNKS):
        here, arrived, first, received, last = pending[chunk]
        terms = list(zip([start for _, start, _ in first], received))
        if last:
            terms = terms[2:] + list(zip([start for _, start, _ in last], send_sums(last)))
        starts, others = zip(*terms)
        if chunk + 1 < CHUNKS:
            others = after(others, [part for _, _, part in pending[chunk + 1][2]])
        sums.append(send_heads(sum_terms(where, attn[chunk], here, arrived, others, starts, n_head)))
    grads = core_grads(where, qkv, grad_core, steps, fwd, bwd)
    return (final_sum(where, hidden_in, sums), *grads)


def solution(mesh):
    in_specs = (
        P("ctx", None),
        P(),
        P(None, None, "head"),
        P(None, None, "head"),
        P("ctx", "head"),
        P("head"),
        P("head", None),
        P(),
        P("ctx", None),
        P("ctx", None),
        P(("ctx", "head"), None, None),
        P(("ctx", "head"), None, None),
        P(("ctx", "head"), None, None),
        P("ctx", "head"),
    )
    out_specs = (P("ctx", "head"), P("ctx", "head"), P("ctx", "head"), P("ctx", "head"))
    return jax.shard_map(body, mesh=mesh, in_specs=in_specs, out_specs=out_specs, check_vma=False)
```

```python
import functools

import jax
import jax.numpy as jnp
from jax import lax
from jax.experimental import pallas as pl
from jax.experimental.pallas import tpu as pltpu
from jax.sharding import PartitionSpec as P

KERNEL = 4
EXP_CTX = 2
LANES = 128
RIM = 16
MIB = 1024 * 1024
HI = lax.Precision.HIGHEST
BF = jnp.bfloat16
F32 = jnp.float32
NT = (((1,), (1,)), ((), ()))
TN = (((0,), (0,)), ((), ()))
NN = (((1,), (0,)), ((), ()))


def params(mib):
    return pltpu.CompilerParams(vmem_limit_bytes=mib * MIB)


def mm(a, b, dims=NN):
    return lax.dot_general(a, b, dims, preferred_element_type=F32)


def pick_block(extent, target):
    return target if extent % target == 0 else extent


def qkv_kernel(x_hbm, gain_ref, w_hbm, mixed_ref, rim_ref, x_ref, w_ref, normed_ref, x_sem, sems):
    kinds, width, chans = w_ref.shape
    load = pltpu.make_async_copy(x_hbm, x_ref, x_sem)
    load.start()
    part = width // sems.shape[1]
    copies = []
    for kind in range(kinds):
        at = [pl.ds(piece * part, part) for piece in range(sems.shape[1])]
        copies.append(
            [
                pltpu.make_async_copy(w_hbm.at[kind, rows], w_ref.at[kind, rows], sems.at[kind, piece])
                for piece, rows in enumerate(at)
            ]
        )
        for copy in copies[kind]:
            copy.start()
    load.wait()
    values = x_ref[...].astype(F32)
    scale = lax.rsqrt(jnp.mean(values * values, axis=-1, keepdims=True) + 1e-06)
    normed_ref[...] = (values * scale * gain_ref[...]).astype(BF)
    for kind in range(kinds):
        for copy in copies[kind]:
            copy.wait()
        out = mm(normed_ref[...], w_ref[kind]).astype(BF)
        mixed_ref[kind] = out
        rim_ref[kind] = out[out.shape[0] - RIM :]


def project(x, gain, weights):
    rows, width = x.shape
    kinds, _, chans = weights.shape
    vmem = pl.BlockSpec(memory_space=pltpu.VMEM)
    hbm = pl.BlockSpec(memory_space=pltpu.HBM)
    return pl.pallas_call(
        qkv_kernel,
        in_specs=[hbm, vmem, hbm],
        out_specs=[vmem, vmem],
        out_shape=[
            jax.ShapeDtypeStruct((kinds, rows, chans), BF),
            jax.ShapeDtypeStruct((kinds, RIM, chans), BF),
        ],
        scratch_shapes=[
            pltpu.VMEM((rows, width), BF),
            pltpu.VMEM((kinds, width, chans), BF),
            pltpu.VMEM((rows, width), BF),
            pltpu.SemaphoreType.DMA,
            pltpu.SemaphoreType.DMA((kinds, 4)),
        ],
        compiler_params=params(60),
        name="qkv_projection",
    )(x, gain.reshape(1, width), weights)


def decay_sums(steps):
    rows = steps.shape[1]
    row_at = lax.broadcasted_iota(jnp.int32, (rows, rows), 0)
    col_at = lax.broadcasted_iota(jnp.int32, (rows, rows), 1)
    lower = row_at >= col_at
    tri = jnp.where(lower, 1.0, 0.0).astype(F32)
    along = lax.dot_general(steps, tri, NT, precision=HI, preferred_element_type=F32)
    down = lax.dot_general(tri, steps, NT, precision=HI, preferred_element_type=F32)
    return along, down, lower


def payload_tail(total, size):
    full = jnp.broadcast_to(total, (RIM, size))
    first = full.astype(BF).astype(F32)
    second = (full - first).astype(BF).astype(F32)
    third = full - first - second
    at = lax.broadcasted_iota(jnp.int32, (RIM, size), 0)
    return jnp.where(at == 0, first, jnp.where(at == 1, second, jnp.where(at == 2, third, 0.0)))


def route_rows(ids_ref, weights_ref, experts):
    top, tok = ids_ref.shape
    expert = lax.broadcasted_iota(jnp.int32, (experts, tok), 0)
    table = jnp.zeros((experts, tok), F32)
    for choice in range(top):
        table += jnp.where(expert == ids_ref[choice : choice + 1, :], weights_ref[choice : choice + 1, :], 0.0)
    first = table.astype(BF).astype(F32)
    second = (table - first).astype(BF).astype(F32)
    return jnp.concatenate([first, second, table - first - second], axis=0)


def conv_kernel(
    experts, mixed_any, rim_ref, taps_ref, steps_ref, cot_ref, ids_ref, weights_ref, qkv_ref, fwd_ref, bwd_ref,
    pad_ref, mixed_ref, sems,
):
    kinds, rows, chans = mixed_ref.shape
    copies = [pltpu.make_async_copy(mixed_any.at[kind], mixed_ref.at[kind], sems.at[kind]) for kind in range(kinds)]
    for copy in copies:
        copy.start()
    heads = steps_ref.shape[0]
    size = chans // heads
    along, down, _ = decay_sums(steps_ref[...])
    for kind in range(kinds):
        copies[kind].wait()
        pad_ref[:RIM] = rim_ref[kind].astype(F32)
        pad_ref[RIM:] = mixed_ref[kind].astype(F32)
        total = taps_ref[kind, 0:1, :] * pad_ref[RIM:]
        for offset in range(1, KERNEL):
            total += taps_ref[kind, offset : offset + 1, :] * pad_ref[RIM - offset : RIM - offset + rows]
        activ = total * jax.nn.sigmoid(total)
        if kind == 0:
            activ = activ * size ** (-0.5)
        qkv_ref[kind] = activ.astype(BF)
    routes = rows // LANES * 3 * experts
    table = route_rows(ids_ref, weights_ref, experts).astype(BF)
    for part in range(rows // LANES):
        fwd_ref[part * 3 * experts : (part + 1) * 3 * experts] = table[:, part * LANES : (part + 1) * LANES]
    for head in range(heads):
        at = slice(head * size, (head + 1) * size)
        base = head * (size + RIM)
        behind = routes + base
        last = along[head : head + 1, rows - 1 : rows]
        lead = jnp.exp(down[:, head : head + 1])
        tail = jnp.exp(last - down[:, head : head + 1])
        key_out = (qkv_ref[1, :, at].astype(F32) * tail).astype(BF)
        query_out = (qkv_ref[0, :, at].astype(F32) * lead).astype(BF)
        ends = payload_tail(last, size).astype(BF)
        fwd_ref[behind : behind + size] = mm(key_out, qkv_ref[2, :, at], TN).astype(BF)
        fwd_ref[behind + size : behind + size + RIM] = ends
        bwd_ref[base : base + size] = mm(query_out, cot_ref[:, at], TN).astype(BF)
        bwd_ref[base + size : base + size + RIM] = ends


def local_states(mixed, rim, taps, steps, cot, ids, weights, experts):
    kinds, rows, chans = mixed.shape
    heads = steps.shape[0]
    size = chans // heads
    states = heads * (size + RIM)
    return pl.pallas_call(
        functools.partial(conv_kernel, experts),
        in_specs=[pl.BlockSpec(memory_space=pl.ANY)] + [pl.BlockSpec(memory_space=pltpu.VMEM)] * 6,
        out_specs=[pl.BlockSpec(memory_space=pltpu.VMEM)] * 3,
        out_shape=[
            jax.ShapeDtypeStruct((kinds, rows, chans), BF),
            jax.ShapeDtypeStruct((states + rows // LANES * 3 * experts, size), BF),
            jax.ShapeDtypeStruct((states, size), BF),
        ],
        scratch_shapes=[
            pltpu.VMEM((rows + RIM, chans), F32),
            pltpu.VMEM(mixed.shape, BF),
            pltpu.SemaphoreType.DMA((kinds,)),
        ],
        compiler_params=params(12),
        name="conv_states",
    )(mixed, rim, taps, steps, cot, ids, weights)


def arrange(me_ref, near_ref, far_ref, held_ref):
    for at in range(near_ref.shape[0]):
        held_ref[me_ref[0] ^ (2 * at)] = near_ref[at]
        held_ref[me_ref[0] ^ (2 * at + 1)] = far_ref[at]


def entering(held_ref, heads, head, size, first, last, step):
    base = held_ref.shape[1] - (heads - head) * (size + RIM)

    def hop(count, total):
        at = first + count * step
        ends = held_ref[at, base + size : base + size + RIM, :].astype(F32)
        factor = jnp.exp(ends[0:1] + ends[1:2] + ends[2:3])
        return factor * total + held_ref[at, base : base + size, :].astype(F32)

    return lax.fori_loop(0, (last - first) * step, hop, jnp.zeros((size, size), F32))


def core_kernel(chunks, me_ref, qkv_ref, steps_ref, gain_ref, near_ref, far_ref, w_ref, *refs):
    out_refs, (headed_ref, held_ref, whole_ref) = refs[:-3], refs[-3:]
    _, rows, chans = qkv_ref.shape
    heads = steps_ref.shape[0]
    size = chans // heads
    arrange(me_ref, near_ref, far_ref, held_ref)
    along, down, lower = decay_sums(steps_ref[...])
    for head in range(heads):
        at = slice(head * size, (head + 1) * size)
        state = entering(held_ref, heads, head, size, 0, me_ref[0], 1).astype(BF)
        diff = down[:, head : head + 1] - along[head : head + 1, :]
        mask = jnp.exp(jnp.where(lower, diff, -jnp.inf))
        query = qkv_ref[0, :, at]
        scores = (mm(query, qkv_ref[1, :, at], NT) * mask).astype(BF)
        attended = mm(scores, qkv_ref[2, :, at])
        attended += mm(query, state) * jnp.exp(down[:, head : head + 1])
        scale = lax.rsqrt(jnp.mean(attended * attended, axis=-1, keepdims=True) + 1e-06)
        headed_ref[:, at] = (attended * scale * gain_ref[:, at]).astype(BF)
    whole_ref[...] = mm(headed_ref[...], w_ref[...]).astype(BF)
    part = rows // len(out_refs) // chunks
    for mask, ref in enumerate(out_refs):
        for chunk in range(chunks):
            start = chunk * len(out_refs) * part + (me_ref[2] ^ mask) * part
            ref[chunk * part : (chunk + 1) * part] = whole_ref[pl.ds(pl.multiple_of(start, part), part), :]


def core_out(where, qkv, steps, near, far, gain, w_out, chunks, parts):
    _, rows, chans = qkv.shape
    width = w_out.shape[1]
    vmem = pl.BlockSpec(memory_space=pltpu.VMEM)
    return pl.pallas_call(
        functools.partial(core_kernel, chunks),
        in_specs=[pl.BlockSpec(memory_space=pltpu.SMEM)] + [vmem] * 6,
        out_shape=[jax.ShapeDtypeStruct((rows // parts, width), BF)] * parts,
        scratch_shapes=[
            pltpu.VMEM((rows, chans), BF),
            pltpu.VMEM((2 * near.shape[0], *near.shape[1:]), BF),
            pltpu.VMEM((rows, width), BF),
        ],
        compiler_params=params(16),
        name="core_out",
    )(where, qkv, steps, gain.reshape(1, chans), near, far, w_out)


def grad_kernel(
    me_ref, qkv_ref, cot_ref, steps_ref, fwd_near, fwd_far, bwd_near, bwd_far, gq_ref, gk_ref, gv_ref, fwd_ref, bwd_ref
):
    _, rows, chans = qkv_ref.shape
    heads = steps_ref.shape[0]
    size = chans // heads
    count = fwd_ref.shape[0]
    arrange(me_ref, fwd_near, fwd_far, fwd_ref)
    arrange(me_ref, bwd_near, bwd_far, bwd_ref)
    along, down, lower = decay_sums(steps_ref[...])
    for head in range(heads):
        at = slice(head * size, (head + 1) * size)
        state = entering(fwd_ref, heads, head, size, 0, me_ref[0], 1).astype(BF)
        after = entering(bwd_ref, heads, head, size, count - 1, me_ref[0], -1).astype(BF)
        here = down[:, head : head + 1]
        lead = jnp.exp(here)
        tail = jnp.exp(along[head : head + 1, rows - 1 : rows] - here)
        mask = jnp.exp(jnp.where(lower, here - along[head : head + 1, :], -jnp.inf))
        query, key, val = qkv_ref[0, :, at], qkv_ref[1, :, at], qkv_ref[2, :, at]
        cot = cot_ref[:, at]
        scores = (mm(query, key, NT) * mask).astype(BF)
        dov = (mm(cot, val, NT) * mask).astype(BF)
        gq_ref[:, at] = (mm(dov, key) + lead * mm(cot, state, NT)).astype(BF)
        gk_ref[:, at] = (mm(dov, query, TN) + tail * mm(val, after, NT)).astype(BF)
        gv_ref[:, at] = (mm(scores, cot, TN) + tail * mm(key, after)).astype(BF)


def core_grads(where, qkv, cot, steps, fwd, bwd):
    _, rows, chans = qkv.shape
    count = 2 * fwd[0].shape[0]
    vmem = pl.BlockSpec(memory_space=pltpu.VMEM)
    return pl.pallas_call(
        grad_kernel,
        in_specs=[pl.BlockSpec(memory_space=pltpu.SMEM)] + [vmem] * 7,
        out_shape=[jax.ShapeDtypeStruct((rows, chans), BF)] * 3,
        scratch_shapes=[pltpu.VMEM((count, *fwd[0].shape[1:]), BF), pltpu.VMEM((count, *bwd[0].shape[1:]), BF)],
        compiler_params=params(24),
        name="core_grads",
    )(where, qkv, cot, steps, *fwd, *bwd)


def norm_kernel(count, where_ref, x_ref, gain_ref, *refs):
    chunks = (len(refs) - count) // 2
    parts, outs, attns = refs[:count], refs[count : count + chunks], refs[count + chunks :]
    rows = outs[0].shape[0]
    for chunk, (out_ref, attn_ref) in enumerate(zip(outs, attns)):
        at = slice(chunk * rows, (chunk + 1) * rows)
        attn = functools.reduce(jnp.add, [part[at].astype(F32) for part in parts])
        attn_ref[...] = attn
        start = pl.multiple_of((chunk * count + where_ref[2]) * rows, rows)
        resid = x_ref[pl.ds(start, rows), :].astype(F32) + attn
        scale = lax.rsqrt(jnp.mean(resid * resid, axis=-1, keepdims=True) + 1e-06)
        out_ref[...] = (resid * scale * gain_ref[...]).astype(BF)


def norm_rows(where, x, parts, gain, chunks):
    rows, width = parts[0].shape[0] // chunks, parts[0].shape[1]
    vmem = pl.BlockSpec(memory_space=pltpu.VMEM)
    outs = pl.pallas_call(
        functools.partial(norm_kernel, len(parts)),
        in_specs=[pl.BlockSpec(memory_space=pltpu.SMEM)] + [vmem] * (2 + len(parts)),
        out_shape=[jax.ShapeDtypeStruct((rows, width), BF)] * chunks
        + [jax.ShapeDtypeStruct((rows, width), F32)] * chunks,
        compiler_params=params(12),
        name="moe_norm",
    )(where, x, gain.reshape(1, width), *parts)
    return list(outs[:chunks]), list(outs[chunks:])


def join_kernel(where_ref, *refs):
    parts, out_ref = refs[:-1], refs[-1]
    rows = parts[0].shape[0]
    for mask, ref in enumerate(parts):
        out_ref[pl.ds(pl.multiple_of((where_ref[2] ^ mask) * rows, rows), rows), :] = ref[...]


def join_rows(where, parts):
    rows, width = parts[0].shape
    vmem = pl.BlockSpec(memory_space=pltpu.VMEM)
    return pl.pallas_call(
        join_kernel,
        in_specs=[pl.BlockSpec(memory_space=pltpu.SMEM)] + [vmem] * len(parts),
        out_shape=jax.ShapeDtypeStruct((len(parts) * rows, width), BF),
        compiler_params=params(16),
        name="join_rows",
    )(where, *parts)


PAIR = 2


def expert_kernel(groups, chunk, experts, where_ref, near_routes, far_routes, gate_ref, up_ref, down_ref, *refs):
    masks = [mask for group in groups for mask in group]
    row_refs, outs, (rows_ref, sems) = refs[: len(masks)], refs[len(masks) : -2], refs[-2:]
    _, tok, width = outs[0].shape
    steps = len(masks) // PAIR
    step = pl.program_id(0)
    slot = lax.rem(step, 2)

    def start(at):
        for part in range(PAIR):
            target = rows_ref.at[at % 2, pl.ds(part * tok, tok)]
            pltpu.make_async_copy(row_refs[PAIR * at + part], target, sems.at[at % 2]).start()

    @pl.when(step == 0)
    def _():
        start(0)

    for at in range(1, steps):

        @pl.when(step == at - 1)
        def _(at=at):
            start(at)

    here = lax.broadcasted_iota(jnp.int32, (3 * experts, LANES), 0)
    mine = (here == where_ref[1]) | (here == where_ref[1] + experts) | (here == where_ref[1] + 2 * experts)
    square = (LANES, LANES)
    diagonal = lax.broadcasted_iota(jnp.int32, square, 0) == lax.broadcasted_iota(jnp.int32, square, 1)
    weights = []
    for part in range(PAIR):
        mask = jnp.int32(masks[part])
        for at in range(1, steps):
            mask = jnp.where(step == at, masks[PAIR * at + part], mask)
        index = lax.shift_right_logical(mask, 1)
        for block in range(tok // LANES):
            base = (chunk // LANES + block) * 3 * experts
            at = slice(base, base + 3 * experts)
            near, far = near_routes[index, at, :].astype(F32), far_routes[index, at, :].astype(F32)
            table = jnp.where((mask & CORE) == 0, near, far)
            row = jnp.sum(jnp.where(mine, table, 0.0), axis=0, keepdims=True)
            weights.append(jnp.sum(jnp.where(diagonal, jnp.broadcast_to(row, square), 0.0), axis=1, keepdims=True))

    pltpu.make_async_copy(rows_ref.at[slot], rows_ref.at[slot], sems.at[slot]).wait()
    tokens = rows_ref[slot]
    gate = mm(tokens, gate_ref[0])
    inner = (gate * jax.nn.sigmoid(gate) * mm(tokens, up_ref[0])).astype(BF)
    cols = pick_block(width, 512)
    per = steps // len(outs)
    for begin in range(0, width, cols):
        piece = mm(inner, down_ref[0, :, begin : begin + cols])
        for at, weight in enumerate(weights):
            part, row = divmod(at * LANES, tok)
            scaled = (piece[at * LANES : (at + 1) * LANES] * weight).astype(BF)
            for group, out_ref in enumerate(outs):

                @pl.when((step >= group * per) & (step < (group + 1) * per))
                def _(scaled=scaled, part=part, row=row, out_ref=out_ref):
                    out_ref[part, row : row + LANES, begin : begin + cols] = scaled


def stage_kernel(where_ref, *refs):
    out_ref = refs[-1]
    for at in range(where_ref.shape[0]):
        out_ref[at] = where_ref[at]


def stage(where, *weights):
    smem = pl.BlockSpec(memory_space=pltpu.SMEM)
    return pl.pallas_call(
        stage_kernel,
        in_specs=[smem] + [pl.BlockSpec(memory_space=pltpu.VMEM)] * len(weights),
        out_specs=smem,
        out_shape=jax.ShapeDtypeStruct(where.shape, where.dtype),
        compiler_params=params(2),
        name="stage_weights",
    )(where, *weights)


def expert_pieces(chunk, where, rows, groups, gate, up, down, routes):
    blocks = [rows[mask] for group in groups for mask in group]
    tok, width = blocks[0].shape
    hidden = gate.shape[2]
    count, each = len(blocks), len(groups[0])
    per = each // PAIR
    experts = EXP_CTX * 2 * routes[0].shape[0]
    route_rows = CHUNKS * tok // LANES * 3 * experts
    vmem = pl.BlockSpec(memory_space=pltpu.VMEM)
    table = pl.BlockSpec((routes[0].shape[0], route_rows, LANES), lambda i: (0, 0, 0))

    def out_spec(group):
        return pl.BlockSpec((PAIR, tok, width), lambda i: (jnp.clip(i - group * per, 0, per - 1), 0, 0))

    return pl.pallas_call(
        functools.partial(expert_kernel, tuple(map(tuple, groups)), chunk, experts),
        grid=(count // PAIR,),
        in_specs=[pl.BlockSpec(memory_space=pltpu.SMEM), table, table]
        + [vmem] * 3
        + [pl.BlockSpec(memory_space=pl.ANY)] * count,
        out_specs=[out_spec(group) for group in range(len(groups))],
        out_shape=[jax.ShapeDtypeStruct((each, tok, width), BF)] * len(groups),
        scratch_shapes=[
            pltpu.VMEM((2, PAIR * tok, width), BF),
            pltpu.SemaphoreType.DMA((2,)),
        ],
        compiler_params=params(20),
        cost_estimate=pl.CostEstimate(
            flops=6 * count * tok * width * hidden,
            bytes_accessed=4 * count * tok * width,
            transcendentals=count * tok * hidden,
        ),
        name="expert_pieces",
    )(where, *routes, gate, up, down, *blocks)


CORE, ROW, COL = 1, 2, 4
PLANE = 8


def swap(value, mask):
    return lax.ppermute(value, "ctx", [(at, at ^ mask) for at in range(lax.axis_size("ctx"))])


def send_heads(parts):
    count = lax.axis_size("head")
    return [parts[0]] + [
        lax.ppermute(parts[mask], "head", [(at, at ^ mask) for at in range(count)]) for mask in range(1, count)
    ]


def spread_near(own):
    return jnp.stack([own] + [swap(own, mask) for mask in range(2, lax.axis_size("ctx"), 2)])


def double(near, mask):
    return jnp.concatenate([near, swap(near, mask)])


def plus(*terms):
    return functools.reduce(jnp.add, [term.astype(F32) for term in terms]).astype(BF)


def after(value, other):
    return lax.optimization_barrier((value, other))[0]


def depart(own):
    masks = (ROW, COL) if lax.axis_size("ctx") == PLANE else range(2, lax.axis_size("ctx"), 2)
    return {mask: swap(own, mask) for mask in masks}


def forward(own, came, leaving=None):
    came = {0: own} | came
    if lax.axis_size("ctx") == PLANE:
        half = own.shape[0] // 2
        halves = [swap(came[ROW][:half], COL), swap(came[COL][half:], ROW)]
        came[ROW | COL] = jnp.concatenate(halves if leaving is None else after(halves, leaving))
    return [came[mask] for mask in range(0, lax.axis_size("ctx"), 2)]


def first_sums(here, arrived):
    if lax.axis_size("ctx") != PLANE:
        return [(2 * at, 0, plus(here[at], arrived[at])) for at in range(1, here.shape[0])]
    half = here.shape[1] // 2
    row, col, across = ROW // 2, COL // 2, (ROW | COL) // 2
    upper, lower = slice(0, half), slice(half, 2 * half)
    return [
        (ROW, 0, plus(here[across, upper], arrived[across, upper])),
        (COL, half, plus(here[across, lower], arrived[across, lower])),
        (ROW, 0, plus(here[row, upper], arrived[row, upper])),
        (COL, half, plus(here[col, lower], arrived[col, lower])),
    ]


def last_sums(here, arrived, came):
    if lax.axis_size("ctx") != PLANE:
        return []
    half = here.shape[1] // 2
    row, col = ROW // 2, COL // 2
    return [
        (COL, 0, plus(here[col, :half], arrived[col, :half], came[0])),
        (ROW, half, plus(here[row, half:], arrived[row, half:], came[1])),
    ]


def send_sums(sums):
    return [swap(rows, mask) for mask, _, rows in sums]


def sum_kernel(starts, where_ref, attn_ref, near_ref, arrived_ref, *refs):
    parts = attn_ref.shape[1] // refs[-1].shape[1]
    others, outs, total_ref = refs[: -parts - 1], refs[-parts - 1 : -1], refs[-1]
    part, width = attn_ref.shape
    cols = width // parts
    own = pl.ds(pl.multiple_of(where_ref[2] * part, part), part)
    for mask, out_ref in enumerate(outs):
        at = pl.ds(pl.multiple_of((where_ref[2] ^ mask) * cols, cols), cols)
        total = near_ref[0, :, at].astype(F32) + arrived_ref[0, :, at].astype(F32)
        total_ref[...] = total
        for start, ref in zip(starts, others):
            total_ref[start : start + ref.shape[0]] += ref[:, at].astype(F32)
        total_ref[own, :] += attn_ref[:, at]
        out_ref[...] = total_ref[...].astype(BF)


def sum_terms(where, attn, near, arrived, others, starts, parts):
    _, tok, width = near.shape
    part = attn.shape[0]
    cols = width // parts
    first = pl.BlockSpec((1, tok, width), lambda i: (0, 0, 0))
    return pl.pallas_call(
        functools.partial(sum_kernel, tuple(starts)),
        grid=(1,),
        in_specs=[
            pl.BlockSpec(memory_space=pltpu.SMEM),
            pl.BlockSpec((part, width), lambda i: (0, 0)),
            first,
            first,
        ]
        + [pl.BlockSpec(part.shape, lambda i: (0, 0)) for part in others],
        out_specs=[pl.BlockSpec((tok, cols), lambda i: (0, 0))] * parts,
        out_shape=[jax.ShapeDtypeStruct((tok, cols), BF)] * parts,
        scratch_shapes=[pltpu.VMEM((tok, cols), F32)],
        compiler_params=params(24),
        name="sum_terms",
    )(where, attn, near, arrived, *others)


def final_kernel(count, where_ref, x_ref, *refs):
    del where_ref
    out_ref = refs[-1]
    rows = refs[0].shape[0]
    for chunk in range((len(refs) - 1) // count):
        at = slice(chunk * rows, (chunk + 1) * rows)
        terms = [x_ref[at]] + [ref[...] for ref in refs[chunk * count : (chunk + 1) * count]]
        out_ref[at] = functools.reduce(jnp.add, [term.astype(F32) for term in terms]).astype(BF)


def final_sum(where, x, parts):
    rows, cols = parts[0][0].shape
    total = len(parts) * rows
    block = pl.BlockSpec((rows, cols), lambda i, where: (0, 0))
    return pl.pallas_call(
        functools.partial(final_kernel, len(parts[0])),
        grid_spec=pltpu.PrefetchScalarGridSpec(
            num_scalar_prefetch=1,
            grid=(1,),
            in_specs=[pl.BlockSpec((total, cols), lambda i, where: (0, where[2]))]
            + [block] * (len(parts) * len(parts[0])),
            out_specs=pl.BlockSpec((total, cols), lambda i, where: (0, 0)),
        ),
        out_shape=jax.ShapeDtypeStruct((total, cols), BF),
        compiler_params=params(12),
        name="layer_out",
    )(where, x, *[part for chunk in parts for part in chunk])


CHUNKS = 2


def body(
    hidden_in,
    gain_attn,
    w_qkv,
    conv_w,
    log_decay,
    norm_gain,
    w_out,
    gain_moe,
    expert_ids,
    route_weights,
    w_gate,
    w_up,
    w_down,
    grad_core,
):
    n_ctx, n_head = lax.axis_size("ctx"), lax.axis_size("head")
    my_ctx, my_head = lax.axis_index("ctx"), lax.axis_index("head")
    experts = EXP_CTX * n_ctx
    shards = n_head // EXP_CTX
    where = jnp.stack([my_ctx, EXP_CTX * my_ctx + my_head // shards, my_head]).astype(jnp.int32)
    steps = log_decay.T
    chunk_rows = hidden_in.shape[0] // CHUNKS

    mixed, rim = project(hidden_in, gain_attn, jnp.transpose(w_qkv, (1, 0, 2)))
    rim = lax.ppermute(rim, "ctx", [(at, at + 1) for at in range(n_ctx - 1)])
    qkv, fwd, bwd = local_states(
        mixed, rim, jnp.transpose(conv_w, (1, 0, 2)), steps, grad_core, expert_ids.T, route_weights.T, experts
    )
    fwd = spread_near(fwd)
    fwd = (fwd, swap(fwd, CORE))
    where = stage(after(where, qkv), w_out)
    parts = core_out(where, qkv, steps, *fwd, norm_gain, w_out, CHUNKS, n_head)
    where = stage(after(where, parts), w_gate, w_up, w_down)
    bwd = double(after(bwd, parts)[None], ROW)
    normed, attn = norm_rows(where, hidden_in, after(send_heads(parts), bwd), gain_moe, CHUNKS)
    bwd = after(bwd, normed)
    while bwd.shape[0] < n_ctx // 2:
        bwd = double(bwd, 2 * bwd.shape[0])

    came, owns = [], []
    own = join_rows(where, after(send_heads([normed[0]] * n_head), bwd))
    bwd = (bwd, swap(after(bwd, own), CORE))
    for chunk in range(CHUNKS):
        owns.append(own)
        came.append(depart(own))
        if chunk + 1 < CHUNKS:
            own = join_rows(where, send_heads([after(normed[chunk + 1], own)] * n_head))
            came[chunk] = after(came[chunk], own)
    evens = list(range(0, n_ctx, 2))
    odds = [mask | CORE for mask in evens]
    pending, sums, first = [], [], None
    for chunk in range(CHUNKS):
        near = forward(owns[chunk], came[chunk], first and [part for _, _, part in first])
        rows = {mask: part for mask, part in zip(evens, near)}
        rows |= {mask | CORE: swap(part, CORE) for mask, part in rows.items()}
        if pending:
            rows = after(rows, [part for _, _, part in first])
        experts_of = functools.partial(
            expert_pieces, chunk * chunk_rows, where, gate=w_gate, up=w_up, down=w_down, routes=fwd
        )
        if chunk + 1 < CHUNKS:
            here, far = experts_of(rows=rows, groups=[evens, odds])
            arrived = swap(after(far, came[chunk + 1]), CORE)
        else:
            (far,) = experts_of(rows=rows, groups=[odds])
            ready = [far]
            arrived = swap(after(far, pending[-1][3]) if pending else far, CORE)
            if pending:
                last = last_sums(*pending[-1][:2], pending[-1][3])
                ready += [part for _, _, part in last]
                last = [(mask, start, swap(part, mask)) for mask, start, part in last]
                pending[-1] += (last,)
                arrived = after(arrived, [part for _, _, part in last])
            (here,) = experts_of(rows=after(rows, ready), groups=[evens])
        first = first_sums(here, arrived)
        pending.append((here, arrived, first, send_sums(first)))
    last = last_sums(*pending[-1][:2], pending[-1][3])
    pending[-1] += ([(mask, start, swap(part, mask)) for mask, start, part in last],)
    for chunk in range(CHUNKS):
        here, arrived, first, received, last = pending[chunk]
        terms = [(start, part) for (_, start, _), part in zip(first, received)]
        if last:
            terms = terms[2:] + [(start, part) for _, start, part in last]
        starts, others = zip(*terms)
        if chunk + 1 < CHUNKS:
            others = after(others, [part for _, _, part in pending[chunk + 1][2]])
        sums.append(send_heads(sum_terms(where, attn[chunk], here, arrived, others, starts, n_head)))
    grads = core_grads(where, qkv, grad_core, steps, fwd, bwd)
    return (final_sum(where, hidden_in, sums), *grads)


def solution(mesh):
    in_specs = (
        P("ctx", None),
        P(),
        P(None, None, "head"),
        P(None, None, "head"),
        P("ctx", "head"),
        P("head"),
        P("head", None),
        P(),
        P("ctx", None),
        P("ctx", None),
        P(("ctx", "head"), None, None),
        P(("ctx", "head"), None, None),
        P(("ctx", "head"), None, None),
        P("ctx", "head"),
    )
    out_specs = (P("ctx", "head"), P("ctx", "head"), P("ctx", "head"), P("ctx", "head"))
    return jax.shard_map(body, mesh=mesh, in_specs=in_specs, out_specs=out_specs, check_vma=False)
```

```python
import functools

import jax
import jax.numpy as jnp
from jax import lax
from jax.experimental import pallas as pl
from jax.experimental.pallas import tpu as pltpu
from jax.sharding import PartitionSpec as P

KERNEL = 4
EXP_CTX = 2
LANES = 128
RIM = 16
MIB = 1024 * 1024
HI = lax.Precision.HIGHEST
BF = jnp.bfloat16
F32 = jnp.float32
NT = (((1,), (1,)), ((), ()))
TN = (((0,), (0,)), ((), ()))
NN = (((1,), (0,)), ((), ()))


def params(mib):
    return pltpu.CompilerParams(vmem_limit_bytes=mib * MIB)


def mm(a, b, dims=NN):
    return lax.dot_general(a, b, dims, preferred_element_type=F32)


def pick_block(extent, target):
    return target if extent % target == 0 else extent


def qkv_kernel(x_hbm, gain_ref, w_hbm, mixed_ref, rim_ref, x_ref, w_ref, normed_ref, x_sem, sems):
    kinds, width, chans = w_ref.shape
    load = pltpu.make_async_copy(x_hbm, x_ref, x_sem)
    load.start()
    part = width // sems.shape[1]
    copies = []
    for kind in range(kinds):
        at = [pl.ds(piece * part, part) for piece in range(sems.shape[1])]
        copies.append(
            [
                pltpu.make_async_copy(w_hbm.at[kind, rows], w_ref.at[kind, rows], sems.at[kind, piece])
                for piece, rows in enumerate(at)
            ]
        )
        for copy in copies[kind]:
            copy.start()
    load.wait()
    values = x_ref[...].astype(F32)
    scale = lax.rsqrt(jnp.mean(values * values, axis=-1, keepdims=True) + 1e-06)
    normed_ref[...] = (values * scale * gain_ref[...]).astype(BF)
    for kind in range(kinds):
        for copy in copies[kind]:
            copy.wait()
        out = mm(normed_ref[...], w_ref[kind]).astype(BF)
        mixed_ref[kind] = out
        rim_ref[kind] = out[out.shape[0] - RIM :]


def project(x, gain, weights):
    rows, width = x.shape
    kinds, _, chans = weights.shape
    vmem = pl.BlockSpec(memory_space=pltpu.VMEM)
    hbm = pl.BlockSpec(memory_space=pltpu.HBM)
    return pl.pallas_call(
        qkv_kernel,
        in_specs=[hbm, vmem, hbm],
        out_specs=[vmem, vmem],
        out_shape=[
            jax.ShapeDtypeStruct((kinds, rows, chans), BF),
            jax.ShapeDtypeStruct((kinds, RIM, chans), BF),
        ],
        scratch_shapes=[
            pltpu.VMEM((rows, width), BF),
            pltpu.VMEM((kinds, width, chans), BF),
            pltpu.VMEM((rows, width), BF),
            pltpu.SemaphoreType.DMA,
            pltpu.SemaphoreType.DMA((kinds, 4)),
        ],
        compiler_params=params(60),
        name="qkv_projection",
    )(x, gain.reshape(1, width), weights)


def decay_sums(steps):
    rows = steps.shape[1]
    row_at = lax.broadcasted_iota(jnp.int32, (rows, rows), 0)
    col_at = lax.broadcasted_iota(jnp.int32, (rows, rows), 1)
    lower = row_at >= col_at
    tri = jnp.where(lower, 1.0, 0.0).astype(F32)
    along = lax.dot_general(steps, tri, NT, precision=HI, preferred_element_type=F32)
    down = lax.dot_general(tri, steps, NT, precision=HI, preferred_element_type=F32)
    return along, down, lower


def payload_tail(total, size):
    full = jnp.broadcast_to(total, (RIM, size))
    first = full.astype(BF).astype(F32)
    second = (full - first).astype(BF).astype(F32)
    third = full - first - second
    at = lax.broadcasted_iota(jnp.int32, (RIM, size), 0)
    return jnp.where(at == 0, first, jnp.where(at == 1, second, jnp.where(at == 2, third, 0.0)))


def route_rows(ids_ref, weights_ref, experts):
    top, tok = ids_ref.shape
    expert = lax.broadcasted_iota(jnp.int32, (experts, tok), 0)
    table = jnp.zeros((experts, tok), F32)
    for choice in range(top):
        table += jnp.where(expert == ids_ref[choice : choice + 1, :], weights_ref[choice : choice + 1, :], 0.0)
    first = table.astype(BF).astype(F32)
    second = (table - first).astype(BF).astype(F32)
    return jnp.concatenate([first, second, table - first - second], axis=0)


def conv_kernel(
    experts, mixed_any, rim_ref, taps_ref, steps_ref, cot_ref, ids_ref, weights_ref, qkv_ref, fwd_ref, bwd_ref,
    pad_ref, mixed_ref, sems,
):
    kinds, rows, chans = mixed_ref.shape
    copies = [pltpu.make_async_copy(mixed_any.at[kind], mixed_ref.at[kind], sems.at[kind]) for kind in range(kinds)]
    for copy in copies:
        copy.start()
    heads = steps_ref.shape[0]
    size = chans // heads
    along, down, _ = decay_sums(steps_ref[...])
    for kind in range(kinds):
        copies[kind].wait()
        pad_ref[:RIM] = rim_ref[kind].astype(F32)
        pad_ref[RIM:] = mixed_ref[kind].astype(F32)
        total = taps_ref[kind, 0:1, :] * pad_ref[RIM:]
        for offset in range(1, KERNEL):
            total += taps_ref[kind, offset : offset + 1, :] * pad_ref[RIM - offset : RIM - offset + rows]
        activ = total * jax.nn.sigmoid(total)
        if kind == 0:
            activ = activ * size ** (-0.5)
        qkv_ref[kind] = activ.astype(BF)
    routes = rows // LANES * 3 * experts
    table = route_rows(ids_ref, weights_ref, experts).astype(BF)
    for part in range(rows // LANES):
        fwd_ref[part * 3 * experts : (part + 1) * 3 * experts] = table[:, part * LANES : (part + 1) * LANES]
    for head in range(heads):
        at = slice(head * size, (head + 1) * size)
        base = head * (size + RIM)
        behind = routes + base
        last = along[head : head + 1, rows - 1 : rows]
        lead = jnp.exp(down[:, head : head + 1])
        tail = jnp.exp(last - down[:, head : head + 1])
        key_out = (qkv_ref[1, :, at].astype(F32) * tail).astype(BF)
        query_out = (qkv_ref[0, :, at].astype(F32) * lead).astype(BF)
        ends = payload_tail(last, size).astype(BF)
        fwd_ref[behind : behind + size] = mm(key_out, qkv_ref[2, :, at], TN).astype(BF)
        fwd_ref[behind + size : behind + size + RIM] = ends
        bwd_ref[base : base + size] = mm(query_out, cot_ref[:, at], TN).astype(BF)
        bwd_ref[base + size : base + size + RIM] = ends


def local_states(mixed, rim, taps, steps, cot, ids, weights, experts):
    kinds, rows, chans = mixed.shape
    heads = steps.shape[0]
    size = chans // heads
    states = heads * (size + RIM)
    return pl.pallas_call(
        functools.partial(conv_kernel, experts),
        in_specs=[pl.BlockSpec(memory_space=pl.ANY)] + [pl.BlockSpec(memory_space=pltpu.VMEM)] * 6,
        out_specs=[pl.BlockSpec(memory_space=pltpu.VMEM)] * 3,
        out_shape=[
            jax.ShapeDtypeStruct((kinds, rows, chans), BF),
            jax.ShapeDtypeStruct((states + rows // LANES * 3 * experts, size), BF),
            jax.ShapeDtypeStruct((states, size), BF),
        ],
        scratch_shapes=[
            pltpu.VMEM((rows + RIM, chans), F32),
            pltpu.VMEM(mixed.shape, BF),
            pltpu.SemaphoreType.DMA((kinds,)),
        ],
        compiler_params=params(12),
        name="conv_states",
    )(mixed, rim, taps, steps, cot, ids, weights)


def arrange(me_ref, near_ref, far_ref, held_ref):
    for at in range(near_ref.shape[0]):
        held_ref[me_ref[0] ^ (2 * at)] = near_ref[at]
        held_ref[me_ref[0] ^ (2 * at + 1)] = far_ref[at]


def entering(held_ref, heads, head, size, first, last, step):
    base = held_ref.shape[1] - (heads - head) * (size + RIM)

    def hop(count, total):
        at = first + count * step
        ends = held_ref[at, base + size : base + size + RIM, :].astype(F32)
        factor = jnp.exp(ends[0:1] + ends[1:2] + ends[2:3])
        return factor * total + held_ref[at, base : base + size, :].astype(F32)

    return lax.fori_loop(0, (last - first) * step, hop, jnp.zeros((size, size), F32))


def core_kernel(chunks, me_ref, qkv_ref, steps_ref, gain_ref, near_ref, far_ref, w_ref, *refs):
    out_refs, (headed_ref, held_ref, whole_ref) = refs[:-3], refs[-3:]
    _, rows, chans = qkv_ref.shape
    heads = steps_ref.shape[0]
    size = chans // heads
    arrange(me_ref, near_ref, far_ref, held_ref)
    along, down, lower = decay_sums(steps_ref[...])
    for head in range(heads):
        at = slice(head * size, (head + 1) * size)
        state = entering(held_ref, heads, head, size, 0, me_ref[0], 1).astype(BF)
        diff = down[:, head : head + 1] - along[head : head + 1, :]
        mask = jnp.exp(jnp.where(lower, diff, -jnp.inf))
        query = qkv_ref[0, :, at]
        scores = (mm(query, qkv_ref[1, :, at], NT) * mask).astype(BF)
        attended = mm(scores, qkv_ref[2, :, at])
        attended += mm(query, state) * jnp.exp(down[:, head : head + 1])
        scale = lax.rsqrt(jnp.mean(attended * attended, axis=-1, keepdims=True) + 1e-06)
        headed_ref[:, at] = (attended * scale * gain_ref[:, at]).astype(BF)
    whole_ref[...] = mm(headed_ref[...], w_ref[...]).astype(BF)
    part = rows // len(out_refs) // chunks
    for mask, ref in enumerate(out_refs):
        for chunk in range(chunks):
            start = chunk * len(out_refs) * part + (me_ref[2] ^ mask) * part
            ref[chunk * part : (chunk + 1) * part] = whole_ref[pl.ds(pl.multiple_of(start, part), part), :]


def core_out(where, qkv, steps, near, far, gain, w_out, chunks, parts):
    _, rows, chans = qkv.shape
    width = w_out.shape[1]
    vmem = pl.BlockSpec(memory_space=pltpu.VMEM)
    return pl.pallas_call(
        functools.partial(core_kernel, chunks),
        in_specs=[pl.BlockSpec(memory_space=pltpu.SMEM)] + [vmem] * 6,
        out_shape=[jax.ShapeDtypeStruct((rows // parts, width), BF)] * parts,
        scratch_shapes=[
            pltpu.VMEM((rows, chans), BF),
            pltpu.VMEM((2 * near.shape[0], *near.shape[1:]), BF),
            pltpu.VMEM((rows, width), BF),
        ],
        compiler_params=params(16),
        name="core_out",
    )(where, qkv, steps, gain.reshape(1, chans), near, far, w_out)


def grad_kernel(
    me_ref, qkv_ref, cot_ref, steps_ref, fwd_near, fwd_far, bwd_near, bwd_far, gq_ref, gk_ref, gv_ref, fwd_ref, bwd_ref
):
    _, rows, chans = qkv_ref.shape
    heads = steps_ref.shape[0]
    size = chans // heads
    count = fwd_ref.shape[0]
    arrange(me_ref, fwd_near, fwd_far, fwd_ref)
    arrange(me_ref, bwd_near, bwd_far, bwd_ref)
    along, down, lower = decay_sums(steps_ref[...])
    for head in range(heads):
        at = slice(head * size, (head + 1) * size)
        state = entering(fwd_ref, heads, head, size, 0, me_ref[0], 1).astype(BF)
        after = entering(bwd_ref, heads, head, size, count - 1, me_ref[0], -1).astype(BF)
        here = down[:, head : head + 1]
        lead = jnp.exp(here)
        tail = jnp.exp(along[head : head + 1, rows - 1 : rows] - here)
        mask = jnp.exp(jnp.where(lower, here - along[head : head + 1, :], -jnp.inf))
        query, key, val = qkv_ref[0, :, at], qkv_ref[1, :, at], qkv_ref[2, :, at]
        cot = cot_ref[:, at]
        scores = (mm(query, key, NT) * mask).astype(BF)
        dov = (mm(cot, val, NT) * mask).astype(BF)
        gq_ref[:, at] = (mm(dov, key) + lead * mm(cot, state, NT)).astype(BF)
        gk_ref[:, at] = (mm(dov, query, TN) + tail * mm(val, after, NT)).astype(BF)
        gv_ref[:, at] = (mm(scores, cot, TN) + tail * mm(key, after)).astype(BF)


def core_grads(where, qkv, cot, steps, fwd, bwd):
    _, rows, chans = qkv.shape
    count = 2 * fwd[0].shape[0]
    vmem = pl.BlockSpec(memory_space=pltpu.VMEM)
    return pl.pallas_call(
        grad_kernel,
        in_specs=[pl.BlockSpec(memory_space=pltpu.SMEM)] + [vmem] * 7,
        out_shape=[jax.ShapeDtypeStruct((rows, chans), BF)] * 3,
        scratch_shapes=[pltpu.VMEM((count, *fwd[0].shape[1:]), BF), pltpu.VMEM((count, *bwd[0].shape[1:]), BF)],
        compiler_params=params(24),
        name="core_grads",
    )(where, qkv, cot, steps, *fwd, *bwd)


def norm_kernel(count, where_ref, x_ref, gain_ref, *refs):
    chunks = (len(refs) - count) // 2
    parts, outs, attns = refs[:count], refs[count : count + chunks], refs[count + chunks :]
    rows = outs[0].shape[0]
    for chunk, (out_ref, attn_ref) in enumerate(zip(outs, attns)):
        at = slice(chunk * rows, (chunk + 1) * rows)
        attn = functools.reduce(jnp.add, [part[at].astype(F32) for part in parts])
        attn_ref[...] = attn
        start = pl.multiple_of((chunk * count + where_ref[2]) * rows, rows)
        resid = x_ref[pl.ds(start, rows), :].astype(F32) + attn
        scale = lax.rsqrt(jnp.mean(resid * resid, axis=-1, keepdims=True) + 1e-06)
        out_ref[...] = (resid * scale * gain_ref[...]).astype(BF)


def norm_rows(where, x, parts, gain, chunks):
    rows, width = parts[0].shape[0] // chunks, parts[0].shape[1]
    vmem = pl.BlockSpec(memory_space=pltpu.VMEM)
    outs = pl.pallas_call(
        functools.partial(norm_kernel, len(parts)),
        in_specs=[pl.BlockSpec(memory_space=pltpu.SMEM)] + [vmem] * (2 + len(parts)),
        out_shape=[jax.ShapeDtypeStruct((rows, width), BF)] * chunks
        + [jax.ShapeDtypeStruct((rows, width), F32)] * chunks,
        compiler_params=params(12),
        name="moe_norm",
    )(where, x, gain.reshape(1, width), *parts)
    return list(outs[:chunks]), list(outs[chunks:])


def join_kernel(where_ref, *refs):
    parts, out_ref = refs[:-1], refs[-1]
    rows = parts[0].shape[0]
    for mask, ref in enumerate(parts):
        out_ref[pl.ds(pl.multiple_of((where_ref[2] ^ mask) * rows, rows), rows), :] = ref[...]


def join_rows(where, parts):
    rows, width = parts[0].shape
    vmem = pl.BlockSpec(memory_space=pltpu.VMEM)
    return pl.pallas_call(
        join_kernel,
        in_specs=[pl.BlockSpec(memory_space=pltpu.SMEM)] + [vmem] * len(parts),
        out_shape=jax.ShapeDtypeStruct((len(parts) * rows, width), BF),
        compiler_params=params(16),
        name="join_rows",
    )(where, *parts)


PAIR = 2


def expert_kernel(groups, chunk, experts, where_ref, near_routes, far_routes, gate_ref, up_ref, down_ref, *refs):
    masks = [mask for group in groups for mask in group]
    row_refs, outs, (rows_ref, sems) = refs[: len(masks)], refs[len(masks) : -2], refs[-2:]
    _, tok, width = outs[0].shape
    steps = len(masks) // PAIR
    step = pl.program_id(0)
    slot = lax.rem(step, 2)

    def start(at):
        for part in range(PAIR):
            target = rows_ref.at[at % 2, pl.ds(part * tok, tok)]
            pltpu.make_async_copy(row_refs[PAIR * at + part], target, sems.at[at % 2]).start()

    @pl.when(step == 0)
    def _():
        start(0)

    for at in range(1, steps):

        @pl.when(step == at - 1)
        def _(at=at):
            start(at)

    here = lax.broadcasted_iota(jnp.int32, (3 * experts, LANES), 0)
    mine = (here == where_ref[1]) | (here == where_ref[1] + experts) | (here == where_ref[1] + 2 * experts)
    square = (LANES, LANES)
    diagonal = lax.broadcasted_iota(jnp.int32, square, 0) == lax.broadcasted_iota(jnp.int32, square, 1)
    weights = []
    for part in range(PAIR):
        mask = jnp.int32(masks[part])
        for at in range(1, steps):
            mask = jnp.where(step == at, masks[PAIR * at + part], mask)
        index = lax.shift_right_logical(mask, 1)
        for block in range(tok // LANES):
            base = (chunk // LANES + block) * 3 * experts
            at = slice(base, base + 3 * experts)
            near, far = near_routes[index, at, :].astype(F32), far_routes[index, at, :].astype(F32)
            table = jnp.where((mask & CORE) == 0, near, far)
            row = jnp.sum(jnp.where(mine, table, 0.0), axis=0, keepdims=True)
            weights.append(jnp.sum(jnp.where(diagonal, jnp.broadcast_to(row, square), 0.0), axis=1, keepdims=True))

    pltpu.make_async_copy(rows_ref.at[slot], rows_ref.at[slot], sems.at[slot]).wait()
    tokens = rows_ref[slot]
    gate = mm(tokens, gate_ref[0])
    inner = (gate * jax.nn.sigmoid(gate) * mm(tokens, up_ref[0])).astype(BF)
    cols = pick_block(width, 512)
    per = steps // len(outs)
    for begin in range(0, width, cols):
        piece = mm(inner, down_ref[0, :, begin : begin + cols])
        for at, weight in enumerate(weights):
            part, row = divmod(at * LANES, tok)
            scaled = (piece[at * LANES : (at + 1) * LANES] * weight).astype(BF)
            for group, out_ref in enumerate(outs):

                @pl.when((step >= group * per) & (step < (group + 1) * per))
                def _(scaled=scaled, part=part, row=row, out_ref=out_ref):
                    out_ref[part, row : row + LANES, begin : begin + cols] = scaled


def stage_kernel(where_ref, *refs):
    out_ref = refs[-1]
    for at in range(where_ref.shape[0]):
        out_ref[at] = where_ref[at]


def stage(where, *weights):
    smem = pl.BlockSpec(memory_space=pltpu.SMEM)
    return pl.pallas_call(
        stage_kernel,
        in_specs=[smem] + [pl.BlockSpec(memory_space=pltpu.VMEM)] * len(weights),
        out_specs=smem,
        out_shape=jax.ShapeDtypeStruct(where.shape, where.dtype),
        compiler_params=params(2),
        name="stage_weights",
    )(where, *weights)


def expert_pieces(chunk, where, rows, groups, gate, up, down, routes):
    blocks = [rows[mask] for group in groups for mask in group]
    tok, width = blocks[0].shape
    hidden = gate.shape[2]
    count, each = len(blocks), len(groups[0])
    per = each // PAIR
    experts = EXP_CTX * 2 * routes[0].shape[0]
    route_rows = CHUNKS * tok // LANES * 3 * experts
    vmem = pl.BlockSpec(memory_space=pltpu.VMEM)
    table = pl.BlockSpec((routes[0].shape[0], route_rows, LANES), lambda i: (0, 0, 0))

    def out_spec(group):
        return pl.BlockSpec((PAIR, tok, width), lambda i: (jnp.clip(i - group * per, 0, per - 1), 0, 0))

    return pl.pallas_call(
        functools.partial(expert_kernel, tuple(map(tuple, groups)), chunk, experts),
        grid=(count // PAIR,),
        in_specs=[pl.BlockSpec(memory_space=pltpu.SMEM), table, table]
        + [vmem] * 3
        + [pl.BlockSpec(memory_space=pl.ANY)] * count,
        out_specs=[out_spec(group) for group in range(len(groups))],
        out_shape=[jax.ShapeDtypeStruct((each, tok, width), BF)] * len(groups),
        scratch_shapes=[
            pltpu.VMEM((2, PAIR * tok, width), BF),
            pltpu.SemaphoreType.DMA((2,)),
        ],
        compiler_params=params(20),
        cost_estimate=pl.CostEstimate(
            flops=6 * count * tok * width * hidden,
            bytes_accessed=4 * count * tok * width,
            transcendentals=count * tok * hidden,
        ),
        name="expert_pieces",
    )(where, *routes, gate, up, down, *blocks)


CORE, ROW, COL = 1, 2, 4
PLANE = 8


def swap(value, mask):
    return lax.ppermute(value, "ctx", [(at, at ^ mask) for at in range(lax.axis_size("ctx"))])


def send_heads(parts):
    count = lax.axis_size("head")
    return [parts[0]] + [
        lax.ppermute(parts[mask], "head", [(at, at ^ mask) for at in range(count)]) for mask in range(1, count)
    ]


def spread_near(own):
    return jnp.stack([own] + [swap(own, mask) for mask in range(2, lax.axis_size("ctx"), 2)])


def double(near, mask):
    return jnp.concatenate([near, swap(near, mask)])


def plus(*terms):
    return functools.reduce(jnp.add, [term.astype(F32) for term in terms]).astype(BF)


def after(value, other):
    return lax.optimization_barrier((value, other))[0]


def depart(own):
    masks = (ROW, COL) if lax.axis_size("ctx") == PLANE else range(2, lax.axis_size("ctx"), 2)
    return {mask: swap(own, mask) for mask in masks}


def forward(came):
    if lax.axis_size("ctx") != PLANE:
        return []
    half = came[ROW].shape[0] // 2
    return [swap(came[ROW][:half], COL), swap(came[COL][half:], ROW)]


def first_sums(here, arrived):
    tok = here.shape[1]
    if lax.axis_size("ctx") != PLANE:
        return [(2 * at, plus(here[at], arrived[at]), [(0, 0, tok)]) for at in range(1, here.shape[0])]
    half, across = tok // 2, (ROW | COL) // 2
    sums = []
    for mask, start in ((ROW, 0), (COL, half)):
        part = slice(start, start + half)
        pieces = [plus(here[at, part], arrived[at, part]) for at in (across, mask // 2)]
        sums.append((mask, jnp.concatenate(pieces), [(half, start, half)]))
    return sums


def last_sums(here, arrived, came):
    if lax.axis_size("ctx") != PLANE:
        return []
    half = here.shape[1] // 2
    row, col = ROW // 2, COL // 2
    return [
        (COL, plus(here[col, :half], arrived[col, :half], came[0][:half]), [(0, 0, half)]),
        (ROW, plus(here[row, half:], arrived[row, half:], came[1][:half]), [(0, half, half)]),
    ]


def send_sums(sums):
    return [swap(rows, mask) for mask, rows, _ in sums]


def arrays(sums):
    return [rows for _, rows, _ in sums]


def terms_of(sums, received):
    return [(rows, places) for (_, _, places), rows in zip(sums, received) if places]


def sum_kernel(places, where_ref, attn_ref, near_ref, arrived_ref, *refs):
    parts = attn_ref.shape[1] // refs[-1].shape[1]
    others, outs, total_ref = refs[: -parts - 1], refs[-parts - 1 : -1], refs[-1]
    part, width = attn_ref.shape
    cols = width // parts
    own = pl.ds(pl.multiple_of(where_ref[2] * part, part), part)
    for mask, out_ref in enumerate(outs):
        at = pl.ds(pl.multiple_of((where_ref[2] ^ mask) * cols, cols), cols)
        total = near_ref[0, :, at].astype(F32) + arrived_ref[0, :, at].astype(F32)
        total_ref[...] = total
        for spots, ref in zip(places, others):
            for source, target, count in spots:
                total_ref[target : target + count] += ref[source : source + count, at].astype(F32)
        total_ref[own, :] += attn_ref[:, at]
        out_ref[...] = total_ref[...].astype(BF)


def sum_terms(where, attn, near, arrived, terms, parts):
    others, places = [rows for rows, _ in terms], tuple(tuple(spots) for _, spots in terms)
    _, tok, width = near.shape
    part = attn.shape[0]
    cols = width // parts
    first = pl.BlockSpec((1, tok, width), lambda i: (0, 0, 0))
    return pl.pallas_call(
        functools.partial(sum_kernel, places),
        grid=(1,),
        in_specs=[
            pl.BlockSpec(memory_space=pltpu.SMEM),
            pl.BlockSpec((part, width), lambda i: (0, 0)),
            first,
            first,
        ]
        + [pl.BlockSpec(part.shape, lambda i: (0, 0)) for part in others],
        out_specs=[pl.BlockSpec((tok, cols), lambda i: (0, 0))] * parts,
        out_shape=[jax.ShapeDtypeStruct((tok, cols), BF)] * parts,
        scratch_shapes=[pltpu.VMEM((tok, cols), F32)],
        compiler_params=params(24),
        name="sum_terms",
    )(where, attn, near, arrived, *others)


def final_kernel(count, where_ref, x_ref, *refs):
    del where_ref
    out_ref = refs[-1]
    rows = refs[0].shape[0]
    for chunk in range((len(refs) - 1) // count):
        at = slice(chunk * rows, (chunk + 1) * rows)
        terms = [x_ref[at]] + [ref[...] for ref in refs[chunk * count : (chunk + 1) * count]]
        out_ref[at] = functools.reduce(jnp.add, [term.astype(F32) for term in terms]).astype(BF)


def final_sum(where, x, parts):
    rows, cols = parts[0][0].shape
    total = len(parts) * rows
    block = pl.BlockSpec((rows, cols), lambda i, where: (0, 0))
    return pl.pallas_call(
        functools.partial(final_kernel, len(parts[0])),
        grid_spec=pltpu.PrefetchScalarGridSpec(
            num_scalar_prefetch=1,
            grid=(1,),
            in_specs=[pl.BlockSpec((total, cols), lambda i, where: (0, where[2]))]
            + [block] * (len(parts) * len(parts[0])),
            out_specs=pl.BlockSpec((total, cols), lambda i, where: (0, 0)),
        ),
        out_shape=jax.ShapeDtypeStruct((total, cols), BF),
        compiler_params=params(12),
        name="layer_out",
    )(where, x, *[part for chunk in parts for part in chunk])


CHUNKS = 2


def body(
    hidden_in,
    gain_attn,
    w_qkv,
    conv_w,
    log_decay,
    norm_gain,
    w_out,
    gain_moe,
    expert_ids,
    route_weights,
    w_gate,
    w_up,
    w_down,
    grad_core,
):
    n_ctx, n_head = lax.axis_size("ctx"), lax.axis_size("head")
    my_ctx, my_head = lax.axis_index("ctx"), lax.axis_index("head")
    experts = EXP_CTX * n_ctx
    shards = n_head // EXP_CTX
    where = jnp.stack([my_ctx, EXP_CTX * my_ctx + my_head // shards, my_head]).astype(jnp.int32)
    steps = log_decay.T
    chunk_rows = hidden_in.shape[0] // CHUNKS

    mixed, rim = project(hidden_in, gain_attn, jnp.transpose(w_qkv, (1, 0, 2)))
    rim = lax.ppermute(rim, "ctx", [(at, at + 1) for at in range(n_ctx - 1)])
    qkv, fwd, bwd = local_states(
        mixed, rim, jnp.transpose(conv_w, (1, 0, 2)), steps, grad_core, expert_ids.T, route_weights.T, experts
    )
    fwd = spread_near(fwd)
    fwd = (fwd, swap(fwd, CORE))
    where = stage(after(where, qkv), w_out)
    parts = core_out(where, qkv, steps, *fwd, norm_gain, w_out, CHUNKS, n_head)
    where = stage(after(where, parts), w_gate, w_up, w_down)
    bwd = double(after(bwd, parts)[None], ROW)
    normed, attn = norm_rows(where, hidden_in, after(send_heads(parts), bwd), gain_moe, CHUNKS)
    bwd = after(bwd, normed)
    while bwd.shape[0] < n_ctx // 2:
        bwd = double(bwd, 2 * bwd.shape[0])

    evens = list(range(0, n_ctx, 2))
    odds = [mask | CORE for mask in evens]
    own = join_rows(where, after(send_heads([normed[0]] * n_head), bwd))
    bwd = (bwd, swap(after(bwd, own), CORE))
    rows = []
    for chunk in range(CHUNKS):
        rows.append({0: own, CORE: swap(own, CORE)} | depart(own))
        if chunk + 1 < CHUNKS:
            parts = send_heads([after(normed[chunk + 1], own)] * n_head)
            own = join_rows(where, after(parts, rows[chunk][CORE]))
            rows[chunk] = after(rows[chunk], own)

    pending, sums, first, arrived = [], [], None, None
    for chunk in range(CHUNKS):
        here_rows = rows[chunk]
        halves = forward(here_rows)
        here_rows |= {mask | CORE: swap(part, CORE) for mask, part in here_rows.items() if mask and not mask & CORE}
        if pending:
            arrived = after(arrived, [part for mask, part in here_rows.items() if mask & CORE])
            first = first_sums(pending[-1][0], arrived)
            pending[-1] += (arrived, first, send_sums(first))
            halves = after(halves, arrays(first))
        if halves:
            across = jnp.concatenate(halves)
            here_rows |= {ROW | COL: across, ROW | COL | CORE: swap(across, CORE)}
        if pending:
            here_rows = after(here_rows, arrays(first))
        experts_of = functools.partial(
            expert_pieces, chunk * chunk_rows, where, gate=w_gate, up=w_up, down=w_down, routes=fwd
        )
        if chunk + 1 < CHUNKS:
            here, far = experts_of(rows=here_rows, groups=[evens, odds])
            arrived = swap(after(far, (rows[chunk + 1], bwd)), CORE)
            pending.append((here,))
        else:
            (far,) = experts_of(rows=here_rows, groups=[odds])
            arrived = swap(after(far, pending[-1][3]), CORE)
            last = last_sums(*pending[-1][:2], pending[-1][3])
            received = send_sums(last)
            pending[-1] += (terms_of(first, pending[-1][3]) + terms_of(last, received),)
            (here,) = experts_of(rows=after(here_rows, [far] + arrays(last)), groups=[evens])
            arrived = after(arrived, received)
            first = first_sums(here, arrived)
            pending.append((here, arrived, first, send_sums(first)))

    for chunk in range(CHUNKS):
        here, arrived, first, received = pending[chunk][:4]
        if chunk + 1 < CHUNKS:
            terms = pending[chunk][4]
            held = after([rows for rows, _ in terms], arrays(pending[chunk + 1][2]))
            terms = list(zip(held, [places for _, places in terms]))
        else:
            last = last_sums(here, arrived, after(received, sums[-1][0]))
            terms = terms_of(first, received) + terms_of(last, send_sums(last))
        sums.append(send_heads(sum_terms(where, attn[chunk], here, arrived, terms, n_head)))
    grads = core_grads(where, qkv, grad_core, steps, fwd, bwd)
    return (final_sum(where, hidden_in, sums), *grads)


def solution(mesh):
    in_specs = (
        P("ctx", None),
        P(),
        P(None, None, "head"),
        P(None, None, "head"),
        P("ctx", "head"),
        P("head"),
        P("head", None),
        P(),
        P("ctx", None),
        P("ctx", None),
        P(("ctx", "head"), None, None),
        P(("ctx", "head"), None, None),
        P(("ctx", "head"), None, None),
        P("ctx", "head"),
    )
    out_specs = (P("ctx", "head"), P("ctx", "head"), P("ctx", "head"), P("ctx", "head"))
    return jax.shard_map(body, mesh=mesh, in_specs=in_specs, out_specs=out_specs, check_vma=False)
```

```python
import functools

import jax
import jax.numpy as jnp
from jax import lax
from jax.experimental import pallas as pl
from jax.experimental.pallas import tpu as pltpu
from jax.sharding import PartitionSpec as P

KERNEL = 4
EXP_CTX = 2
LANES = 128
RIM = 16
MIB = 1024 * 1024
HI = lax.Precision.HIGHEST
BF = jnp.bfloat16
F32 = jnp.float32
NT = (((1,), (1,)), ((), ()))
TN = (((0,), (0,)), ((), ()))
NN = (((1,), (0,)), ((), ()))


def params(mib):
    return pltpu.CompilerParams(vmem_limit_bytes=mib * MIB)


def mm(a, b, dims=NN):
    return lax.dot_general(a, b, dims, preferred_element_type=F32)


def pick_block(extent, target):
    return target if extent % target == 0 else extent


def qkv_kernel(x_hbm, gain_ref, w_hbm, mixed_ref, rim_ref, x_ref, w_ref, normed_ref, x_sem, sems):
    kinds, width, chans = w_ref.shape
    load = pltpu.make_async_copy(x_hbm, x_ref, x_sem)
    load.start()
    part = width // sems.shape[1]
    copies = []
    for kind in range(kinds):
        at = [pl.ds(piece * part, part) for piece in range(sems.shape[1])]
        copies.append(
            [
                pltpu.make_async_copy(w_hbm.at[kind, rows], w_ref.at[kind, rows], sems.at[kind, piece])
                for piece, rows in enumerate(at)
            ]
        )
        for copy in copies[kind]:
            copy.start()
    load.wait()
    values = x_ref[...].astype(F32)
    scale = lax.rsqrt(jnp.mean(values * values, axis=-1, keepdims=True) + 1e-06)
    normed_ref[...] = (values * scale * gain_ref[...]).astype(BF)
    for kind in range(kinds):
        for copy in copies[kind]:
            copy.wait()
        out = mm(normed_ref[...], w_ref[kind]).astype(BF)
        mixed_ref[kind] = out
        rim_ref[kind] = out[out.shape[0] - RIM :]


def project(x, gain, weights):
    rows, width = x.shape
    kinds, _, chans = weights.shape
    vmem = pl.BlockSpec(memory_space=pltpu.VMEM)
    hbm = pl.BlockSpec(memory_space=pltpu.HBM)
    return pl.pallas_call(
        qkv_kernel,
        in_specs=[hbm, vmem, hbm],
        out_specs=[vmem, vmem],
        out_shape=[
            jax.ShapeDtypeStruct((kinds, rows, chans), BF),
            jax.ShapeDtypeStruct((kinds, RIM, chans), BF),
        ],
        scratch_shapes=[
            pltpu.VMEM((rows, width), BF),
            pltpu.VMEM((kinds, width, chans), BF),
            pltpu.VMEM((rows, width), BF),
            pltpu.SemaphoreType.DMA,
            pltpu.SemaphoreType.DMA((kinds, 4)),
        ],
        compiler_params=params(60),
        name="qkv_projection",
    )(x, gain.reshape(1, width), weights)


def decay_sums(steps):
    rows = steps.shape[1]
    row_at = lax.broadcasted_iota(jnp.int32, (rows, rows), 0)
    col_at = lax.broadcasted_iota(jnp.int32, (rows, rows), 1)
    lower = row_at >= col_at
    tri = jnp.where(lower, 1.0, 0.0).astype(F32)
    along = lax.dot_general(steps, tri, NT, precision=HI, preferred_element_type=F32)
    down = lax.dot_general(tri, steps, NT, precision=HI, preferred_element_type=F32)
    return along, down, lower


def payload_tail(total, size):
    full = jnp.broadcast_to(total, (RIM, size))
    first = full.astype(BF).astype(F32)
    second = (full - first).astype(BF).astype(F32)
    third = full - first - second
    at = lax.broadcasted_iota(jnp.int32, (RIM, size), 0)
    return jnp.where(at == 0, first, jnp.where(at == 1, second, jnp.where(at == 2, third, 0.0)))


def route_rows(ids_ref, weights_ref, experts):
    top, tok = ids_ref.shape
    expert = lax.broadcasted_iota(jnp.int32, (experts, tok), 0)
    table = jnp.zeros((experts, tok), F32)
    for choice in range(top):
        table += jnp.where(expert == ids_ref[choice : choice + 1, :], weights_ref[choice : choice + 1, :], 0.0)
    first = table.astype(BF).astype(F32)
    second = (table - first).astype(BF).astype(F32)
    return jnp.concatenate([first, second, table - first - second], axis=0)


def conv_kernel(
    experts, mixed_any, rim_ref, taps_ref, steps_ref, cot_ref, ids_ref, weights_ref, qkv_ref, fwd_ref, bwd_ref,
    pad_ref, mixed_ref, sems,
):
    kinds, rows, chans = mixed_ref.shape
    copies = [pltpu.make_async_copy(mixed_any.at[kind], mixed_ref.at[kind], sems.at[kind]) for kind in range(kinds)]
    for copy in copies:
        copy.start()
    heads = steps_ref.shape[0]
    size = chans // heads
    along, down, _ = decay_sums(steps_ref[...])
    for kind in range(kinds):
        copies[kind].wait()
        pad_ref[:RIM] = rim_ref[kind].astype(F32)
        pad_ref[RIM:] = mixed_ref[kind].astype(F32)
        total = taps_ref[kind, 0:1, :] * pad_ref[RIM:]
        for offset in range(1, KERNEL):
            total += taps_ref[kind, offset : offset + 1, :] * pad_ref[RIM - offset : RIM - offset + rows]
        activ = total * jax.nn.sigmoid(total)
        if kind == 0:
            activ = activ * size ** (-0.5)
        qkv_ref[kind] = activ.astype(BF)
    routes = rows // LANES * 3 * experts
    table = route_rows(ids_ref, weights_ref, experts).astype(BF)
    for part in range(rows // LANES):
        fwd_ref[part * 3 * experts : (part + 1) * 3 * experts] = table[:, part * LANES : (part + 1) * LANES]
    for head in range(heads):
        at = slice(head * size, (head + 1) * size)
        base = head * (size + RIM)
        behind = routes + base
        last = along[head : head + 1, rows - 1 : rows]
        lead = jnp.exp(down[:, head : head + 1])
        tail = jnp.exp(last - down[:, head : head + 1])
        key_out = (qkv_ref[1, :, at].astype(F32) * tail).astype(BF)
        query_out = (qkv_ref[0, :, at].astype(F32) * lead).astype(BF)
        ends = payload_tail(last, size).astype(BF)
        fwd_ref[behind : behind + size] = mm(key_out, qkv_ref[2, :, at], TN).astype(BF)
        fwd_ref[behind + size : behind + size + RIM] = ends
        bwd_ref[base : base + size] = mm(query_out, cot_ref[:, at], TN).astype(BF)
        bwd_ref[base + size : base + size + RIM] = ends


def local_states(mixed, rim, taps, steps, cot, ids, weights, experts):
    kinds, rows, chans = mixed.shape
    heads = steps.shape[0]
    size = chans // heads
    states = heads * (size + RIM)
    return pl.pallas_call(
        functools.partial(conv_kernel, experts),
        in_specs=[pl.BlockSpec(memory_space=pl.ANY)] + [pl.BlockSpec(memory_space=pltpu.VMEM)] * 6,
        out_specs=[pl.BlockSpec(memory_space=pltpu.VMEM)] * 3,
        out_shape=[
            jax.ShapeDtypeStruct((kinds, rows, chans), BF),
            jax.ShapeDtypeStruct((states + rows // LANES * 3 * experts, size), BF),
            jax.ShapeDtypeStruct((states, size), BF),
        ],
        scratch_shapes=[
            pltpu.VMEM((rows + RIM, chans), F32),
            pltpu.VMEM(mixed.shape, BF),
            pltpu.SemaphoreType.DMA((kinds,)),
        ],
        compiler_params=params(12),
        name="conv_states",
    )(mixed, rim, taps, steps, cot, ids, weights)


def arrange(me_ref, near_ref, far_ref, held_ref):
    for at in range(near_ref.shape[0]):
        held_ref[me_ref[0] ^ (2 * at)] = near_ref[at]
        held_ref[me_ref[0] ^ (2 * at + 1)] = far_ref[at]


def entering(held_ref, heads, head, size, first, last, step):
    base = held_ref.shape[1] - (heads - head) * (size + RIM)

    def hop(count, total):
        at = first + count * step
        ends = held_ref[at, base + size : base + size + RIM, :].astype(F32)
        factor = jnp.exp(ends[0:1] + ends[1:2] + ends[2:3])
        return factor * total + held_ref[at, base : base + size, :].astype(F32)

    return lax.fori_loop(0, (last - first) * step, hop, jnp.zeros((size, size), F32))


def core_kernel(chunks, me_ref, qkv_ref, steps_ref, gain_ref, near_ref, far_ref, w_ref, *refs):
    out_refs, (headed_ref, held_ref, whole_ref) = refs[:-3], refs[-3:]
    _, rows, chans = qkv_ref.shape
    heads = steps_ref.shape[0]
    size = chans // heads
    arrange(me_ref, near_ref, far_ref, held_ref)
    along, down, lower = decay_sums(steps_ref[...])
    for head in range(heads):
        at = slice(head * size, (head + 1) * size)
        state = entering(held_ref, heads, head, size, 0, me_ref[0], 1).astype(BF)
        diff = down[:, head : head + 1] - along[head : head + 1, :]
        mask = jnp.exp(jnp.where(lower, diff, -jnp.inf))
        query = qkv_ref[0, :, at]
        scores = (mm(query, qkv_ref[1, :, at], NT) * mask).astype(BF)
        attended = mm(scores, qkv_ref[2, :, at])
        attended += mm(query, state) * jnp.exp(down[:, head : head + 1])
        scale = lax.rsqrt(jnp.mean(attended * attended, axis=-1, keepdims=True) + 1e-06)
        headed_ref[:, at] = (attended * scale * gain_ref[:, at]).astype(BF)
    whole_ref[...] = mm(headed_ref[...], w_ref[...]).astype(BF)
    part = rows // len(out_refs) // chunks
    for mask, ref in enumerate(out_refs):
        for chunk in range(chunks):
            start = chunk * len(out_refs) * part + (me_ref[2] ^ mask) * part
            ref[chunk * part : (chunk + 1) * part] = whole_ref[pl.ds(pl.multiple_of(start, part), part), :]


def core_out(where, qkv, steps, near, far, gain, w_out, chunks, parts):
    _, rows, chans = qkv.shape
    width = w_out.shape[1]
    vmem = pl.BlockSpec(memory_space=pltpu.VMEM)
    return pl.pallas_call(
        functools.partial(core_kernel, chunks),
        in_specs=[pl.BlockSpec(memory_space=pltpu.SMEM)] + [vmem] * 6,
        out_shape=[jax.ShapeDtypeStruct((rows // parts, width), BF)] * parts,
        scratch_shapes=[
            pltpu.VMEM((rows, chans), BF),
            pltpu.VMEM((2 * near.shape[0], *near.shape[1:]), BF),
            pltpu.VMEM((rows, width), BF),
        ],
        compiler_params=params(16),
        name="core_out",
    )(where, qkv, steps, gain.reshape(1, chans), near, far, w_out)


def grad_kernel(
    me_ref, qkv_ref, cot_ref, steps_ref, fwd_near, fwd_far, bwd_near, bwd_far, gq_ref, gk_ref, gv_ref, fwd_ref, bwd_ref
):
    _, rows, chans = qkv_ref.shape
    heads = steps_ref.shape[0]
    size = chans // heads
    count = fwd_ref.shape[0]
    arrange(me_ref, fwd_near, fwd_far, fwd_ref)
    arrange(me_ref, bwd_near, bwd_far, bwd_ref)
    along, down, lower = decay_sums(steps_ref[...])
    for head in range(heads):
        at = slice(head * size, (head + 1) * size)
        state = entering(fwd_ref, heads, head, size, 0, me_ref[0], 1).astype(BF)
        after = entering(bwd_ref, heads, head, size, count - 1, me_ref[0], -1).astype(BF)
        here = down[:, head : head + 1]
        lead = jnp.exp(here)
        tail = jnp.exp(along[head : head + 1, rows - 1 : rows] - here)
        mask = jnp.exp(jnp.where(lower, here - along[head : head + 1, :], -jnp.inf))
        query, key, val = qkv_ref[0, :, at], qkv_ref[1, :, at], qkv_ref[2, :, at]
        cot = cot_ref[:, at]
        scores = (mm(query, key, NT) * mask).astype(BF)
        dov = (mm(cot, val, NT) * mask).astype(BF)
        gq_ref[:, at] = (mm(dov, key) + lead * mm(cot, state, NT)).astype(BF)
        gk_ref[:, at] = (mm(dov, query, TN) + tail * mm(val, after, NT)).astype(BF)
        gv_ref[:, at] = (mm(scores, cot, TN) + tail * mm(key, after)).astype(BF)


def core_grads(where, qkv, cot, steps, fwd, bwd):
    _, rows, chans = qkv.shape
    count = 2 * fwd[0].shape[0]
    vmem = pl.BlockSpec(memory_space=pltpu.VMEM)
    return pl.pallas_call(
        grad_kernel,
        in_specs=[pl.BlockSpec(memory_space=pltpu.SMEM)] + [vmem] * 7,
        out_shape=[jax.ShapeDtypeStruct((rows, chans), BF)] * 3,
        scratch_shapes=[pltpu.VMEM((count, *fwd[0].shape[1:]), BF), pltpu.VMEM((count, *bwd[0].shape[1:]), BF)],
        compiler_params=params(24),
        name="core_grads",
    )(where, qkv, cot, steps, *fwd, *bwd)


def norm_kernel(count, where_ref, x_ref, gain_ref, *refs):
    chunks = (len(refs) - count) // 2
    parts, outs, attns = refs[:count], refs[count : count + chunks], refs[count + chunks :]
    rows = outs[0].shape[0]
    for chunk, (out_ref, attn_ref) in enumerate(zip(outs, attns)):
        at = slice(chunk * rows, (chunk + 1) * rows)
        attn = functools.reduce(jnp.add, [part[at].astype(F32) for part in parts])
        attn_ref[...] = attn
        start = pl.multiple_of((chunk * count + where_ref[2]) * rows, rows)
        resid = x_ref[pl.ds(start, rows), :].astype(F32) + attn
        scale = lax.rsqrt(jnp.mean(resid * resid, axis=-1, keepdims=True) + 1e-06)
        out_ref[...] = (resid * scale * gain_ref[...]).astype(BF)


def norm_rows(where, x, parts, gain, chunks):
    rows, width = parts[0].shape[0] // chunks, parts[0].shape[1]
    vmem = pl.BlockSpec(memory_space=pltpu.VMEM)
    outs = pl.pallas_call(
        functools.partial(norm_kernel, len(parts)),
        in_specs=[pl.BlockSpec(memory_space=pltpu.SMEM)] + [vmem] * (2 + len(parts)),
        out_shape=[jax.ShapeDtypeStruct((rows, width), BF)] * chunks
        + [jax.ShapeDtypeStruct((rows, width), F32)] * chunks,
        compiler_params=params(12),
        name="moe_norm",
    )(where, x, gain.reshape(1, width), *parts)
    return list(outs[:chunks]), list(outs[chunks:])


def join_kernel(where_ref, *refs):
    parts, out_ref = refs[:-1], refs[-1]
    rows = parts[0].shape[0]
    for mask, ref in enumerate(parts):
        out_ref[pl.ds(pl.multiple_of((where_ref[2] ^ mask) * rows, rows), rows), :] = ref[...]


def join_rows(where, parts):
    rows, width = parts[0].shape
    vmem = pl.BlockSpec(memory_space=pltpu.VMEM)
    return pl.pallas_call(
        join_kernel,
        in_specs=[pl.BlockSpec(memory_space=pltpu.SMEM)] + [vmem] * len(parts),
        out_shape=jax.ShapeDtypeStruct((len(parts) * rows, width), BF),
        compiler_params=params(16),
        name="join_rows",
    )(where, *parts)


PAIR = 2


def expert_kernel(masks, chunk, experts, where_ref, near_routes, far_routes, gate_ref, up_ref, down_ref, *refs):
    row_refs, (near_ref, far_ref, rows_ref, sems) = refs[: PAIR * len(masks)], refs[PAIR * len(masks) :]
    _, tok, width = near_ref.shape
    steps = len(masks)
    step = pl.program_id(0)
    slot = lax.rem(step, 2)

    def start(at):
        for part in range(PAIR):
            target = rows_ref.at[at % 2, pl.ds(part * tok, tok)]
            pltpu.make_async_copy(row_refs[PAIR * at + part], target, sems.at[at % 2]).start()

    @pl.when(step == 0)
    def _():
        start(0)

    for at in range(1, steps):

        @pl.when(step == at - 1)
        def _(at=at):
            start(at)

    here = lax.broadcasted_iota(jnp.int32, (3 * experts, LANES), 0)
    mine = (here == where_ref[1]) | (here == where_ref[1] + experts) | (here == where_ref[1] + 2 * experts)
    square = (LANES, LANES)
    diagonal = lax.broadcasted_iota(jnp.int32, square, 0) == lax.broadcasted_iota(jnp.int32, square, 1)
    index = jnp.int32(masks[0] // 2)
    for at in range(1, steps):
        index = jnp.where(step == at, masks[at] // 2, index)
    weights = []
    for routes_ref in (near_routes, far_routes):
        for block in range(tok // LANES):
            base = (chunk // LANES + block) * 3 * experts
            table = routes_ref[index, base : base + 3 * experts, :].astype(F32)
            row = jnp.sum(jnp.where(mine, table, 0.0), axis=0, keepdims=True)
            weights.append(jnp.sum(jnp.where(diagonal, jnp.broadcast_to(row, square), 0.0), axis=1, keepdims=True))

    pltpu.make_async_copy(rows_ref.at[slot], rows_ref.at[slot], sems.at[slot]).wait()
    tokens = rows_ref[slot]
    gate = mm(tokens, gate_ref[0])
    inner = (gate * jax.nn.sigmoid(gate) * mm(tokens, up_ref[0])).astype(BF)
    cols = pick_block(width, 512)
    for begin in range(0, width, cols):
        piece = mm(inner, down_ref[0, :, begin : begin + cols])
        for at, weight in enumerate(weights):
            part, row = divmod(at * LANES, tok)
            scaled = (piece[at * LANES : (at + 1) * LANES] * weight).astype(BF)
            (near_ref, far_ref)[part][0, row : row + LANES, begin : begin + cols] = scaled


def stage_kernel(where_ref, *refs):
    out_ref = refs[-1]
    for at in range(where_ref.shape[0]):
        out_ref[at] = where_ref[at]


def stage(where, *weights):
    smem = pl.BlockSpec(memory_space=pltpu.SMEM)
    return pl.pallas_call(
        stage_kernel,
        in_specs=[smem] + [pl.BlockSpec(memory_space=pltpu.VMEM)] * len(weights),
        out_specs=smem,
        out_shape=jax.ShapeDtypeStruct(where.shape, where.dtype),
        compiler_params=params(2),
        name="stage_weights",
    )(where, *weights)


def expert_pieces(chunk, where, rows, masks, gate, up, down, routes):
    blocks = [rows[mask | core] for mask in masks for core in (0, CORE)]
    tok, width = blocks[0].shape
    hidden = gate.shape[2]
    count = len(masks)
    experts = EXP_CTX * 2 * routes[0].shape[0]
    route_rows = CHUNKS * tok // LANES * 3 * experts
    vmem = pl.BlockSpec(memory_space=pltpu.VMEM)
    table = pl.BlockSpec((routes[0].shape[0], route_rows, LANES), lambda i: (0, 0, 0))
    return pl.pallas_call(
        functools.partial(expert_kernel, tuple(masks), chunk, experts),
        grid=(count,),
        in_specs=[pl.BlockSpec(memory_space=pltpu.SMEM), table, table]
        + [vmem] * 3
        + [pl.BlockSpec(memory_space=pl.ANY)] * (PAIR * count),
        out_specs=[pl.BlockSpec((1, tok, width), lambda i: (i, 0, 0))] * PAIR,
        out_shape=[jax.ShapeDtypeStruct((count, tok, width), BF)] * PAIR,
        scratch_shapes=[
            pltpu.VMEM((2, PAIR * tok, width), BF),
            pltpu.SemaphoreType.DMA((2,)),
        ],
        compiler_params=params(20),
        cost_estimate=pl.CostEstimate(
            flops=6 * PAIR * count * tok * width * hidden,
            bytes_accessed=4 * PAIR * count * tok * width,
            transcendentals=PAIR * count * tok * hidden,
        ),
        name="expert_pieces",
    )(where, *routes, gate, up, down, *blocks)


CORE, ROW, COL = 1, 2, 4
PLANE = 8


def swap(value, mask):
    return lax.ppermute(value, "ctx", [(at, at ^ mask) for at in range(lax.axis_size("ctx"))])


def send_heads(parts):
    count = lax.axis_size("head")
    return [parts[0]] + [
        lax.ppermute(parts[mask], "head", [(at, at ^ mask) for at in range(count)]) for mask in range(1, count)
    ]


def spread_near(own):
    return jnp.stack([own] + [swap(own, mask) for mask in range(2, lax.axis_size("ctx"), 2)])


def double(near, mask):
    return jnp.concatenate([near, swap(near, mask)])


def plus(*terms):
    return functools.reduce(jnp.add, [term.astype(F32) for term in terms]).astype(BF)


def after(value, other):
    return lax.optimization_barrier((value, other))[0]


def depart(own):
    masks = (ROW, COL) if lax.axis_size("ctx") == PLANE else range(2, lax.axis_size("ctx"), 2)
    return {mask: swap(own, mask) for mask in masks}


def forward(came):
    if lax.axis_size("ctx") != PLANE:
        return []
    half = came[ROW].shape[0] // 2
    return [swap(came[ROW][:half], COL), swap(came[COL][half:], ROW)]


def first_sums(pieces):
    tok = pieces[0][0].shape[0]
    if lax.axis_size("ctx") != PLANE:
        return [(mask, plus(*parts), [(0, 0, tok)]) for mask, parts in pieces.items() if mask]
    half = tok // 2
    sums = []
    for mask, start in ((ROW, 0), (COL, half)):
        both = [plus(*[part[start : start + half] for part in pieces[at]]) for at in (ROW | COL, mask)]
        sums.append((mask, jnp.concatenate(both), [(half, start, half)]))
    return sums


def last_sums(pieces, came):
    if lax.axis_size("ctx") != PLANE:
        return []
    half = pieces[0][0].shape[0] // 2
    return [
        (mask, plus(*[part[start : start + half] for part in pieces[mask]], rows[:half]), [(0, start, half)])
        for mask, start, rows in ((COL, 0, came[0]), (ROW, half, came[1]))
    ]


def send_sums(sums):
    return [swap(rows, mask) for mask, rows, _ in sums]


def arrays(sums):
    return [rows for _, rows, _ in sums]


def terms_of(sums, received):
    return [(rows, places) for (_, _, places), rows in zip(sums, received) if places]


def sum_kernel(places, where_ref, attn_ref, near_ref, arrived_ref, *refs):
    parts = attn_ref.shape[1] // refs[-1].shape[1]
    others, outs, total_ref = refs[: -parts - 1], refs[-parts - 1 : -1], refs[-1]
    part, width = attn_ref.shape
    cols = width // parts
    own = pl.ds(pl.multiple_of(where_ref[2] * part, part), part)
    for mask, out_ref in enumerate(outs):
        at = pl.ds(pl.multiple_of((where_ref[2] ^ mask) * cols, cols), cols)
        total = near_ref[0, :, at].astype(F32) + arrived_ref[0, :, at].astype(F32)
        total_ref[...] = total
        for spots, ref in zip(places, others):
            for source, target, count in spots:
                total_ref[target : target + count] += ref[source : source + count, at].astype(F32)
        total_ref[own, :] += attn_ref[:, at]
        out_ref[...] = total_ref[...].astype(BF)


def sum_terms(where, attn, near, arrived, terms, parts):
    others, places = [rows for rows, _ in terms], tuple(tuple(spots) for _, spots in terms)
    _, tok, width = near.shape
    part = attn.shape[0]
    cols = width // parts
    first = pl.BlockSpec((1, tok, width), lambda i: (0, 0, 0))
    return pl.pallas_call(
        functools.partial(sum_kernel, places),
        grid=(1,),
        in_specs=[
            pl.BlockSpec(memory_space=pltpu.SMEM),
            pl.BlockSpec((part, width), lambda i: (0, 0)),
            first,
            first,
        ]
        + [pl.BlockSpec(part.shape, lambda i: (0, 0)) for part in others],
        out_specs=[pl.BlockSpec((tok, cols), lambda i: (0, 0))] * parts,
        out_shape=[jax.ShapeDtypeStruct((tok, cols), BF)] * parts,
        scratch_shapes=[pltpu.VMEM((tok, cols), F32)],
        compiler_params=params(24),
        name="sum_terms",
    )(where, attn, near, arrived, *others)


def final_kernel(count, where_ref, x_ref, *refs):
    del where_ref
    out_ref = refs[-1]
    rows = refs[0].shape[0]
    for chunk in range((len(refs) - 1) // count):
        at = slice(chunk * rows, (chunk + 1) * rows)
        terms = [x_ref[at]] + [ref[...] for ref in refs[chunk * count : (chunk + 1) * count]]
        out_ref[at] = functools.reduce(jnp.add, [term.astype(F32) for term in terms]).astype(BF)


def final_sum(where, x, parts):
    rows, cols = parts[0][0].shape
    total = len(parts) * rows
    block = pl.BlockSpec((rows, cols), lambda i, where: (0, 0))
    return pl.pallas_call(
        functools.partial(final_kernel, len(parts[0])),
        grid_spec=pltpu.PrefetchScalarGridSpec(
            num_scalar_prefetch=1,
            grid=(1,),
            in_specs=[pl.BlockSpec((total, cols), lambda i, where: (0, where[2]))]
            + [block] * (len(parts) * len(parts[0])),
            out_specs=pl.BlockSpec((total, cols), lambda i, where: (0, 0)),
        ),
        out_shape=jax.ShapeDtypeStruct((total, cols), BF),
        compiler_params=params(12),
        name="layer_out",
    )(where, x, *[part for chunk in parts for part in chunk])


CHUNKS = 2


def body(
    hidden_in,
    gain_attn,
    w_qkv,
    conv_w,
    log_decay,
    norm_gain,
    w_out,
    gain_moe,
    expert_ids,
    route_weights,
    w_gate,
    w_up,
    w_down,
    grad_core,
):
    n_ctx, n_head = lax.axis_size("ctx"), lax.axis_size("head")
    my_ctx, my_head = lax.axis_index("ctx"), lax.axis_index("head")
    experts = EXP_CTX * n_ctx
    shards = n_head // EXP_CTX
    where = jnp.stack([my_ctx, EXP_CTX * my_ctx + my_head // shards, my_head]).astype(jnp.int32)
    steps = log_decay.T
    chunk_rows = hidden_in.shape[0] // CHUNKS

    mixed, rim = project(hidden_in, gain_attn, jnp.transpose(w_qkv, (1, 0, 2)))
    rim = lax.ppermute(rim, "ctx", [(at, at + 1) for at in range(n_ctx - 1)])
    qkv, fwd, bwd = local_states(
        mixed, rim, jnp.transpose(conv_w, (1, 0, 2)), steps, grad_core, expert_ids.T, route_weights.T, experts
    )
    fwd = spread_near(fwd)
    fwd = (fwd, swap(fwd, CORE))
    where = stage(after(where, qkv), w_out)
    parts = core_out(where, qkv, steps, *fwd, norm_gain, w_out, CHUNKS, n_head)
    where = stage(after(where, parts), w_gate, w_up, w_down)
    bwd = double(after(bwd, parts)[None], ROW)
    normed, attn = norm_rows(where, hidden_in, after(send_heads(parts), bwd), gain_moe, CHUNKS)
    bwd = after(bwd, normed)
    while bwd.shape[0] < n_ctx // 2:
        bwd = double(bwd, 2 * bwd.shape[0])

    own = join_rows(where, after(send_heads([normed[0]] * n_head), bwd))
    bwd = (bwd, swap(after(bwd, own), CORE))
    rows = []
    for chunk in range(CHUNKS):
        rows.append({0: own} | depart(own))
        if chunk + 1 < CHUNKS:
            own = join_rows(where, send_heads([after(normed[chunk + 1], own)] * n_head))
            rows[chunk] = after(rows[chunk], own)

    state = []
    for chunk in range(CHUNKS):
        experts_of = functools.partial(
            expert_pieces, chunk * chunk_rows, where, gate=w_gate, up=w_up, down=w_down, routes=fwd
        )
        halves = forward(rows[chunk]) if chunk == 0 else halves
        masks = list(rows[chunk])
        here = rows[chunk] | {mask | CORE: swap(part, CORE) for mask, part in rows[chunk].items()}
        if state:
            if halves:
                across = jnp.concatenate(halves)
                pair = {ROW | COL: across, ROW | COL | CORE: swap(across, CORE)}
                here = after(here, pair)
            here = after(here, arrays(state[-1]["first"]))
        near, far = experts_of(rows=here, masks=masks)
        if state:
            before = state[-1]
            far = after(far, (before["came"], bwd))
            before["last"] = last_sums(before["pieces"], before["came"])
            before["came_last"] = send_sums(before["last"])
        arrived = swap(far, CORE)
        pieces = {mask: (near[at], arrived[at]) for at, mask in enumerate(masks)}
        if halves:
            if not state:
                across = jnp.concatenate(after(halves, near))
                pair = {ROW | COL: across, ROW | COL | CORE: swap(across, CORE)}
            pair = after(pair, [far] + arrays(before["last"]) if state else rows[chunk + 1])
            near_across, far_across = experts_of(rows=pair, masks=[ROW | COL])
            arrived_across = swap(after(far_across, before["came_last"]) if state else far_across, CORE)
            if chunk + 1 < CHUNKS:
                halves = forward(rows[chunk + 1])
                arrived_across = after(arrived_across, halves)
            pieces[ROW | COL] = (near_across[0], arrived_across[0])
        first = first_sums(pieces)
        state.append(
            {"first": first, "came": send_sums(first), "pieces": pieces, "own": (near, arrived), "came_last": []}
        )

    sums = []
    for chunk, made in enumerate(state):
        if chunk + 1 == CHUNKS:
            made["last"] = last_sums(made["pieces"], after(made["came"], sums[-1][0]))
            made["came_last"] = send_sums(made["last"])
        terms = terms_of(made["first"], made["came"]) + terms_of(made["last"], made["came_last"])
        if chunk + 1 < CHUNKS:
            held = after([part for part, _ in terms], arrays(state[chunk + 1]["first"]))
            terms = list(zip(held, [places for _, places in terms]))
        sums.append(send_heads(sum_terms(where, attn[chunk], *made["own"], terms, n_head)))
    grads = core_grads(where, qkv, grad_core, steps, fwd, bwd)
    return (final_sum(where, hidden_in, sums), *grads)


def solution(mesh):
    in_specs = (
        P("ctx", None),
        P(),
        P(None, None, "head"),
        P(None, None, "head"),
        P("ctx", "head"),
        P("head"),
        P("head", None),
        P(),
        P("ctx", None),
        P("ctx", None),
        P(("ctx", "head"), None, None),
        P(("ctx", "head"), None, None),
        P(("ctx", "head"), None, None),
        P("ctx", "head"),
    )
    out_specs = (P("ctx", "head"), P("ctx", "head"), P("ctx", "head"), P("ctx", "head"))
    return jax.shard_map(body, mesh=mesh, in_specs=in_specs, out_specs=out_specs, check_vma=False)
```

```python
import functools

import jax
import jax.numpy as jnp
from jax import lax
from jax.experimental import pallas as pl
from jax.experimental.pallas import tpu as pltpu
from jax.sharding import PartitionSpec as P

KERNEL = 4
EXP_CTX = 2
LANES = 128
RIM = 16
MIB = 1024 * 1024
HI = lax.Precision.HIGHEST
BF = jnp.bfloat16
F32 = jnp.float32
NT = (((1,), (1,)), ((), ()))
TN = (((0,), (0,)), ((), ()))
NN = (((1,), (0,)), ((), ()))


def params(mib):
    return pltpu.CompilerParams(vmem_limit_bytes=mib * MIB)


def mm(a, b, dims=NN):
    return lax.dot_general(a, b, dims, preferred_element_type=F32)


def pick_block(extent, target):
    return target if extent % target == 0 else extent


def qkv_kernel(x_hbm, gain_ref, w_hbm, mixed_ref, rim_ref, x_ref, w_ref, normed_ref, x_sem, sems):
    kinds, width, chans = w_ref.shape
    load = pltpu.make_async_copy(x_hbm, x_ref, x_sem)
    load.start()
    part = width // sems.shape[1]
    copies = []
    for kind in range(kinds):
        at = [pl.ds(piece * part, part) for piece in range(sems.shape[1])]
        copies.append(
            [
                pltpu.make_async_copy(w_hbm.at[kind, rows], w_ref.at[kind, rows], sems.at[kind, piece])
                for piece, rows in enumerate(at)
            ]
        )
        for copy in copies[kind]:
            copy.start()
    load.wait()
    values = x_ref[...].astype(F32)
    scale = lax.rsqrt(jnp.mean(values * values, axis=-1, keepdims=True) + 1e-06)
    normed_ref[...] = (values * scale * gain_ref[...]).astype(BF)
    for kind in range(kinds):
        for copy in copies[kind]:
            copy.wait()
        out = mm(normed_ref[...], w_ref[kind]).astype(BF)
        mixed_ref[kind] = out
        rim_ref[kind] = out[out.shape[0] - RIM :]


def project(x, gain, weights):
    rows, width = x.shape
    kinds, _, chans = weights.shape
    vmem = pl.BlockSpec(memory_space=pltpu.VMEM)
    hbm = pl.BlockSpec(memory_space=pltpu.HBM)
    return pl.pallas_call(
        qkv_kernel,
        in_specs=[hbm, vmem, hbm],
        out_specs=[vmem, vmem],
        out_shape=[
            jax.ShapeDtypeStruct((kinds, rows, chans), BF),
            jax.ShapeDtypeStruct((kinds, RIM, chans), BF),
        ],
        scratch_shapes=[
            pltpu.VMEM((rows, width), BF),
            pltpu.VMEM((kinds, width, chans), BF),
            pltpu.VMEM((rows, width), BF),
            pltpu.SemaphoreType.DMA,
            pltpu.SemaphoreType.DMA((kinds, 4)),
        ],
        compiler_params=params(60),
        name="qkv_projection",
    )(x, gain.reshape(1, width), weights)


def decay_sums(steps):
    rows = steps.shape[1]
    row_at = lax.broadcasted_iota(jnp.int32, (rows, rows), 0)
    col_at = lax.broadcasted_iota(jnp.int32, (rows, rows), 1)
    lower = row_at >= col_at
    tri = jnp.where(lower, 1.0, 0.0).astype(F32)
    along = lax.dot_general(steps, tri, NT, precision=HI, preferred_element_type=F32)
    down = lax.dot_general(tri, steps, NT, precision=HI, preferred_element_type=F32)
    return along, down, lower


def payload_tail(total, size):
    full = jnp.broadcast_to(total, (RIM, size))
    first = full.astype(BF).astype(F32)
    second = (full - first).astype(BF).astype(F32)
    third = full - first - second
    at = lax.broadcasted_iota(jnp.int32, (RIM, size), 0)
    return jnp.where(at == 0, first, jnp.where(at == 1, second, jnp.where(at == 2, third, 0.0)))


def route_rows(ids_ref, weights_ref, experts):
    top, tok = ids_ref.shape
    expert = lax.broadcasted_iota(jnp.int32, (experts, tok), 0)
    table = jnp.zeros((experts, tok), F32)
    for choice in range(top):
        table += jnp.where(expert == ids_ref[choice : choice + 1, :], weights_ref[choice : choice + 1, :], 0.0)
    first = table.astype(BF).astype(F32)
    second = (table - first).astype(BF).astype(F32)
    return jnp.concatenate([first, second, table - first - second], axis=0)


def conv_kernel(
    experts, mixed_any, rim_ref, taps_ref, steps_ref, cot_ref, ids_ref, weights_ref, qkv_ref, fwd_ref, bwd_ref,
    pad_ref, mixed_ref, sems,
):
    kinds, rows, chans = mixed_ref.shape
    copies = [pltpu.make_async_copy(mixed_any.at[kind], mixed_ref.at[kind], sems.at[kind]) for kind in range(kinds)]
    for copy in copies:
        copy.start()
    heads = steps_ref.shape[0]
    size = chans // heads
    along, down, _ = decay_sums(steps_ref[...])
    for kind in range(kinds):
        copies[kind].wait()
        pad_ref[:RIM] = rim_ref[kind].astype(F32)
        pad_ref[RIM:] = mixed_ref[kind].astype(F32)
        total = taps_ref[kind, 0:1, :] * pad_ref[RIM:]
        for offset in range(1, KERNEL):
            total += taps_ref[kind, offset : offset + 1, :] * pad_ref[RIM - offset : RIM - offset + rows]
        activ = total * jax.nn.sigmoid(total)
        if kind == 0:
            activ = activ * size ** (-0.5)
        qkv_ref[kind] = activ.astype(BF)
    routes = rows // LANES * 3 * experts
    table = route_rows(ids_ref, weights_ref, experts).astype(BF)
    for part in range(rows // LANES):
        fwd_ref[part * 3 * experts : (part + 1) * 3 * experts] = table[:, part * LANES : (part + 1) * LANES]
    for head in range(heads):
        at = slice(head * size, (head + 1) * size)
        base = head * (size + RIM)
        behind = routes + base
        last = along[head : head + 1, rows - 1 : rows]
        lead = jnp.exp(down[:, head : head + 1])
        tail = jnp.exp(last - down[:, head : head + 1])
        key_out = (qkv_ref[1, :, at].astype(F32) * tail).astype(BF)
        query_out = (qkv_ref[0, :, at].astype(F32) * lead).astype(BF)
        ends = payload_tail(last, size).astype(BF)
        fwd_ref[behind : behind + size] = mm(key_out, qkv_ref[2, :, at], TN).astype(BF)
        fwd_ref[behind + size : behind + size + RIM] = ends
        bwd_ref[base : base + size] = mm(query_out, cot_ref[:, at], TN).astype(BF)
        bwd_ref[base + size : base + size + RIM] = ends


def local_states(mixed, rim, taps, steps, cot, ids, weights, experts):
    kinds, rows, chans = mixed.shape
    heads = steps.shape[0]
    size = chans // heads
    states = heads * (size + RIM)
    return pl.pallas_call(
        functools.partial(conv_kernel, experts),
        in_specs=[pl.BlockSpec(memory_space=pl.ANY)] + [pl.BlockSpec(memory_space=pltpu.VMEM)] * 6,
        out_specs=[pl.BlockSpec(memory_space=pltpu.VMEM)] * 3,
        out_shape=[
            jax.ShapeDtypeStruct((kinds, rows, chans), BF),
            jax.ShapeDtypeStruct((states + rows // LANES * 3 * experts, size), BF),
            jax.ShapeDtypeStruct((states, size), BF),
        ],
        scratch_shapes=[
            pltpu.VMEM((rows + RIM, chans), F32),
            pltpu.VMEM(mixed.shape, BF),
            pltpu.SemaphoreType.DMA((kinds,)),
        ],
        compiler_params=params(12),
        name="conv_states",
    )(mixed, rim, taps, steps, cot, ids, weights)


def arrange(me_ref, near_ref, far_ref, held_ref):
    for at in range(near_ref.shape[0]):
        held_ref[me_ref[0] ^ (2 * at)] = near_ref[at]
        held_ref[me_ref[0] ^ (2 * at + 1)] = far_ref[at]


def entering(held_ref, heads, head, size, first, last, step):
    base = held_ref.shape[1] - (heads - head) * (size + RIM)

    def hop(count, total):
        at = first + count * step
        ends = held_ref[at, base + size : base + size + RIM, :].astype(F32)
        factor = jnp.exp(ends[0:1] + ends[1:2] + ends[2:3])
        return factor * total + held_ref[at, base : base + size, :].astype(F32)

    return lax.fori_loop(0, (last - first) * step, hop, jnp.zeros((size, size), F32))


def core_kernel(chunks, me_ref, qkv_ref, steps_ref, gain_ref, near_ref, far_ref, w_ref, *refs):
    out_refs, (headed_ref, held_ref, whole_ref) = refs[:-3], refs[-3:]
    _, rows, chans = qkv_ref.shape
    heads = steps_ref.shape[0]
    size = chans // heads
    arrange(me_ref, near_ref, far_ref, held_ref)
    along, down, lower = decay_sums(steps_ref[...])
    for head in range(heads):
        at = slice(head * size, (head + 1) * size)
        state = entering(held_ref, heads, head, size, 0, me_ref[0], 1).astype(BF)
        diff = down[:, head : head + 1] - along[head : head + 1, :]
        mask = jnp.exp(jnp.where(lower, diff, -jnp.inf))
        query = qkv_ref[0, :, at]
        scores = (mm(query, qkv_ref[1, :, at], NT) * mask).astype(BF)
        attended = mm(scores, qkv_ref[2, :, at])
        attended += mm(query, state) * jnp.exp(down[:, head : head + 1])
        scale = lax.rsqrt(jnp.mean(attended * attended, axis=-1, keepdims=True) + 1e-06)
        headed_ref[:, at] = (attended * scale * gain_ref[:, at]).astype(BF)
    whole_ref[...] = mm(headed_ref[...], w_ref[...]).astype(BF)
    part = rows // len(out_refs) // chunks
    for mask, ref in enumerate(out_refs):
        for chunk in range(chunks):
            start = chunk * len(out_refs) * part + (me_ref[2] ^ mask) * part
            ref[chunk * part : (chunk + 1) * part] = whole_ref[pl.ds(pl.multiple_of(start, part), part), :]


def core_out(where, qkv, steps, near, far, gain, w_out, chunks, parts):
    _, rows, chans = qkv.shape
    width = w_out.shape[1]
    vmem = pl.BlockSpec(memory_space=pltpu.VMEM)
    return pl.pallas_call(
        functools.partial(core_kernel, chunks),
        in_specs=[pl.BlockSpec(memory_space=pltpu.SMEM)] + [vmem] * 6,
        out_shape=[jax.ShapeDtypeStruct((rows // parts, width), BF)] * parts,
        scratch_shapes=[
            pltpu.VMEM((rows, chans), BF),
            pltpu.VMEM((2 * near.shape[0], *near.shape[1:]), BF),
            pltpu.VMEM((rows, width), BF),
        ],
        compiler_params=params(16),
        name="core_out",
    )(where, qkv, steps, gain.reshape(1, chans), near, far, w_out)


def grad_kernel(
    me_ref, qkv_ref, cot_ref, steps_ref, fwd_near, fwd_far, bwd_near, bwd_far, gq_ref, gk_ref, gv_ref, fwd_ref, bwd_ref
):
    _, rows, chans = qkv_ref.shape
    heads = steps_ref.shape[0]
    size = chans // heads
    count = fwd_ref.shape[0]
    arrange(me_ref, fwd_near, fwd_far, fwd_ref)
    arrange(me_ref, bwd_near, bwd_far, bwd_ref)
    along, down, lower = decay_sums(steps_ref[...])
    for head in range(heads):
        at = slice(head * size, (head + 1) * size)
        state = entering(fwd_ref, heads, head, size, 0, me_ref[0], 1).astype(BF)
        after = entering(bwd_ref, heads, head, size, count - 1, me_ref[0], -1).astype(BF)
        here = down[:, head : head + 1]
        lead = jnp.exp(here)
        tail = jnp.exp(along[head : head + 1, rows - 1 : rows] - here)
        mask = jnp.exp(jnp.where(lower, here - along[head : head + 1, :], -jnp.inf))
        query, key, val = qkv_ref[0, :, at], qkv_ref[1, :, at], qkv_ref[2, :, at]
        cot = cot_ref[:, at]
        scores = (mm(query, key, NT) * mask).astype(BF)
        dov = (mm(cot, val, NT) * mask).astype(BF)
        gq_ref[:, at] = (mm(dov, key) + lead * mm(cot, state, NT)).astype(BF)
        gk_ref[:, at] = (mm(dov, query, TN) + tail * mm(val, after, NT)).astype(BF)
        gv_ref[:, at] = (mm(scores, cot, TN) + tail * mm(key, after)).astype(BF)


def core_grads(where, qkv, cot, steps, fwd, bwd):
    _, rows, chans = qkv.shape
    count = 2 * fwd[0].shape[0]
    vmem = pl.BlockSpec(memory_space=pltpu.VMEM)
    return pl.pallas_call(
        grad_kernel,
        in_specs=[pl.BlockSpec(memory_space=pltpu.SMEM)] + [vmem] * 7,
        out_shape=[jax.ShapeDtypeStruct((rows, chans), BF)] * 3,
        scratch_shapes=[pltpu.VMEM((count, *fwd[0].shape[1:]), BF), pltpu.VMEM((count, *bwd[0].shape[1:]), BF)],
        compiler_params=params(24),
        name="core_grads",
    )(where, qkv, cot, steps, *fwd, *bwd)


def norm_kernel(count, where_ref, x_ref, gain_ref, *refs):
    chunks = (len(refs) - count) // 2
    parts, outs, attns = refs[:count], refs[count : count + chunks], refs[count + chunks :]
    rows = outs[0].shape[0]
    for chunk, (out_ref, attn_ref) in enumerate(zip(outs, attns)):
        at = slice(chunk * rows, (chunk + 1) * rows)
        attn = functools.reduce(jnp.add, [part[at].astype(F32) for part in parts])
        attn_ref[...] = attn
        start = pl.multiple_of((chunk * count + where_ref[2]) * rows, rows)
        resid = x_ref[pl.ds(start, rows), :].astype(F32) + attn
        scale = lax.rsqrt(jnp.mean(resid * resid, axis=-1, keepdims=True) + 1e-06)
        out_ref[...] = (resid * scale * gain_ref[...]).astype(BF)


def norm_rows(where, x, parts, gain, chunks):
    rows, width = parts[0].shape[0] // chunks, parts[0].shape[1]
    vmem = pl.BlockSpec(memory_space=pltpu.VMEM)
    outs = pl.pallas_call(
        functools.partial(norm_kernel, len(parts)),
        in_specs=[pl.BlockSpec(memory_space=pltpu.SMEM)] + [vmem] * (2 + len(parts)),
        out_shape=[jax.ShapeDtypeStruct((rows, width), BF)] * chunks
        + [jax.ShapeDtypeStruct((rows, width), F32)] * chunks,
        compiler_params=params(12),
        name="moe_norm",
    )(where, x, gain.reshape(1, width), *parts)
    return list(outs[:chunks]), list(outs[chunks:])


def join_kernel(where_ref, *refs):
    parts, out_ref = refs[:-1], refs[-1]
    rows = parts[0].shape[0]
    for mask, ref in enumerate(parts):
        out_ref[pl.ds(pl.multiple_of((where_ref[2] ^ mask) * rows, rows), rows), :] = ref[...]


def join_rows(where, parts):
    rows, width = parts[0].shape
    vmem = pl.BlockSpec(memory_space=pltpu.VMEM)
    return pl.pallas_call(
        join_kernel,
        in_specs=[pl.BlockSpec(memory_space=pltpu.SMEM)] + [vmem] * len(parts),
        out_shape=jax.ShapeDtypeStruct((len(parts) * rows, width), BF),
        compiler_params=params(16),
        name="join_rows",
    )(where, *parts)


PAIR = 2


def expert_kernel(masks, chunk, experts, where_ref, near_routes, far_routes, gate_ref, up_ref, down_ref, *refs):
    row_refs, (near_ref, far_ref, rows_ref, sems) = refs[: PAIR * len(masks)], refs[PAIR * len(masks) :]
    _, tok, width = near_ref.shape
    steps = len(masks)
    step = pl.program_id(0)
    slot = lax.rem(step, 2)

    def start(at):
        for part in range(PAIR):
            target = rows_ref.at[at % 2, pl.ds(part * tok, tok)]
            pltpu.make_async_copy(row_refs[PAIR * at + part], target, sems.at[at % 2]).start()

    @pl.when(step == 0)
    def _():
        start(0)

    for at in range(1, steps):

        @pl.when(step == at - 1)
        def _(at=at):
            start(at)

    here = lax.broadcasted_iota(jnp.int32, (3 * experts, LANES), 0)
    mine = (here == where_ref[1]) | (here == where_ref[1] + experts) | (here == where_ref[1] + 2 * experts)
    square = (LANES, LANES)
    diagonal = lax.broadcasted_iota(jnp.int32, square, 0) == lax.broadcasted_iota(jnp.int32, square, 1)
    index = jnp.int32(masks[0] // 2)
    for at in range(1, steps):
        index = jnp.where(step == at, masks[at] // 2, index)
    weights = []
    for routes_ref in (near_routes, far_routes):
        for block in range(tok // LANES):
            base = (chunk // LANES + block) * 3 * experts
            table = routes_ref[index, base : base + 3 * experts, :].astype(F32)
            row = jnp.sum(jnp.where(mine, table, 0.0), axis=0, keepdims=True)
            weights.append(jnp.sum(jnp.where(diagonal, jnp.broadcast_to(row, square), 0.0), axis=1, keepdims=True))

    pltpu.make_async_copy(rows_ref.at[slot], rows_ref.at[slot], sems.at[slot]).wait()
    tokens = rows_ref[slot]
    gate = mm(tokens, gate_ref[0])
    inner = (gate * jax.nn.sigmoid(gate) * mm(tokens, up_ref[0])).astype(BF)
    cols = pick_block(width, 512)
    for begin in range(0, width, cols):
        piece = mm(inner, down_ref[0, :, begin : begin + cols])
        for at, weight in enumerate(weights):
            part, row = divmod(at * LANES, tok)
            scaled = (piece[at * LANES : (at + 1) * LANES] * weight).astype(BF)
            (near_ref, far_ref)[part][0, row : row + LANES, begin : begin + cols] = scaled


def stage_kernel(where_ref, *refs):
    out_ref = refs[-1]
    for at in range(where_ref.shape[0]):
        out_ref[at] = where_ref[at]


def stage(where, *weights):
    smem = pl.BlockSpec(memory_space=pltpu.SMEM)
    return pl.pallas_call(
        stage_kernel,
        in_specs=[smem] + [pl.BlockSpec(memory_space=pltpu.VMEM)] * len(weights),
        out_specs=smem,
        out_shape=jax.ShapeDtypeStruct(where.shape, where.dtype),
        compiler_params=params(2),
        name="stage_weights",
    )(where, *weights)


def expert_pieces(chunk, where, rows, masks, gate, up, down, routes):
    blocks = [rows[mask | core] for mask in masks for core in (0, CORE)]
    tok, width = blocks[0].shape
    hidden = gate.shape[2]
    count = len(masks)
    experts = EXP_CTX * 2 * routes[0].shape[0]
    route_rows = CHUNKS * tok // LANES * 3 * experts
    vmem = pl.BlockSpec(memory_space=pltpu.VMEM)
    table = pl.BlockSpec((routes[0].shape[0], route_rows, LANES), lambda i: (0, 0, 0))
    return pl.pallas_call(
        functools.partial(expert_kernel, tuple(masks), chunk, experts),
        grid=(count,),
        in_specs=[pl.BlockSpec(memory_space=pltpu.SMEM), table, table]
        + [vmem] * 3
        + [pl.BlockSpec(memory_space=pl.ANY)] * (PAIR * count),
        out_specs=[pl.BlockSpec((1, tok, width), lambda i: (i, 0, 0))] * PAIR,
        out_shape=[jax.ShapeDtypeStruct((count, tok, width), BF)] * PAIR,
        scratch_shapes=[
            pltpu.VMEM((2, PAIR * tok, width), BF),
            pltpu.SemaphoreType.DMA((2,)),
        ],
        compiler_params=params(20),
        cost_estimate=pl.CostEstimate(
            flops=6 * PAIR * count * tok * width * hidden,
            bytes_accessed=4 * PAIR * count * tok * width,
            transcendentals=PAIR * count * tok * hidden,
        ),
        name="expert_pieces",
    )(where, *routes, gate, up, down, *blocks)


CORE, ROW, COL = 1, 2, 4
PLANE = 8


def swap(value, mask):
    return lax.ppermute(value, "ctx", [(at, at ^ mask) for at in range(lax.axis_size("ctx"))])


def send_heads(parts):
    count = lax.axis_size("head")
    return [parts[0]] + [
        lax.ppermute(parts[mask], "head", [(at, at ^ mask) for at in range(count)]) for mask in range(1, count)
    ]


def spread_near(own):
    return jnp.stack([own] + [swap(own, mask) for mask in range(2, lax.axis_size("ctx"), 2)])


def double(near, mask):
    return jnp.concatenate([near, swap(near, mask)])


def plus(*terms):
    return functools.reduce(jnp.add, [term.astype(F32) for term in terms]).astype(BF)


def after(value, other):
    return lax.optimization_barrier((value, other))[0]


def depart(own):
    masks = (ROW, COL) if lax.axis_size("ctx") == PLANE else range(2, lax.axis_size("ctx"), 2)
    return {mask: swap(own, mask) for mask in masks}


def forward(came):
    if lax.axis_size("ctx") != PLANE:
        return []
    half = came[ROW].shape[0] // 2
    return [swap(came[ROW][:half], COL), swap(came[COL][half:], ROW)]


def first_sums(pieces):
    tok = pieces[0][0].shape[0]
    if lax.axis_size("ctx") != PLANE:
        return [(mask, plus(*parts), [(0, 0, tok)]) for mask, parts in pieces.items() if mask]
    half = tok // 2
    sums = []
    for mask, start in ((ROW, 0), (COL, half)):
        both = [plus(*[part[start : start + half] for part in pieces[at]]) for at in (ROW | COL, mask)]
        sums.append((mask, jnp.concatenate(both), [(half, start, half)]))
    return sums


def last_sums(pieces, came):
    if lax.axis_size("ctx") != PLANE:
        return []
    half = pieces[0][0].shape[0] // 2
    return [
        (mask, plus(*[part[start : start + half] for part in pieces[mask]], rows[:half]), [(0, start, half)])
        for mask, start, rows in ((COL, 0, came[0]), (ROW, half, came[1]))
    ]


def send_sums(sums):
    return [swap(rows, mask) for mask, rows, _ in sums]


def arrays(sums):
    return [rows for _, rows, _ in sums]


def terms_of(sums, received):
    return [(rows, places) for (_, _, places), rows in zip(sums, received) if places]


def sum_kernel(places, where_ref, attn_ref, near_ref, arrived_ref, *refs):
    parts = attn_ref.shape[1] // refs[-1].shape[1]
    others, outs, total_ref = refs[: -parts - 1], refs[-parts - 1 : -1], refs[-1]
    part, width = attn_ref.shape
    cols = width // parts
    own = pl.ds(pl.multiple_of(where_ref[2] * part, part), part)
    for mask, out_ref in enumerate(outs):
        at = pl.ds(pl.multiple_of((where_ref[2] ^ mask) * cols, cols), cols)
        total = near_ref[0, :, at].astype(F32) + arrived_ref[0, :, at].astype(F32)
        total_ref[...] = total
        for spots, ref in zip(places, others):
            for source, target, count in spots:
                total_ref[target : target + count] += ref[source : source + count, at].astype(F32)
        total_ref[own, :] += attn_ref[:, at]
        out_ref[...] = total_ref[...].astype(BF)


def sum_terms(where, attn, near, arrived, terms, parts):
    others, places = [rows for rows, _ in terms], tuple(tuple(spots) for _, spots in terms)
    _, tok, width = near.shape
    part = attn.shape[0]
    cols = width // parts
    first = pl.BlockSpec((1, tok, width), lambda i: (0, 0, 0))
    return pl.pallas_call(
        functools.partial(sum_kernel, places),
        grid=(1,),
        in_specs=[
            pl.BlockSpec(memory_space=pltpu.SMEM),
            pl.BlockSpec((part, width), lambda i: (0, 0)),
            first,
            first,
        ]
        + [pl.BlockSpec(part.shape, lambda i: (0, 0)) for part in others],
        out_specs=[pl.BlockSpec((tok, cols), lambda i: (0, 0))] * parts,
        out_shape=[jax.ShapeDtypeStruct((tok, cols), BF)] * parts,
        scratch_shapes=[pltpu.VMEM((tok, cols), F32)],
        compiler_params=params(24),
        name="sum_terms",
    )(where, attn, near, arrived, *others)


def final_kernel(count, where_ref, x_ref, *refs):
    del where_ref
    out_ref = refs[-1]
    rows = refs[0].shape[0]
    for chunk in range((len(refs) - 1) // count):
        at = slice(chunk * rows, (chunk + 1) * rows)
        terms = [x_ref[at]] + [ref[...] for ref in refs[chunk * count : (chunk + 1) * count]]
        out_ref[at] = functools.reduce(jnp.add, [term.astype(F32) for term in terms]).astype(BF)


def final_sum(where, x, parts):
    rows, cols = parts[0][0].shape
    total = len(parts) * rows
    block = pl.BlockSpec((rows, cols), lambda i, where: (0, 0))
    return pl.pallas_call(
        functools.partial(final_kernel, len(parts[0])),
        grid_spec=pltpu.PrefetchScalarGridSpec(
            num_scalar_prefetch=1,
            grid=(1,),
            in_specs=[pl.BlockSpec((total, cols), lambda i, where: (0, where[2]))]
            + [block] * (len(parts) * len(parts[0])),
            out_specs=pl.BlockSpec((total, cols), lambda i, where: (0, 0)),
        ),
        out_shape=jax.ShapeDtypeStruct((total, cols), BF),
        compiler_params=params(12),
        name="layer_out",
    )(where, x, *[part for chunk in parts for part in chunk])


CHUNKS = 2


def body(
    hidden_in,
    gain_attn,
    w_qkv,
    conv_w,
    log_decay,
    norm_gain,
    w_out,
    gain_moe,
    expert_ids,
    route_weights,
    w_gate,
    w_up,
    w_down,
    grad_core,
):
    n_ctx, n_head = lax.axis_size("ctx"), lax.axis_size("head")
    my_ctx, my_head = lax.axis_index("ctx"), lax.axis_index("head")
    experts = EXP_CTX * n_ctx
    shards = n_head // EXP_CTX
    where = jnp.stack([my_ctx, EXP_CTX * my_ctx + my_head // shards, my_head]).astype(jnp.int32)
    steps = log_decay.T
    chunk_rows = hidden_in.shape[0] // CHUNKS

    mixed, rim = project(hidden_in, gain_attn, jnp.transpose(w_qkv, (1, 0, 2)))
    rim = lax.ppermute(rim, "ctx", [(at, at + 1) for at in range(n_ctx - 1)])
    qkv, fwd, bwd = local_states(
        mixed, rim, jnp.transpose(conv_w, (1, 0, 2)), steps, grad_core, expert_ids.T, route_weights.T, experts
    )
    fwd = spread_near(fwd)
    fwd = (fwd, swap(fwd, CORE))
    where = stage(after(where, qkv), w_out)
    parts = core_out(where, qkv, steps, *fwd, norm_gain, w_out, CHUNKS, n_head)
    where = stage(after(where, parts), w_gate, w_up, w_down)
    bwd = double(after(bwd, parts)[None], ROW)
    normed, attn = norm_rows(where, hidden_in, after(send_heads(parts), bwd), gain_moe, CHUNKS)
    bwd = after(bwd, normed)
    while bwd.shape[0] < n_ctx // 2:
        bwd = double(bwd, 2 * bwd.shape[0])

    own = join_rows(where, after(send_heads([normed[0]] * n_head), bwd))
    bwd = (bwd, swap(after(bwd, own), CORE))
    rows = []
    for chunk in range(CHUNKS):
        rows.append({0: own} | depart(own))
        if chunk + 1 < CHUNKS:
            own = join_rows(where, send_heads([after(normed[chunk + 1], own)] * n_head))
            rows[chunk] = after(rows[chunk], own)

    def experts_of(chunk, rows):
        masks = [mask for mask in rows if not mask & CORE]
        return expert_pieces(chunk * chunk_rows, where, rows, masks, w_gate, w_up, w_down, fwd)

    def with_cores(rows):
        return rows | {mask | CORE: swap(part, CORE) for mask, part in rows.items()}

    halves, pieces, owns = [], [], []
    for chunk in range(CHUNKS):
        here = rows[chunk] if chunk == 0 else after(rows[chunk], near)
        halves.append(forward(here))
        near, far = experts_of(chunk, with_cores(here))
        arrived = swap(far if chunk == 0 else after(far, bwd), CORE)
        pieces.append({mask: (near[at], arrived[at]) for at, mask in enumerate(here)})
        owns.append((near, arrived))
    halves = after(halves, near)
    for chunk in range(CHUNKS):
        if halves[chunk]:
            across = with_cores({ROW | COL: jnp.concatenate(halves[chunk])})
            if chunk:
                across = after(across, near)
            near, far = experts_of(chunk, across)
            pieces[chunk][ROW | COL] = (near[0], swap(far, CORE)[0])
    firsts = [first_sums(part) for part in pieces]
    came = [send_sums(first) for first in firsts]
    lasts = [last_sums(*both) for both in zip(pieces, came)]
    came_last = [send_sums(last) for last in lasts]
    sums = []
    for chunk in range(CHUNKS):
        terms = terms_of(firsts[chunk], came[chunk]) + terms_of(lasts[chunk], came_last[chunk])
        if chunk + 1 < CHUNKS:
            held = after([part for part, _ in terms], arrays(firsts[chunk + 1]))
            terms = list(zip(held, [places for _, places in terms]))
        sums.append(send_heads(sum_terms(where, attn[chunk], *owns[chunk], terms, n_head)))
    grads = core_grads(where, qkv, grad_core, steps, fwd, bwd)
    return (final_sum(where, hidden_in, sums), *grads)


def solution(mesh):
    in_specs = (
        P("ctx", None),
        P(),
        P(None, None, "head"),
        P(None, None, "head"),
        P("ctx", "head"),
        P("head"),
        P("head", None),
        P(),
        P("ctx", None),
        P("ctx", None),
        P(("ctx", "head"), None, None),
        P(("ctx", "head"), None, None),
        P(("ctx", "head"), None, None),
        P("ctx", "head"),
    )
    out_specs = (P("ctx", "head"), P("ctx", "head"), P("ctx", "head"), P("ctx", "head"))
    return jax.shard_map(body, mesh=mesh, in_specs=in_specs, out_specs=out_specs, check_vma=False)
```

```python
import functools

import jax
import jax.numpy as jnp
from jax import lax
from jax.experimental import pallas as pl
from jax.experimental.pallas import tpu as pltpu
from jax.sharding import PartitionSpec as P

KERNEL = 4
EXP_CTX = 2
LANES = 128
RIM = 16
MIB = 1024 * 1024
HI = lax.Precision.HIGHEST
BF = jnp.bfloat16
F32 = jnp.float32
NT = (((1,), (1,)), ((), ()))
TN = (((0,), (0,)), ((), ()))
NN = (((1,), (0,)), ((), ()))


def params(mib):
    return pltpu.CompilerParams(vmem_limit_bytes=mib * MIB)


def mm(a, b, dims=NN):
    return lax.dot_general(a, b, dims, preferred_element_type=F32)


def pick_block(extent, target):
    return target if extent % target == 0 else extent


def qkv_kernel(x_hbm, gain_ref, w_hbm, mixed_ref, rim_ref, x_ref, w_ref, normed_ref, x_sem, sems):
    kinds, width, chans = w_ref.shape
    load = pltpu.make_async_copy(x_hbm, x_ref, x_sem)
    load.start()
    part = width // sems.shape[1]
    copies = []
    for kind in range(kinds):
        at = [pl.ds(piece * part, part) for piece in range(sems.shape[1])]
        copies.append(
            [
                pltpu.make_async_copy(w_hbm.at[kind, rows], w_ref.at[kind, rows], sems.at[kind, piece])
                for piece, rows in enumerate(at)
            ]
        )
        for copy in copies[kind]:
            copy.start()
    load.wait()
    values = x_ref[...].astype(F32)
    scale = lax.rsqrt(jnp.mean(values * values, axis=-1, keepdims=True) + 1e-06)
    normed_ref[...] = (values * scale * gain_ref[...]).astype(BF)
    for kind in range(kinds):
        for copy in copies[kind]:
            copy.wait()
        out = mm(normed_ref[...], w_ref[kind]).astype(BF)
        mixed_ref[kind] = out
        rim_ref[kind] = out[out.shape[0] - RIM :]


def project(x, gain, weights):
    rows, width = x.shape
    kinds, _, chans = weights.shape
    vmem = pl.BlockSpec(memory_space=pltpu.VMEM)
    hbm = pl.BlockSpec(memory_space=pltpu.HBM)
    return pl.pallas_call(
        qkv_kernel,
        in_specs=[hbm, vmem, hbm],
        out_specs=[vmem, vmem],
        out_shape=[
            jax.ShapeDtypeStruct((kinds, rows, chans), BF),
            jax.ShapeDtypeStruct((kinds, RIM, chans), BF),
        ],
        scratch_shapes=[
            pltpu.VMEM((rows, width), BF),
            pltpu.VMEM((kinds, width, chans), BF),
            pltpu.VMEM((rows, width), BF),
            pltpu.SemaphoreType.DMA,
            pltpu.SemaphoreType.DMA((kinds, 4)),
        ],
        compiler_params=params(60),
        name="qkv_projection",
    )(x, gain.reshape(1, width), weights)


def decay_sums(steps):
    rows = steps.shape[1]
    row_at = lax.broadcasted_iota(jnp.int32, (rows, rows), 0)
    col_at = lax.broadcasted_iota(jnp.int32, (rows, rows), 1)
    lower = row_at >= col_at
    tri = jnp.where(lower, 1.0, 0.0).astype(F32)
    along = lax.dot_general(steps, tri, NT, precision=HI, preferred_element_type=F32)
    down = lax.dot_general(tri, steps, NT, precision=HI, preferred_element_type=F32)
    return along, down, lower


def payload_tail(total, size):
    full = jnp.broadcast_to(total, (RIM, size))
    first = full.astype(BF).astype(F32)
    second = (full - first).astype(BF).astype(F32)
    third = full - first - second
    at = lax.broadcasted_iota(jnp.int32, (RIM, size), 0)
    return jnp.where(at == 0, first, jnp.where(at == 1, second, jnp.where(at == 2, third, 0.0)))


def route_rows(ids_ref, weights_ref, experts):
    top, tok = ids_ref.shape
    expert = lax.broadcasted_iota(jnp.int32, (experts, tok), 0)
    table = jnp.zeros((experts, tok), F32)
    for choice in range(top):
        table += jnp.where(expert == ids_ref[choice : choice + 1, :], weights_ref[choice : choice + 1, :], 0.0)
    first = table.astype(BF).astype(F32)
    second = (table - first).astype(BF).astype(F32)
    return jnp.concatenate([first, second, table - first - second], axis=0)


def conv_kernel(
    experts, mixed_any, rim_ref, taps_ref, steps_ref, cot_ref, ids_ref, weights_ref, qkv_ref, fwd_ref, bwd_ref,
    pad_ref, mixed_ref, sems,
):
    kinds, rows, chans = mixed_ref.shape
    copies = [pltpu.make_async_copy(mixed_any.at[kind], mixed_ref.at[kind], sems.at[kind]) for kind in range(kinds)]
    for copy in copies:
        copy.start()
    heads = steps_ref.shape[0]
    size = chans // heads
    along, down, _ = decay_sums(steps_ref[...])
    for kind in range(kinds):
        copies[kind].wait()
        pad_ref[:RIM] = rim_ref[kind].astype(F32)
        pad_ref[RIM:] = mixed_ref[kind].astype(F32)
        total = taps_ref[kind, 0:1, :] * pad_ref[RIM:]
        for offset in range(1, KERNEL):
            total += taps_ref[kind, offset : offset + 1, :] * pad_ref[RIM - offset : RIM - offset + rows]
        activ = total * jax.nn.sigmoid(total)
        if kind == 0:
            activ = activ * size ** (-0.5)
        qkv_ref[kind] = activ.astype(BF)
    routes = rows // LANES * 3 * experts
    table = route_rows(ids_ref, weights_ref, experts).astype(BF)
    for part in range(rows // LANES):
        fwd_ref[part * 3 * experts : (part + 1) * 3 * experts] = table[:, part * LANES : (part + 1) * LANES]
    for head in range(heads):
        at = slice(head * size, (head + 1) * size)
        base = head * (size + RIM)
        behind = routes + base
        last = along[head : head + 1, rows - 1 : rows]
        lead = jnp.exp(down[:, head : head + 1])
        tail = jnp.exp(last - down[:, head : head + 1])
        key_out = (qkv_ref[1, :, at].astype(F32) * tail).astype(BF)
        query_out = (qkv_ref[0, :, at].astype(F32) * lead).astype(BF)
        ends = payload_tail(last, size).astype(BF)
        fwd_ref[behind : behind + size] = mm(key_out, qkv_ref[2, :, at], TN).astype(BF)
        fwd_ref[behind + size : behind + size + RIM] = ends
        bwd_ref[base : base + size] = mm(query_out, cot_ref[:, at], TN).astype(BF)
        bwd_ref[base + size : base + size + RIM] = ends


def local_states(mixed, rim, taps, steps, cot, ids, weights, experts):
    kinds, rows, chans = mixed.shape
    heads = steps.shape[0]
    size = chans // heads
    states = heads * (size + RIM)
    return pl.pallas_call(
        functools.partial(conv_kernel, experts),
        in_specs=[pl.BlockSpec(memory_space=pl.ANY)] + [pl.BlockSpec(memory_space=pltpu.VMEM)] * 6,
        out_specs=[pl.BlockSpec(memory_space=pltpu.VMEM)] * 3,
        out_shape=[
            jax.ShapeDtypeStruct((kinds, rows, chans), BF),
            jax.ShapeDtypeStruct((states + rows // LANES * 3 * experts, size), BF),
            jax.ShapeDtypeStruct((states, size), BF),
        ],
        scratch_shapes=[
            pltpu.VMEM((rows + RIM, chans), F32),
            pltpu.VMEM(mixed.shape, BF),
            pltpu.SemaphoreType.DMA((kinds,)),
        ],
        compiler_params=params(12),
        name="conv_states",
    )(mixed, rim, taps, steps, cot, ids, weights)


def arrange(me_ref, near_ref, far_ref, held_ref):
    for at in range(near_ref.shape[0]):
        held_ref[me_ref[0] ^ (2 * at)] = near_ref[at]
        held_ref[me_ref[0] ^ (2 * at + 1)] = far_ref[at]


def entering(held_ref, heads, head, size, first, last, step):
    base = held_ref.shape[1] - (heads - head) * (size + RIM)

    def hop(count, total):
        at = first + count * step
        ends = held_ref[at, base + size : base + size + RIM, :].astype(F32)
        factor = jnp.exp(ends[0:1] + ends[1:2] + ends[2:3])
        return factor * total + held_ref[at, base : base + size, :].astype(F32)

    return lax.fori_loop(0, (last - first) * step, hop, jnp.zeros((size, size), F32))


def core_kernel(chunks, me_ref, qkv_ref, steps_ref, gain_ref, near_ref, far_ref, w_ref, *refs):
    out_refs, (headed_ref, held_ref, whole_ref) = refs[:-3], refs[-3:]
    _, rows, chans = qkv_ref.shape
    heads = steps_ref.shape[0]
    size = chans // heads
    arrange(me_ref, near_ref, far_ref, held_ref)
    along, down, lower = decay_sums(steps_ref[...])
    for head in range(heads):
        at = slice(head * size, (head + 1) * size)
        state = entering(held_ref, heads, head, size, 0, me_ref[0], 1).astype(BF)
        diff = down[:, head : head + 1] - along[head : head + 1, :]
        mask = jnp.exp(jnp.where(lower, diff, -jnp.inf))
        query = qkv_ref[0, :, at]
        scores = (mm(query, qkv_ref[1, :, at], NT) * mask).astype(BF)
        attended = mm(scores, qkv_ref[2, :, at])
        attended += mm(query, state) * jnp.exp(down[:, head : head + 1])
        scale = lax.rsqrt(jnp.mean(attended * attended, axis=-1, keepdims=True) + 1e-06)
        headed_ref[:, at] = (attended * scale * gain_ref[:, at]).astype(BF)
    whole_ref[...] = mm(headed_ref[...], w_ref[...]).astype(BF)
    part = rows // len(out_refs) // chunks
    for mask, ref in enumerate(out_refs):
        for chunk in range(chunks):
            start = chunk * len(out_refs) * part + (me_ref[2] ^ mask) * part
            ref[chunk * part : (chunk + 1) * part] = whole_ref[pl.ds(pl.multiple_of(start, part), part), :]


def core_out(where, qkv, steps, near, far, gain, w_out, chunks, parts):
    _, rows, chans = qkv.shape
    width = w_out.shape[1]
    vmem = pl.BlockSpec(memory_space=pltpu.VMEM)
    return pl.pallas_call(
        functools.partial(core_kernel, chunks),
        in_specs=[pl.BlockSpec(memory_space=pltpu.SMEM)] + [vmem] * 6,
        out_shape=[jax.ShapeDtypeStruct((rows // parts, width), BF)] * parts,
        scratch_shapes=[
            pltpu.VMEM((rows, chans), BF),
            pltpu.VMEM((2 * near.shape[0], *near.shape[1:]), BF),
            pltpu.VMEM((rows, width), BF),
        ],
        compiler_params=params(16),
        name="core_out",
    )(where, qkv, steps, gain.reshape(1, chans), near, far, w_out)


def grad_kernel(
    me_ref, qkv_ref, cot_ref, steps_ref, fwd_near, fwd_far, bwd_near, bwd_far, gq_ref, gk_ref, gv_ref, fwd_ref, bwd_ref
):
    _, rows, chans = qkv_ref.shape
    heads = steps_ref.shape[0]
    size = chans // heads
    count = fwd_ref.shape[0]
    arrange(me_ref, fwd_near, fwd_far, fwd_ref)
    arrange(me_ref, bwd_near, bwd_far, bwd_ref)
    along, down, lower = decay_sums(steps_ref[...])
    for head in range(heads):
        at = slice(head * size, (head + 1) * size)
        state = entering(fwd_ref, heads, head, size, 0, me_ref[0], 1).astype(BF)
        after = entering(bwd_ref, heads, head, size, count - 1, me_ref[0], -1).astype(BF)
        here = down[:, head : head + 1]
        lead = jnp.exp(here)
        tail = jnp.exp(along[head : head + 1, rows - 1 : rows] - here)
        mask = jnp.exp(jnp.where(lower, here - along[head : head + 1, :], -jnp.inf))
        query, key, val = qkv_ref[0, :, at], qkv_ref[1, :, at], qkv_ref[2, :, at]
        cot = cot_ref[:, at]
        scores = (mm(query, key, NT) * mask).astype(BF)
        dov = (mm(cot, val, NT) * mask).astype(BF)
        gq_ref[:, at] = (mm(dov, key) + lead * mm(cot, state, NT)).astype(BF)
        gk_ref[:, at] = (mm(dov, query, TN) + tail * mm(val, after, NT)).astype(BF)
        gv_ref[:, at] = (mm(scores, cot, TN) + tail * mm(key, after)).astype(BF)


def core_grads(where, qkv, cot, steps, fwd, bwd):
    _, rows, chans = qkv.shape
    count = 2 * fwd[0].shape[0]
    vmem = pl.BlockSpec(memory_space=pltpu.VMEM)
    return pl.pallas_call(
        grad_kernel,
        in_specs=[pl.BlockSpec(memory_space=pltpu.SMEM)] + [vmem] * 7,
        out_shape=[jax.ShapeDtypeStruct((rows, chans), BF)] * 3,
        scratch_shapes=[pltpu.VMEM((count, *fwd[0].shape[1:]), BF), pltpu.VMEM((count, *bwd[0].shape[1:]), BF)],
        compiler_params=params(24),
        name="core_grads",
    )(where, qkv, cot, steps, *fwd, *bwd)


def norm_kernel(count, where_ref, x_ref, gain_ref, *refs):
    chunks = (len(refs) - count) // 2
    parts, outs, attns = refs[:count], refs[count : count + chunks], refs[count + chunks :]
    rows = outs[0].shape[0]
    for chunk, (out_ref, attn_ref) in enumerate(zip(outs, attns)):
        at = slice(chunk * rows, (chunk + 1) * rows)
        attn = functools.reduce(jnp.add, [part[at].astype(F32) for part in parts])
        attn_ref[...] = attn
        start = pl.multiple_of((chunk * count + where_ref[2]) * rows, rows)
        resid = x_ref[pl.ds(start, rows), :].astype(F32) + attn
        scale = lax.rsqrt(jnp.mean(resid * resid, axis=-1, keepdims=True) + 1e-06)
        out_ref[...] = (resid * scale * gain_ref[...]).astype(BF)


def norm_rows(where, x, parts, gain, chunks):
    rows, width = parts[0].shape[0] // chunks, parts[0].shape[1]
    vmem = pl.BlockSpec(memory_space=pltpu.VMEM)
    outs = pl.pallas_call(
        functools.partial(norm_kernel, len(parts)),
        in_specs=[pl.BlockSpec(memory_space=pltpu.SMEM)] + [vmem] * (2 + len(parts)),
        out_shape=[jax.ShapeDtypeStruct((rows, width), BF)] * chunks
        + [jax.ShapeDtypeStruct((rows, width), F32)] * chunks,
        compiler_params=params(12),
        name="moe_norm",
    )(where, x, gain.reshape(1, width), *parts)
    return list(outs[:chunks]), list(outs[chunks:])


def join_kernel(where_ref, *refs):
    parts, out_ref = refs[:-1], refs[-1]
    rows = parts[0].shape[0]
    for mask, ref in enumerate(parts):
        out_ref[pl.ds(pl.multiple_of((where_ref[2] ^ mask) * rows, rows), rows), :] = ref[...]


def join_rows(where, parts):
    rows, width = parts[0].shape
    vmem = pl.BlockSpec(memory_space=pltpu.VMEM)
    return pl.pallas_call(
        join_kernel,
        in_specs=[pl.BlockSpec(memory_space=pltpu.SMEM)] + [vmem] * len(parts),
        out_shape=jax.ShapeDtypeStruct((len(parts) * rows, width), BF),
        compiler_params=params(16),
        name="join_rows",
    )(where, *parts)


PAIR = 2


def expert_kernel(masks, chunk, experts, where_ref, near_routes, far_routes, gate_ref, up_ref, down_ref, *refs):
    row_refs, (near_ref, far_ref, rows_ref, sems) = refs[: PAIR * len(masks)], refs[PAIR * len(masks) :]
    _, tok, width = near_ref.shape
    steps = len(masks)
    step = pl.program_id(0)
    slot = lax.rem(step, 2)

    def start(at):
        for part in range(PAIR):
            target = rows_ref.at[at % 2, pl.ds(part * tok, tok)]
            pltpu.make_async_copy(row_refs[PAIR * at + part], target, sems.at[at % 2]).start()

    @pl.when(step == 0)
    def _():
        start(0)

    for at in range(1, steps):

        @pl.when(step == at - 1)
        def _(at=at):
            start(at)

    here = lax.broadcasted_iota(jnp.int32, (3 * experts, LANES), 0)
    mine = (here == where_ref[1]) | (here == where_ref[1] + experts) | (here == where_ref[1] + 2 * experts)
    square = (LANES, LANES)
    diagonal = lax.broadcasted_iota(jnp.int32, square, 0) == lax.broadcasted_iota(jnp.int32, square, 1)
    index = jnp.int32(masks[0] // 2)
    for at in range(1, steps):
        index = jnp.where(step == at, masks[at] // 2, index)
    weights = []
    for routes_ref in (near_routes, far_routes):
        for block in range(tok // LANES):
            base = (chunk // LANES + block) * 3 * experts
            table = routes_ref[index, base : base + 3 * experts, :].astype(F32)
            row = jnp.sum(jnp.where(mine, table, 0.0), axis=0, keepdims=True)
            weights.append(jnp.sum(jnp.where(diagonal, jnp.broadcast_to(row, square), 0.0), axis=1, keepdims=True))

    pltpu.make_async_copy(rows_ref.at[slot], rows_ref.at[slot], sems.at[slot]).wait()
    tokens = rows_ref[slot]
    gate = mm(tokens, gate_ref[0])
    inner = (gate * jax.nn.sigmoid(gate) * mm(tokens, up_ref[0])).astype(BF)
    cols = pick_block(width, 512)
    for begin in range(0, width, cols):
        piece = mm(inner, down_ref[0, :, begin : begin + cols])
        for at, weight in enumerate(weights):
            part, row = divmod(at * LANES, tok)
            scaled = (piece[at * LANES : (at + 1) * LANES] * weight).astype(BF)
            (near_ref, far_ref)[part][0, row : row + LANES, begin : begin + cols] = scaled


def stage_kernel(where_ref, *refs):
    out_ref = refs[-1]
    for at in range(where_ref.shape[0]):
        out_ref[at] = where_ref[at]


def stage(where, *weights):
    smem = pl.BlockSpec(memory_space=pltpu.SMEM)
    return pl.pallas_call(
        stage_kernel,
        in_specs=[smem] + [pl.BlockSpec(memory_space=pltpu.VMEM)] * len(weights),
        out_specs=smem,
        out_shape=jax.ShapeDtypeStruct(where.shape, where.dtype),
        compiler_params=params(2),
        name="stage_weights",
    )(where, *weights)


def expert_pieces(chunk, where, rows, masks, gate, up, down, routes):
    blocks = [rows[mask | core] for mask in masks for core in (0, CORE)]
    tok, width = blocks[0].shape
    hidden = gate.shape[2]
    count = len(masks)
    experts = EXP_CTX * 2 * routes[0].shape[0]
    route_rows = CHUNKS * tok // LANES * 3 * experts
    vmem = pl.BlockSpec(memory_space=pltpu.VMEM)
    table = pl.BlockSpec((routes[0].shape[0], route_rows, LANES), lambda i: (0, 0, 0))
    return pl.pallas_call(
        functools.partial(expert_kernel, tuple(masks), chunk, experts),
        grid=(count,),
        in_specs=[pl.BlockSpec(memory_space=pltpu.SMEM), table, table]
        + [vmem] * 3
        + [pl.BlockSpec(memory_space=pl.ANY)] * (PAIR * count),
        out_specs=[pl.BlockSpec((1, tok, width), lambda i: (i, 0, 0))] * PAIR,
        out_shape=[jax.ShapeDtypeStruct((count, tok, width), BF)] * PAIR,
        scratch_shapes=[
            pltpu.VMEM((2, PAIR * tok, width), BF),
            pltpu.SemaphoreType.DMA((2,)),
        ],
        compiler_params=params(20),
        cost_estimate=pl.CostEstimate(
            flops=6 * PAIR * count * tok * width * hidden,
            bytes_accessed=4 * PAIR * count * tok * width,
            transcendentals=PAIR * count * tok * hidden,
        ),
        name="expert_pieces",
    )(where, *routes, gate, up, down, *blocks)


CORE, ROW, COL = 1, 2, 4
PLANE = 8


def swap(value, mask):
    return lax.ppermute(value, "ctx", [(at, at ^ mask) for at in range(lax.axis_size("ctx"))])


def send_heads(parts):
    count = lax.axis_size("head")
    return [parts[0]] + [
        lax.ppermute(parts[mask], "head", [(at, at ^ mask) for at in range(count)]) for mask in range(1, count)
    ]


def spread_near(own):
    return jnp.stack([own] + [swap(own, mask) for mask in range(2, lax.axis_size("ctx"), 2)])


def double(near, mask):
    return jnp.concatenate([near, swap(near, mask)])


def plus(*terms):
    return functools.reduce(jnp.add, [term.astype(F32) for term in terms]).astype(BF)


def after(value, other):
    return lax.optimization_barrier((value, other))[0]


def depart(own):
    masks = (ROW, COL) if lax.axis_size("ctx") == PLANE else range(2, lax.axis_size("ctx"), 2)
    return {mask: swap(own, mask) for mask in masks}


def forward(came):
    if lax.axis_size("ctx") != PLANE:
        return []
    half = came[ROW].shape[0] // 2
    return [swap(came[ROW][:half], COL), swap(came[COL][half:], ROW)]


def direct_sums(pieces):
    tok = pieces[0][0].shape[0]
    if lax.axis_size("ctx") != PLANE:
        return [(mask, plus(*parts), [(0, 0, tok)]) for mask, parts in pieces.items() if mask]
    half = tok // 2
    return [
        (mask, plus(*[part[start : start + half] for part in pieces[mask]]), [(0, start, half)])
        for mask, start in ((ROW, 0), (COL, half))
    ]


def through_sums(pieces):
    if lax.axis_size("ctx") != PLANE:
        return []
    half = pieces[0][0].shape[0] // 2
    return [
        (mask, plus(*[part[start : start + half] for part in pieces[ROW | COL]]), [])
        for mask, start in ((ROW, 0), (COL, half))
    ]


def last_sums(pieces, came):
    if lax.axis_size("ctx") != PLANE:
        return []
    half = pieces[0][0].shape[0] // 2
    return [
        (mask, plus(*[part[start : start + half] for part in pieces[mask]], rows), [(0, start, half)])
        for mask, start, rows in ((COL, 0, came[0]), (ROW, half, came[1]))
    ]


def send_sums(sums):
    return [swap(rows, mask) for mask, rows, _ in sums]


def arrays(sums):
    return [rows for _, rows, _ in sums]


def terms_of(sums, received):
    return [(rows, places) for (_, _, places), rows in zip(sums, received) if places]


def sum_kernel(places, where_ref, attn_ref, near_ref, arrived_ref, *refs):
    parts = attn_ref.shape[1] // refs[-1].shape[1]
    others, outs, total_ref = refs[: -parts - 1], refs[-parts - 1 : -1], refs[-1]
    part, width = attn_ref.shape
    cols = width // parts
    own = pl.ds(pl.multiple_of(where_ref[2] * part, part), part)
    for mask, out_ref in enumerate(outs):
        at = pl.ds(pl.multiple_of((where_ref[2] ^ mask) * cols, cols), cols)
        total = near_ref[0, :, at].astype(F32) + arrived_ref[0, :, at].astype(F32)
        total_ref[...] = total
        for spots, ref in zip(places, others):
            for source, target, count in spots:
                total_ref[target : target + count] += ref[source : source + count, at].astype(F32)
        total_ref[own, :] += attn_ref[:, at]
        out_ref[...] = total_ref[...].astype(BF)


def sum_terms(where, attn, near, arrived, terms, parts):
    others, places = [rows for rows, _ in terms], tuple(tuple(spots) for _, spots in terms)
    _, tok, width = near.shape
    part = attn.shape[0]
    cols = width // parts
    first = pl.BlockSpec((1, tok, width), lambda i: (0, 0, 0))
    return pl.pallas_call(
        functools.partial(sum_kernel, places),
        grid=(1,),
        in_specs=[
            pl.BlockSpec(memory_space=pltpu.SMEM),
            pl.BlockSpec((part, width), lambda i: (0, 0)),
            first,
            first,
        ]
        + [pl.BlockSpec(part.shape, lambda i: (0, 0)) for part in others],
        out_specs=[pl.BlockSpec((tok, cols), lambda i: (0, 0))] * parts,
        out_shape=[jax.ShapeDtypeStruct((tok, cols), BF)] * parts,
        scratch_shapes=[pltpu.VMEM((tok, cols), F32)],
        compiler_params=params(24),
        name="sum_terms",
    )(where, attn, near, arrived, *others)


def final_kernel(count, where_ref, x_ref, *refs):
    del where_ref
    out_ref = refs[-1]
    rows = refs[0].shape[0]
    for chunk in range((len(refs) - 1) // count):
        at = slice(chunk * rows, (chunk + 1) * rows)
        terms = [x_ref[at]] + [ref[...] for ref in refs[chunk * count : (chunk + 1) * count]]
        out_ref[at] = functools.reduce(jnp.add, [term.astype(F32) for term in terms]).astype(BF)


def final_sum(where, x, parts):
    rows, cols = parts[0][0].shape
    total = len(parts) * rows
    block = pl.BlockSpec((rows, cols), lambda i, where: (0, 0))
    return pl.pallas_call(
        functools.partial(final_kernel, len(parts[0])),
        grid_spec=pltpu.PrefetchScalarGridSpec(
            num_scalar_prefetch=1,
            grid=(1,),
            in_specs=[pl.BlockSpec((total, cols), lambda i, where: (0, where[2]))]
            + [block] * (len(parts) * len(parts[0])),
            out_specs=pl.BlockSpec((total, cols), lambda i, where: (0, 0)),
        ),
        out_shape=jax.ShapeDtypeStruct((total, cols), BF),
        compiler_params=params(12),
        name="layer_out",
    )(where, x, *[part for chunk in parts for part in chunk])


CHUNKS = 2


def body(
    hidden_in,
    gain_attn,
    w_qkv,
    conv_w,
    log_decay,
    norm_gain,
    w_out,
    gain_moe,
    expert_ids,
    route_weights,
    w_gate,
    w_up,
    w_down,
    grad_core,
):
    n_ctx, n_head = lax.axis_size("ctx"), lax.axis_size("head")
    my_ctx, my_head = lax.axis_index("ctx"), lax.axis_index("head")
    experts = EXP_CTX * n_ctx
    shards = n_head // EXP_CTX
    where = jnp.stack([my_ctx, EXP_CTX * my_ctx + my_head // shards, my_head]).astype(jnp.int32)
    steps = log_decay.T
    chunk_rows = hidden_in.shape[0] // CHUNKS

    mixed, rim = project(hidden_in, gain_attn, jnp.transpose(w_qkv, (1, 0, 2)))
    rim = lax.ppermute(rim, "ctx", [(at, at + 1) for at in range(n_ctx - 1)])
    qkv, fwd, bwd = local_states(
        mixed, rim, jnp.transpose(conv_w, (1, 0, 2)), steps, grad_core, expert_ids.T, route_weights.T, experts
    )
    fwd = spread_near(fwd)
    fwd = (fwd, swap(fwd, CORE))
    where = stage(after(where, qkv), w_out)
    parts = core_out(where, qkv, steps, *fwd, norm_gain, w_out, CHUNKS, n_head)
    where = stage(after(where, parts), w_gate, w_up, w_down)
    bwd = double(after(bwd, parts)[None], ROW)
    normed, attn = norm_rows(where, hidden_in, after(send_heads(parts), bwd), gain_moe, CHUNKS)
    bwd = after(bwd, normed)
    while bwd.shape[0] < n_ctx // 2:
        bwd = double(bwd, 2 * bwd.shape[0])

    own = join_rows(where, after(send_heads([normed[0]] * n_head), bwd))
    bwd = (bwd, swap(after(bwd, own), CORE))
    rows = []
    for chunk in range(CHUNKS):
        rows.append({0: own} | depart(own))
        if chunk + 1 < CHUNKS:
            own = join_rows(where, send_heads([after(normed[chunk + 1], own)] * n_head))
            rows[chunk] = after(rows[chunk], own)

    def experts_of(chunk, rows):
        masks = [mask for mask in rows if not mask & CORE]
        return expert_pieces(chunk * chunk_rows, where, rows, masks, w_gate, w_up, w_down, fwd)

    def with_cores(rows):
        return rows | {mask | CORE: swap(part, CORE) for mask, part in rows.items()}

    halves, pieces, owns = [], [], []
    for chunk in range(CHUNKS):
        here = rows[chunk] if chunk == 0 else after(rows[chunk], near)
        halves.append(forward(here))
        near, far = experts_of(chunk, with_cores(here))
        arrived = swap(far if chunk == 0 else after(far, bwd), CORE)
        pieces.append({mask: (near[at], arrived[at]) for at, mask in enumerate(here)})
        owns.append((near, arrived))
    halves = after(halves, near)
    direct = [direct_sums(part) for part in pieces]
    came = [send_sums(part) for part in direct]
    through, came_through = [], []
    ahead = [rows for part in direct for rows in arrays(part)]
    for chunk in range(CHUNKS):
        if halves[chunk]:
            across = after(with_cores({ROW | COL: jnp.concatenate(halves[chunk])}), near if chunk else ahead)
            near, far = experts_of(chunk, across)
            pieces[chunk][ROW | COL] = (near[0], swap(after(far, came[chunk]), CORE)[0])
    for chunk in range(CHUNKS):
        through.append(through_sums(pieces[chunk]))
        came_through.append(send_sums(through[chunk]))
    last = [last_sums(*both) for both in zip(pieces, came_through)]
    came_last = [send_sums(part) for part in last]
    sums = []
    for chunk in range(CHUNKS):
        terms = terms_of(direct[chunk], came[chunk]) + terms_of(last[chunk], came_last[chunk])
        if chunk + 1 < CHUNKS and through[chunk + 1]:
            held = after([part for part, _ in terms], arrays(through[chunk + 1]))
            terms = list(zip(held, [places for _, places in terms]))
        sums.append(send_heads(sum_terms(where, attn[chunk], *owns[chunk], terms, n_head)))
    grads = core_grads(where, qkv, grad_core, steps, fwd, bwd)
    return (final_sum(where, hidden_in, sums), *grads)


def solution(mesh):
    in_specs = (
        P("ctx", None),
        P(),
        P(None, None, "head"),
        P(None, None, "head"),
        P("ctx", "head"),
        P("head"),
        P("head", None),
        P(),
        P("ctx", None),
        P("ctx", None),
        P(("ctx", "head"), None, None),
        P(("ctx", "head"), None, None),
        P(("ctx", "head"), None, None),
        P("ctx", "head"),
    )
    out_specs = (P("ctx", "head"), P("ctx", "head"), P("ctx", "head"), P("ctx", "head"))
    return jax.shard_map(body, mesh=mesh, in_specs=in_specs, out_specs=out_specs, check_vma=False)
```

```python
import functools

import jax
import jax.numpy as jnp
from jax import lax
from jax.experimental import pallas as pl
from jax.experimental.pallas import tpu as pltpu
from jax.sharding import PartitionSpec as P

KERNEL = 4
EXP_CTX = 2
LANES = 128
RIM = 16
MIB = 1024 * 1024
HI = lax.Precision.HIGHEST
BF = jnp.bfloat16
F32 = jnp.float32
NT = (((1,), (1,)), ((), ()))
TN = (((0,), (0,)), ((), ()))
NN = (((1,), (0,)), ((), ()))


def params(mib):
    return pltpu.CompilerParams(vmem_limit_bytes=mib * MIB)


def mm(a, b, dims=NN):
    return lax.dot_general(a, b, dims, preferred_element_type=F32)


def pick_block(extent, target):
    return target if extent % target == 0 else extent


def qkv_kernel(x_hbm, gain_ref, w_hbm, mixed_ref, rim_ref, x_ref, w_ref, normed_ref, x_sem, sems):
    kinds, width, chans = w_ref.shape
    load = pltpu.make_async_copy(x_hbm, x_ref, x_sem)
    load.start()
    part = width // sems.shape[1]
    copies = []
    for kind in range(kinds):
        at = [pl.ds(piece * part, part) for piece in range(sems.shape[1])]
        copies.append(
            [
                pltpu.make_async_copy(w_hbm.at[kind, rows], w_ref.at[kind, rows], sems.at[kind, piece])
                for piece, rows in enumerate(at)
            ]
        )
        for copy in copies[kind]:
            copy.start()
    load.wait()
    values = x_ref[...].astype(F32)
    scale = lax.rsqrt(jnp.mean(values * values, axis=-1, keepdims=True) + 1e-06)
    normed_ref[...] = (values * scale * gain_ref[...]).astype(BF)
    for kind in range(kinds):
        for copy in copies[kind]:
            copy.wait()
        out = mm(normed_ref[...], w_ref[kind]).astype(BF)
        mixed_ref[kind] = out
        rim_ref[kind] = out[out.shape[0] - RIM :]


def project(x, gain, weights):
    rows, width = x.shape
    kinds, _, chans = weights.shape
    vmem = pl.BlockSpec(memory_space=pltpu.VMEM)
    hbm = pl.BlockSpec(memory_space=pltpu.HBM)
    return pl.pallas_call(
        qkv_kernel,
        in_specs=[hbm, vmem, hbm],
        out_specs=[vmem, vmem],
        out_shape=[
            jax.ShapeDtypeStruct((kinds, rows, chans), BF),
            jax.ShapeDtypeStruct((kinds, RIM, chans), BF),
        ],
        scratch_shapes=[
            pltpu.VMEM((rows, width), BF),
            pltpu.VMEM((kinds, width, chans), BF),
            pltpu.VMEM((rows, width), BF),
            pltpu.SemaphoreType.DMA,
            pltpu.SemaphoreType.DMA((kinds, 4)),
        ],
        compiler_params=params(60),
        name="qkv_projection",
    )(x, gain.reshape(1, width), weights)


def decay_sums(steps):
    rows = steps.shape[1]
    row_at = lax.broadcasted_iota(jnp.int32, (rows, rows), 0)
    col_at = lax.broadcasted_iota(jnp.int32, (rows, rows), 1)
    lower = row_at >= col_at
    tri = jnp.where(lower, 1.0, 0.0).astype(F32)
    along = lax.dot_general(steps, tri, NT, precision=HI, preferred_element_type=F32)
    down = lax.dot_general(tri, steps, NT, precision=HI, preferred_element_type=F32)
    return along, down, lower


def payload_tail(total, size):
    full = jnp.broadcast_to(total, (RIM, size))
    first = full.astype(BF).astype(F32)
    second = (full - first).astype(BF).astype(F32)
    third = full - first - second
    at = lax.broadcasted_iota(jnp.int32, (RIM, size), 0)
    return jnp.where(at == 0, first, jnp.where(at == 1, second, jnp.where(at == 2, third, 0.0)))


def route_rows(ids_ref, weights_ref, experts):
    top, tok = ids_ref.shape
    expert = lax.broadcasted_iota(jnp.int32, (experts, tok), 0)
    table = jnp.zeros((experts, tok), F32)
    for choice in range(top):
        table += jnp.where(expert == ids_ref[choice : choice + 1, :], weights_ref[choice : choice + 1, :], 0.0)
    first = table.astype(BF).astype(F32)
    second = (table - first).astype(BF).astype(F32)
    return jnp.concatenate([first, second, table - first - second], axis=0)


def conv_kernel(
    experts, mixed_ref, rim_ref, taps_ref, steps_ref, cot_ref, ids_ref, weights_ref, qkv_ref, fwd_ref, bwd_ref, pad_ref
):
    kinds, rows, chans = mixed_ref.shape
    heads = steps_ref.shape[0]
    size = chans // heads
    along, down, _ = decay_sums(steps_ref[...])
    for kind in range(kinds):
        pad_ref[:RIM] = rim_ref[kind].astype(F32)
        pad_ref[RIM:] = mixed_ref[kind].astype(F32)
        total = taps_ref[kind, 0:1, :] * pad_ref[RIM:]
        for offset in range(1, KERNEL):
            total += taps_ref[kind, offset : offset + 1, :] * pad_ref[RIM - offset : RIM - offset + rows]
        activ = total * jax.nn.sigmoid(total)
        if kind == 0:
            activ = activ * size ** (-0.5)
        qkv_ref[kind] = activ.astype(BF)
    routes = rows // LANES * 3 * experts
    table = route_rows(ids_ref, weights_ref, experts).astype(BF)
    for part in range(rows // LANES):
        fwd_ref[part * 3 * experts : (part + 1) * 3 * experts] = table[:, part * LANES : (part + 1) * LANES]
    for head in range(heads):
        at = slice(head * size, (head + 1) * size)
        base = head * (size + RIM)
        behind = routes + base
        last = along[head : head + 1, rows - 1 : rows]
        lead = jnp.exp(down[:, head : head + 1])
        tail = jnp.exp(last - down[:, head : head + 1])
        key_out = (qkv_ref[1, :, at].astype(F32) * tail).astype(BF)
        query_out = (qkv_ref[0, :, at].astype(F32) * lead).astype(BF)
        ends = payload_tail(last, size).astype(BF)
        fwd_ref[behind : behind + size] = mm(key_out, qkv_ref[2, :, at], TN).astype(BF)
        fwd_ref[behind + size : behind + size + RIM] = ends
        bwd_ref[base : base + size] = mm(query_out, cot_ref[:, at], TN).astype(BF)
        bwd_ref[base + size : base + size + RIM] = ends


def local_states(mixed, rim, taps, steps, cot, ids, weights, experts):
    kinds, rows, chans = mixed.shape
    heads = steps.shape[0]
    size = chans // heads
    states = heads * (size + RIM)
    return pl.pallas_call(
        functools.partial(conv_kernel, experts),
        out_specs=[pl.BlockSpec(memory_space=pltpu.VMEM)] * 3,
        out_shape=[
            jax.ShapeDtypeStruct((kinds, rows, chans), BF),
            jax.ShapeDtypeStruct((states + rows // LANES * 3 * experts, size), BF),
            jax.ShapeDtypeStruct((states, size), BF),
        ],
        scratch_shapes=[pltpu.VMEM((rows + RIM, chans), F32)],
        compiler_params=params(12),
        name="conv_states",
    )(mixed, rim, taps, steps, cot, ids, weights)


def arrange(me_ref, near_ref, far_ref, held_ref):
    for at in range(near_ref.shape[0]):
        held_ref[me_ref[0] ^ (2 * at)] = near_ref[at]
        held_ref[me_ref[0] ^ (2 * at + 1)] = far_ref[at]


def entering(held_ref, heads, head, size, first, last, step):
    base = held_ref.shape[1] - (heads - head) * (size + RIM)

    def hop(count, total):
        at = first + count * step
        ends = held_ref[at, base + size : base + size + RIM, :].astype(F32)
        factor = jnp.exp(ends[0:1] + ends[1:2] + ends[2:3])
        return factor * total + held_ref[at, base : base + size, :].astype(F32)

    return lax.fori_loop(0, (last - first) * step, hop, jnp.zeros((size, size), F32))


def core_kernel(chunks, me_ref, qkv_ref, steps_ref, gain_ref, near_ref, far_ref, w_ref, *refs):
    out_refs, (headed_ref, held_ref, whole_ref) = refs[:-3], refs[-3:]
    _, rows, chans = qkv_ref.shape
    heads = steps_ref.shape[0]
    size = chans // heads
    arrange(me_ref, near_ref, far_ref, held_ref)
    along, down, lower = decay_sums(steps_ref[...])
    for head in range(heads):
        at = slice(head * size, (head + 1) * size)
        state = entering(held_ref, heads, head, size, 0, me_ref[0], 1).astype(BF)
        diff = down[:, head : head + 1] - along[head : head + 1, :]
        mask = jnp.exp(jnp.where(lower, diff, -jnp.inf))
        query = qkv_ref[0, :, at]
        scores = (mm(query, qkv_ref[1, :, at], NT) * mask).astype(BF)
        attended = mm(scores, qkv_ref[2, :, at])
        attended += mm(query, state) * jnp.exp(down[:, head : head + 1])
        scale = lax.rsqrt(jnp.mean(attended * attended, axis=-1, keepdims=True) + 1e-06)
        headed_ref[:, at] = (attended * scale * gain_ref[:, at]).astype(BF)
    whole_ref[...] = mm(headed_ref[...], w_ref[...]).astype(BF)
    part = rows // len(out_refs) // chunks
    for mask, ref in enumerate(out_refs):
        for chunk in range(chunks):
            start = chunk * len(out_refs) * part + (me_ref[2] ^ mask) * part
            ref[chunk * part : (chunk + 1) * part] = whole_ref[pl.ds(pl.multiple_of(start, part), part), :]


def core_out(where, qkv, steps, near, far, gain, w_out, chunks, parts):
    _, rows, chans = qkv.shape
    width = w_out.shape[1]
    vmem = pl.BlockSpec(memory_space=pltpu.VMEM)
    return pl.pallas_call(
        functools.partial(core_kernel, chunks),
        in_specs=[pl.BlockSpec(memory_space=pltpu.SMEM)] + [vmem] * 6,
        out_shape=[jax.ShapeDtypeStruct((rows // parts, width), BF)] * parts,
        scratch_shapes=[
            pltpu.VMEM((rows, chans), BF),
            pltpu.VMEM((2 * near.shape[0], *near.shape[1:]), BF),
            pltpu.VMEM((rows, width), BF),
        ],
        compiler_params=params(16),
        name="core_out",
    )(where, qkv, steps, gain.reshape(1, chans), near, far, w_out)


def grad_kernel(
    me_ref, qkv_ref, cot_ref, steps_ref, fwd_near, fwd_far, bwd_near, bwd_far, gq_ref, gk_ref, gv_ref, fwd_ref, bwd_ref
):
    _, rows, chans = qkv_ref.shape
    heads = steps_ref.shape[0]
    size = chans // heads
    count = fwd_ref.shape[0]
    arrange(me_ref, fwd_near, fwd_far, fwd_ref)
    arrange(me_ref, bwd_near, bwd_far, bwd_ref)
    along, down, lower = decay_sums(steps_ref[...])
    for head in range(heads):
        at = slice(head * size, (head + 1) * size)
        state = entering(fwd_ref, heads, head, size, 0, me_ref[0], 1).astype(BF)
        after = entering(bwd_ref, heads, head, size, count - 1, me_ref[0], -1).astype(BF)
        here = down[:, head : head + 1]
        lead = jnp.exp(here)
        tail = jnp.exp(along[head : head + 1, rows - 1 : rows] - here)
        mask = jnp.exp(jnp.where(lower, here - along[head : head + 1, :], -jnp.inf))
        query, key, val = qkv_ref[0, :, at], qkv_ref[1, :, at], qkv_ref[2, :, at]
        cot = cot_ref[:, at]
        scores = (mm(query, key, NT) * mask).astype(BF)
        dov = (mm(cot, val, NT) * mask).astype(BF)
        gq_ref[:, at] = (mm(dov, key) + lead * mm(cot, state, NT)).astype(BF)
        gk_ref[:, at] = (mm(dov, query, TN) + tail * mm(val, after, NT)).astype(BF)
        gv_ref[:, at] = (mm(scores, cot, TN) + tail * mm(key, after)).astype(BF)


def core_grads(where, qkv, cot, steps, fwd, bwd):
    _, rows, chans = qkv.shape
    count = 2 * fwd[0].shape[0]
    vmem = pl.BlockSpec(memory_space=pltpu.VMEM)
    return pl.pallas_call(
        grad_kernel,
        in_specs=[pl.BlockSpec(memory_space=pltpu.SMEM)] + [vmem] * 7,
        out_shape=[jax.ShapeDtypeStruct((rows, chans), BF)] * 3,
        scratch_shapes=[pltpu.VMEM((count, *fwd[0].shape[1:]), BF), pltpu.VMEM((count, *bwd[0].shape[1:]), BF)],
        compiler_params=params(24),
        name="core_grads",
    )(where, qkv, cot, steps, *fwd, *bwd)


def norm_kernel(count, where_ref, x_ref, gain_ref, *refs):
    chunks = (len(refs) - count) // 2
    parts, outs, attns = refs[:count], refs[count : count + chunks], refs[count + chunks :]
    rows = outs[0].shape[0]
    for chunk, (out_ref, attn_ref) in enumerate(zip(outs, attns)):
        at = slice(chunk * rows, (chunk + 1) * rows)
        attn = functools.reduce(jnp.add, [part[at].astype(F32) for part in parts])
        attn_ref[...] = attn
        start = pl.multiple_of((chunk * count + where_ref[2]) * rows, rows)
        resid = x_ref[pl.ds(start, rows), :].astype(F32) + attn
        scale = lax.rsqrt(jnp.mean(resid * resid, axis=-1, keepdims=True) + 1e-06)
        out_ref[...] = (resid * scale * gain_ref[...]).astype(BF)


def norm_rows(where, x, parts, gain, chunks):
    rows, width = parts[0].shape[0] // chunks, parts[0].shape[1]
    vmem = pl.BlockSpec(memory_space=pltpu.VMEM)
    outs = pl.pallas_call(
        functools.partial(norm_kernel, len(parts)),
        in_specs=[pl.BlockSpec(memory_space=pltpu.SMEM)] + [vmem] * (2 + len(parts)),
        out_shape=[jax.ShapeDtypeStruct((rows, width), BF)] * chunks
        + [jax.ShapeDtypeStruct((rows, width), F32)] * chunks,
        compiler_params=params(12),
        name="moe_norm",
    )(where, x, gain.reshape(1, width), *parts)
    return list(outs[:chunks]), list(outs[chunks:])


def join_kernel(where_ref, *refs):
    parts, out_ref = refs[:-1], refs[-1]
    rows = parts[0].shape[0]
    for mask, ref in enumerate(parts):
        out_ref[pl.ds(pl.multiple_of((where_ref[2] ^ mask) * rows, rows), rows), :] = ref[...]


def join_rows(where, parts):
    rows, width = parts[0].shape
    vmem = pl.BlockSpec(memory_space=pltpu.VMEM)
    return pl.pallas_call(
        join_kernel,
        in_specs=[pl.BlockSpec(memory_space=pltpu.SMEM)] + [vmem] * len(parts),
        out_shape=jax.ShapeDtypeStruct((len(parts) * rows, width), BF),
        compiler_params=params(16),
        name="join_rows",
    )(where, *parts)


PAIR = 2


def expert_kernel(masks, chunk, experts, where_ref, near_routes, far_routes, gate_ref, up_ref, down_ref, *refs):
    row_refs, outs, (rows_ref, sems) = refs[: len(masks)], refs[len(masks) : -2], refs[-2:]
    _, tok, width = outs[0].shape
    steps = len(masks) // PAIR
    step = pl.program_id(0)
    slot = lax.rem(step, 2)

    def start(at):
        for part in range(PAIR):
            target = rows_ref.at[at % 2, pl.ds(part * tok, tok)]
            pltpu.make_async_copy(row_refs[PAIR * at + part], target, sems.at[at % 2]).start()

    @pl.when(step == 0)
    def _():
        start(0)

    for at in range(1, steps):

        @pl.when(step == at - 1)
        def _(at=at):
            start(at)

    here = lax.broadcasted_iota(jnp.int32, (3 * experts, LANES), 0)
    mine = (here == where_ref[1]) | (here == where_ref[1] + experts) | (here == where_ref[1] + 2 * experts)
    square = (LANES, LANES)
    diagonal = lax.broadcasted_iota(jnp.int32, square, 0) == lax.broadcasted_iota(jnp.int32, square, 1)
    weights = []
    for part in range(PAIR):
        index = jnp.int32(masks[part] // 2)
        for at in range(1, steps):
            index = jnp.where(step == at, masks[PAIR * at + part] // 2, index)
        routes_ref = far_routes if masks[part] & CORE else near_routes
        for block in range(tok // LANES):
            base = (chunk // LANES + block) * 3 * experts
            table = routes_ref[index, base : base + 3 * experts, :].astype(F32)
            row = jnp.sum(jnp.where(mine, table, 0.0), axis=0, keepdims=True)
            weights.append(jnp.sum(jnp.where(diagonal, jnp.broadcast_to(row, square), 0.0), axis=1, keepdims=True))

    pltpu.make_async_copy(rows_ref.at[slot], rows_ref.at[slot], sems.at[slot]).wait()
    tokens = rows_ref[slot]
    gate = mm(tokens, gate_ref[0])
    inner = (gate * jax.nn.sigmoid(gate) * mm(tokens, up_ref[0])).astype(BF)
    cols = pick_block(width, 512)
    for begin in range(0, width, cols):
        piece = mm(inner, down_ref[0, :, begin : begin + cols])
        for at, weight in enumerate(weights):
            part, row = divmod(at * LANES, tok)
            scaled = (piece[at * LANES : (at + 1) * LANES] * weight).astype(BF)
            if len(outs) > 1:
                outs[part][0, row : row + LANES, begin : begin + cols] = scaled
            else:
                outs[0][part, row : row + LANES, begin : begin + cols] = scaled


def stage_kernel(where_ref, *refs):
    out_ref = refs[-1]
    for at in range(where_ref.shape[0]):
        out_ref[at] = where_ref[at]


def stage(where, *weights):
    smem = pl.BlockSpec(memory_space=pltpu.SMEM)
    return pl.pallas_call(
        stage_kernel,
        in_specs=[smem] + [pl.BlockSpec(memory_space=pltpu.VMEM)] * len(weights),
        out_specs=smem,
        out_shape=jax.ShapeDtypeStruct(where.shape, where.dtype),
        compiler_params=params(2),
        name="stage_weights",
    )(where, *weights)


def expert_pieces(chunk, where, rows, groups, gate, up, down, routes):
    split = len(groups)
    masks = groups[0] if split == 1 else [mask for pair in zip(*groups) for mask in pair]
    blocks = [rows[mask] for mask in masks]
    tok, width = blocks[0].shape
    hidden = gate.shape[2]
    count, each, per = len(blocks), len(groups[0]), PAIR // split
    experts = EXP_CTX * 2 * routes[0].shape[0]
    route_rows = CHUNKS * tok // LANES * 3 * experts
    vmem = pl.BlockSpec(memory_space=pltpu.VMEM)
    table = pl.BlockSpec((routes[0].shape[0], route_rows, LANES), lambda i: (0, 0, 0))
    return pl.pallas_call(
        functools.partial(expert_kernel, tuple(masks), chunk, experts),
        grid=(count // PAIR,),
        in_specs=[pl.BlockSpec(memory_space=pltpu.SMEM), table, table]
        + [vmem] * 3
        + [pl.BlockSpec(memory_space=pl.ANY)] * count,
        out_specs=[pl.BlockSpec((per, tok, width), lambda i: (i, 0, 0))] * split,
        out_shape=[jax.ShapeDtypeStruct((each, tok, width), BF)] * split,
        scratch_shapes=[
            pltpu.VMEM((2, PAIR * tok, width), BF),
            pltpu.SemaphoreType.DMA((2,)),
        ],
        compiler_params=params(20),
        cost_estimate=pl.CostEstimate(
            flops=6 * count * tok * width * hidden,
            bytes_accessed=4 * count * tok * width,
            transcendentals=count * tok * hidden,
        ),
        name="expert_pieces",
    )(where, *routes, gate, up, down, *blocks)


CORE, ROW, COL = 1, 2, 4
PLANE = 8


def swap(value, mask):
    return lax.ppermute(value, "ctx", [(at, at ^ mask) for at in range(lax.axis_size("ctx"))])


def send_heads(parts):
    count = lax.axis_size("head")
    return [parts[0]] + [
        lax.ppermute(parts[mask], "head", [(at, at ^ mask) for at in range(count)]) for mask in range(1, count)
    ]


def spread_near(own):
    return jnp.stack([own] + [swap(own, mask) for mask in range(2, lax.axis_size("ctx"), 2)])


def double(near, mask):
    return jnp.concatenate([near, swap(near, mask)])


def plus(*terms):
    return functools.reduce(jnp.add, [term.astype(F32) for term in terms]).astype(BF)


def after(value, other):
    return lax.optimization_barrier((value, other))[0]


def depart(own):
    masks = (ROW, COL) if lax.axis_size("ctx") == PLANE else range(2, lax.axis_size("ctx"), 2)
    return {mask: swap(own, mask) for mask in masks}


def forward(came):
    if lax.axis_size("ctx") != PLANE:
        return []
    half = came[ROW].shape[0] // 2
    return [swap(came[ROW][:half], COL), swap(came[COL][half:], ROW)]


def first_sums(here, arrived):
    tok = here.shape[1]
    if lax.axis_size("ctx") != PLANE:
        return [(2 * at, plus(here[at], arrived[at]), [(0, 0, tok)]) for at in range(1, here.shape[0])]
    half, across = tok // 2, (ROW | COL) // 2
    sums = []
    for mask, start in ((ROW, 0), (COL, half)):
        part = slice(start, start + half)
        pieces = [plus(here[at, part], arrived[at, part]) for at in (across, mask // 2)]
        sums.append((mask, jnp.concatenate(pieces), [(half, start, half)]))
    return sums


def last_sums(here, arrived, came):
    if lax.axis_size("ctx") != PLANE:
        return []
    half = here.shape[1] // 2
    row, col = ROW // 2, COL // 2
    return [
        (COL, plus(here[col, :half], arrived[col, :half], came[0][:half]), [(0, 0, half)]),
        (ROW, plus(here[row, half:], arrived[row, half:], came[1][:half]), [(0, half, half)]),
    ]


def send_sums(sums):
    return [swap(rows, mask) for mask, rows, _ in sums]


def arrays(sums):
    return [rows for _, rows, _ in sums]


def terms_of(sums, received):
    return [(rows, places) for (_, _, places), rows in zip(sums, received) if places]


def sum_kernel(places, where_ref, attn_ref, near_ref, arrived_ref, *refs):
    parts = attn_ref.shape[1] // refs[-1].shape[1]
    others, outs, total_ref = refs[: -parts - 1], refs[-parts - 1 : -1], refs[-1]
    part, width = attn_ref.shape
    cols = width // parts
    own = pl.ds(pl.multiple_of(where_ref[2] * part, part), part)
    for mask, out_ref in enumerate(outs):
        at = pl.ds(pl.multiple_of((where_ref[2] ^ mask) * cols, cols), cols)
        total = near_ref[0, :, at].astype(F32) + arrived_ref[0, :, at].astype(F32)
        total_ref[...] = total
        for spots, ref in zip(places, others):
            for source, target, count in spots:
                total_ref[target : target + count] += ref[source : source + count, at].astype(F32)
        total_ref[own, :] += attn_ref[:, at]
        out_ref[...] = total_ref[...].astype(BF)


def sum_terms(where, attn, near, arrived, terms, parts):
    others, places = [rows for rows, _ in terms], tuple(tuple(spots) for _, spots in terms)
    _, tok, width = near.shape
    part = attn.shape[0]
    cols = width // parts
    first = pl.BlockSpec((1, tok, width), lambda i: (0, 0, 0))
    return pl.pallas_call(
        functools.partial(sum_kernel, places),
        grid=(1,),
        in_specs=[
            pl.BlockSpec(memory_space=pltpu.SMEM),
            pl.BlockSpec((part, width), lambda i: (0, 0)),
            first,
            first,
        ]
        + [pl.BlockSpec(part.shape, lambda i: (0, 0)) for part in others],
        out_specs=[pl.BlockSpec((tok, cols), lambda i: (0, 0))] * parts,
        out_shape=[jax.ShapeDtypeStruct((tok, cols), BF)] * parts,
        scratch_shapes=[pltpu.VMEM((tok, cols), F32)],
        compiler_params=params(24),
        name="sum_terms",
    )(where, attn, near, arrived, *others)


def final_kernel(count, where_ref, x_ref, *refs):
    del where_ref
    out_ref = refs[-1]
    rows = refs[0].shape[0]
    for chunk in range((len(refs) - 1) // count):
        at = slice(chunk * rows, (chunk + 1) * rows)
        terms = [x_ref[at]] + [ref[...] for ref in refs[chunk * count : (chunk + 1) * count]]
        out_ref[at] = functools.reduce(jnp.add, [term.astype(F32) for term in terms]).astype(BF)


def final_sum(where, x, parts):
    rows, cols = parts[0][0].shape
    total = len(parts) * rows
    block = pl.BlockSpec((rows, cols), lambda i, where: (0, 0))
    return pl.pallas_call(
        functools.partial(final_kernel, len(parts[0])),
        grid_spec=pltpu.PrefetchScalarGridSpec(
            num_scalar_prefetch=1,
            grid=(1,),
            in_specs=[pl.BlockSpec((total, cols), lambda i, where: (0, where[2]))]
            + [block] * (len(parts) * len(parts[0])),
            out_specs=pl.BlockSpec((total, cols), lambda i, where: (0, 0)),
        ),
        out_shape=jax.ShapeDtypeStruct((total, cols), BF),
        compiler_params=params(12),
        name="layer_out",
    )(where, x, *[part for chunk in parts for part in chunk])


CHUNKS = 2


def body(
    hidden_in,
    gain_attn,
    w_qkv,
    conv_w,
    log_decay,
    norm_gain,
    w_out,
    gain_moe,
    expert_ids,
    route_weights,
    w_gate,
    w_up,
    w_down,
    grad_core,
):
    n_ctx, n_head = lax.axis_size("ctx"), lax.axis_size("head")
    my_ctx, my_head = lax.axis_index("ctx"), lax.axis_index("head")
    experts = EXP_CTX * n_ctx
    shards = n_head // EXP_CTX
    where = jnp.stack([my_ctx, EXP_CTX * my_ctx + my_head // shards, my_head]).astype(jnp.int32)
    steps = log_decay.T
    chunk_rows = hidden_in.shape[0] // CHUNKS

    mixed, rim = project(hidden_in, gain_attn, jnp.transpose(w_qkv, (1, 0, 2)))
    rim = lax.ppermute(rim, "ctx", [(at, at + 1) for at in range(n_ctx - 1)])
    qkv, fwd, bwd = local_states(
        mixed, rim, jnp.transpose(conv_w, (1, 0, 2)), steps, grad_core, expert_ids.T, route_weights.T, experts
    )
    fwd = spread_near(fwd)
    fwd = (fwd, swap(fwd, CORE))
    where = stage(after(where, qkv), w_out)
    parts = core_out(where, qkv, steps, *fwd, norm_gain, w_out, CHUNKS, n_head)
    where = stage(after(where, parts), w_gate, w_up, w_down)
    bwd = double(after(bwd, parts)[None], ROW)
    normed, attn = norm_rows(where, hidden_in, after(send_heads(parts), bwd), gain_moe, CHUNKS)
    bwd = after(bwd, normed)
    while bwd.shape[0] < n_ctx // 2:
        bwd = double(bwd, 2 * bwd.shape[0])

    evens = list(range(0, n_ctx, 2))
    odds = [mask | CORE for mask in evens]
    own = join_rows(where, after(send_heads([normed[0]] * n_head), bwd))
    bwd = (bwd, swap(after(bwd, own), CORE))
    rows = []
    for chunk in range(CHUNKS):
        rows.append({0: own} | ({CORE: swap(own, CORE)} if chunk else {}) | depart(own))
        if chunk + 1 < CHUNKS:
            parts = send_heads([after(normed[chunk + 1], own)] * n_head)
            own = join_rows(where, parts)
            rows[chunk] = after(rows[chunk], own)

    pending, sums, first, arrived = [], [], None, None
    for chunk in range(CHUNKS):
        here_rows = rows[chunk]
        halves = forward(here_rows)
        lacking = [mask for mask in here_rows if mask | CORE not in here_rows]
        here_rows |= {mask | CORE: swap(here_rows[mask], CORE) for mask in lacking}
        if pending:
            arrived = after(arrived, [part for mask, part in here_rows.items() if mask & CORE])
            first = first_sums(pending[-1][0], arrived)
            pending[-1] += (arrived, first, send_sums(first))
            halves = after(halves, arrays(first))
        if halves:
            across = jnp.concatenate(halves)
            here_rows |= {ROW | COL: across, ROW | COL | CORE: swap(across, CORE)}
        if pending:
            here_rows = after(here_rows, arrays(first))
        experts_of = functools.partial(
            expert_pieces, chunk * chunk_rows, where, gate=w_gate, up=w_up, down=w_down, routes=fwd
        )
        if chunk + 1 < CHUNKS:
            here, far = experts_of(rows=here_rows, groups=[evens, odds])
            arrived = swap(after(far, (rows[chunk + 1], bwd)), CORE)
            pending.append((here,))
        else:
            (far,) = experts_of(rows=here_rows, groups=[odds])
            arrived = swap(after(far, pending[-1][3]), CORE)
            last = last_sums(*pending[-1][:2], pending[-1][3])
            received = send_sums(last)
            pending[-1] += (terms_of(first, pending[-1][3]) + terms_of(last, received),)
            (here,) = experts_of(rows=after(here_rows, [far] + arrays(last)), groups=[evens])
            arrived = after(arrived, received)
            first = first_sums(here, arrived)
            pending.append((here, arrived, first, send_sums(first)))

    for chunk in range(CHUNKS):
        here, arrived, first, received = pending[chunk][:4]
        if chunk + 1 < CHUNKS:
            terms = pending[chunk][4]
            held = after([rows for rows, _ in terms], arrays(pending[chunk + 1][2]))
            terms = list(zip(held, [places for _, places in terms]))
        else:
            last = last_sums(here, arrived, after(received, sums[-1][0]))
            terms = terms_of(first, received) + terms_of(last, send_sums(last))
        sums.append(send_heads(sum_terms(where, attn[chunk], here, arrived, terms, n_head)))
    grads = core_grads(where, qkv, grad_core, steps, fwd, bwd)
    return (final_sum(where, hidden_in, sums), *grads)


def solution(mesh):
    in_specs = (
        P("ctx", None),
        P(),
        P(None, None, "head"),
        P(None, None, "head"),
        P("ctx", "head"),
        P("head"),
        P("head", None),
        P(),
        P("ctx", None),
        P("ctx", None),
        P(("ctx", "head"), None, None),
        P(("ctx", "head"), None, None),
        P(("ctx", "head"), None, None),
        P("ctx", "head"),
    )
    out_specs = (P("ctx", "head"), P("ctx", "head"), P("ctx", "head"), P("ctx", "head"))
    return jax.shard_map(body, mesh=mesh, in_specs=in_specs, out_specs=out_specs, check_vma=False)
```

```python
import functools

import jax
import jax.numpy as jnp
from jax import lax
from jax.experimental import pallas as pl
from jax.experimental.pallas import tpu as pltpu
from jax.sharding import PartitionSpec as P

KERNEL = 4
EXP_CTX = 2
LANES = 128
RIM = 16
MIB = 1024 * 1024
HI = lax.Precision.HIGHEST
BF = jnp.bfloat16
F32 = jnp.float32
NT = (((1,), (1,)), ((), ()))
TN = (((0,), (0,)), ((), ()))
NN = (((1,), (0,)), ((), ()))


def params(mib):
    return pltpu.CompilerParams(vmem_limit_bytes=mib * MIB)


def mm(a, b, dims=NN):
    return lax.dot_general(a, b, dims, preferred_element_type=F32)


def pick_block(extent, target):
    return target if extent % target == 0 else extent


def qkv_kernel(x_hbm, gain_ref, w_hbm, mixed_ref, rim_ref, x_ref, w_ref, normed_ref, x_sem, sems):
    kinds, width, chans = w_ref.shape
    load = pltpu.make_async_copy(x_hbm, x_ref, x_sem)
    load.start()
    part = width // sems.shape[1]
    copies = []
    for kind in range(kinds):
        at = [pl.ds(piece * part, part) for piece in range(sems.shape[1])]
        copies.append(
            [
                pltpu.make_async_copy(w_hbm.at[kind, rows], w_ref.at[kind, rows], sems.at[kind, piece])
                for piece, rows in enumerate(at)
            ]
        )
        for copy in copies[kind]:
            copy.start()
    load.wait()
    values = x_ref[...].astype(F32)
    scale = lax.rsqrt(jnp.mean(values * values, axis=-1, keepdims=True) + 1e-06)
    normed_ref[...] = (values * scale * gain_ref[...]).astype(BF)
    for kind in range(kinds):
        for copy in copies[kind]:
            copy.wait()
        out = mm(normed_ref[...], w_ref[kind]).astype(BF)
        mixed_ref[kind] = out
        rim_ref[kind] = out[out.shape[0] - RIM :]


def project(x, gain, weights):
    rows, width = x.shape
    kinds, _, chans = weights.shape
    vmem = pl.BlockSpec(memory_space=pltpu.VMEM)
    hbm = pl.BlockSpec(memory_space=pltpu.HBM)
    return pl.pallas_call(
        qkv_kernel,
        in_specs=[hbm, vmem, hbm],
        out_specs=[vmem, vmem],
        out_shape=[
            jax.ShapeDtypeStruct((kinds, rows, chans), BF),
            jax.ShapeDtypeStruct((kinds, RIM, chans), BF),
        ],
        scratch_shapes=[
            pltpu.VMEM((rows, width), BF),
            pltpu.VMEM((kinds, width, chans), BF),
            pltpu.VMEM((rows, width), BF),
            pltpu.SemaphoreType.DMA,
            pltpu.SemaphoreType.DMA((kinds, 4)),
        ],
        compiler_params=params(60),
        name="qkv_projection",
    )(x, gain.reshape(1, width), weights)


def decay_sums(steps):
    rows = steps.shape[1]
    row_at = lax.broadcasted_iota(jnp.int32, (rows, rows), 0)
    col_at = lax.broadcasted_iota(jnp.int32, (rows, rows), 1)
    lower = row_at >= col_at
    tri = jnp.where(lower, 1.0, 0.0).astype(F32)
    along = lax.dot_general(steps, tri, NT, precision=HI, preferred_element_type=F32)
    down = lax.dot_general(tri, steps, NT, precision=HI, preferred_element_type=F32)
    return along, down, lower


def payload_tail(total, size):
    full = jnp.broadcast_to(total, (RIM, size))
    first = full.astype(BF).astype(F32)
    second = (full - first).astype(BF).astype(F32)
    third = full - first - second
    at = lax.broadcasted_iota(jnp.int32, (RIM, size), 0)
    return jnp.where(at == 0, first, jnp.where(at == 1, second, jnp.where(at == 2, third, 0.0)))


def route_rows(ids_ref, weights_ref, experts):
    top, tok = ids_ref.shape
    expert = lax.broadcasted_iota(jnp.int32, (experts, tok), 0)
    table = jnp.zeros((experts, tok), F32)
    for choice in range(top):
        table += jnp.where(expert == ids_ref[choice : choice + 1, :], weights_ref[choice : choice + 1, :], 0.0)
    first = table.astype(BF).astype(F32)
    second = (table - first).astype(BF).astype(F32)
    return jnp.concatenate([first, second, table - first - second], axis=0)


def conv_kernel(
    experts, mixed_ref, rim_ref, taps_ref, steps_ref, cot_ref, ids_ref, weights_ref, qkv_ref, fwd_ref, bwd_ref, pad_ref
):
    kinds, rows, chans = mixed_ref.shape
    heads = steps_ref.shape[0]
    size = chans // heads
    along, down, _ = decay_sums(steps_ref[...])
    for kind in range(kinds):
        pad_ref[:RIM] = rim_ref[kind].astype(F32)
        pad_ref[RIM:] = mixed_ref[kind].astype(F32)
        total = taps_ref[kind, 0:1, :] * pad_ref[RIM:]
        for offset in range(1, KERNEL):
            total += taps_ref[kind, offset : offset + 1, :] * pad_ref[RIM - offset : RIM - offset + rows]
        activ = total * jax.nn.sigmoid(total)
        if kind == 0:
            activ = activ * size ** (-0.5)
        qkv_ref[kind] = activ.astype(BF)
    routes = rows // LANES * 3 * experts
    table = route_rows(ids_ref, weights_ref, experts).astype(BF)
    for part in range(rows // LANES):
        fwd_ref[part * 3 * experts : (part + 1) * 3 * experts] = table[:, part * LANES : (part + 1) * LANES]
    for head in range(heads):
        at = slice(head * size, (head + 1) * size)
        base = head * (size + RIM)
        behind = routes + base
        last = along[head : head + 1, rows - 1 : rows]
        lead = jnp.exp(down[:, head : head + 1])
        tail = jnp.exp(last - down[:, head : head + 1])
        key_out = (qkv_ref[1, :, at].astype(F32) * tail).astype(BF)
        query_out = (qkv_ref[0, :, at].astype(F32) * lead).astype(BF)
        ends = payload_tail(last, size).astype(BF)
        fwd_ref[behind : behind + size] = mm(key_out, qkv_ref[2, :, at], TN).astype(BF)
        fwd_ref[behind + size : behind + size + RIM] = ends
        bwd_ref[base : base + size] = mm(query_out, cot_ref[:, at], TN).astype(BF)
        bwd_ref[base + size : base + size + RIM] = ends


def local_states(mixed, rim, taps, steps, cot, ids, weights, experts):
    kinds, rows, chans = mixed.shape
    heads = steps.shape[0]
    size = chans // heads
    states = heads * (size + RIM)
    return pl.pallas_call(
        functools.partial(conv_kernel, experts),
        out_specs=[pl.BlockSpec(memory_space=pltpu.VMEM)] * 3,
        out_shape=[
            jax.ShapeDtypeStruct((kinds, rows, chans), BF),
            jax.ShapeDtypeStruct((states + rows // LANES * 3 * experts, size), BF),
            jax.ShapeDtypeStruct((states, size), BF),
        ],
        scratch_shapes=[pltpu.VMEM((rows + RIM, chans), F32)],
        compiler_params=params(12),
        name="conv_states",
    )(mixed, rim, taps, steps, cot, ids, weights)


def arrange(me_ref, near_ref, far_ref, held_ref):
    for at in range(near_ref.shape[0]):
        held_ref[me_ref[0] ^ (2 * at)] = near_ref[at]
        held_ref[me_ref[0] ^ (2 * at + 1)] = far_ref[at]


def entering(held_ref, heads, head, size, first, last, step):
    base = held_ref.shape[1] - (heads - head) * (size + RIM)

    def hop(count, total):
        at = first + count * step
        ends = held_ref[at, base + size : base + size + RIM, :].astype(F32)
        factor = jnp.exp(ends[0:1] + ends[1:2] + ends[2:3])
        return factor * total + held_ref[at, base : base + size, :].astype(F32)

    return lax.fori_loop(0, (last - first) * step, hop, jnp.zeros((size, size), F32))


def core_kernel(chunks, me_ref, qkv_ref, steps_ref, gain_ref, near_ref, far_ref, w_ref, *refs):
    out_refs, (headed_ref, held_ref, whole_ref) = refs[:-3], refs[-3:]
    _, rows, chans = qkv_ref.shape
    heads = steps_ref.shape[0]
    size = chans // heads
    arrange(me_ref, near_ref, far_ref, held_ref)
    along, down, lower = decay_sums(steps_ref[...])
    for head in range(heads):
        at = slice(head * size, (head + 1) * size)
        state = entering(held_ref, heads, head, size, 0, me_ref[0], 1).astype(BF)
        diff = down[:, head : head + 1] - along[head : head + 1, :]
        mask = jnp.exp(jnp.where(lower, diff, -jnp.inf))
        query = qkv_ref[0, :, at]
        scores = (mm(query, qkv_ref[1, :, at], NT) * mask).astype(BF)
        attended = mm(scores, qkv_ref[2, :, at])
        attended += mm(query, state) * jnp.exp(down[:, head : head + 1])
        scale = lax.rsqrt(jnp.mean(attended * attended, axis=-1, keepdims=True) + 1e-06)
        headed_ref[:, at] = (attended * scale * gain_ref[:, at]).astype(BF)
    whole_ref[...] = mm(headed_ref[...], w_ref[...]).astype(BF)
    part = rows // len(out_refs) // chunks
    for mask, ref in enumerate(out_refs):
        for chunk in range(chunks):
            start = chunk * len(out_refs) * part + (me_ref[2] ^ mask) * part
            ref[chunk * part : (chunk + 1) * part] = whole_ref[pl.ds(pl.multiple_of(start, part), part), :]


def core_out(where, qkv, steps, near, far, gain, w_out, chunks, parts):
    _, rows, chans = qkv.shape
    width = w_out.shape[1]
    vmem = pl.BlockSpec(memory_space=pltpu.VMEM)
    return pl.pallas_call(
        functools.partial(core_kernel, chunks),
        in_specs=[pl.BlockSpec(memory_space=pltpu.SMEM)] + [vmem] * 6,
        out_shape=[jax.ShapeDtypeStruct((rows // parts, width), BF)] * parts,
        scratch_shapes=[
            pltpu.VMEM((rows, chans), BF),
            pltpu.VMEM((2 * near.shape[0], *near.shape[1:]), BF),
            pltpu.VMEM((rows, width), BF),
        ],
        compiler_params=params(16),
        name="core_out",
    )(where, qkv, steps, gain.reshape(1, chans), near, far, w_out)


def grad_kernel(
    me_ref, qkv_ref, cot_ref, steps_ref, fwd_near, fwd_far, bwd_near, bwd_far, gq_ref, gk_ref, gv_ref, fwd_ref, bwd_ref
):
    _, rows, chans = qkv_ref.shape
    heads = steps_ref.shape[0]
    size = chans // heads
    count = fwd_ref.shape[0]
    arrange(me_ref, fwd_near, fwd_far, fwd_ref)
    arrange(me_ref, bwd_near, bwd_far, bwd_ref)
    along, down, lower = decay_sums(steps_ref[...])
    for head in range(heads):
        at = slice(head * size, (head + 1) * size)
        state = entering(fwd_ref, heads, head, size, 0, me_ref[0], 1).astype(BF)
        after = entering(bwd_ref, heads, head, size, count - 1, me_ref[0], -1).astype(BF)
        here = down[:, head : head + 1]
        lead = jnp.exp(here)
        tail = jnp.exp(along[head : head + 1, rows - 1 : rows] - here)
        mask = jnp.exp(jnp.where(lower, here - along[head : head + 1, :], -jnp.inf))
        query, key, val = qkv_ref[0, :, at], qkv_ref[1, :, at], qkv_ref[2, :, at]
        cot = cot_ref[:, at]
        scores = (mm(query, key, NT) * mask).astype(BF)
        dov = (mm(cot, val, NT) * mask).astype(BF)
        gq_ref[:, at] = (mm(dov, key) + lead * mm(cot, state, NT)).astype(BF)
        gk_ref[:, at] = (mm(dov, query, TN) + tail * mm(val, after, NT)).astype(BF)
        gv_ref[:, at] = (mm(scores, cot, TN) + tail * mm(key, after)).astype(BF)


def core_grads(where, qkv, cot, steps, fwd, bwd):
    _, rows, chans = qkv.shape
    count = 2 * fwd[0].shape[0]
    vmem = pl.BlockSpec(memory_space=pltpu.VMEM)
    return pl.pallas_call(
        grad_kernel,
        in_specs=[pl.BlockSpec(memory_space=pltpu.SMEM)] + [vmem] * 7,
        out_shape=[jax.ShapeDtypeStruct((rows, chans), BF)] * 3,
        scratch_shapes=[pltpu.VMEM((count, *fwd[0].shape[1:]), BF), pltpu.VMEM((count, *bwd[0].shape[1:]), BF)],
        compiler_params=params(24),
        name="core_grads",
    )(where, qkv, cot, steps, *fwd, *bwd)


def norm_kernel(count, where_ref, x_ref, gain_ref, *refs):
    chunks = (len(refs) - count) // 2
    parts, outs, attns = refs[:count], refs[count : count + chunks], refs[count + chunks :]
    rows = outs[0].shape[0]
    for chunk, (out_ref, attn_ref) in enumerate(zip(outs, attns)):
        at = slice(chunk * rows, (chunk + 1) * rows)
        attn = functools.reduce(jnp.add, [part[at].astype(F32) for part in parts])
        attn_ref[...] = attn
        start = pl.multiple_of((chunk * count + where_ref[2]) * rows, rows)
        resid = x_ref[pl.ds(start, rows), :].astype(F32) + attn
        scale = lax.rsqrt(jnp.mean(resid * resid, axis=-1, keepdims=True) + 1e-06)
        out_ref[...] = (resid * scale * gain_ref[...]).astype(BF)


def norm_rows(where, x, parts, gain, chunks):
    rows, width = parts[0].shape[0] // chunks, parts[0].shape[1]
    vmem = pl.BlockSpec(memory_space=pltpu.VMEM)
    outs = pl.pallas_call(
        functools.partial(norm_kernel, len(parts)),
        in_specs=[pl.BlockSpec(memory_space=pltpu.SMEM)] + [vmem] * (2 + len(parts)),
        out_shape=[jax.ShapeDtypeStruct((rows, width), BF)] * chunks
        + [jax.ShapeDtypeStruct((rows, width), F32)] * chunks,
        compiler_params=params(12),
        name="moe_norm",
    )(where, x, gain.reshape(1, width), *parts)
    return list(outs[:chunks]), list(outs[chunks:])


def join_kernel(where_ref, *refs):
    parts, out_ref = refs[:-1], refs[-1]
    rows = parts[0].shape[0]
    for mask, ref in enumerate(parts):
        out_ref[pl.ds(pl.multiple_of((where_ref[2] ^ mask) * rows, rows), rows), :] = ref[...]


def join_rows(where, parts):
    rows, width = parts[0].shape
    vmem = pl.BlockSpec(memory_space=pltpu.VMEM)
    return pl.pallas_call(
        join_kernel,
        in_specs=[pl.BlockSpec(memory_space=pltpu.SMEM)] + [vmem] * len(parts),
        out_shape=jax.ShapeDtypeStruct((len(parts) * rows, width), BF),
        compiler_params=params(16),
        name="join_rows",
    )(where, *parts)


PAIR = 2


def expert_kernel(masks, chunk, experts, where_ref, near_routes, far_routes, gate_ref, up_ref, down_ref, *refs):
    row_refs, outs, (rows_ref, sems) = refs[: len(masks)], refs[len(masks) : -2], refs[-2:]
    _, tok, width = outs[0].shape
    steps = len(masks) // PAIR
    step = pl.program_id(0)
    slot = lax.rem(step, 2)

    def start(at):
        for part in range(PAIR):
            target = rows_ref.at[at % 2, pl.ds(part * tok, tok)]
            pltpu.make_async_copy(row_refs[PAIR * at + part], target, sems.at[at % 2]).start()

    @pl.when(step == 0)
    def _():
        start(0)

    for at in range(1, steps):

        @pl.when(step == at - 1)
        def _(at=at):
            start(at)

    here = lax.broadcasted_iota(jnp.int32, (3 * experts, LANES), 0)
    mine = (here == where_ref[1]) | (here == where_ref[1] + experts) | (here == where_ref[1] + 2 * experts)
    square = (LANES, LANES)
    diagonal = lax.broadcasted_iota(jnp.int32, square, 0) == lax.broadcasted_iota(jnp.int32, square, 1)
    weights = []
    for part in range(PAIR):
        index = jnp.int32(masks[part] // 2)
        for at in range(1, steps):
            index = jnp.where(step == at, masks[PAIR * at + part] // 2, index)
        routes_ref = far_routes if masks[part] & CORE else near_routes
        for block in range(tok // LANES):
            base = (chunk // LANES + block) * 3 * experts
            table = routes_ref[index, base : base + 3 * experts, :].astype(F32)
            row = jnp.sum(jnp.where(mine, table, 0.0), axis=0, keepdims=True)
            weights.append(jnp.sum(jnp.where(diagonal, jnp.broadcast_to(row, square), 0.0), axis=1, keepdims=True))

    pltpu.make_async_copy(rows_ref.at[slot], rows_ref.at[slot], sems.at[slot]).wait()
    tokens = rows_ref[slot]
    gate = mm(tokens, gate_ref[0])
    inner = (gate * jax.nn.sigmoid(gate) * mm(tokens, up_ref[0])).astype(BF)
    cols = pick_block(width, 512)
    for begin in range(0, width, cols):
        piece = mm(inner, down_ref[0, :, begin : begin + cols])
        for at, weight in enumerate(weights):
            part, row = divmod(at * LANES, tok)
            scaled = (piece[at * LANES : (at + 1) * LANES] * weight).astype(BF)
            if len(outs) > 1:
                outs[part][0, row : row + LANES, begin : begin + cols] = scaled
            else:
                outs[0][part, row : row + LANES, begin : begin + cols] = scaled


def stage_kernel(where_ref, *refs):
    out_ref = refs[-1]
    for at in range(where_ref.shape[0]):
        out_ref[at] = where_ref[at]


def stage(where, *weights):
    smem = pl.BlockSpec(memory_space=pltpu.SMEM)
    return pl.pallas_call(
        stage_kernel,
        in_specs=[smem] + [pl.BlockSpec(memory_space=pltpu.VMEM)] * len(weights),
        out_specs=smem,
        out_shape=jax.ShapeDtypeStruct(where.shape, where.dtype),
        compiler_params=params(2),
        name="stage_weights",
    )(where, *weights)


def expert_pieces(chunk, where, rows, groups, gate, up, down, routes):
    split = len(groups)
    masks = groups[0] if split == 1 else [mask for pair in zip(*groups) for mask in pair]
    blocks = [rows[mask] for mask in masks]
    tok, width = blocks[0].shape
    hidden = gate.shape[2]
    count, each, per = len(blocks), len(groups[0]), PAIR // split
    experts = EXP_CTX * 2 * routes[0].shape[0]
    route_rows = CHUNKS * tok // LANES * 3 * experts
    vmem = pl.BlockSpec(memory_space=pltpu.VMEM)
    table = pl.BlockSpec((routes[0].shape[0], route_rows, LANES), lambda i: (0, 0, 0))
    return pl.pallas_call(
        functools.partial(expert_kernel, tuple(masks), chunk, experts),
        grid=(count // PAIR,),
        in_specs=[pl.BlockSpec(memory_space=pltpu.SMEM), table, table]
        + [vmem] * 3
        + [pl.BlockSpec(memory_space=pl.ANY)] * count,
        out_specs=[pl.BlockSpec((per, tok, width), lambda i: (i, 0, 0))] * split,
        out_shape=[jax.ShapeDtypeStruct((each, tok, width), BF)] * split,
        scratch_shapes=[
            pltpu.VMEM((2, PAIR * tok, width), BF),
            pltpu.SemaphoreType.DMA((2,)),
        ],
        compiler_params=params(20),
        cost_estimate=pl.CostEstimate(
            flops=6 * count * tok * width * hidden,
            bytes_accessed=4 * count * tok * width,
            transcendentals=count * tok * hidden,
        ),
        name="expert_pieces",
    )(where, *routes, gate, up, down, *blocks)


CORE, ROW, COL = 1, 2, 4
PLANE = 8


def swap(value, mask):
    return lax.ppermute(value, "ctx", [(at, at ^ mask) for at in range(lax.axis_size("ctx"))])


def send_heads(parts):
    count = lax.axis_size("head")
    return [parts[0]] + [
        lax.ppermute(parts[mask], "head", [(at, at ^ mask) for at in range(count)]) for mask in range(1, count)
    ]


def spread_near(own):
    return jnp.stack([own] + [swap(own, mask) for mask in range(2, lax.axis_size("ctx"), 2)])


def double(near, mask):
    return jnp.concatenate([near, swap(near, mask)])


def plus(*terms):
    return functools.reduce(jnp.add, [term.astype(F32) for term in terms]).astype(BF)


def after(value, other):
    return lax.optimization_barrier((value, other))[0]


def depart(own):
    masks = (ROW, COL) if lax.axis_size("ctx") == PLANE else range(2, lax.axis_size("ctx"), 2)
    return {mask: swap(own, mask) for mask in masks}


def forward(came):
    if lax.axis_size("ctx") != PLANE:
        return []
    half = came[ROW].shape[0] // 2
    return [swap(came[ROW][:half], COL), swap(came[COL][half:], ROW)]


def first_sums(here, arrived):
    tok = here.shape[1]
    if lax.axis_size("ctx") != PLANE:
        return [(2 * at, plus(here[at], arrived[at]), [(0, 0, tok)]) for at in range(1, here.shape[0])]
    half, across = tok // 2, (ROW | COL) // 2
    sums = []
    for mask, start in ((ROW, 0), (COL, half)):
        part = slice(start, start + half)
        pieces = [plus(here[at, part], arrived[at, part]) for at in (across, mask // 2)]
        sums.append((mask, jnp.concatenate(pieces), [(half, start, half)]))
    return sums


def last_sums(here, arrived, came):
    if lax.axis_size("ctx") != PLANE:
        return []
    half = here.shape[1] // 2
    row, col = ROW // 2, COL // 2
    return [
        (COL, plus(here[col, :half], arrived[col, :half], came[0][:half]), [(0, 0, half)]),
        (ROW, plus(here[row, half:], arrived[row, half:], came[1][:half]), [(0, half, half)]),
    ]


def send_sums(sums):
    return [swap(rows, mask) for mask, rows, _ in sums]


def arrays(sums):
    return [rows for _, rows, _ in sums]


def terms_of(sums, received):
    return [(rows, places) for (_, _, places), rows in zip(sums, received) if places]


def sum_kernel(places, where_ref, attn_ref, near_ref, arrived_ref, *refs):
    parts = attn_ref.shape[1] // refs[-1].shape[1]
    others, outs, total_ref = refs[: -parts - 1], refs[-parts - 1 : -1], refs[-1]
    part, width = attn_ref.shape
    cols = width // parts
    own = pl.ds(pl.multiple_of(where_ref[2] * part, part), part)
    for mask, out_ref in enumerate(outs):
        at = pl.ds(pl.multiple_of((where_ref[2] ^ mask) * cols, cols), cols)
        total = near_ref[0, :, at].astype(F32) + arrived_ref[0, :, at].astype(F32)
        total_ref[...] = total
        for spots, ref in zip(places, others):
            for source, target, count in spots:
                total_ref[target : target + count] += ref[source : source + count, at].astype(F32)
        total_ref[own, :] += attn_ref[:, at]
        out_ref[...] = total_ref[...].astype(BF)


def sum_terms(where, attn, near, arrived, terms, parts):
    others, places = [rows for rows, _ in terms], tuple(tuple(spots) for _, spots in terms)
    _, tok, width = near.shape
    part = attn.shape[0]
    cols = width // parts
    first = pl.BlockSpec((1, tok, width), lambda i: (0, 0, 0))
    return pl.pallas_call(
        functools.partial(sum_kernel, places),
        grid=(1,),
        in_specs=[
            pl.BlockSpec(memory_space=pltpu.SMEM),
            pl.BlockSpec((part, width), lambda i: (0, 0)),
            first,
            first,
        ]
        + [pl.BlockSpec(part.shape, lambda i: (0, 0)) for part in others],
        out_specs=[pl.BlockSpec((tok, cols), lambda i: (0, 0))] * parts,
        out_shape=[jax.ShapeDtypeStruct((tok, cols), BF)] * parts,
        scratch_shapes=[pltpu.VMEM((tok, cols), F32)],
        compiler_params=params(24),
        name="sum_terms",
    )(where, attn, near, arrived, *others)


def final_kernel(count, where_ref, x_ref, *refs):
    del where_ref
    out_ref = refs[-1]
    rows = refs[0].shape[0]
    for chunk in range((len(refs) - 1) // count):
        at = slice(chunk * rows, (chunk + 1) * rows)
        terms = [x_ref[at]] + [ref[...] for ref in refs[chunk * count : (chunk + 1) * count]]
        out_ref[at] = functools.reduce(jnp.add, [term.astype(F32) for term in terms]).astype(BF)


def final_sum(where, x, parts):
    rows, cols = parts[0][0].shape
    total = len(parts) * rows
    block = pl.BlockSpec((rows, cols), lambda i, where: (0, 0))
    return pl.pallas_call(
        functools.partial(final_kernel, len(parts[0])),
        grid_spec=pltpu.PrefetchScalarGridSpec(
            num_scalar_prefetch=1,
            grid=(1,),
            in_specs=[pl.BlockSpec((total, cols), lambda i, where: (0, where[2]))]
            + [block] * (len(parts) * len(parts[0])),
            out_specs=pl.BlockSpec((total, cols), lambda i, where: (0, 0)),
        ),
        out_shape=jax.ShapeDtypeStruct((total, cols), BF),
        compiler_params=params(12),
        name="layer_out",
    )(where, x, *[part for chunk in parts for part in chunk])


CHUNKS = 2


def body(
    hidden_in,
    gain_attn,
    w_qkv,
    conv_w,
    log_decay,
    norm_gain,
    w_out,
    gain_moe,
    expert_ids,
    route_weights,
    w_gate,
    w_up,
    w_down,
    grad_core,
):
    n_ctx, n_head = lax.axis_size("ctx"), lax.axis_size("head")
    my_ctx, my_head = lax.axis_index("ctx"), lax.axis_index("head")
    experts = EXP_CTX * n_ctx
    shards = n_head // EXP_CTX
    where = jnp.stack([my_ctx, EXP_CTX * my_ctx + my_head // shards, my_head]).astype(jnp.int32)
    steps = log_decay.T
    chunk_rows = hidden_in.shape[0] // CHUNKS

    mixed, rim = project(hidden_in, gain_attn, jnp.transpose(w_qkv, (1, 0, 2)))
    rim = lax.ppermute(rim, "ctx", [(at, at + 1) for at in range(n_ctx - 1)])
    qkv, fwd, bwd = local_states(
        mixed, rim, jnp.transpose(conv_w, (1, 0, 2)), steps, grad_core, expert_ids.T, route_weights.T, experts
    )
    fwd = spread_near(fwd)
    fwd = (fwd, swap(fwd, CORE))
    where = stage(after(where, qkv), w_out)
    parts = core_out(where, qkv, steps, *fwd, norm_gain, w_out, CHUNKS, n_head)
    where = stage(after(where, parts), w_gate, w_up, w_down)
    bwd = double(after(bwd, parts)[None], ROW)
    normed, attn = norm_rows(where, hidden_in, after(send_heads(parts), bwd), gain_moe, CHUNKS)
    bwd = after(bwd, normed)
    while bwd.shape[0] < n_ctx // 2:
        bwd = double(bwd, 2 * bwd.shape[0])

    evens = list(range(0, n_ctx, 2))
    odds = [mask | CORE for mask in evens]
    own = join_rows(where, after(send_heads([normed[0]] * n_head), bwd))
    bwd = (bwd, swap(after(bwd, own), CORE))
    rows = []
    for chunk in range(CHUNKS):
        rows.append({0: own} | ({CORE: swap(own, CORE)} if chunk else {}) | depart(own))
        if chunk + 1 < CHUNKS:
            parts = send_heads([after(normed[chunk + 1], own)] * n_head)
            own = join_rows(where, parts)
            rows[chunk] = after(rows[chunk], own)

    pending, sums, first, arrived = [], [], None, None
    for chunk in range(CHUNKS):
        here_rows = rows[chunk]
        halves = forward(here_rows)
        lacking = [mask for mask in here_rows if mask | CORE not in here_rows]
        here_rows |= {mask | CORE: swap(here_rows[mask], CORE) for mask in lacking}
        if pending:
            arrived = after(arrived, [part for mask, part in here_rows.items() if mask & CORE])
            first = first_sums(pending[-1][0], arrived)
            pending[-1] += (arrived, first, send_sums(first))
            halves = after(halves, arrays(first))
        if halves:
            across = jnp.concatenate(halves)
            here_rows |= {ROW | COL: across, ROW | COL | CORE: swap(across, CORE)}
        if pending:
            here_rows = after(here_rows, arrays(first))
        experts_of = functools.partial(
            expert_pieces, chunk * chunk_rows, where, gate=w_gate, up=w_up, down=w_down, routes=fwd
        )
        here, far = experts_of(rows=here_rows, groups=[evens, odds])
        beside = (rows[chunk + 1], bwd) if chunk + 1 < CHUNKS else pending[-1][3]
        arrived = swap(after(far, beside), CORE)
        if chunk + 1 < CHUNKS:
            pending.append((here,))
        else:
            last = last_sums(*pending[-1][:2], pending[-1][3])
            received = send_sums(last)
            pending[-1] += (terms_of(first, pending[-1][3]) + terms_of(last, received),)
            arrived = after(arrived, received)
            first = first_sums(here, arrived)
            pending.append((here, arrived, first, send_sums(first)))

    for chunk in range(CHUNKS):
        here, arrived, first, received = pending[chunk][:4]
        if chunk + 1 < CHUNKS:
            terms = pending[chunk][4]
            held = after([rows for rows, _ in terms], arrays(pending[chunk + 1][2]))
            terms = list(zip(held, [places for _, places in terms]))
        else:
            last = last_sums(here, arrived, after(received, sums[-1][:-1]))
            terms = terms_of(first, received) + terms_of(last, send_sums(last))
        sums.append(send_heads(sum_terms(where, attn[chunk], here, arrived, terms, n_head)))
    grads = core_grads(where, qkv, grad_core, steps, fwd, bwd)
    return (final_sum(where, hidden_in, sums), *grads)


def solution(mesh):
    in_specs = (
        P("ctx", None),
        P(),
        P(None, None, "head"),
        P(None, None, "head"),
        P("ctx", "head"),
        P("head"),
        P("head", None),
        P(),
        P("ctx", None),
        P("ctx", None),
        P(("ctx", "head"), None, None),
        P(("ctx", "head"), None, None),
        P(("ctx", "head"), None, None),
        P("ctx", "head"),
    )
    out_specs = (P("ctx", "head"), P("ctx", "head"), P("ctx", "head"), P("ctx", "head"))
    return jax.shard_map(body, mesh=mesh, in_specs=in_specs, out_specs=out_specs, check_vma=False)
```

```python
import functools

import jax
import jax.numpy as jnp
from jax import lax
from jax.experimental import pallas as pl
from jax.experimental.pallas import tpu as pltpu
from jax.sharding import PartitionSpec as P

KERNEL = 4
EXP_CTX = 2
LANES = 128
RIM = 16
MIB = 1024 * 1024
HI = lax.Precision.HIGHEST
BF = jnp.bfloat16
F32 = jnp.float32
NT = (((1,), (1,)), ((), ()))
TN = (((0,), (0,)), ((), ()))
NN = (((1,), (0,)), ((), ()))


def params(mib):
    return pltpu.CompilerParams(vmem_limit_bytes=mib * MIB)


def mm(a, b, dims=NN):
    return lax.dot_general(a, b, dims, preferred_element_type=F32)


def pick_block(extent, target):
    return target if extent % target == 0 else extent


def qkv_kernel(x_hbm, gain_ref, w_hbm, mixed_ref, rim_ref, x_ref, w_ref, normed_ref, x_sem, sems):
    kinds, width, chans = w_ref.shape
    load = pltpu.make_async_copy(x_hbm, x_ref, x_sem)
    load.start()
    part = width // sems.shape[1]
    copies = []
    for kind in range(kinds):
        at = [pl.ds(piece * part, part) for piece in range(sems.shape[1])]
        copies.append(
            [
                pltpu.make_async_copy(w_hbm.at[kind, rows], w_ref.at[kind, rows], sems.at[kind, piece])
                for piece, rows in enumerate(at)
            ]
        )
        for copy in copies[kind]:
            copy.start()
    load.wait()
    values = x_ref[...].astype(F32)
    scale = lax.rsqrt(jnp.mean(values * values, axis=-1, keepdims=True) + 1e-06)
    normed_ref[...] = (values * scale * gain_ref[...]).astype(BF)
    for kind in range(kinds):
        for copy in copies[kind]:
            copy.wait()
        out = mm(normed_ref[...], w_ref[kind]).astype(BF)
        mixed_ref[kind] = out
        rim_ref[kind] = out[out.shape[0] - RIM :]


def project(x, gain, weights):
    rows, width = x.shape
    kinds, _, chans = weights.shape
    vmem = pl.BlockSpec(memory_space=pltpu.VMEM)
    hbm = pl.BlockSpec(memory_space=pltpu.HBM)
    return pl.pallas_call(
        qkv_kernel,
        in_specs=[hbm, vmem, hbm],
        out_specs=[vmem, vmem],
        out_shape=[
            jax.ShapeDtypeStruct((kinds, rows, chans), BF),
            jax.ShapeDtypeStruct((kinds, RIM, chans), BF),
        ],
        scratch_shapes=[
            pltpu.VMEM((rows, width), BF),
            pltpu.VMEM((kinds, width, chans), BF),
            pltpu.VMEM((rows, width), BF),
            pltpu.SemaphoreType.DMA,
            pltpu.SemaphoreType.DMA((kinds, 4)),
        ],
        compiler_params=params(60),
        name="qkv_projection",
    )(x, gain.reshape(1, width), weights)


def decay_sums(steps):
    rows = steps.shape[1]
    row_at = lax.broadcasted_iota(jnp.int32, (rows, rows), 0)
    col_at = lax.broadcasted_iota(jnp.int32, (rows, rows), 1)
    lower = row_at >= col_at
    tri = jnp.where(lower, 1.0, 0.0).astype(F32)
    along = lax.dot_general(steps, tri, NT, precision=HI, preferred_element_type=F32)
    down = lax.dot_general(tri, steps, NT, precision=HI, preferred_element_type=F32)
    return along, down, lower


def payload_tail(total, size):
    full = jnp.broadcast_to(total, (RIM, size))
    first = full.astype(BF).astype(F32)
    second = (full - first).astype(BF).astype(F32)
    third = full - first - second
    at = lax.broadcasted_iota(jnp.int32, (RIM, size), 0)
    return jnp.where(at == 0, first, jnp.where(at == 1, second, jnp.where(at == 2, third, 0.0)))


def route_rows(ids_ref, weights_ref, experts):
    top, tok = ids_ref.shape
    expert = lax.broadcasted_iota(jnp.int32, (experts, tok), 0)
    table = jnp.zeros((experts, tok), F32)
    for choice in range(top):
        table += jnp.where(expert == ids_ref[choice : choice + 1, :], weights_ref[choice : choice + 1, :], 0.0)
    first = table.astype(BF).astype(F32)
    second = (table - first).astype(BF).astype(F32)
    return jnp.concatenate([first, second, table - first - second], axis=0)


def conv_kernel(
    experts, mixed_ref, rim_ref, taps_ref, steps_ref, cot_ref, ids_ref, weights_ref, qkv_ref, fwd_ref, bwd_ref, pad_ref
):
    kinds, rows, chans = mixed_ref.shape
    heads = steps_ref.shape[0]
    size = chans // heads
    along, down, _ = decay_sums(steps_ref[...])
    for kind in range(kinds):
        pad_ref[:RIM] = rim_ref[kind].astype(F32)
        pad_ref[RIM:] = mixed_ref[kind].astype(F32)
        total = taps_ref[kind, 0:1, :] * pad_ref[RIM:]
        for offset in range(1, KERNEL):
            total += taps_ref[kind, offset : offset + 1, :] * pad_ref[RIM - offset : RIM - offset + rows]
        activ = total * jax.nn.sigmoid(total)
        if kind == 0:
            activ = activ * size ** (-0.5)
        qkv_ref[kind] = activ.astype(BF)
    routes = rows // LANES * 3 * experts
    table = route_rows(ids_ref, weights_ref, experts).astype(BF)
    for part in range(rows // LANES):
        fwd_ref[part * 3 * experts : (part + 1) * 3 * experts] = table[:, part * LANES : (part + 1) * LANES]
    for head in range(heads):
        at = slice(head * size, (head + 1) * size)
        base = head * (size + RIM)
        behind = routes + base
        last = along[head : head + 1, rows - 1 : rows]
        lead = jnp.exp(down[:, head : head + 1])
        tail = jnp.exp(last - down[:, head : head + 1])
        key_out = (qkv_ref[1, :, at].astype(F32) * tail).astype(BF)
        query_out = (qkv_ref[0, :, at].astype(F32) * lead).astype(BF)
        ends = payload_tail(last, size).astype(BF)
        fwd_ref[behind : behind + size] = mm(key_out, qkv_ref[2, :, at], TN).astype(BF)
        fwd_ref[behind + size : behind + size + RIM] = ends
        bwd_ref[base : base + size] = mm(query_out, cot_ref[:, at], TN).astype(BF)
        bwd_ref[base + size : base + size + RIM] = ends


def local_states(mixed, rim, taps, steps, cot, ids, weights, experts):
    kinds, rows, chans = mixed.shape
    heads = steps.shape[0]
    size = chans // heads
    states = heads * (size + RIM)
    return pl.pallas_call(
        functools.partial(conv_kernel, experts),
        out_specs=[pl.BlockSpec(memory_space=pltpu.VMEM)] * 3,
        out_shape=[
            jax.ShapeDtypeStruct((kinds, rows, chans), BF),
            jax.ShapeDtypeStruct((states + rows // LANES * 3 * experts, size), BF),
            jax.ShapeDtypeStruct((states, size), BF),
        ],
        scratch_shapes=[pltpu.VMEM((rows + RIM, chans), F32)],
        compiler_params=params(12),
        name="conv_states",
    )(mixed, rim, taps, steps, cot, ids, weights)


def arrange(me_ref, near_ref, far_ref, held_ref):
    for at in range(near_ref.shape[0]):
        held_ref[me_ref[0] ^ (2 * at)] = near_ref[at]
        held_ref[me_ref[0] ^ (2 * at + 1)] = far_ref[at]


def entering(held_ref, heads, head, size, first, last, step):
    base = held_ref.shape[1] - (heads - head) * (size + RIM)

    def hop(count, total):
        at = first + count * step
        ends = held_ref[at, base + size : base + size + RIM, :].astype(F32)
        factor = jnp.exp(ends[0:1] + ends[1:2] + ends[2:3])
        return factor * total + held_ref[at, base : base + size, :].astype(F32)

    return lax.fori_loop(0, (last - first) * step, hop, jnp.zeros((size, size), F32))


def core_kernel(chunks, me_ref, qkv_ref, steps_ref, gain_ref, near_ref, far_ref, w_ref, *refs):
    out_refs, (headed_ref, held_ref, whole_ref) = refs[:-3], refs[-3:]
    _, rows, chans = qkv_ref.shape
    heads = steps_ref.shape[0]
    size = chans // heads
    arrange(me_ref, near_ref, far_ref, held_ref)
    along, down, lower = decay_sums(steps_ref[...])
    for head in range(heads):
        at = slice(head * size, (head + 1) * size)
        state = entering(held_ref, heads, head, size, 0, me_ref[0], 1).astype(BF)
        diff = down[:, head : head + 1] - along[head : head + 1, :]
        mask = jnp.exp(jnp.where(lower, diff, -jnp.inf))
        query = qkv_ref[0, :, at]
        scores = (mm(query, qkv_ref[1, :, at], NT) * mask).astype(BF)
        attended = mm(scores, qkv_ref[2, :, at])
        attended += mm(query, state) * jnp.exp(down[:, head : head + 1])
        scale = lax.rsqrt(jnp.mean(attended * attended, axis=-1, keepdims=True) + 1e-06)
        headed_ref[:, at] = (attended * scale * gain_ref[:, at]).astype(BF)
    whole_ref[...] = mm(headed_ref[...], w_ref[...]).astype(BF)
    part = rows // len(out_refs) // chunks
    for mask, ref in enumerate(reversed(out_refs)):
        for chunk in range(chunks):
            start = chunk * len(out_refs) * part + (me_ref[2] ^ mask) * part
            ref[chunk * part : (chunk + 1) * part] = whole_ref[pl.ds(pl.multiple_of(start, part), part), :]


def core_out(where, qkv, steps, near, far, gain, w_out, chunks, parts):
    _, rows, chans = qkv.shape
    width = w_out.shape[1]
    vmem = pl.BlockSpec(memory_space=pltpu.VMEM)
    return pl.pallas_call(
        functools.partial(core_kernel, chunks),
        in_specs=[pl.BlockSpec(memory_space=pltpu.SMEM)] + [vmem] * 6,
        out_shape=[jax.ShapeDtypeStruct((rows // parts, width), BF)] * parts,
        scratch_shapes=[
            pltpu.VMEM((rows, chans), BF),
            pltpu.VMEM((2 * near.shape[0], *near.shape[1:]), BF),
            pltpu.VMEM((rows, width), BF),
        ],
        compiler_params=params(16),
        name="core_out",
    )(where, qkv, steps, gain.reshape(1, chans), near, far, w_out)


def grad_kernel(
    me_ref, qkv_ref, cot_ref, steps_ref, fwd_near, fwd_far, bwd_near, bwd_far, gq_ref, gk_ref, gv_ref, fwd_ref, bwd_ref
):
    _, rows, chans = qkv_ref.shape
    heads = steps_ref.shape[0]
    size = chans // heads
    count = fwd_ref.shape[0]
    arrange(me_ref, fwd_near, fwd_far, fwd_ref)
    arrange(me_ref, bwd_near, bwd_far, bwd_ref)
    along, down, lower = decay_sums(steps_ref[...])
    for head in range(heads):
        at = slice(head * size, (head + 1) * size)
        state = entering(fwd_ref, heads, head, size, 0, me_ref[0], 1).astype(BF)
        after = entering(bwd_ref, heads, head, size, count - 1, me_ref[0], -1).astype(BF)
        here = down[:, head : head + 1]
        lead = jnp.exp(here)
        tail = jnp.exp(along[head : head + 1, rows - 1 : rows] - here)
        mask = jnp.exp(jnp.where(lower, here - along[head : head + 1, :], -jnp.inf))
        query, key, val = qkv_ref[0, :, at], qkv_ref[1, :, at], qkv_ref[2, :, at]
        cot = cot_ref[:, at]
        scores = (mm(query, key, NT) * mask).astype(BF)
        dov = (mm(cot, val, NT) * mask).astype(BF)
        gq_ref[:, at] = (mm(dov, key) + lead * mm(cot, state, NT)).astype(BF)
        gk_ref[:, at] = (mm(dov, query, TN) + tail * mm(val, after, NT)).astype(BF)
        gv_ref[:, at] = (mm(scores, cot, TN) + tail * mm(key, after)).astype(BF)


def core_grads(where, qkv, cot, steps, fwd, bwd):
    _, rows, chans = qkv.shape
    count = 2 * fwd[0].shape[0]
    vmem = pl.BlockSpec(memory_space=pltpu.VMEM)
    return pl.pallas_call(
        grad_kernel,
        in_specs=[pl.BlockSpec(memory_space=pltpu.SMEM)] + [vmem] * 7,
        out_shape=[jax.ShapeDtypeStruct((rows, chans), BF)] * 3,
        scratch_shapes=[pltpu.VMEM((count, *fwd[0].shape[1:]), BF), pltpu.VMEM((count, *bwd[0].shape[1:]), BF)],
        compiler_params=params(24),
        name="core_grads",
    )(where, qkv, cot, steps, *fwd, *bwd)


def norm_kernel(count, where_ref, x_ref, gain_ref, *refs):
    chunks = (len(refs) - count) // 2
    parts, outs, attns = refs[:count], refs[count : count + chunks], refs[count + chunks :]
    rows = outs[0].shape[0]
    for chunk, (out_ref, attn_ref) in enumerate(zip(outs, attns)):
        at = slice(chunk * rows, (chunk + 1) * rows)
        attn = functools.reduce(jnp.add, [part[at].astype(F32) for part in parts])
        attn_ref[...] = attn
        start = pl.multiple_of((chunk * count + where_ref[2]) * rows, rows)
        resid = x_ref[pl.ds(start, rows), :].astype(F32) + attn
        scale = lax.rsqrt(jnp.mean(resid * resid, axis=-1, keepdims=True) + 1e-06)
        out_ref[...] = (resid * scale * gain_ref[...]).astype(BF)


def norm_rows(where, x, parts, gain, chunks):
    rows, width = parts[0].shape[0] // chunks, parts[0].shape[1]
    vmem = pl.BlockSpec(memory_space=pltpu.VMEM)
    outs = pl.pallas_call(
        functools.partial(norm_kernel, len(parts)),
        in_specs=[pl.BlockSpec(memory_space=pltpu.SMEM)] + [vmem] * (2 + len(parts)),
        out_shape=[jax.ShapeDtypeStruct((rows, width), BF)] * chunks
        + [jax.ShapeDtypeStruct((rows, width), F32)] * chunks,
        compiler_params=params(12),
        name="moe_norm",
    )(where, x, gain.reshape(1, width), *parts)
    return list(outs[:chunks]), list(outs[chunks:])


def join_kernel(where_ref, *refs):
    parts, out_ref = refs[:-1], refs[-1]
    rows = parts[0].shape[0]
    for mask, ref in enumerate(parts):
        out_ref[pl.ds(pl.multiple_of((where_ref[2] ^ mask) * rows, rows), rows), :] = ref[...]


def join_rows(where, parts):
    rows, width = parts[0].shape
    vmem = pl.BlockSpec(memory_space=pltpu.VMEM)
    return pl.pallas_call(
        join_kernel,
        in_specs=[pl.BlockSpec(memory_space=pltpu.SMEM)] + [vmem] * len(parts),
        out_shape=jax.ShapeDtypeStruct((len(parts) * rows, width), BF),
        compiler_params=params(16),
        name="join_rows",
    )(where, *parts)


PAIR = 2


def expert_kernel(masks, chunk, experts, where_ref, near_routes, far_routes, gate_ref, up_ref, down_ref, *refs):
    row_refs, outs, (rows_ref, sems) = refs[: len(masks)], refs[len(masks) : -2], refs[-2:]
    _, tok, width = outs[0].shape
    steps = len(masks) // PAIR
    step = pl.program_id(0)
    slot = lax.rem(step, 2)

    def start(at):
        for part in range(PAIR):
            target = rows_ref.at[at % 2, pl.ds(part * tok, tok)]
            pltpu.make_async_copy(row_refs[PAIR * at + part], target, sems.at[at % 2]).start()

    @pl.when(step == 0)
    def _():
        start(0)

    for at in range(1, steps):

        @pl.when(step == at - 1)
        def _(at=at):
            start(at)

    here = lax.broadcasted_iota(jnp.int32, (3 * experts, LANES), 0)
    mine = (here == where_ref[1]) | (here == where_ref[1] + experts) | (here == where_ref[1] + 2 * experts)
    square = (LANES, LANES)
    diagonal = lax.broadcasted_iota(jnp.int32, square, 0) == lax.broadcasted_iota(jnp.int32, square, 1)
    weights = []
    for part in range(PAIR):
        index = jnp.int32(masks[part] // 2)
        for at in range(1, steps):
            index = jnp.where(step == at, masks[PAIR * at + part] // 2, index)
        routes_ref = far_routes if masks[part] & CORE else near_routes
        for block in range(tok // LANES):
            base = (chunk // LANES + block) * 3 * experts
            table = routes_ref[index, base : base + 3 * experts, :].astype(F32)
            row = jnp.sum(jnp.where(mine, table, 0.0), axis=0, keepdims=True)
            weights.append(jnp.sum(jnp.where(diagonal, jnp.broadcast_to(row, square), 0.0), axis=1, keepdims=True))

    pltpu.make_async_copy(rows_ref.at[slot], rows_ref.at[slot], sems.at[slot]).wait()
    tokens = rows_ref[slot]
    gate = mm(tokens, gate_ref[0])
    inner = (gate * jax.nn.sigmoid(gate) * mm(tokens, up_ref[0])).astype(BF)
    cols = pick_block(width, 512)
    for begin in range(0, width, cols):
        piece = mm(inner, down_ref[0, :, begin : begin + cols])
        for at, weight in enumerate(weights):
            part, row = divmod(at * LANES, tok)
            scaled = (piece[at * LANES : (at + 1) * LANES] * weight).astype(BF)
            if len(outs) > 1:
                outs[part][0, row : row + LANES, begin : begin + cols] = scaled
            else:
                outs[0][part, row : row + LANES, begin : begin + cols] = scaled


def stage_kernel(where_ref, *refs):
    out_ref = refs[-1]
    for at in range(where_ref.shape[0]):
        out_ref[at] = where_ref[at]


def stage(where, *weights):
    smem = pl.BlockSpec(memory_space=pltpu.SMEM)
    return pl.pallas_call(
        stage_kernel,
        in_specs=[smem] + [pl.BlockSpec(memory_space=pltpu.VMEM)] * len(weights),
        out_specs=smem,
        out_shape=jax.ShapeDtypeStruct(where.shape, where.dtype),
        compiler_params=params(2),
        name="stage_weights",
    )(where, *weights)


def expert_pieces(chunk, where, rows, groups, gate, up, down, routes):
    split = len(groups)
    masks = groups[0] if split == 1 else [mask for pair in zip(*groups) for mask in pair]
    blocks = [rows[mask] for mask in masks]
    tok, width = blocks[0].shape
    hidden = gate.shape[2]
    count, each, per = len(blocks), len(groups[0]), PAIR // split
    experts = EXP_CTX * 2 * routes[0].shape[0]
    route_rows = CHUNKS * tok // LANES * 3 * experts
    vmem = pl.BlockSpec(memory_space=pltpu.VMEM)
    table = pl.BlockSpec((routes[0].shape[0], route_rows, LANES), lambda i: (0, 0, 0))
    return pl.pallas_call(
        functools.partial(expert_kernel, tuple(masks), chunk, experts),
        grid=(count // PAIR,),
        in_specs=[pl.BlockSpec(memory_space=pltpu.SMEM), table, table]
        + [vmem] * 3
        + [pl.BlockSpec(memory_space=pl.ANY)] * count,
        out_specs=[pl.BlockSpec((per, tok, width), lambda i: (i, 0, 0))] * split,
        out_shape=[jax.ShapeDtypeStruct((each, tok, width), BF)] * split,
        scratch_shapes=[
            pltpu.VMEM((2, PAIR * tok, width), BF),
            pltpu.SemaphoreType.DMA((2,)),
        ],
        compiler_params=params(20),
        cost_estimate=pl.CostEstimate(
            flops=6 * count * tok * width * hidden,
            bytes_accessed=4 * count * tok * width,
            transcendentals=count * tok * hidden,
        ),
        name="expert_pieces",
    )(where, *routes, gate, up, down, *blocks)


CORE, ROW, COL = 1, 2, 4
PLANE = 8


def swap(value, mask):
    return lax.ppermute(value, "ctx", [(at, at ^ mask) for at in range(lax.axis_size("ctx"))])


def send_heads(parts):
    count = lax.axis_size("head")
    return [parts[0]] + [
        lax.ppermute(parts[mask], "head", [(at, at ^ mask) for at in range(count)]) for mask in range(1, count)
    ]


def spread_near(own):
    return jnp.stack([own] + [swap(own, mask) for mask in range(2, lax.axis_size("ctx"), 2)])


def double(near, mask):
    return jnp.concatenate([near, swap(near, mask)])


def plus(*terms):
    return functools.reduce(jnp.add, [term.astype(F32) for term in terms]).astype(BF)


def after(value, other):
    return lax.optimization_barrier((value, other))[0]


def depart(own):
    masks = (ROW, COL) if lax.axis_size("ctx") == PLANE else range(2, lax.axis_size("ctx"), 2)
    return {mask: swap(own, mask) for mask in masks}


def forward(came):
    if lax.axis_size("ctx") != PLANE:
        return []
    half = came[ROW].shape[0] // 2
    return [swap(came[ROW][:half], COL), swap(came[COL][half:], ROW)]


def first_sums(here, arrived):
    tok = here.shape[1]
    if lax.axis_size("ctx") != PLANE:
        return [(2 * at, plus(here[at], arrived[at]), [(0, 0, tok)]) for at in range(1, here.shape[0])]
    half, across = tok // 2, (ROW | COL) // 2
    sums = []
    for mask, start in ((ROW, 0), (COL, half)):
        part = slice(start, start + half)
        pieces = [plus(here[at, part], arrived[at, part]) for at in (across, mask // 2)]
        sums.append((mask, jnp.concatenate(pieces), [(half, start, half)]))
    return sums


def last_sums(here, arrived, came):
    if lax.axis_size("ctx") != PLANE:
        return []
    half = here.shape[1] // 2
    row, col = ROW // 2, COL // 2
    return [
        (COL, plus(here[col, :half], arrived[col, :half], came[0][:half]), [(0, 0, half)]),
        (ROW, plus(here[row, half:], arrived[row, half:], came[1][:half]), [(0, half, half)]),
    ]


def send_sums(sums):
    return [swap(rows, mask) for mask, rows, _ in sums]


def arrays(sums):
    return [rows for _, rows, _ in sums]


def terms_of(sums, received):
    return [(rows, places) for (_, _, places), rows in zip(sums, received) if places]


def sum_kernel(places, where_ref, attn_ref, near_ref, arrived_ref, *refs):
    parts = attn_ref.shape[1] // refs[-1].shape[1]
    others, outs, total_ref = refs[: -parts - 1], refs[-parts - 1 : -1], refs[-1]
    part, width = attn_ref.shape
    cols = width // parts
    own = pl.ds(pl.multiple_of(where_ref[2] * part, part), part)
    for mask, out_ref in enumerate(reversed(outs)):
        at = pl.ds(pl.multiple_of((where_ref[2] ^ mask) * cols, cols), cols)
        total = near_ref[0, :, at].astype(F32) + arrived_ref[0, :, at].astype(F32)
        total_ref[...] = total
        for spots, ref in zip(places, others):
            for source, target, count in spots:
                total_ref[target : target + count] += ref[source : source + count, at].astype(F32)
        total_ref[own, :] += attn_ref[:, at]
        out_ref[...] = total_ref[...].astype(BF)


def sum_terms(where, attn, near, arrived, terms, parts):
    others, places = [rows for rows, _ in terms], tuple(tuple(spots) for _, spots in terms)
    _, tok, width = near.shape
    part = attn.shape[0]
    cols = width // parts
    first = pl.BlockSpec((1, tok, width), lambda i: (0, 0, 0))
    return pl.pallas_call(
        functools.partial(sum_kernel, places),
        grid=(1,),
        in_specs=[
            pl.BlockSpec(memory_space=pltpu.SMEM),
            pl.BlockSpec((part, width), lambda i: (0, 0)),
            first,
            first,
        ]
        + [pl.BlockSpec(part.shape, lambda i: (0, 0)) for part in others],
        out_specs=[pl.BlockSpec((tok, cols), lambda i: (0, 0))] * parts,
        out_shape=[jax.ShapeDtypeStruct((tok, cols), BF)] * parts,
        scratch_shapes=[pltpu.VMEM((tok, cols), F32)],
        compiler_params=params(24),
        name="sum_terms",
    )(where, attn, near, arrived, *others)


def final_kernel(count, where_ref, x_ref, *refs):
    del where_ref
    out_ref = refs[-1]
    rows = refs[0].shape[0]
    for chunk in range((len(refs) - 1) // count):
        at = slice(chunk * rows, (chunk + 1) * rows)
        terms = [x_ref[at]] + [ref[...] for ref in refs[chunk * count : (chunk + 1) * count]]
        out_ref[at] = functools.reduce(jnp.add, [term.astype(F32) for term in terms]).astype(BF)


def final_sum(where, x, parts):
    rows, cols = parts[0][0].shape
    total = len(parts) * rows
    block = pl.BlockSpec((rows, cols), lambda i, where: (0, 0))
    return pl.pallas_call(
        functools.partial(final_kernel, len(parts[0])),
        grid_spec=pltpu.PrefetchScalarGridSpec(
            num_scalar_prefetch=1,
            grid=(1,),
            in_specs=[pl.BlockSpec((total, cols), lambda i, where: (0, where[2]))]
            + [block] * (len(parts) * len(parts[0])),
            out_specs=pl.BlockSpec((total, cols), lambda i, where: (0, 0)),
        ),
        out_shape=jax.ShapeDtypeStruct((total, cols), BF),
        compiler_params=params(12),
        name="layer_out",
    )(where, x, *[part for chunk in parts for part in chunk])


CHUNKS = 2


def body(
    hidden_in,
    gain_attn,
    w_qkv,
    conv_w,
    log_decay,
    norm_gain,
    w_out,
    gain_moe,
    expert_ids,
    route_weights,
    w_gate,
    w_up,
    w_down,
    grad_core,
):
    n_ctx, n_head = lax.axis_size("ctx"), lax.axis_size("head")
    my_ctx, my_head = lax.axis_index("ctx"), lax.axis_index("head")
    experts = EXP_CTX * n_ctx
    shards = n_head // EXP_CTX
    where = jnp.stack([my_ctx, EXP_CTX * my_ctx + my_head // shards, my_head]).astype(jnp.int32)
    steps = log_decay.T
    chunk_rows = hidden_in.shape[0] // CHUNKS

    mixed, rim = project(hidden_in, gain_attn, jnp.transpose(w_qkv, (1, 0, 2)))
    rim = lax.ppermute(rim, "ctx", [(at, at + 1) for at in range(n_ctx - 1)])
    qkv, fwd, bwd = local_states(
        mixed, rim, jnp.transpose(conv_w, (1, 0, 2)), steps, grad_core, expert_ids.T, route_weights.T, experts
    )
    fwd = spread_near(fwd)
    fwd = (fwd, swap(fwd, CORE))
    where = stage(after(where, qkv), w_out)
    parts = core_out(where, qkv, steps, *fwd, norm_gain, w_out, CHUNKS, n_head)
    where = stage(after(where, parts), w_gate, w_up, w_down)
    bwd = double(after(bwd, parts)[None], ROW)
    normed, attn = norm_rows(where, hidden_in, after(send_heads(parts[::-1]), bwd), gain_moe, CHUNKS)
    bwd = after(bwd, normed)
    while bwd.shape[0] < n_ctx // 2:
        bwd = double(bwd, 2 * bwd.shape[0])

    evens = list(range(0, n_ctx, 2))
    odds = [mask | CORE for mask in evens]
    own = join_rows(where, after(send_heads([normed[0]] * n_head), bwd))
    bwd = (bwd, swap(after(bwd, own), CORE))
    rows = []
    for chunk in range(CHUNKS):
        rows.append({0: own} | ({CORE: swap(own, CORE)} if chunk else {}) | depart(own))
        if chunk + 1 < CHUNKS:
            parts = send_heads([after(normed[chunk + 1], own)] * n_head)
            own = join_rows(where, parts)
            rows[chunk] = after(rows[chunk], own)

    pending, sums, first, arrived = [], [], None, None
    for chunk in range(CHUNKS):
        here_rows = rows[chunk]
        halves = forward(here_rows)
        lacking = [mask for mask in here_rows if mask | CORE not in here_rows]
        here_rows |= {mask | CORE: swap(here_rows[mask], CORE) for mask in lacking}
        if pending:
            arrived = after(arrived, [part for mask, part in here_rows.items() if mask & CORE])
            first = first_sums(pending[-1][0], arrived)
            pending[-1] += (arrived, first, send_sums(first))
            halves = after(halves, arrays(first))
        if halves:
            across = jnp.concatenate(halves)
            here_rows |= {ROW | COL: across, ROW | COL | CORE: swap(across, CORE)}
        if pending:
            here_rows = after(here_rows, arrays(first))
        experts_of = functools.partial(
            expert_pieces, chunk * chunk_rows, where, gate=w_gate, up=w_up, down=w_down, routes=fwd
        )
        here, far = experts_of(rows=here_rows, groups=[evens, odds])
        beside = (rows[chunk + 1], bwd) if chunk + 1 < CHUNKS else pending[-1][3]
        arrived = swap(after(far, beside), CORE)
        if chunk + 1 < CHUNKS:
            pending.append((here,))
        else:
            last = last_sums(*pending[-1][:2], pending[-1][3])
            received = send_sums(last)
            pending[-1] += (terms_of(first, pending[-1][3]) + terms_of(last, received),)
            arrived = after(arrived, received)
            first = first_sums(here, arrived)
            pending.append((here, arrived, first, send_sums(first)))

    for chunk in range(CHUNKS):
        here, arrived, first, received = pending[chunk][:4]
        if chunk + 1 < CHUNKS:
            terms = pending[chunk][4]
            held = after([rows for rows, _ in terms], arrays(pending[chunk + 1][2]))
            terms = list(zip(held, [places for _, places in terms]))
        else:
            last = last_sums(here, arrived, after(received, sums[-1][:-1]))
            terms = terms_of(first, received) + terms_of(last, send_sums(last))
        sums.append(send_heads(sum_terms(where, attn[chunk], here, arrived, terms, n_head)[::-1]))
    grads = core_grads(where, qkv, grad_core, steps, fwd, bwd)
    return (final_sum(where, hidden_in, [part[::-1] for part in sums]), *grads)


def solution(mesh):
    in_specs = (
        P("ctx", None),
        P(),
        P(None, None, "head"),
        P(None, None, "head"),
        P("ctx", "head"),
        P("head"),
        P("head", None),
        P(),
        P("ctx", None),
        P("ctx", None),
        P(("ctx", "head"), None, None),
        P(("ctx", "head"), None, None),
        P(("ctx", "head"), None, None),
        P("ctx", "head"),
    )
    out_specs = (P("ctx", "head"), P("ctx", "head"), P("ctx", "head"), P("ctx", "head"))
    return jax.shard_map(body, mesh=mesh, in_specs=in_specs, out_specs=out_specs, check_vma=False)
```

```python
import functools

import jax
import jax.numpy as jnp
from jax import lax
from jax.experimental import pallas as pl
from jax.experimental.pallas import tpu as pltpu
from jax.sharding import PartitionSpec as P

KERNEL = 4
EXP_CTX = 2
LANES = 128
RIM = 16
MIB = 1024 * 1024
HI = lax.Precision.HIGHEST
BF = jnp.bfloat16
F32 = jnp.float32
NT = (((1,), (1,)), ((), ()))
TN = (((0,), (0,)), ((), ()))
NN = (((1,), (0,)), ((), ()))


def params(mib):
    return pltpu.CompilerParams(vmem_limit_bytes=mib * MIB)


def mm(a, b, dims=NN):
    return lax.dot_general(a, b, dims, preferred_element_type=F32)


def pick_block(extent, target):
    return target if extent % target == 0 else extent


def qkv_kernel(x_hbm, gain_ref, w_hbm, mixed_ref, rim_ref, x_ref, w_ref, normed_ref, x_sem, sems):
    kinds, width, chans = w_ref.shape
    load = pltpu.make_async_copy(x_hbm, x_ref, x_sem)
    load.start()
    part = width // sems.shape[1]
    copies = []
    for kind in range(kinds):
        at = [pl.ds(piece * part, part) for piece in range(sems.shape[1])]
        copies.append(
            [
                pltpu.make_async_copy(w_hbm.at[kind, rows], w_ref.at[kind, rows], sems.at[kind, piece])
                for piece, rows in enumerate(at)
            ]
        )
        for copy in copies[kind]:
            copy.start()
    load.wait()
    values = x_ref[...].astype(F32)
    scale = lax.rsqrt(jnp.mean(values * values, axis=-1, keepdims=True) + 1e-06)
    normed_ref[...] = (values * scale * gain_ref[...]).astype(BF)
    for kind in range(kinds):
        for copy in copies[kind]:
            copy.wait()
        out = mm(normed_ref[...], w_ref[kind]).astype(BF)
        mixed_ref[kind] = out
        rim_ref[kind] = out[out.shape[0] - RIM :]


def project(x, gain, weights):
    rows, width = x.shape
    kinds, _, chans = weights.shape
    vmem = pl.BlockSpec(memory_space=pltpu.VMEM)
    hbm = pl.BlockSpec(memory_space=pltpu.HBM)
    return pl.pallas_call(
        qkv_kernel,
        in_specs=[hbm, vmem, hbm],
        out_specs=[vmem, vmem],
        out_shape=[
            jax.ShapeDtypeStruct((kinds, rows, chans), BF),
            jax.ShapeDtypeStruct((kinds, RIM, chans), BF),
        ],
        scratch_shapes=[
            pltpu.VMEM((rows, width), BF),
            pltpu.VMEM((kinds, width, chans), BF),
            pltpu.VMEM((rows, width), BF),
            pltpu.SemaphoreType.DMA,
            pltpu.SemaphoreType.DMA((kinds, 1)),
        ],
        compiler_params=params(60),
        name="qkv_projection",
    )(x, gain.reshape(1, width), weights)


def decay_sums(steps):
    rows = steps.shape[1]
    row_at = lax.broadcasted_iota(jnp.int32, (rows, rows), 0)
    col_at = lax.broadcasted_iota(jnp.int32, (rows, rows), 1)
    lower = row_at >= col_at
    tri = jnp.where(lower, 1.0, 0.0).astype(F32)
    along = lax.dot_general(steps, tri, NT, precision=HI, preferred_element_type=F32)
    down = lax.dot_general(tri, steps, NT, precision=HI, preferred_element_type=F32)
    return along, down, lower


def payload_tail(total, size):
    full = jnp.broadcast_to(total, (RIM, size))
    first = full.astype(BF).astype(F32)
    second = (full - first).astype(BF).astype(F32)
    third = full - first - second
    at = lax.broadcasted_iota(jnp.int32, (RIM, size), 0)
    return jnp.where(at == 0, first, jnp.where(at == 1, second, jnp.where(at == 2, third, 0.0)))


def route_rows(ids_ref, weights_ref, experts):
    top, tok = ids_ref.shape
    expert = lax.broadcasted_iota(jnp.int32, (experts, tok), 0)
    table = jnp.zeros((experts, tok), F32)
    for choice in range(top):
        table += jnp.where(expert == ids_ref[choice : choice + 1, :], weights_ref[choice : choice + 1, :], 0.0)
    first = table.astype(BF).astype(F32)
    second = (table - first).astype(BF).astype(F32)
    return jnp.concatenate([first, second, table - first - second], axis=0)


def conv_kernel(
    experts, mixed_ref, rim_ref, taps_ref, steps_ref, cot_ref, ids_ref, weights_ref, qkv_ref, fwd_ref, bwd_ref, pad_ref
):
    kinds, rows, chans = mixed_ref.shape
    heads = steps_ref.shape[0]
    size = chans // heads
    along, down, _ = decay_sums(steps_ref[...])
    for kind in range(kinds):
        pad_ref[:RIM] = rim_ref[kind].astype(F32)
        pad_ref[RIM:] = mixed_ref[kind].astype(F32)
        total = taps_ref[kind, 0:1, :] * pad_ref[RIM:]
        for offset in range(1, KERNEL):
            total += taps_ref[kind, offset : offset + 1, :] * pad_ref[RIM - offset : RIM - offset + rows]
        activ = total * jax.nn.sigmoid(total)
        if kind == 0:
            activ = activ * size ** (-0.5)
        qkv_ref[kind] = activ.astype(BF)
    routes = rows // LANES * 3 * experts
    table = route_rows(ids_ref, weights_ref, experts).astype(BF)
    for part in range(rows // LANES):
        fwd_ref[part * 3 * experts : (part + 1) * 3 * experts] = table[:, part * LANES : (part + 1) * LANES]
    for head in range(heads):
        at = slice(head * size, (head + 1) * size)
        base = head * (size + RIM)
        behind = routes + base
        last = along[head : head + 1, rows - 1 : rows]
        lead = jnp.exp(down[:, head : head + 1])
        tail = jnp.exp(last - down[:, head : head + 1])
        key_out = (qkv_ref[1, :, at].astype(F32) * tail).astype(BF)
        query_out = (qkv_ref[0, :, at].astype(F32) * lead).astype(BF)
        ends = payload_tail(last, size).astype(BF)
        fwd_ref[behind : behind + size] = mm(key_out, qkv_ref[2, :, at], TN).astype(BF)
        fwd_ref[behind + size : behind + size + RIM] = ends
        bwd_ref[base : base + size] = mm(query_out, cot_ref[:, at], TN).astype(BF)
        bwd_ref[base + size : base + size + RIM] = ends


def local_states(mixed, rim, taps, steps, cot, ids, weights, experts):
    kinds, rows, chans = mixed.shape
    heads = steps.shape[0]
    size = chans // heads
    states = heads * (size + RIM)
    return pl.pallas_call(
        functools.partial(conv_kernel, experts),
        out_specs=[pl.BlockSpec(memory_space=pltpu.VMEM)] * 3,
        out_shape=[
            jax.ShapeDtypeStruct((kinds, rows, chans), BF),
            jax.ShapeDtypeStruct((states + rows // LANES * 3 * experts, size), BF),
            jax.ShapeDtypeStruct((states, size), BF),
        ],
        scratch_shapes=[pltpu.VMEM((rows + RIM, chans), F32)],
        compiler_params=params(12),
        name="conv_states",
    )(mixed, rim, taps, steps, cot, ids, weights)


def arrange(me_ref, near_ref, far_ref, held_ref):
    for at in range(near_ref.shape[0]):
        held_ref[me_ref[0] ^ (2 * at)] = near_ref[at]
        held_ref[me_ref[0] ^ (2 * at + 1)] = far_ref[at]


def entering(held_ref, heads, head, size, first, last, step):
    base = held_ref.shape[1] - (heads - head) * (size + RIM)

    def hop(count, total):
        at = first + count * step
        ends = held_ref[at, base + size : base + size + RIM, :].astype(F32)
        factor = jnp.exp(ends[0:1] + ends[1:2] + ends[2:3])
        return factor * total + held_ref[at, base : base + size, :].astype(F32)

    return lax.fori_loop(0, (last - first) * step, hop, jnp.zeros((size, size), F32))


def core_kernel(chunks, me_ref, qkv_ref, steps_ref, gain_ref, near_ref, far_ref, w_ref, *refs):
    out_refs, (headed_ref, held_ref, whole_ref) = refs[:-3], refs[-3:]
    _, rows, chans = qkv_ref.shape
    heads = steps_ref.shape[0]
    size = chans // heads
    arrange(me_ref, near_ref, far_ref, held_ref)
    along, down, lower = decay_sums(steps_ref[...])
    for head in range(heads):
        at = slice(head * size, (head + 1) * size)
        state = entering(held_ref, heads, head, size, 0, me_ref[0], 1).astype(BF)
        diff = down[:, head : head + 1] - along[head : head + 1, :]
        mask = jnp.exp(jnp.where(lower, diff, -jnp.inf))
        query = qkv_ref[0, :, at]
        scores = (mm(query, qkv_ref[1, :, at], NT) * mask).astype(BF)
        attended = mm(scores, qkv_ref[2, :, at])
        attended += mm(query, state) * jnp.exp(down[:, head : head + 1])
        scale = lax.rsqrt(jnp.mean(attended * attended, axis=-1, keepdims=True) + 1e-06)
        headed_ref[:, at] = (attended * scale * gain_ref[:, at]).astype(BF)
    whole_ref[...] = mm(headed_ref[...], w_ref[...]).astype(BF)
    part = rows // len(out_refs) // chunks
    for mask, ref in enumerate(out_refs):
        for chunk in range(chunks):
            start = chunk * len(out_refs) * part + (me_ref[2] ^ mask) * part
            ref[chunk * part : (chunk + 1) * part] = whole_ref[pl.ds(pl.multiple_of(start, part), part), :]


def core_out(where, qkv, steps, near, far, gain, w_out, chunks, parts):
    _, rows, chans = qkv.shape
    width = w_out.shape[1]
    vmem = pl.BlockSpec(memory_space=pltpu.VMEM)
    return pl.pallas_call(
        functools.partial(core_kernel, chunks),
        in_specs=[pl.BlockSpec(memory_space=pltpu.SMEM)] + [vmem] * 6,
        out_shape=[jax.ShapeDtypeStruct((rows // parts, width), BF)] * parts,
        scratch_shapes=[
            pltpu.VMEM((rows, chans), BF),
            pltpu.VMEM((2 * near.shape[0], *near.shape[1:]), BF),
            pltpu.VMEM((rows, width), BF),
        ],
        compiler_params=params(16),
        name="core_out",
    )(where, qkv, steps, gain.reshape(1, chans), near, far, w_out)


def grad_kernel(
    me_ref, qkv_ref, cot_ref, steps_ref, fwd_near, fwd_far, bwd_near, bwd_far, gq_ref, gk_ref, gv_ref, fwd_ref, bwd_ref
):
    _, rows, chans = qkv_ref.shape
    heads = steps_ref.shape[0]
    size = chans // heads
    count = fwd_ref.shape[0]
    arrange(me_ref, fwd_near, fwd_far, fwd_ref)
    arrange(me_ref, bwd_near, bwd_far, bwd_ref)
    along, down, lower = decay_sums(steps_ref[...])
    for head in range(heads):
        at = slice(head * size, (head + 1) * size)
        state = entering(fwd_ref, heads, head, size, 0, me_ref[0], 1).astype(BF)
        after = entering(bwd_ref, heads, head, size, count - 1, me_ref[0], -1).astype(BF)
        here = down[:, head : head + 1]
        lead = jnp.exp(here)
        tail = jnp.exp(along[head : head + 1, rows - 1 : rows] - here)
        mask = jnp.exp(jnp.where(lower, here - along[head : head + 1, :], -jnp.inf))
        query, key, val = qkv_ref[0, :, at], qkv_ref[1, :, at], qkv_ref[2, :, at]
        cot = cot_ref[:, at]
        scores = (mm(query, key, NT) * mask).astype(BF)
        dov = (mm(cot, val, NT) * mask).astype(BF)
        gq_ref[:, at] = (mm(dov, key) + lead * mm(cot, state, NT)).astype(BF)
        gk_ref[:, at] = (mm(dov, query, TN) + tail * mm(val, after, NT)).astype(BF)
        gv_ref[:, at] = (mm(scores, cot, TN) + tail * mm(key, after)).astype(BF)


def core_grads(where, qkv, cot, steps, fwd, bwd):
    _, rows, chans = qkv.shape
    count = 2 * fwd[0].shape[0]
    vmem = pl.BlockSpec(memory_space=pltpu.VMEM)
    return pl.pallas_call(
        grad_kernel,
        in_specs=[pl.BlockSpec(memory_space=pltpu.SMEM)] + [vmem] * 7,
        out_shape=[jax.ShapeDtypeStruct((rows, chans), BF)] * 3,
        scratch_shapes=[pltpu.VMEM((count, *fwd[0].shape[1:]), BF), pltpu.VMEM((count, *bwd[0].shape[1:]), BF)],
        compiler_params=params(24),
        name="core_grads",
    )(where, qkv, cot, steps, *fwd, *bwd)


def norm_kernel(count, where_ref, x_ref, gain_ref, *refs):
    chunks = (len(refs) - count) // 2
    parts, outs, attns = refs[:count], refs[count : count + chunks], refs[count + chunks :]
    rows = outs[0].shape[0]
    for chunk, (out_ref, attn_ref) in enumerate(zip(outs, attns)):
        at = slice(chunk * rows, (chunk + 1) * rows)
        attn = functools.reduce(jnp.add, [part[at].astype(F32) for part in parts])
        attn_ref[...] = attn
        start = pl.multiple_of((chunk * count + where_ref[2]) * rows, rows)
        resid = x_ref[pl.ds(start, rows), :].astype(F32) + attn
        scale = lax.rsqrt(jnp.mean(resid * resid, axis=-1, keepdims=True) + 1e-06)
        out_ref[...] = (resid * scale * gain_ref[...]).astype(BF)


def norm_rows(where, x, parts, gain, chunks):
    rows, width = parts[0].shape[0] // chunks, parts[0].shape[1]
    vmem = pl.BlockSpec(memory_space=pltpu.VMEM)
    outs = pl.pallas_call(
        functools.partial(norm_kernel, len(parts)),
        in_specs=[pl.BlockSpec(memory_space=pltpu.SMEM)] + [vmem] * (2 + len(parts)),
        out_shape=[jax.ShapeDtypeStruct((rows, width), BF)] * chunks
        + [jax.ShapeDtypeStruct((rows, width), F32)] * chunks,
        compiler_params=params(12),
        name="moe_norm",
    )(where, x, gain.reshape(1, width), *parts)
    return list(outs[:chunks]), list(outs[chunks:])


def join_kernel(where_ref, *refs):
    parts, out_ref = refs[:-1], refs[-1]
    rows = parts[0].shape[0]
    for mask, ref in enumerate(parts):
        out_ref[pl.ds(pl.multiple_of((where_ref[2] ^ mask) * rows, rows), rows), :] = ref[...]


def join_rows(where, parts):
    rows, width = parts[0].shape
    vmem = pl.BlockSpec(memory_space=pltpu.VMEM)
    return pl.pallas_call(
        join_kernel,
        in_specs=[pl.BlockSpec(memory_space=pltpu.SMEM)] + [vmem] * len(parts),
        out_shape=jax.ShapeDtypeStruct((len(parts) * rows, width), BF),
        compiler_params=params(16),
        name="join_rows",
    )(where, *parts)


PAIR = 2


def expert_kernel(masks, chunk, experts, where_ref, near_routes, far_routes, gate_ref, up_ref, down_ref, *refs):
    row_refs, outs, (rows_ref, sems) = refs[: len(masks)], refs[len(masks) : -2], refs[-2:]
    _, tok, width = outs[0].shape
    steps = len(masks) // PAIR
    step = pl.program_id(0)
    slot = lax.rem(step, 2)

    def start(at):
        for part in range(PAIR):
            target = rows_ref.at[at % 2, pl.ds(part * tok, tok)]
            pltpu.make_async_copy(row_refs[PAIR * at + part], target, sems.at[at % 2]).start()

    @pl.when(step == 0)
    def _():
        start(0)

    for at in range(1, steps):

        @pl.when(step == at - 1)
        def _(at=at):
            start(at)

    here = lax.broadcasted_iota(jnp.int32, (3 * experts, LANES), 0)
    mine = (here == where_ref[1]) | (here == where_ref[1] + experts) | (here == where_ref[1] + 2 * experts)
    square = (LANES, LANES)
    diagonal = lax.broadcasted_iota(jnp.int32, square, 0) == lax.broadcasted_iota(jnp.int32, square, 1)
    weights = []
    for part in range(PAIR):
        index = jnp.int32(masks[part] // 2)
        for at in range(1, steps):
            index = jnp.where(step == at, masks[PAIR * at + part] // 2, index)
        routes_ref = far_routes if masks[part] & CORE else near_routes
        for block in range(tok // LANES):
            base = (chunk // LANES + block) * 3 * experts
            table = routes_ref[index, base : base + 3 * experts, :].astype(F32)
            row = jnp.sum(jnp.where(mine, table, 0.0), axis=0, keepdims=True)
            weights.append(jnp.sum(jnp.where(diagonal, jnp.broadcast_to(row, square), 0.0), axis=1, keepdims=True))

    pltpu.make_async_copy(rows_ref.at[slot], rows_ref.at[slot], sems.at[slot]).wait()
    tokens = rows_ref[slot]
    gate = mm(tokens, gate_ref[0])
    inner = (gate * jax.nn.sigmoid(gate) * mm(tokens, up_ref[0])).astype(BF)
    cols = pick_block(width, 512)
    for begin in range(0, width, cols):
        piece = mm(inner, down_ref[0, :, begin : begin + cols])
        for at, weight in enumerate(weights):
            part, row = divmod(at * LANES, tok)
            scaled = (piece[at * LANES : (at + 1) * LANES] * weight).astype(BF)
            if len(outs) > 1:
                outs[part][0, row : row + LANES, begin : begin + cols] = scaled
            else:
                outs[0][part, row : row + LANES, begin : begin + cols] = scaled


def stage_kernel(where_ref, *refs):
    out_ref = refs[-1]
    for at in range(where_ref.shape[0]):
        out_ref[at] = where_ref[at]


def stage(where, *weights):
    smem = pl.BlockSpec(memory_space=pltpu.SMEM)
    return pl.pallas_call(
        stage_kernel,
        in_specs=[smem] + [pl.BlockSpec(memory_space=pltpu.VMEM)] * len(weights),
        out_specs=smem,
        out_shape=jax.ShapeDtypeStruct(where.shape, where.dtype),
        compiler_params=params(2),
        name="stage_weights",
    )(where, *weights)


def expert_pieces(chunk, where, rows, groups, gate, up, down, routes):
    split = len(groups)
    masks = groups[0] if split == 1 else [mask for pair in zip(*groups) for mask in pair]
    blocks = [rows[mask] for mask in masks]
    tok, width = blocks[0].shape
    hidden = gate.shape[2]
    count, each, per = len(blocks), len(groups[0]), PAIR // split
    experts = EXP_CTX * 2 * routes[0].shape[0]
    route_rows = CHUNKS * tok // LANES * 3 * experts
    vmem = pl.BlockSpec(memory_space=pltpu.VMEM)
    table = pl.BlockSpec((routes[0].shape[0], route_rows, LANES), lambda i: (0, 0, 0))
    return pl.pallas_call(
        functools.partial(expert_kernel, tuple(masks), chunk, experts),
        grid=(count // PAIR,),
        in_specs=[pl.BlockSpec(memory_space=pltpu.SMEM), table, table]
        + [vmem] * 3
        + [pl.BlockSpec(memory_space=pl.ANY)] * count,
        out_specs=[pl.BlockSpec((per, tok, width), lambda i: (i, 0, 0))] * split,
        out_shape=[jax.ShapeDtypeStruct((each, tok, width), BF)] * split,
        scratch_shapes=[
            pltpu.VMEM((2, PAIR * tok, width), BF),
            pltpu.SemaphoreType.DMA((2,)),
        ],
        compiler_params=params(20),
        cost_estimate=pl.CostEstimate(
            flops=6 * count * tok * width * hidden,
            bytes_accessed=4 * count * tok * width,
            transcendentals=count * tok * hidden,
        ),
        name="expert_pieces",
    )(where, *routes, gate, up, down, *blocks)


CORE, ROW, COL = 1, 2, 4
PLANE = 8


def swap(value, mask):
    return lax.ppermute(value, "ctx", [(at, at ^ mask) for at in range(lax.axis_size("ctx"))])


def send_heads(parts):
    count = lax.axis_size("head")
    return [parts[0]] + [
        lax.ppermute(parts[mask], "head", [(at, at ^ mask) for at in range(count)]) for mask in range(1, count)
    ]


def spread_near(own):
    return jnp.stack([own] + [swap(own, mask) for mask in range(2, lax.axis_size("ctx"), 2)])


def double(near, mask):
    return jnp.concatenate([near, swap(near, mask)])


def plus(*terms):
    return functools.reduce(jnp.add, [term.astype(F32) for term in terms]).astype(BF)


def after(value, other):
    return lax.optimization_barrier((value, other))[0]


def depart(own):
    masks = (ROW, COL) if lax.axis_size("ctx") == PLANE else range(2, lax.axis_size("ctx"), 2)
    return {mask: swap(own, mask) for mask in masks}


def forward(came):
    if lax.axis_size("ctx") != PLANE:
        return []
    half = came[ROW].shape[0] // 2
    return [swap(came[ROW][:half], COL), swap(came[COL][half:], ROW)]


def first_sums(here, arrived):
    tok = here.shape[1]
    if lax.axis_size("ctx") != PLANE:
        return [(2 * at, plus(here[at], arrived[at]), [(0, 0, tok)]) for at in range(1, here.shape[0])]
    half, across = tok // 2, (ROW | COL) // 2
    sums = []
    for mask, start in ((ROW, 0), (COL, half)):
        part = slice(start, start + half)
        pieces = [plus(here[at, part], arrived[at, part]) for at in (across, mask // 2)]
        sums.append((mask, jnp.concatenate(pieces), [(half, start, half)]))
    return sums


def last_sums(here, arrived, came):
    if lax.axis_size("ctx") != PLANE:
        return []
    half = here.shape[1] // 2
    row, col = ROW // 2, COL // 2
    return [
        (COL, plus(here[col, :half], arrived[col, :half], came[0][:half]), [(0, 0, half)]),
        (ROW, plus(here[row, half:], arrived[row, half:], came[1][:half]), [(0, half, half)]),
    ]


def send_sums(sums):
    return [swap(rows, mask) for mask, rows, _ in sums]


def arrays(sums):
    return [rows for _, rows, _ in sums]


def terms_of(sums, received):
    return [(rows, places) for (_, _, places), rows in zip(sums, received) if places]


def sum_kernel(places, where_ref, attn_ref, near_ref, arrived_ref, *refs):
    parts = attn_ref.shape[1] // refs[-1].shape[1]
    others, outs, total_ref = refs[: -parts - 1], refs[-parts - 1 : -1], refs[-1]
    part, width = attn_ref.shape
    cols = width // parts
    own = pl.ds(pl.multiple_of(where_ref[2] * part, part), part)
    for mask, out_ref in enumerate(outs):
        at = pl.ds(pl.multiple_of((where_ref[2] ^ mask) * cols, cols), cols)
        total = near_ref[0, :, at].astype(F32) + arrived_ref[0, :, at].astype(F32)
        total_ref[...] = total
        for spots, ref in zip(places, others):
            for source, target, count in spots:
                total_ref[target : target + count] += ref[source : source + count, at].astype(F32)
        total_ref[own, :] += attn_ref[:, at]
        out_ref[...] = total_ref[...].astype(BF)


def sum_terms(where, attn, near, arrived, terms, parts):
    others, places = [rows for rows, _ in terms], tuple(tuple(spots) for _, spots in terms)
    _, tok, width = near.shape
    part = attn.shape[0]
    cols = width // parts
    first = pl.BlockSpec((1, tok, width), lambda i: (0, 0, 0))
    return pl.pallas_call(
        functools.partial(sum_kernel, places),
        grid=(1,),
        in_specs=[
            pl.BlockSpec(memory_space=pltpu.SMEM),
            pl.BlockSpec((part, width), lambda i: (0, 0)),
            first,
            first,
        ]
        + [pl.BlockSpec(part.shape, lambda i: (0, 0)) for part in others],
        out_specs=[pl.BlockSpec((tok, cols), lambda i: (0, 0))] * parts,
        out_shape=[jax.ShapeDtypeStruct((tok, cols), BF)] * parts,
        scratch_shapes=[pltpu.VMEM((tok, cols), F32)],
        compiler_params=params(24),
        name="sum_terms",
    )(where, attn, near, arrived, *others)


def final_kernel(count, where_ref, x_ref, *refs):
    del where_ref
    out_ref = refs[-1]
    rows = refs[0].shape[0]
    for chunk in range((len(refs) - 1) // count):
        at = slice(chunk * rows, (chunk + 1) * rows)
        terms = [x_ref[at]] + [ref[...] for ref in refs[chunk * count : (chunk + 1) * count]]
        out_ref[at] = functools.reduce(jnp.add, [term.astype(F32) for term in terms]).astype(BF)


def final_sum(where, x, parts):
    rows, cols = parts[0][0].shape
    total = len(parts) * rows
    block = pl.BlockSpec((rows, cols), lambda i, where: (0, 0))
    return pl.pallas_call(
        functools.partial(final_kernel, len(parts[0])),
        grid_spec=pltpu.PrefetchScalarGridSpec(
            num_scalar_prefetch=1,
            grid=(1,),
            in_specs=[pl.BlockSpec((total, cols), lambda i, where: (0, where[2]))]
            + [block] * (len(parts) * len(parts[0])),
            out_specs=pl.BlockSpec((total, cols), lambda i, where: (0, 0)),
        ),
        out_shape=jax.ShapeDtypeStruct((total, cols), BF),
        compiler_params=params(12),
        name="layer_out",
    )(where, x, *[part for chunk in parts for part in chunk])


CHUNKS = 2


def body(
    hidden_in,
    gain_attn,
    w_qkv,
    conv_w,
    log_decay,
    norm_gain,
    w_out,
    gain_moe,
    expert_ids,
    route_weights,
    w_gate,
    w_up,
    w_down,
    grad_core,
):
    n_ctx, n_head = lax.axis_size("ctx"), lax.axis_size("head")
    my_ctx, my_head = lax.axis_index("ctx"), lax.axis_index("head")
    experts = EXP_CTX * n_ctx
    shards = n_head // EXP_CTX
    where = jnp.stack([my_ctx, EXP_CTX * my_ctx + my_head // shards, my_head]).astype(jnp.int32)
    steps = log_decay.T
    chunk_rows = hidden_in.shape[0] // CHUNKS

    mixed, rim = project(hidden_in, gain_attn, jnp.transpose(w_qkv, (1, 0, 2)))
    rim = lax.ppermute(rim, "ctx", [(at, at + 1) for at in range(n_ctx - 1)])
    qkv, fwd, bwd = local_states(
        mixed, rim, jnp.transpose(conv_w, (1, 0, 2)), steps, grad_core, expert_ids.T, route_weights.T, experts
    )
    fwd = spread_near(fwd)
    fwd = (fwd, swap(fwd, CORE))
    where = stage(after(where, qkv), w_out)
    parts = core_out(where, qkv, steps, *fwd, norm_gain, w_out, CHUNKS, n_head)
    where = stage(after(where, parts), w_gate, w_up, w_down)
    bwd = double(after(bwd, parts)[None], ROW)
    normed, attn = norm_rows(where, hidden_in, after(send_heads(parts), bwd), gain_moe, CHUNKS)
    bwd = after(bwd, normed)
    while bwd.shape[0] < n_ctx // 2:
        bwd = double(bwd, 2 * bwd.shape[0])

    evens = list(range(0, n_ctx, 2))
    odds = [mask | CORE for mask in evens]
    own = join_rows(where, after(send_heads([normed[0]] * n_head), bwd))
    bwd = (bwd, swap(after(bwd, own), CORE))
    rows = []
    for chunk in range(CHUNKS):
        rows.append({0: own} | ({CORE: swap(own, CORE)} if chunk else {}) | depart(own))
        if chunk + 1 < CHUNKS:
            parts = send_heads([after(normed[chunk + 1], own)] * n_head)
            own = join_rows(where, parts)
            rows[chunk] = after(rows[chunk], own)

    pending, sums, first, arrived = [], [], None, None
    for chunk in range(CHUNKS):
        here_rows = rows[chunk]
        halves = forward(here_rows)
        lacking = [mask for mask in here_rows if mask | CORE not in here_rows]
        here_rows |= {mask | CORE: swap(here_rows[mask], CORE) for mask in lacking}
        if pending:
            arrived = after(arrived, [part for mask, part in here_rows.items() if mask & CORE])
            first = first_sums(pending[-1][0], arrived)
            pending[-1] += (arrived, first, send_sums(first))
            halves = after(halves, arrays(first))
        if halves:
            across = jnp.concatenate(halves)
            here_rows |= {ROW | COL: across, ROW | COL | CORE: swap(across, CORE)}
        if pending:
            here_rows = after(here_rows, arrays(first))
        experts_of = functools.partial(
            expert_pieces, chunk * chunk_rows, where, gate=w_gate, up=w_up, down=w_down, routes=fwd
        )
        here, far = experts_of(rows=here_rows, groups=[evens, odds])
        beside = (rows[chunk + 1], bwd) if chunk + 1 < CHUNKS else pending[-1][3]
        arrived = swap(after(far, beside), CORE)
        if chunk + 1 < CHUNKS:
            pending.append((here,))
        else:
            last = last_sums(*pending[-1][:2], pending[-1][3])
            received = send_sums(last)
            pending[-1] += (terms_of(first, pending[-1][3]) + terms_of(last, received),)
            arrived = after(arrived, received)
            first = first_sums(here, arrived)
            pending.append((here, arrived, first, send_sums(first)))

    for chunk in range(CHUNKS):
        here, arrived, first, received = pending[chunk][:4]
        if chunk + 1 < CHUNKS:
            terms = pending[chunk][4]
            held = after([rows for rows, _ in terms], arrays(pending[chunk + 1][2]))
            terms = list(zip(held, [places for _, places in terms]))
        else:
            last = last_sums(here, arrived, after(received, sums[-1][:-1]))
            terms = terms_of(first, received) + terms_of(last, send_sums(last))
        sums.append(send_heads(sum_terms(where, attn[chunk], here, arrived, terms, n_head)))
    grads = core_grads(where, qkv, grad_core, steps, fwd, bwd)
    return (final_sum(where, hidden_in, sums), *grads)


def solution(mesh):
    in_specs = (
        P("ctx", None),
        P(),
        P(None, None, "head"),
        P(None, None, "head"),
        P("ctx", "head"),
        P("head"),
        P("head", None),
        P(),
        P("ctx", None),
        P("ctx", None),
        P(("ctx", "head"), None, None),
        P(("ctx", "head"), None, None),
        P(("ctx", "head"), None, None),
        P("ctx", "head"),
    )
    out_specs = (P("ctx", "head"), P("ctx", "head"), P("ctx", "head"), P("ctx", "head"))
    return jax.shard_map(body, mesh=mesh, in_specs=in_specs, out_specs=out_specs, check_vma=False)
```
